32 devices in a mesh: dp: 8 (over z, y), fsdp: 4 (over x, core).
Axes of the slice: x: 2, y: 2, z: 4, core: 2. Of those that a mesh axis runs over, the one named last changes fastest.
Arguments:
- hidden: bfloat16 [2, 32, 256, 768], P(None, ('dp', 'fsdp')), may hold values from -6 to 6, as said below
- memory: bfloat16 [2, 32, 256, 768], P(None, ('dp', 'fsdp')), may hold values from -6 to 6, as said below
- cotangent: bfloat16 [2, 32, 256, 768], P(None, ('dp', 'fsdp')), may hold values from -6 to 6, as said below
- target_lengths: int32 [2, 32], P(None, ('dp', 'fsdp')), may hold values from 64 to 256, as said below
- memory_lengths: int32 [2, 32], P(None, ('dp', 'fsdp')), may hold values from 64 to 256, as said below
- qk_master: float32 [4, 768, 768], P(None, ('dp', 'fsdp')), may hold values from -0.21875 to 0.21875
- value_master: float32 [2, 768, 768], P(None, ('dp', 'fsdp')), may hold values from -0.21875 to 0.21875
- output_master: float32 [2, 768, 768], P(None, ('dp', 'fsdp')), may hold values from -1.25 to 1.25
- inner_master: float32 [768, 3072], P(('dp', 'fsdp')), may hold values from -0.21875 to 0.21875
- outer_master: float32 [3072, 768], P(('dp', 'fsdp')), may hold values from -0.109375 to 0.109375
- gain_master: float32 [3, 768], P(None, ('dp', 'fsdp')), may hold values from 0.5 to 1.5
- table_master: float32 [32, 12], replicated, may hold values from -6 to 6
- qk_first: float32 [4, 768, 768], P(None, ('dp', 'fsdp')), may hold values from -40 to 40
- value_first: float32 [2, 768, 768], P(None, ('dp', 'fsdp')), may hold values from -160 to 160
- output_first: float32 [2, 768, 768], P(None, ('dp', 'fsdp')), may hold values from -12 to 12
- inner_first: float32 [768, 3072], P(('dp', 'fsdp')), may hold values from -12 to 12
- outer_first: float32 [3072, 768], P(('dp', 'fsdp')), may hold values from -32 to 32
- gain_first: float32 [3, 768], P(None, ('dp', 'fsdp')), may hold values from -80 to 80
- table_first: float32 [32, 12], replicated, may hold values from -64 to 64
- qk_second: float32 [4, 768, 768], P(None, ('dp', 'fsdp')), may hold values from 2.048 to 32.768
- value_second: float32 [2, 768, 768], P(None, ('dp', 'fsdp')), may hold values from 32.768 to 524.288
- output_second: float32 [2, 768, 768], P(None, ('dp', 'fsdp')), may hold values from 0.18432 to 2.94912
- inner_second: float32 [768, 3072], P(('dp', 'fsdp')), may hold values from 0.18432 to 2.94912
- outer_second: float32 [3072, 768], P(('dp', 'fsdp')), may hold values from 1.31072 to 20.97152
- gain_second: float32 [3, 768], P(None, ('dp', 'fsdp')), may hold values from 8.192 to 131.072
- table_second: float32 [32, 12], replicated, may hold values from 5.89824 to 94.37184
Outputs:
- layer_out: bfloat16 [2, 32, 256, 768], P(None, ('dp', 'fsdp'))
- hidden_grad: float32 [2, 32, 256, 768], P(None, ('dp', 'fsdp'))
- memory_grad: float32 [2, 32, 256, 768], P(None, ('dp', 'fsdp'))
- qk_new: float32 [4, 768, 768], P(None, ('dp', 'fsdp'))
- value_new: float32 [2, 768, 768], P(None, ('dp', 'fsdp'))
- output_new: float32 [2, 768, 768], P(None, ('dp', 'fsdp'))
- inner_new: float32 [768, 3072], P(('dp', 'fsdp'))
- outer_new: float32 [3072, 768], P(('dp', 'fsdp'))
- gain_new: float32 [3, 768], P(None, ('dp', 'fsdp'))
- table_new: float32 [32, 12], replicated
- qk_first_new: float32 [4, 768, 768], P(None, ('dp', 'fsdp'))
- value_first_new: float32 [2, 768, 768], P(None, ('dp', 'fsdp'))
- output_first_new: float32 [2, 768, 768], P(None, ('dp', 'fsdp'))
- inner_first_new: float32 [768, 3072], P(('dp', 'fsdp'))
- outer_first_new: float32 [3072, 768], P(('dp', 'fsdp'))
- gain_first_new: float32 [3, 768], P(None, ('dp', 'fsdp'))
- table_first_new: float32 [32, 12], replicated
- qk_second_new: float32 [4, 768, 768], P(None, ('dp', 'fsdp'))
- value_second_new: float32 [2, 768, 768], P(None, ('dp', 'fsdp'))
- output_second_new: float32 [2, 768, 768], P(None, ('dp', 'fsdp'))
- inner_second_new: float32 [768, 3072], P(('dp', 'fsdp'))
- outer_second_new: float32 [3072, 768], P(('dp', 'fsdp'))
- gain_second_new: float32 [3, 768], P(None, ('dp', 'fsdp'))
- table_second_new: float32 [32, 12], replicated
- qk_copy: bfloat16 [4, 768, 768], P(None, ('dp', 'fsdp'))
- value_copy: bfloat16 [2, 768, 768], P(None, ('dp', 'fsdp'))
- output_copy: bfloat16 [2, 768, 768], P(None, ('dp', 'fsdp'))
- inner_copy: bfloat16 [768, 3072], P(('dp', 'fsdp'))
- outer_copy: bfloat16 [3072, 768], P(('dp', 'fsdp'))
- gain_copy: bfloat16 [3, 768], P(None, ('dp', 'fsdp'))
- table_copy: bfloat16 [32, 12], replicated
The draws below stay inside these ranges and needn't reach their ends.
Inputs may be any that keep to these rules, and one draw needn't show every extreme that they name: `target_lengths`: each is at least 64, and some sequence has exactly 256. `memory_lengths`: each is at least 64, and some sequence has exactly 256. `hidden`: independent entries of mean 0 and deviation 1. `memory`: independent entries of mean 0 and deviation 1. `cotangent`: independent entries of mean 0 and deviation 1.
All inputs are finite; a program needn't handle non-finite values.
Results may differ from the reference program's by a relative error of at most 0.015.
The reference program's roundings to bfloat16 on the way count: a program that leaves them out, or rounds other values in their place, can miss the bound.
Values may be sent and summed in bfloat16 or wider, within the bound.
A program may use at most 256 MiB of HBM per device.

```python
import math
import jax
import jax.numpy as jnp
from jax import lax

D = 768
FF = 3072
HEADS = 12
HEAD_DIM = 64
BUCKETS = 32
MAX_DIST = 128
LEN = 256
MEM = 256
MICRO = 2
STEP = 10
BATCH = 32


def ragged_lengths(key, longest):
    pick_key, value_key = jax.random.split(key)
    values = jax.random.randint(value_key, (MICRO, BATCH), longest // 4, longest + 1)
    chosen = jax.random.randint(pick_key, (), 0, MICRO * BATCH)
    flat_index = jnp.arange(MICRO * BATCH, dtype=jnp.int32).reshape(MICRO, BATCH)
    return jnp.where(flat_index == chosen, longest, values).astype(jnp.int32)


def draw_target_lengths(key, part):
    key = jax.random.fold_in(key, 11)
    return ragged_lengths(key, LEN)


def draw_memory_lengths(key, part):
    key = jax.random.fold_in(key, 23)
    return ragged_lengths(key, MEM)


def normal_field(key, shape):
    return jnp.clip(jax.random.normal(key, shape, jnp.float32), -6.0, 6.0)


def draw_hidden(key, part):
    key = jax.random.fold_in(key, 31)
    values = normal_field(key, (MICRO, BATCH, LEN, D))
    return values.astype(jnp.bfloat16)


def draw_memory(key, part):
    key = jax.random.fold_in(key, 37)
    values = normal_field(key, (MICRO, BATCH, MEM, D))
    return values.astype(jnp.bfloat16)


def draw_cotangent(key, part):
    key = jax.random.fold_in(key, 41)
    values = normal_field(key, (MICRO, BATCH, LEN, D))
    return values.astype(jnp.bfloat16)


def shard_levels(stream_key, dims, cuts, low, top_value):
    gain = 1.0
    for position, parts in cuts:
        draws = jax.random.uniform(jax.random.fold_in(jax.random.fold_in(stream_key, 6), position), (parts,), jnp.float32, low / len(cuts), top_value / len(cuts))
        gain = gain * jnp.repeat(jnp.exp(draws), dims[position] // parts).reshape((-1,) + (1,) * (len(dims) - 1 - position))
    return gain


def gaussian(stream_key, dims, width, bound, cuts=(), kind=jnp.bfloat16):
    result = width * jax.random.normal(stream_key, dims, jnp.float32)
    if cuts:
        result = result * shard_levels(stream_key, dims, cuts, -0.22, 0.18)
    return jnp.clip(result, -bound, bound).astype(kind)


def setup_inputs(seed: int = 0) -> dict:
    arg_keys = jax.random.split(jax.random.key(seed), 27)
    return {
        "hidden": draw_hidden(jax.random.fold_in(arg_keys[26], 71), 0),
        "memory": draw_memory(jax.random.fold_in(arg_keys[26], 71), 0),
        "cotangent": draw_cotangent(jax.random.fold_in(arg_keys[26], 71), 0),
        "target_lengths": draw_target_lengths(jax.random.fold_in(arg_keys[26], 71), 0),
        "memory_lengths": draw_memory_lengths(jax.random.fold_in(arg_keys[26], 71), 0),
        "qk_master": gaussian(arg_keys[5], (4, D, D), D ** -0.5, 0.21875, ((1, 32),), jnp.float32),
        "value_master": gaussian(arg_keys[6], (2, D, D), D ** -0.5, 0.21875, ((1, 32),), jnp.float32),
        "output_master": gaussian(arg_keys[7], (2, D, D), (D // 32) ** -0.5, 1.25, ((1, 32),), jnp.float32),
        "inner_master": gaussian(arg_keys[8], (D, FF), D ** -0.5, 0.21875, ((0, 32),), jnp.float32),
        "outer_master": gaussian(arg_keys[9], (FF, D), FF ** -0.5, 0.109375, ((0, 32),), jnp.float32),
        "gain_master": jnp.clip(1.0 + 0.1 * jax.random.normal(arg_keys[10], (3, D), jnp.float32), 0.5, 1.5),
        "table_master": gaussian(arg_keys[11], (BUCKETS, HEADS), 1.0, 6.0, (), jnp.float32),
        "qk_first": gaussian(arg_keys[12], (4, D, D), (0.055 * (MICRO * BATCH * LEN) ** 0.5), 40.0, ((1, 32),), jnp.float32),
        "value_first": gaussian(arg_keys[13], (2, D, D), (0.22 * (MICRO * BATCH * LEN) ** 0.5), 160.0, ((1, 32),), jnp.float32),
        "output_first": gaussian(arg_keys[14], (2, D, D), (0.0165 * (MICRO * BATCH * LEN) ** 0.5), 12.0, ((1, 32),), jnp.float32),
        "inner_first": gaussian(arg_keys[15], (D, FF), (0.0165 * (MICRO * BATCH * LEN) ** 0.5), 12.0, ((0, 32),), jnp.float32),
        "outer_first": gaussian(arg_keys[16], (FF, D), (0.044 * (MICRO * BATCH * LEN) ** 0.5), 32.0, ((0, 32),), jnp.float32),
        "gain_first": gaussian(arg_keys[17], (3, D), (0.11 * (MICRO * BATCH * LEN) ** 0.5), 80.0, ((1, 32),), jnp.float32),
        "table_first": gaussian(arg_keys[18], (BUCKETS, HEADS), (0.033 * (MICRO * BATCH * LEN * LEN / 32) ** 0.5), 64.0, (), jnp.float32),
        "qk_second": jnp.clip(jnp.exp(math.log(32.768) - 2.7725887 * jax.random.uniform(arg_keys[19], (4, D, D), jnp.float32) ** shard_levels(arg_keys[19], (4, D, D), ((1, 32),), -0.2, 0.2)), 2.048, 32.768),
        "value_second": jnp.clip(jnp.exp(math.log(524.288) - 2.7725887 * jax.random.uniform(arg_keys[20], (2, D, D), jnp.float32) ** shard_levels(arg_keys[20], (2, D, D), ((1, 32),), -0.2, 0.2)), 32.768, 524.288),
        "output_second": jnp.clip(jnp.exp(math.log(2.94912) - 2.7725887 * jax.random.uniform(arg_keys[21], (2, D, D), jnp.float32) ** shard_levels(arg_keys[21], (2, D, D), ((1, 32),), -0.2, 0.2)), 0.18432, 2.94912),
        "inner_second": jnp.clip(jnp.exp(math.log(2.94912) - 2.7725887 * jax.random.uniform(arg_keys[22], (D, FF), jnp.float32) ** shard_levels(arg_keys[22], (D, FF), ((0, 32),), -0.2, 0.2)), 0.18432, 2.94912),
        "outer_second": jnp.clip(jnp.exp(math.log(20.97152) - 2.7725887 * jax.random.uniform(arg_keys[23], (FF, D), jnp.float32) ** shard_levels(arg_keys[23], (FF, D), ((0, 32),), -0.2, 0.2)), 1.31072, 20.97152),
        "gain_second": jnp.clip(jnp.exp(math.log(131.072) - 2.7725887 * jax.random.uniform(arg_keys[24], (3, D), jnp.float32) ** shard_levels(arg_keys[24], (3, D), ((1, 32),), -0.2, 0.2)), 8.192, 131.072),
        "table_second": jnp.clip(jnp.exp(jax.random.uniform(arg_keys[25], (BUCKETS, HEADS), jnp.float32, math.log(5.89824), math.log(94.37184))), 5.89824, 94.37184),
    }


epsilon_norm = 1e-06
score_scale = 0.125
masked_score = -1e+30
beta_first = 0.9
beta_second = 0.999
adam_epsilon = 1e-08
rate_matrix = 0.15
rate_small = 1.0
weight_decay = 0.01
highest = lax.Precision.HIGHEST

@jax.custom_vjp
def low(v):
    return lax.optimization_barrier(v.astype(jnp.bfloat16)).astype(jnp.float32)

@jax.custom_vjp
def low_back(v):
    return v

def low_keep(v):
    return (low(v), None)

def low_pass(kept, grad):
    return (grad,)

def back_keep(v):
    return (v, None)

def back_low(kept, grad):
    return (low(grad),)
low.defvjp(low_keep, low_pass)
low_back.defvjp(back_keep, back_low)

def rounded_both(value):
    return low_back(low(value))

def bucket_onehot():
    places = jnp.arange(LEN, dtype=jnp.int32)
    distance = jnp.maximum(places[:, None] - places[None, :], 0)
    exact_range = BUCKETS // 2
    safe_distance = jnp.maximum(distance, 1).astype(jnp.float32)
    spread = jnp.log(safe_distance / exact_range) / math.log(MAX_DIST / exact_range) * (BUCKETS - exact_range)
    far_bucket = jnp.minimum(exact_range + spread.astype(jnp.int32), BUCKETS - 1)
    bucket = jnp.where(distance < exact_range, distance, far_bucket)
    labels = jnp.arange(BUCKETS, dtype=jnp.int32)
    return (bucket[None, :, :] == labels[:, None, None]).astype(jnp.float32)

def norm_rows(values, gain_row):
    return values * lax.rsqrt(lax.optimization_barrier(jnp.mean(values * values, axis=-1, keepdims=True)) + epsilon_norm) * gain_row

def project(inputs, weight):
    return jnp.einsum('gtd,de->gte', inputs, weight, precision=highest)

def to_heads(inputs):
    return inputs.reshape(inputs.shape[0], inputs.shape[1], HEADS, HEAD_DIM)

def attention(queries, key_rows, value_rows, bias_term, allowed):
    scores = jnp.einsum('gihe,gjhe->ghij', to_heads(queries), to_heads(key_rows), precision=highest) * score_scale + bias_term
    scores = low_back(scores)
    scores = jnp.where(allowed, scores, masked_score)
    row_max = lax.optimization_barrier(jnp.max(scores, axis=-1, keepdims=True))
    expanded = jnp.exp(scores - row_max)
    weights = expanded / lax.optimization_barrier(jnp.sum(expanded, axis=-1, keepdims=True))
    mixed_heads = jnp.einsum('ghij,gjhe->gihe', low(weights), to_heads(value_rows), precision=highest)
    return mixed_heads.reshape(queries.shape[0], queries.shape[1], HEADS * HEAD_DIM)

def layer(qk_weight, value_weight, output_weight, inner_weight, outer_weight, gain_values, table_values, hidden_rows, memory_rows, onehot, target_rows, memory_len_rows):
    qk_weight = low(qk_weight)
    value_weight = low(value_weight)
    output_weight = low(output_weight)
    inner_weight = low(inner_weight)
    outer_weight = low(outer_weight)
    gain_values = low(gain_values)
    bias_heads = jnp.einsum('bij,bh->hij', onehot, table_values, precision=highest)[None]
    places = jnp.arange(LEN, dtype=jnp.int32)
    causal = (places[None, :] <= places[:, None])[None, None]
    self_allowed = causal & (places[None, None, None, :] < target_rows[:, None, None, None])
    memory_places = jnp.arange(MEM, dtype=jnp.int32)
    cross_allowed = (memory_places[None, :] < memory_len_rows[:, None])[:, None, None, :]
    normed = low(norm_rows(hidden_rows, gain_values[0]))
    queries = rounded_both(project(normed, qk_weight[0]))
    key_rows = rounded_both(project(normed, qk_weight[1]))
    value_rows = rounded_both(project(normed, value_weight[0]))
    attended = rounded_both(attention(queries, key_rows, value_rows, bias_heads, self_allowed))
    first_sum = hidden_rows + low_back(project(attended, output_weight[0]))
    normed = low(norm_rows(first_sum, gain_values[1]))
    queries = rounded_both(project(normed, qk_weight[2]))
    key_rows = rounded_both(project(memory_rows, qk_weight[3]))
    value_rows = rounded_both(project(memory_rows, value_weight[1]))
    attended = rounded_both(attention(queries, key_rows, value_rows, 0.0, cross_allowed))
    second_sum = first_sum + low_back(project(attended, output_weight[1]))
    normed = low(norm_rows(second_sum, gain_values[2]))
    inner_act = low_back(project(normed, inner_weight))
    activated = low(jax.nn.gelu(inner_act, approximate=True))
    return second_sum + low_back(project(activated, outer_weight))

def adam_step(master, first_moment, second_moment, gradient, rate, decay):
    first_next = beta_first * first_moment + (1.0 - beta_first) * gradient
    second_next = beta_second * second_moment + (1.0 - beta_second) * gradient * gradient
    corrected = first_next / (1.0 - beta_first ** STEP) / (jnp.sqrt(second_next / (1.0 - beta_second ** STEP)) + adam_epsilon)
    master_next = master - rate * (corrected + decay * master)
    return (master_next, first_next, second_next)

def reference(hidden, memory, cotangent, target_lengths, memory_lengths, qk_master, value_master, output_master, inner_master, outer_master, gain_master, table_master, qk_first, value_first, output_first, inner_first, outer_first, gain_first, table_first, qk_second, value_second, output_second, inner_second, outer_second, gain_second, table_second):
    onehot = bucket_onehot()
    sequences = MICRO * BATCH
    group_size = math.gcd(sequences, max(1, 4096 // LEN))
    rounds = sequences // group_size

    def regroup(array):
        return array.reshape((rounds, group_size) + array.shape[2:])
    live_rows = (jnp.arange(LEN, dtype=jnp.int32)[None, None, :] < target_lengths[:, :, None]).astype(jnp.float32)
    pulled = cotangent.astype(jnp.float32) * live_rows[:, :, :, None]
    masters = (qk_master, value_master, output_master, inner_master, outer_master, gain_master, table_master)

    def one_group(totals, group_items):
        hidden_rows, memory_rows, pulled_rows, target_rows, memory_len_rows = group_items

        def forward(*operands):
            return layer(*operands, onehot, target_rows, memory_len_rows)
        produced, pullback = jax.vjp(forward, *masters, hidden_rows, memory_rows)
        gradients = pullback(pulled_rows)
        totals = tuple((total + grad_part for total, grad_part in zip(totals, gradients[:7])))
        return (totals, (produced.astype(jnp.bfloat16), gradients[7], gradients[8]))
    zero_totals = tuple((jnp.zeros_like(master) for master in masters))
    group_items = (regroup(hidden.astype(jnp.float32)), regroup(memory.astype(jnp.float32)), regroup(pulled), regroup(target_lengths), regroup(memory_lengths))
    totals, (produced, hidden_grads, memory_grads) = lax.scan(one_group, zero_totals, group_items)
    layer_out = produced.reshape(MICRO, BATCH, LEN, D)
    hidden_grad = hidden_grads.reshape(MICRO, BATCH, LEN, D)
    memory_grad = memory_grads.reshape(MICRO, BATCH, MEM, D)
    firsts = (qk_first, value_first, output_first, inner_first, outer_first, gain_first, table_first)
    seconds = (qk_second, value_second, output_second, inner_second, outer_second, gain_second, table_second)
    rates = (rate_matrix, rate_matrix, rate_matrix, rate_matrix, rate_matrix, rate_small, rate_small)
    decays = (weight_decay, weight_decay, weight_decay, weight_decay, weight_decay, 0.0, 0.0)
    updated = [adam_step(masters[index], firsts[index], seconds[index], totals[index], rates[index], decays[index]) for index in range(7)]
    news = [entry[0] for entry in updated]
    first_news = [entry[1] for entry in updated]
    second_news = [entry[2] for entry in updated]
    copies = [entry.astype(jnp.bfloat16) for entry in news]
    return (layer_out, hidden_grad, memory_grad, news[0], news[1], news[2], news[3], news[4], news[5], news[6], first_news[0], first_news[1], first_news[2], first_news[3], first_news[4], first_news[5], first_news[6], second_news[0], second_news[1], second_news[2], second_news[3], second_news[4], second_news[5], second_news[6], copies[0], copies[1], copies[2], copies[3], copies[4], copies[5], copies[6])
```

```python
import functools
import math

import jax
import jax.numpy as jnp
from jax import lax
from jax.experimental import pallas as pl
from jax.experimental.pallas import tpu as pltpu
from jax.sharding import PartitionSpec as P

HEADS = 12
HEAD_DIM = 64
BUCKETS = 32
MAX_DIST = 128
STEP = 10


epsilon_norm = 1e-06
score_scale = 0.125
masked_score = -1e30
beta_first = 0.9
beta_second = 0.999
adam_epsilon = 1e-08
rate_matrix = 0.15
rate_small = 1.0
weight_decay = 0.01
highest = lax.Precision.HIGHEST


def bucket_onehot(length):
    places = jnp.arange(length, dtype=jnp.int32)
    distance = jnp.maximum(places[:, None] - places[None, :], 0)
    exact_range = BUCKETS // 2
    safe_distance = jnp.maximum(distance, 1).astype(jnp.float32)
    spread = (
        jnp.log(safe_distance / exact_range)
        / math.log(MAX_DIST / exact_range)
        * (BUCKETS - exact_range)
    )
    far_bucket = jnp.minimum(exact_range + spread.astype(jnp.int32), BUCKETS - 1)
    bucket = jnp.where(distance < exact_range, distance, far_bucket)
    labels = jnp.arange(BUCKETS, dtype=jnp.int32)
    return (bucket[None, :, :] == labels[:, None, None]).astype(jnp.float32)


def product(left_side, right_side):
    return jnp.dot(left_side, right_side, preferred_element_type=jnp.float32)


def product_over_rows(left_side, right_side):
    return lax.dot_general(
        left_side, right_side, (((0,), (0,)), ((), ())), preferred_element_type=jnp.float32
    )


def product_transposed(left_side, right_side):
    return lax.dot_general(
        left_side, right_side, (((1,), (1,)), ((), ())), preferred_element_type=jnp.float32
    )


def to_heads(values, sequences):
    return values.reshape(sequences, -1, HEADS, HEAD_DIM)


def normalize(values, gain_row):
    scale_rows = lax.rsqrt(jnp.mean(values * values, axis=-1, keepdims=True) + epsilon_norm)
    unit_rows = values * scale_rows
    return ((unit_rows * gain_row).astype(jnp.bfloat16), unit_rows, scale_rows)


def normalize_back(grad_norm, unit_rows, scale_rows, gain_row):
    gain_grad = jnp.sum(grad_norm * unit_rows, axis=0)
    grad_unit = grad_norm * gain_row
    grad_values = scale_rows * (
        grad_unit - unit_rows * jnp.mean(grad_unit * unit_rows, axis=-1, keepdims=True)
    )
    return (grad_values, gain_grad)


def attend_scores(queries, key_heads, bias_term, allowed):
    scores = (
        jnp.einsum("sihe,sjhe->shij", queries, key_heads, preferred_element_type=jnp.float32)
        * score_scale
        + bias_term
    )
    return jnp.where(allowed, scores, masked_score)


def attend_forward(queries, key_heads, value_heads, bias_term, allowed):
    scores = attend_scores(queries, key_heads, bias_term, allowed)
    row_max = jnp.max(scores, axis=-1, keepdims=True)
    expanded = jnp.exp(scores - row_max)
    row_total = jnp.sum(expanded, axis=-1, keepdims=True)
    weights = (expanded / row_total).astype(jnp.bfloat16)
    mixed_heads = jnp.einsum(
        "shij,sjhe->sihe", weights, value_heads, preferred_element_type=jnp.float32
    )
    return (mixed_heads, row_max + jnp.log(row_total))


def attend_back(queries, key_heads, value_heads, bias_term, allowed, summary, grad_mixed):
    scores = attend_scores(queries, key_heads, bias_term, allowed)
    weights = jnp.exp(scores - summary)
    grad_weights = jnp.einsum(
        "sihe,sjhe->shij", grad_mixed, value_heads, preferred_element_type=jnp.float32
    )
    grad_values = jnp.einsum(
        "shij,sihe->sjhe",
        weights.astype(jnp.bfloat16),
        grad_mixed,
        preferred_element_type=jnp.float32,
    )
    grad_scores = (
        weights * (grad_weights - jnp.sum(weights * grad_weights, axis=-1, keepdims=True))
    ).astype(jnp.bfloat16)
    grad_queries = (
        jnp.einsum("shij,sjhe->sihe", grad_scores, key_heads, preferred_element_type=jnp.float32)
        * score_scale
    )
    grad_keys = (
        jnp.einsum("shij,sihe->sjhe", grad_scores, queries, preferred_element_type=jnp.float32)
        * score_scale
    )
    return (grad_queries, grad_keys, grad_values, grad_scores)


def forward_pass(gathered, bias_heads, hidden_seq, memory_seq, target_len, memory_len):
    qk_full, value_full, output_full, inner_full, outer_full, gain_full = gathered
    gain_rows = gain_full.astype(jnp.float32)
    sequences, length, model_width = hidden_seq.shape
    memory_span = memory_seq.shape[1]
    row_count = sequences * length
    residual = hidden_seq.astype(jnp.float32).reshape(row_count, model_width)
    memory_rows = memory_seq.reshape(sequences * memory_span, model_width)
    places = jnp.arange(length, dtype=jnp.int32)
    self_mask = (places[None, :] <= places[:, None])[None, None] & (
        places[None, None, None, :] < target_len[:, None, None, None]
    )
    memory_places = jnp.arange(memory_span, dtype=jnp.int32)
    cross_mask = (memory_places[None, :] < memory_len[:, None])[:, None, None, :]
    normed_first, unit_first, scale_first = normalize(residual, gain_rows[0])
    query_first = product(normed_first, qk_full[0]).astype(jnp.bfloat16)
    key_first = product(normed_first, qk_full[1]).astype(jnp.bfloat16)
    value_first = product(normed_first, value_full[0]).astype(jnp.bfloat16)
    mixed_first, summary_first = attend_forward(
        to_heads(query_first, sequences),
        to_heads(key_first, sequences),
        to_heads(value_first, sequences),
        bias_heads,
        self_mask,
    )
    mixed_first = mixed_first.reshape(row_count, model_width).astype(jnp.bfloat16)
    first_sum = residual + product(mixed_first, output_full[0])
    normed_second, unit_second, scale_second = normalize(first_sum, gain_rows[1])
    query_second = product(normed_second, qk_full[2]).astype(jnp.bfloat16)
    key_second = product(memory_rows, qk_full[3]).astype(jnp.bfloat16)
    value_second = product(memory_rows, value_full[1]).astype(jnp.bfloat16)
    mixed_second, summary_second = attend_forward(
        to_heads(query_second, sequences),
        to_heads(key_second, sequences),
        to_heads(value_second, sequences),
        0.0,
        cross_mask,
    )
    mixed_second = mixed_second.reshape(row_count, model_width).astype(jnp.bfloat16)
    second_sum = first_sum + product(mixed_second, output_full[1])
    normed_third, unit_third, scale_third = normalize(second_sum, gain_rows[2])
    inner_act = product(normed_third, inner_full)
    activated = jax.nn.gelu(inner_act, approximate=True).astype(jnp.bfloat16)
    produced = (second_sum + product(activated, outer_full)).astype(jnp.bfloat16)
    stored = (
        self_mask,
        cross_mask,
        memory_rows,
        normed_first,
        unit_first,
        scale_first,
        query_first,
        key_first,
        value_first,
        summary_first,
        mixed_first,
        normed_second,
        unit_second,
        scale_second,
        query_second,
        key_second,
        value_second,
        summary_second,
        mixed_second,
        normed_third,
        unit_third,
        scale_third,
        inner_act,
        activated,
    )
    return (stored, produced.reshape(sequences, length, model_width))


def backward_pass(gathered, bias_heads, stored, cotangent_seq, target_len):
    qk_full, value_full, output_full, inner_full, outer_full, gain_full = gathered
    gain_rows = gain_full.astype(jnp.float32)
    (
        self_mask,
        cross_mask,
        memory_rows,
        normed_first,
        unit_first,
        scale_first,
        query_first,
        key_first,
        value_first,
        summary_first,
        mixed_first,
        normed_second,
        unit_second,
        scale_second,
        query_second,
        key_second,
        value_second,
        summary_second,
        mixed_second,
        normed_third,
        unit_third,
        scale_third,
        inner_act,
        activated,
    ) = stored
    sequences, length, model_width = cotangent_seq.shape
    row_count = sequences * length
    places = jnp.arange(length, dtype=jnp.int32)
    live_rows = (places[None, :] < target_len[:, None]).astype(jnp.float32).reshape(row_count, 1)
    grad_out = cotangent_seq.astype(jnp.float32).reshape(row_count, model_width) * live_rows
    branch = grad_out.astype(jnp.bfloat16)
    outer_grad = product_over_rows(activated, branch)
    grad_act = product_transposed(branch, outer_full)
    unused_value, gelu_pull = jax.vjp(
        lambda inputs: jax.nn.gelu(inputs, approximate=True), inner_act
    )
    grad_inner = gelu_pull(grad_act)[0].astype(jnp.bfloat16)
    inner_grad = product_over_rows(normed_third, grad_inner)
    grad_from_third, gain_third = normalize_back(
        product_transposed(grad_inner, inner_full), unit_third, scale_third, gain_rows[2]
    )
    grad_second = grad_out + grad_from_third
    branch = grad_second.astype(jnp.bfloat16)
    output_grad_second = product_over_rows(mixed_second, branch)
    grad_mixed = product_transposed(branch, output_full[1]).astype(jnp.bfloat16)
    grad_query, grad_key, grad_value, unused_scores = attend_back(
        to_heads(query_second, sequences),
        to_heads(key_second, sequences),
        to_heads(value_second, sequences),
        0.0,
        cross_mask,
        summary_second,
        to_heads(grad_mixed, sequences),
    )
    grad_query = grad_query.reshape(row_count, model_width).astype(jnp.bfloat16)
    grad_key = grad_key.reshape(memory_rows.shape[0], model_width).astype(jnp.bfloat16)
    grad_value = grad_value.reshape(memory_rows.shape[0], model_width).astype(jnp.bfloat16)
    qk_grad_two = product_over_rows(normed_second, grad_query)
    qk_grad_three = product_over_rows(memory_rows, grad_key)
    value_grad_one = product_over_rows(memory_rows, grad_value)
    memory_grad = product_transposed(grad_key, qk_full[3]) + product_transposed(
        grad_value, value_full[1]
    )
    grad_from_second, gain_second = normalize_back(
        product_transposed(grad_query, qk_full[2]), unit_second, scale_second, gain_rows[1]
    )
    grad_first = grad_second + grad_from_second
    branch = grad_first.astype(jnp.bfloat16)
    output_grad_first = product_over_rows(mixed_first, branch)
    grad_mixed = product_transposed(branch, output_full[0]).astype(jnp.bfloat16)
    grad_query, grad_key, grad_value, grad_scores = attend_back(
        to_heads(query_first, sequences),
        to_heads(key_first, sequences),
        to_heads(value_first, sequences),
        bias_heads,
        self_mask,
        summary_first,
        to_heads(grad_mixed, sequences),
    )
    grad_query = grad_query.reshape(row_count, model_width).astype(jnp.bfloat16)
    grad_key = grad_key.reshape(row_count, model_width).astype(jnp.bfloat16)
    grad_value = grad_value.reshape(row_count, model_width).astype(jnp.bfloat16)
    qk_grad_zero = product_over_rows(normed_first, grad_query)
    qk_grad_one = product_over_rows(normed_first, grad_key)
    value_grad_zero = product_over_rows(normed_first, grad_value)
    grad_norm = (
        product_transposed(grad_query, qk_full[0])
        + product_transposed(grad_key, qk_full[1])
        + product_transposed(grad_value, value_full[0])
    )
    grad_from_first, gain_first = normalize_back(grad_norm, unit_first, scale_first, gain_rows[0])
    hidden_grad = grad_first + grad_from_first
    score_term = jnp.sum(grad_scores.astype(jnp.float32), axis=0)
    grad_terms = (
        jnp.stack([qk_grad_zero, qk_grad_one, qk_grad_two, qk_grad_three]),
        jnp.stack([value_grad_zero, value_grad_one]),
        jnp.stack([output_grad_first, output_grad_second]),
        inner_grad,
        outer_grad,
        jnp.stack([gain_first, gain_second, gain_third]),
    )
    return (
        grad_terms,
        score_term,
        hidden_grad.reshape(sequences, length, model_width),
        memory_grad.reshape(sequences, -1, model_width),
    )


def adam_step(master, first_moment, second_moment, gradient, rate, decay):
    first_next = beta_first * first_moment + (1.0 - beta_first) * gradient
    second_next = beta_second * second_moment + (1.0 - beta_second) * gradient * gradient
    corrected = (
        first_next
        / (1.0 - beta_first**STEP)
        / (jnp.sqrt(second_next / (1.0 - beta_second**STEP)) + adam_epsilon)
    )
    master_next = master - rate * (corrected + decay * master)
    return (master_next, first_next, second_next)


def shards(
    hidden,
    memory,
    cotangent,
    target_lengths,
    memory_lengths,
    qk_master,
    value_master,
    output_master,
    inner_master,
    outer_master,
    gain_master,
    table_master,
    qk_first,
    value_first,
    output_first,
    inner_first,
    outer_first,
    gain_first,
    table_first,
    qk_second,
    value_second,
    output_second,
    inner_second,
    outer_second,
    gain_second,
    table_second,
):
    micro_count = hidden.shape[0]
    length = hidden.shape[2]
    model_width = hidden.shape[3]
    hidden_units = inner_master.shape[1]
    qk_low = qk_master.astype(jnp.bfloat16)
    value_low = value_master.astype(jnp.bfloat16)
    output_low = output_master.astype(jnp.bfloat16)
    inner_low = inner_master.astype(jnp.bfloat16)
    outer_low = outer_master.astype(jnp.bfloat16)
    gain_low = gain_master.astype(jnp.bfloat16)
    onehot = bucket_onehot(length)
    bias_heads = jnp.einsum("bij,bh->hij", onehot, table_master, precision=highest)
    masters = (qk_master, value_master, output_master, inner_master, outer_master, gain_master)
    totals = (
        jnp.zeros((4, model_width, model_width), jnp.float32),
        jnp.zeros((2, model_width, model_width), jnp.float32),
        jnp.zeros((2, model_width, model_width), jnp.float32),
        jnp.zeros((model_width, hidden_units), jnp.float32),
        jnp.zeros((hidden_units, model_width), jnp.float32),
        jnp.zeros((3, model_width), jnp.float32),
    )
    reduced = tuple((jnp.zeros_like(master) for master in masters))
    score_total = jnp.zeros((HEADS, length, length), jnp.float32)
    produced_list = []
    hidden_list = []
    memory_list = []
    for micro_index in range(micro_count):
        gathered = (
            lax.all_gather(qk_low, ("dp", "fsdp"), axis=1, tiled=True),
            lax.all_gather(value_low, ("dp", "fsdp"), axis=1, tiled=True),
            lax.all_gather(output_low, ("dp", "fsdp"), axis=1, tiled=True),
            lax.all_gather(inner_low, ("dp", "fsdp"), axis=0, tiled=True),
            lax.all_gather(outer_low, ("dp", "fsdp"), axis=0, tiled=True),
            lax.all_gather(gain_low, ("dp", "fsdp"), axis=1, tiled=True),
        )
        stored, produced = forward_pass(
            gathered,
            bias_heads,
            hidden[micro_index],
            memory[micro_index],
            target_lengths[micro_index],
            memory_lengths[micro_index],
        )
        gathered = (
            lax.all_gather(qk_low, ("dp", "fsdp"), axis=1, tiled=True),
            lax.all_gather(value_low, ("dp", "fsdp"), axis=1, tiled=True),
            lax.all_gather(output_low, ("dp", "fsdp"), axis=1, tiled=True),
            lax.all_gather(inner_low, ("dp", "fsdp"), axis=0, tiled=True),
            lax.all_gather(outer_low, ("dp", "fsdp"), axis=0, tiled=True),
            lax.all_gather(gain_low, ("dp", "fsdp"), axis=1, tiled=True),
        )
        grad_terms, score_term, hidden_grad, memory_grad = backward_pass(
            gathered, bias_heads, stored, cotangent[micro_index], target_lengths[micro_index]
        )
        totals = tuple((running + addition for running, addition in zip(totals, grad_terms)))
        score_total = score_total + score_term
        produced_list.append(produced)
        hidden_list.append(hidden_grad)
        memory_list.append(memory_grad)
    reduced = (
        lax.psum_scatter(totals[0], ("dp", "fsdp"), scatter_dimension=1, tiled=True),
        lax.psum_scatter(totals[1], ("dp", "fsdp"), scatter_dimension=1, tiled=True),
        lax.psum_scatter(totals[2], ("dp", "fsdp"), scatter_dimension=1, tiled=True),
        lax.psum_scatter(totals[3], ("dp", "fsdp"), scatter_dimension=0, tiled=True),
        lax.psum_scatter(totals[4], ("dp", "fsdp"), scatter_dimension=0, tiled=True),
        lax.psum_scatter(totals[5], ("dp", "fsdp"), scatter_dimension=1, tiled=True),
    )
    table_grad = jnp.einsum("bij,hij->bh", onehot, score_total, precision=highest)
    table_grad = lax.psum(table_grad, ("dp", "fsdp"))
    all_masters = (
        qk_master,
        value_master,
        output_master,
        inner_master,
        outer_master,
        gain_master,
        table_master,
    )
    firsts = (
        qk_first,
        value_first,
        output_first,
        inner_first,
        outer_first,
        gain_first,
        table_first,
    )
    seconds = (
        qk_second,
        value_second,
        output_second,
        inner_second,
        outer_second,
        gain_second,
        table_second,
    )
    gradients = (reduced[0], reduced[1], reduced[2], reduced[3], reduced[4], reduced[5], table_grad)
    rates = (
        rate_matrix,
        rate_matrix,
        rate_matrix,
        rate_matrix,
        rate_matrix,
        rate_small,
        rate_small,
    )
    decays = (weight_decay, weight_decay, weight_decay, weight_decay, weight_decay, 0.0, 0.0)
    updated = [
        adam_step(
            all_masters[index],
            firsts[index],
            seconds[index],
            gradients[index],
            rates[index],
            decays[index],
        )
        for index in range(7)
    ]
    news = [entry[0] for entry in updated]
    first_news = [entry[1] for entry in updated]
    second_news = [entry[2] for entry in updated]
    copies = [entry.astype(jnp.bfloat16) for entry in news]
    layer_out = jnp.stack(produced_list)
    hidden_out = jnp.stack(hidden_list)
    memory_out = jnp.stack(memory_list)
    return (
        layer_out,
        hidden_out,
        memory_out,
        news[0],
        news[1],
        news[2],
        news[3],
        news[4],
        news[5],
        news[6],
        first_news[0],
        first_news[1],
        first_news[2],
        first_news[3],
        first_news[4],
        first_news[5],
        first_news[6],
        second_news[0],
        second_news[1],
        second_news[2],
        second_news[3],
        second_news[4],
        second_news[5],
        second_news[6],
        copies[0],
        copies[1],
        copies[2],
        copies[3],
        copies[4],
        copies[5],
        copies[6],
    )


MESH = pl.DeviceIdType.MESH
PAIRS = 6
ORDERS = ("ax", "ay", "ax", "ay", "ax", "ay", "cx", "cy")


class Place:
    def __init__(self, wa, wf):
        self.wa, self.wf = wa, wf
        dp, fs = lax.axis_index("dp"), lax.axis_index("fsdp")
        self.z, self.y = dp // 2, dp % 2
        self.x, self.c = fs // 2, fs % 2
        self.to = {
            "x": (dp, (1 - self.x) * 2 + self.c),
            "y": (self.z * 2 + 1 - self.y, fs),
            "c": (dp, self.x * 2 + 1 - self.c),
            "r": (dp + 2, fs),
            "l": (dp - 2, fs),
        }

    def enter(self):
        bar = pltpu.get_barrier_semaphore()

        def greet(way):
            pl.semaphore_signal(bar, inc=1, device_id=self.to[way], device_id_type=MESH)

        for way in ("x", "y", "c"):
            greet(way)

        @pl.when(self.z < 3)
        def _():
            greet("r")

        @pl.when(self.z > 0)
        def _():
            greet("l")

        inner = (self.z > 0) & (self.z < 3)

        @pl.when(inner)
        def _():
            pl.semaphore_wait(bar, 5)

        @pl.when(jnp.logical_not(inner))
        def _():
            pl.semaphore_wait(bar, 4)

    def pick(self, f, zs, ps, qs, core=None):
        c = self.c if core is None else core
        xs, ys = (ps, qs) if ORDERS[f][1] == "x" else (qs, ps)
        if f < PAIRS:
            return self.wa.at[2 * f + c, zs, ys, xs]
        return self.wf.at[zs, ys, xs, c, f - PAIRS]

    def own(self, f):
        return (self.x, self.y) if ORDERS[f][1] == "x" else (self.y, self.x)

    def ways(self, f):
        return ("x", "y") if ORDERS[f][1] == "x" else ("y", "x")


def push(place, src, dst, send, recv, way):
    pltpu.make_async_remote_copy(
        src_ref=src, dst_ref=dst, send_sem=send, recv_sem=recv,
        device_id=place.to[way], device_id_type=MESH,
    ).start()


def got(place, ref, sem, way):
    pltpu.make_async_remote_copy(
        src_ref=ref, dst_ref=ref, send_sem=sem, recv_sem=sem,
        device_id=place.to[way], device_id_type=MESH,
    ).wait_recv()


def left_out(place, ref, sem, way):
    pltpu.make_async_remote_copy(
        src_ref=ref, dst_ref=ref, send_sem=sem, recv_sem=sem,
        device_id=place.to[way], device_id_type=MESH,
    ).wait_send()


ALL = slice(None)


class Gather:
    def __init__(self, place, f, send, recv):
        self.k, self.f = place, f
        self.send, self.recv = send, recv
        self.first_cross = ORDERS[f][0] == "a"
        self.stages = [self.start, self.cross if self.first_cross else (lambda: self.step(1)),
                       (lambda: self.step(1 if self.first_cross else 2)),
                       (lambda: self.step(2 if self.first_cross else 3)),
                       (lambda: self.step(3)) if self.first_cross else self.cross,
                       self.second, self.finish]

    def blk(self, zi):
        p, q = self.k.own(self.f)
        return self.k.pick(self.f, zi, ALL if self.first_cross else p, q)

    def move(self, ref, s, r, way):
        push(self.k, ref, ref, self.send.at[self.f, s], self.recv.at[self.f, r], way)

    def start(self):
        p, q = self.k.own(self.f)
        pw, qw = self.k.ways(self.f)
        if self.first_cross:
            self.move(self.k.pick(self.f, self.k.z, p, q), 0, 0, pw)
        else:
            self.spread(self.k.z, 1)

    def cross(self):
        p, q = self.k.own(self.f)
        pw, qw = self.k.ways(self.f)
        if self.first_cross:
            got(self.k, self.k.pick(self.f, self.k.z, 1 - p, q), self.recv.at[self.f, 0], pw)
            self.spread(self.k.z, 1)
        else:
            got(self.k, self.k.pick(self.f, ALL, 1 - p, q), self.recv.at[self.f, 0], pw)
            half = self.k.pick(self.f, ALL, ALL, q)
            self.move(half, 3, 7, qw)
            self.move(half, 4, 8, "c")

    def sideways(self, zi):
        pw, qw = self.k.ways(self.f)
        if self.first_cross:
            self.move(self.blk(zi), 3, 7, qw)
            self.move(self.blk(zi), 4, 8, "c")
        else:
            self.move(self.blk(zi), 0, 0, pw)

    def spread(self, zi, t):
        z = self.k.z

        @pl.when(z < 3)
        def _():
            self.move(self.blk(zi), 1, t, "r")

        @pl.when(z > 0)
        def _():
            self.move(self.blk(zi), 2, 3 + t, "l")

        self.sideways(zi)

    def step(self, t):
        z = self.k.z

        @pl.when(z >= t)
        def _():
            got(self.k, self.blk(z - t), self.recv.at[self.f, t], "l")

            if t < 3:
                @pl.when(z < 3)
                def _():
                    self.move(self.blk(z - t), 1, t + 1, "r")

            self.sideways(z - t)

        @pl.when(z <= 3 - t)
        def _():
            got(self.k, self.blk(z + t), self.recv.at[self.f, 3 + t], "r")

            if t < 3:
                @pl.when(z > 0)
                def _():
                    self.move(self.blk(z + t), 2, 3 + t + 1, "l")

            self.sideways(z + t)

    def second(self):
        p, q = self.k.own(self.f)
        pw, qw = self.k.ways(self.f)
        other = self.k.pick(self.f, ALL, ALL, 1 - q)
        got(self.k, other, self.recv.at[self.f, 7], qw)
        self.move(other, 4, 8, "c")

    def finish(self):
        theirs = self.k.pick(self.f, ALL, ALL, ALL, 1 - self.k.c)
        got(self.k, theirs, self.recv.at[self.f, 8], "c")

    def drain(self):
        p, q = self.k.own(self.f)
        pw, qw = self.k.ways(self.f)
        z, f = self.k.z, self.f
        some = (lambda n: self.k.pick(f, pl.ds(0, n), ALL if self.first_cross else p, q))
        first = self.k.pick(f, z, p, q) if self.first_cross else self.k.pick(f, ALL, p, q)
        left_out(self.k, first, self.send.at[f, 0], pw)
        for n in (1, 2, 3):
            @pl.when(z == n - 1)
            def _():
                left_out(self.k, some(n), self.send.at[f, 1], "r")

            @pl.when(z == 4 - n)
            def _():
                left_out(self.k, some(n), self.send.at[f, 2], "l")
        left_out(self.k, self.k.pick(f, ALL, ALL, q), self.send.at[f, 3], qw)
        left_out(self.k, self.k.pick(f, ALL, ALL, ALL), self.send.at[f, 4], "c")


def add_into(dst, srcs, lead):
    sizes = lead
    count = 1
    for s in sizes:
        count *= s

    def body(i, _):
        idx, rest = [], i
        for s in reversed(sizes):
            idx.append(rest % s)
            rest = rest // s
        idx = tuple(reversed(idx)) or Ellipsis
        total = dst[idx].astype(jnp.float32)
        for src in srcs:
            total = total + src[idx].astype(jnp.float32)
        dst[idx] = total.astype(jnp.bfloat16)
        return 0

    lax.fori_loop(0, count, body, 0)


class Scatter:
    def __init__(self, place, f, send, recv, slots, final, result):
        self.k, self.f = place, f
        self.send, self.recv = send, recv
        self.rd, self.rq, self.rp, self.rl, self.rr = slots
        self.final, self.result = final, result
        self.wide = ORDERS[f][0] == "a"
        self.stages = [self.start, self.core, self.half,
                       *([] if self.wide else [self.cross_in]),
                       (lambda: self.step_in(1)), (lambda: self.step_in(2)), (lambda: self.step_in(3)),
                       *([self.last] if self.wide else []), self.finish]

    def move(self, src, dst, s, way):
        push(self.k, src, dst, self.send.at[self.f, s], self.recv.at[self.f, s], way)

    def blk(self, zi):
        p, q = self.k.own(self.f)
        return self.k.pick(self.f, zi, ALL if self.wide else p, q)

    def start(self):
        self.move(self.k.pick(self.f, ALL, ALL, ALL, 1 - self.k.c), self.rd, 0, "c")

    def rpick(self, ps, qs):
        xs, ys = (ps, qs) if ORDERS[self.f][1] == "x" else (qs, ps)
        return self.rd.at[:, ys, xs]

    def core(self):
        p, q = self.k.own(self.f)
        pw, qw = self.k.ways(self.f)
        got(self.k, self.rd, self.recv.at[self.f, 0], "c")
        away = self.k.pick(self.f, ALL, ALL, 1 - q)
        add_into(away, [self.rpick(ALL, 1 - q)], (4, 2))
        self.move(away, self.rq, 1, qw)

    def half(self):
        p, q = self.k.own(self.f)
        pw, qw = self.k.ways(self.f)
        got(self.k, self.rq, self.recv.at[self.f, 1], qw)
        add_into(self.k.pick(self.f, ALL, ALL, q), [self.rpick(ALL, q), self.rq], (4, 2))
        if self.wide:
            self.step_out(1)
        else:
            self.move(self.k.pick(self.f, ALL, 1 - p, q), self.rp, 2, pw)

    def cross_in(self):
        p, q = self.k.own(self.f)
        pw, qw = self.k.ways(self.f)
        got(self.k, self.rp, self.recv.at[self.f, 2], pw)
        add_into(self.k.pick(self.f, ALL, p, q), [self.rp], (4,))
        self.step_out(1)

    def step_out(self, t):
        z = self.k.z

        @pl.when(z <= t - 1)
        def _():
            self.move(self.blk(z + 4 - t), self.rl.at[t - 1], 2 + t, "r")

        @pl.when(z >= 4 - t)
        def _():
            self.move(self.blk(z - 4 + t), self.rr.at[t - 1], 5 + t, "l")

    def step_in(self, t):
        z, f = self.k.z, self.f
        lead = (2,) if self.wide else ()

        @pl.when((z >= 1) & (z <= t))
        def _():
            got(self.k, self.rl.at[t - 1], self.recv.at[f, 2 + t], "l")
            add_into(self.blk(z + 3 - t), [self.rl.at[t - 1]], lead)

        @pl.when((z <= 2) & (z >= 3 - t))
        def _():
            got(self.k, self.rr.at[t - 1], self.recv.at[f, 5 + t], "r")
            add_into(self.blk(z - 3 + t), [self.rr.at[t - 1]], lead)

        if t < 3:
            self.step_out(t + 1)
        else:
            p, q = self.k.own(f)
            pw, qw = self.k.ways(f)
            if self.wide:
                self.move(self.k.pick(f, z, 1 - p, q), self.rp, 2, pw)
            else:
                self.total(None)

    def last(self):
        pw, qw = self.k.ways(self.f)
        got(self.k, self.rp, self.recv.at[self.f, 2], pw)
        self.total(self.rp)

    def total(self, more):
        p, q = self.k.own(self.f)
        c = self.k.c
        mine = self.k.pick(self.f, self.k.z, p, q)[...].astype(jnp.float32)
        if more is not None:
            mine = mine + more[...].astype(jnp.float32)
        if self.f < PAIRS:
            self.final[...] = mine
            kept = pl.ds(pl.multiple_of(c * 24, 8), 24)
            away = pl.ds(pl.multiple_of(24 - c * 24, 8), 24)
            self.move(self.final.at[away], self.result.at[2 * self.f + c], 9, "c")
            self.result[2 * self.f + c] = self.final[kept]
        else:
            self.final[...] = mine

    def finish(self):
        if self.f < PAIRS:
            got(self.k, self.result.at[2 * self.f + 1 - self.k.c], self.recv.at[self.f, 9], "c")

    def drain(self):
        p, q = self.k.own(self.f)
        pw, qw = self.k.ways(self.f)
        z, f, k = self.k.z, self.f, self.k
        left_out(k, self.rd, self.send.at[f, 0], "c")
        left_out(k, self.rq, self.send.at[f, 1], qw)
        left_out(k, self.rp, self.send.at[f, 2], pw)
        for t in (1, 2, 3):
            @pl.when(z <= t - 1)
            def _():
                left_out(k, self.rl.at[t - 1], self.send.at[f, 2 + t], "r")

            @pl.when(z >= 4 - t)
            def _():
                left_out(k, self.rr.at[t - 1], self.send.at[f, 5 + t], "l")
        if f < PAIRS:
            left_out(k, self.final.at[pl.ds(0, 24)], self.send.at[f, 9], "c")


def weave(flows, gap=0):
    out = []
    rounds = max(i * gap + len(flow.stages) for i, flow in enumerate(flows))
    for r in range(rounds):
        for i, flow in enumerate(flows):
            s = r - i * gap
            if 0 <= s < len(flow.stages):
                out.append(flow.stages[s])
    return out


def gather_kernel(m_ref, o_ref, wa, wf, xch, send, recv, xs, xr):
    k = Place(wa, wf)
    k.enter()
    z, y, x, c = k.z, k.y, k.x, k.c
    row = pl.ds(pl.multiple_of(24 * c, 8), 24)
    push(k, m_ref.at[:, 1 - c], xch.at[:, row], xs, xr, "c")
    for h in range(2):
        wf[z, y, x, c, h] = o_ref[48 * h:48 * h + 48].astype(jnp.bfloat16)
    flows = [Gather(k, f, send, recv) for f in range(8)]
    for f in (6, 7):
        flows[f].start()
    for p in range(PAIRS):
        xch[p, row] = m_ref[p, c]
    other = pl.ds(pl.multiple_of(24 - 24 * c, 8), 24)
    got(k, xch.at[:, other], xr, "c")
    for p in range(PAIRS):
        wa[2 * p + c, z, y, x] = xch[p].astype(jnp.bfloat16)
        flows[p].start()
    left_out(k, m_ref.at[:, 1 - c], xs, "c")
    for flow in flows:
        flow.stages = flow.stages[1:]
    for stage in weave(flows):
        stage()
    for flow in flows:
        flow.drain()


def gather_all(m, o):
    return pl.pallas_call(
        gather_kernel,
        out_shape=(jax.ShapeDtypeStruct((12, 4, 2, 2, 48, 768), jnp.bfloat16),
                   jax.ShapeDtypeStruct((4, 2, 2, 2, 2, 48, 768), jnp.bfloat16)),
        in_specs=[pl.BlockSpec(memory_space=pltpu.VMEM)] * 2,
        out_specs=[pl.BlockSpec(memory_space=pltpu.VMEM)] * 2,
        scratch_shapes=[
            pltpu.VMEM((6, 48, 768), jnp.float32),
            pltpu.SemaphoreType.DMA((8, 5)),
            pltpu.SemaphoreType.DMA((8, 9)),
            pltpu.SemaphoreType.DMA,
            pltpu.SemaphoreType.DMA,
        ],
        compiler_params=pltpu.CompilerParams(collective_id=0, has_side_effects=True, vmem_limit_bytes=60 * 2**20),
    )(m, o)


def scatter_kernel(ga_in, gf_in, res, fin, wa, wf, rd, rq, rlw, rrw, rpw, rln, rrn, rpn, send, recv, cs):
    ca = pltpu.make_async_copy(ga_in, wa, cs.at[0])
    cf = pltpu.make_async_copy(gf_in, wf, cs.at[1])
    ca.start()
    cf.start()
    k = Place(wa, wf)
    k.enter()
    ca.wait()
    cf.wait()
    flows = []
    for f in (6, 7, 5, 4, 3, 2, 1, 0):
        if f < PAIRS:
            slots = (rd.at[f], rq.at[f], rpw.at[f], rlw.at[f], rrw.at[f])
        else:
            slots = (rd.at[f], rq.at[f], rpn.at[f - PAIRS], rln.at[f - PAIRS], rrn.at[f - PAIRS])
        flows.append(Scatter(k, f, send, recv, slots, fin.at[f], res))
    for flow in flows:
        flow.stages[0]()
        flow.stages = flow.stages[1:]
    for stage in weave(flows):
        stage()
    for flow in flows:
        flow.drain()


def scatter_all(ga, gf):
    bf, f32 = jnp.bfloat16, jnp.float32
    return pl.pallas_call(
        scatter_kernel,
        out_shape=(jax.ShapeDtypeStruct((12, 24, 768), f32), jax.ShapeDtypeStruct((8, 48, 768), f32)),
        in_specs=[pl.BlockSpec(memory_space=pl.ANY)] * 2,
        out_specs=[pl.BlockSpec(memory_space=pltpu.VMEM)] * 2,
        scratch_shapes=[
            pltpu.VMEM((12, 4, 2, 2, 48, 768), bf),
            pltpu.VMEM((4, 2, 2, 2, 2, 48, 768), bf),
            pltpu.VMEM((8, 4, 2, 2, 48, 768), bf),
            pltpu.VMEM((8, 4, 2, 48, 768), bf),
            pltpu.VMEM((6, 3, 2, 48, 768), bf),
            pltpu.VMEM((6, 3, 2, 48, 768), bf),
            pltpu.VMEM((6, 48, 768), bf),
            pltpu.VMEM((2, 3, 48, 768), bf),
            pltpu.VMEM((2, 3, 48, 768), bf),
            pltpu.VMEM((2, 4, 48, 768), bf),
            pltpu.SemaphoreType.DMA((8, 10)),
            pltpu.SemaphoreType.DMA((8, 10)),
            pltpu.SemaphoreType.DMA((2,)),
        ],
        compiler_params=pltpu.CompilerParams(collective_id=1, has_side_effects=True, vmem_limit_bytes=60 * 2**20),
    )(ga, gf)


def shards_block(
    hidden, memory, cotangent, target_lengths, memory_lengths,
    qk_master, value_master, output_master, inner_master, outer_master, gain_master, table_master,
    qk_first, value_first, output_first, inner_first, outer_first, gain_first, table_first,
    qk_second, value_second, output_second, inner_second, outer_second, gain_second, table_second,
):
    axes = ("dp", "fsdp")
    micro, _, length, width = hidden.shape
    inner4 = inner_master.reshape(24, 4, 768).transpose(1, 0, 2)
    m = jnp.concatenate(
        [qk_master[0:2], value_master[0:1], output_master[0:1], qk_master[3:4], value_master[1:2],
         qk_master[2:3], output_master[1:2], inner4]
    ).reshape(6, 2, 24, 768)
    wa, wf = gather_all(m, outer_master)
    wa = wa.reshape(12, 768, 768)
    gain_full = lax.all_gather(gain_master.astype(jnp.bfloat16), axes, axis=1, tiled=True)
    gathered = (
        jnp.stack([wa[0], wa[1], wa[6], wa[4]]),
        jnp.stack([wa[2], wa[5]]),
        jnp.stack([wa[3], wa[7]]),
        jnp.concatenate([wa[8], wa[9], wa[10], wa[11]], axis=1),
        wf.reshape(3072, 768),
        gain_full,
    )
    onehot = bucket_onehot(length)
    bias_heads = jnp.einsum("bij,bh->hij", onehot, table_master, precision=highest)
    stored, produced = forward_pass(
        gathered, bias_heads, hidden[:, 0], memory[:, 0], target_lengths[:, 0], memory_lengths[:, 0]
    )
    grad_terms, score_term, hidden_grad, memory_grad = backward_pass(
        gathered, bias_heads, stored, cotangent[:, 0], target_lengths[:, 0]
    )
    gqk, gv, go, gi, gw, gg = grad_terms
    ga = jnp.concatenate(
        [gqk[0:2], gv[0:1], go[0:1], gqk[3:4], gv[1:2], gqk[2:3], go[1:2],
         gi.reshape(768, 4, 768).transpose(1, 0, 2)]
    ).astype(jnp.bfloat16).reshape(12, 4, 2, 2, 48, 768)
    res, fin = scatter_all(ga, gw.astype(jnp.bfloat16).reshape(4, 2, 2, 2, 2, 48, 768))
    table_grad = jnp.einsum("bij,hij->bh", onehot, score_term, precision=highest)
    small = lax.psum(jnp.concatenate([gg.reshape(-1), table_grad.reshape(-1)]), axes)
    device = lax.axis_index(axes)
    gain_grad = lax.dynamic_slice(small[:2304].reshape(3, 768), (0, 24 * device), (3, 24))
    gradients = (
        jnp.stack([res[0], res[1], res[6], res[4]]),
        jnp.stack([res[2], res[5]]),
        jnp.stack([res[3], res[7]]),
        res[8:12].transpose(1, 0, 2).reshape(24, 3072),
        fin[6:].reshape(96, 768),
        gain_grad,
        small[2304:].reshape(BUCKETS, HEADS),
    )
    masters = (qk_master, value_master, output_master, inner_master, outer_master, gain_master, table_master)
    firsts = (qk_first, value_first, output_first, inner_first, outer_first, gain_first, table_first)
    seconds = (qk_second, value_second, output_second, inner_second, outer_second, gain_second, table_second)
    updated = [
        adam_step(a, b, c, g, rate_matrix if i < 5 else rate_small, weight_decay if i < 5 else 0.0)
        for i, (a, b, c, g) in enumerate(zip(masters, firsts, seconds, gradients))
    ]
    return (
        produced[:, None],
        hidden_grad[:, None],
        memory_grad[:, None],
        *[u[0] for u in updated],
        *[u[1] for u in updated],
        *[u[2] for u in updated],
        *[u[0].astype(jnp.bfloat16) for u in updated],
    )


def solution(mesh):
    placed = (
        P(None, ("dp", "fsdp"), None, None),
        P(None, ("dp", "fsdp"), None, None),
        P(None, ("dp", "fsdp"), None, None),
        P(None, ("dp", "fsdp")),
        P(None, ("dp", "fsdp")),
        P(None, ("dp", "fsdp"), None),
        P(None, ("dp", "fsdp"), None),
        P(None, ("dp", "fsdp"), None),
        P(("dp", "fsdp"), None),
        P(("dp", "fsdp"), None),
        P(None, ("dp", "fsdp")),
        P(),
        P(None, ("dp", "fsdp"), None),
        P(None, ("dp", "fsdp"), None),
        P(None, ("dp", "fsdp"), None),
        P(("dp", "fsdp"), None),
        P(("dp", "fsdp"), None),
        P(None, ("dp", "fsdp")),
        P(),
        P(None, ("dp", "fsdp"), None),
        P(None, ("dp", "fsdp"), None),
        P(None, ("dp", "fsdp"), None),
        P(("dp", "fsdp"), None),
        P(("dp", "fsdp"), None),
        P(None, ("dp", "fsdp")),
        P(),
    )
    small_slice = dict(mesh.shape) == {"dp": 8, "fsdp": 4}
    return jax.shard_map(
        shards_block if small_slice else shards,
        mesh=mesh,
        in_specs=placed,
        out_specs=(
            P(None, ("dp", "fsdp"), None, None),
            P(None, ("dp", "fsdp"), None, None),
            P(None, ("dp", "fsdp"), None, None),
            P(None, ("dp", "fsdp"), None),
            P(None, ("dp", "fsdp"), None),
            P(None, ("dp", "fsdp"), None),
            P(("dp", "fsdp"), None),
            P(("dp", "fsdp"), None),
            P(None, ("dp", "fsdp")),
            P(),
            P(None, ("dp", "fsdp"), None),
            P(None, ("dp", "fsdp"), None),
            P(None, ("dp", "fsdp"), None),
            P(("dp", "fsdp"), None),
            P(("dp", "fsdp"), None),
            P(None, ("dp", "fsdp")),
            P(),
            P(None, ("dp", "fsdp"), None),
            P(None, ("dp", "fsdp"), None),
            P(None, ("dp", "fsdp"), None),
            P(("dp", "fsdp"), None),
            P(("dp", "fsdp"), None),
            P(None, ("dp", "fsdp")),
            P(),
            P(None, ("dp", "fsdp"), None),
            P(None, ("dp", "fsdp"), None),
            P(None, ("dp", "fsdp"), None),
            P(("dp", "fsdp"), None),
            P(("dp", "fsdp"), None),
            P(None, ("dp", "fsdp")),
            P(),
        ),
        check_vma=False,
    )
```

```python
import functools
import math

import jax
import jax.numpy as jnp
from jax import lax
from jax.experimental import pallas as pl
from jax.experimental.pallas import tpu as pltpu
from jax.sharding import PartitionSpec as P

HEADS = 12
HEAD_DIM = 64
BUCKETS = 32
MAX_DIST = 128
STEP = 10


epsilon_norm = 1e-06
score_scale = 0.125
masked_score = -1e30
beta_first = 0.9
beta_second = 0.999
adam_epsilon = 1e-08
rate_matrix = 0.15
rate_small = 1.0
weight_decay = 0.01
highest = lax.Precision.HIGHEST


def bucket_onehot(length):
    places = jnp.arange(length, dtype=jnp.int32)
    distance = jnp.maximum(places[:, None] - places[None, :], 0)
    exact_range = BUCKETS // 2
    safe_distance = jnp.maximum(distance, 1).astype(jnp.float32)
    spread = (
        jnp.log(safe_distance / exact_range)
        / math.log(MAX_DIST / exact_range)
        * (BUCKETS - exact_range)
    )
    far_bucket = jnp.minimum(exact_range + spread.astype(jnp.int32), BUCKETS - 1)
    bucket = jnp.where(distance < exact_range, distance, far_bucket)
    labels = jnp.arange(BUCKETS, dtype=jnp.int32)
    return (bucket[None, :, :] == labels[:, None, None]).astype(jnp.float32)


def product(left_side, right_side):
    return jnp.dot(left_side, right_side, preferred_element_type=jnp.float32)


def product_over_rows(left_side, right_side):
    return lax.dot_general(
        left_side, right_side, (((0,), (0,)), ((), ())), preferred_element_type=jnp.float32
    )


def product_transposed(left_side, right_side):
    return lax.dot_general(
        left_side, right_side, (((1,), (1,)), ((), ())), preferred_element_type=jnp.float32
    )


def to_heads(values, sequences):
    return values.reshape(sequences, -1, HEADS, HEAD_DIM)


def normalize(values, gain_row):
    scale_rows = lax.rsqrt(jnp.mean(values * values, axis=-1, keepdims=True) + epsilon_norm)
    unit_rows = values * scale_rows
    return ((unit_rows * gain_row).astype(jnp.bfloat16), unit_rows, scale_rows)


def normalize_back(grad_norm, unit_rows, scale_rows, gain_row):
    gain_grad = jnp.sum(grad_norm * unit_rows, axis=0)
    grad_unit = grad_norm * gain_row
    grad_values = scale_rows * (
        grad_unit - unit_rows * jnp.mean(grad_unit * unit_rows, axis=-1, keepdims=True)
    )
    return (grad_values, gain_grad)


def attend_scores(queries, key_heads, bias_term, allowed):
    scores = (
        jnp.einsum("sihe,sjhe->shij", queries, key_heads, preferred_element_type=jnp.float32)
        * score_scale
        + bias_term
    )
    return jnp.where(allowed, scores, masked_score)


def attend_forward(queries, key_heads, value_heads, bias_term, allowed):
    scores = attend_scores(queries, key_heads, bias_term, allowed)
    row_max = jnp.max(scores, axis=-1, keepdims=True)
    expanded = jnp.exp(scores - row_max)
    row_total = jnp.sum(expanded, axis=-1, keepdims=True)
    weights = (expanded / row_total).astype(jnp.bfloat16)
    mixed_heads = jnp.einsum(
        "shij,sjhe->sihe", weights, value_heads, preferred_element_type=jnp.float32
    )
    return (mixed_heads, row_max + jnp.log(row_total))


def attend_back(queries, key_heads, value_heads, bias_term, allowed, summary, grad_mixed):
    scores = attend_scores(queries, key_heads, bias_term, allowed)
    weights = jnp.exp(scores - summary)
    grad_weights = jnp.einsum(
        "sihe,sjhe->shij", grad_mixed, value_heads, preferred_element_type=jnp.float32
    )
    grad_values = jnp.einsum(
        "shij,sihe->sjhe",
        weights.astype(jnp.bfloat16),
        grad_mixed,
        preferred_element_type=jnp.float32,
    )
    grad_scores = (
        weights * (grad_weights - jnp.sum(weights * grad_weights, axis=-1, keepdims=True))
    ).astype(jnp.bfloat16)
    grad_queries = (
        jnp.einsum("shij,sjhe->sihe", grad_scores, key_heads, preferred_element_type=jnp.float32)
        * score_scale
    )
    grad_keys = (
        jnp.einsum("shij,sihe->sjhe", grad_scores, queries, preferred_element_type=jnp.float32)
        * score_scale
    )
    return (grad_queries, grad_keys, grad_values, grad_scores)


def forward_pass(gathered, bias_heads, hidden_seq, memory_seq, target_len, memory_len):
    qk_full, value_full, output_full, inner_full, outer_full, gain_full = gathered
    gain_rows = gain_full.astype(jnp.float32)
    sequences, length, model_width = hidden_seq.shape
    memory_span = memory_seq.shape[1]
    row_count = sequences * length
    residual = hidden_seq.astype(jnp.float32).reshape(row_count, model_width)
    memory_rows = memory_seq.reshape(sequences * memory_span, model_width)
    places = jnp.arange(length, dtype=jnp.int32)
    self_mask = (places[None, :] <= places[:, None])[None, None] & (
        places[None, None, None, :] < target_len[:, None, None, None]
    )
    memory_places = jnp.arange(memory_span, dtype=jnp.int32)
    cross_mask = (memory_places[None, :] < memory_len[:, None])[:, None, None, :]
    normed_first, unit_first, scale_first = normalize(residual, gain_rows[0])
    query_first = product(normed_first, qk_full[0]).astype(jnp.bfloat16)
    key_first = product(normed_first, qk_full[1]).astype(jnp.bfloat16)
    value_first = product(normed_first, value_full[0]).astype(jnp.bfloat16)
    mixed_first, summary_first = attend_forward(
        to_heads(query_first, sequences),
        to_heads(key_first, sequences),
        to_heads(value_first, sequences),
        bias_heads,
        self_mask,
    )
    mixed_first = mixed_first.reshape(row_count, model_width).astype(jnp.bfloat16)
    first_sum = residual + product(mixed_first, output_full[0])
    normed_second, unit_second, scale_second = normalize(first_sum, gain_rows[1])
    query_second = product(normed_second, qk_full[2]).astype(jnp.bfloat16)
    key_second = product(memory_rows, qk_full[3]).astype(jnp.bfloat16)
    value_second = product(memory_rows, value_full[1]).astype(jnp.bfloat16)
    mixed_second, summary_second = attend_forward(
        to_heads(query_second, sequences),
        to_heads(key_second, sequences),
        to_heads(value_second, sequences),
        0.0,
        cross_mask,
    )
    mixed_second = mixed_second.reshape(row_count, model_width).astype(jnp.bfloat16)
    second_sum = first_sum + product(mixed_second, output_full[1])
    normed_third, unit_third, scale_third = normalize(second_sum, gain_rows[2])
    inner_act = product(normed_third, inner_full)
    activated = jax.nn.gelu(inner_act, approximate=True).astype(jnp.bfloat16)
    produced = (second_sum + product(activated, outer_full)).astype(jnp.bfloat16)
    stored = (
        self_mask,
        cross_mask,
        memory_rows,
        normed_first,
        unit_first,
        scale_first,
        query_first,
        key_first,
        value_first,
        summary_first,
        mixed_first,
        normed_second,
        unit_second,
        scale_second,
        query_second,
        key_second,
        value_second,
        summary_second,
        mixed_second,
        normed_third,
        unit_third,
        scale_third,
        inner_act,
        activated,
    )
    return (stored, produced.reshape(sequences, length, model_width))


def backward_pass(gathered, bias_heads, stored, cotangent_seq, target_len):
    qk_full, value_full, output_full, inner_full, outer_full, gain_full = gathered
    gain_rows = gain_full.astype(jnp.float32)
    (
        self_mask,
        cross_mask,
        memory_rows,
        normed_first,
        unit_first,
        scale_first,
        query_first,
        key_first,
        value_first,
        summary_first,
        mixed_first,
        normed_second,
        unit_second,
        scale_second,
        query_second,
        key_second,
        value_second,
        summary_second,
        mixed_second,
        normed_third,
        unit_third,
        scale_third,
        inner_act,
        activated,
    ) = stored
    sequences, length, model_width = cotangent_seq.shape
    row_count = sequences * length
    places = jnp.arange(length, dtype=jnp.int32)
    live_rows = (places[None, :] < target_len[:, None]).astype(jnp.float32).reshape(row_count, 1)
    grad_out = cotangent_seq.astype(jnp.float32).reshape(row_count, model_width) * live_rows
    branch = grad_out.astype(jnp.bfloat16)
    outer_grad = product_over_rows(activated, branch)
    grad_act = product_transposed(branch, outer_full)
    unused_value, gelu_pull = jax.vjp(
        lambda inputs: jax.nn.gelu(inputs, approximate=True), inner_act
    )
    grad_inner = gelu_pull(grad_act)[0].astype(jnp.bfloat16)
    inner_grad = product_over_rows(normed_third, grad_inner)
    grad_from_third, gain_third = normalize_back(
        product_transposed(grad_inner, inner_full), unit_third, scale_third, gain_rows[2]
    )
    grad_second = grad_out + grad_from_third
    branch = grad_second.astype(jnp.bfloat16)
    output_grad_second = product_over_rows(mixed_second, branch)
    grad_mixed = product_transposed(branch, output_full[1]).astype(jnp.bfloat16)
    grad_query, grad_key, grad_value, unused_scores = attend_back(
        to_heads(query_second, sequences),
        to_heads(key_second, sequences),
        to_heads(value_second, sequences),
        0.0,
        cross_mask,
        summary_second,
        to_heads(grad_mixed, sequences),
    )
    grad_query = grad_query.reshape(row_count, model_width).astype(jnp.bfloat16)
    grad_key = grad_key.reshape(memory_rows.shape[0], model_width).astype(jnp.bfloat16)
    grad_value = grad_value.reshape(memory_rows.shape[0], model_width).astype(jnp.bfloat16)
    qk_grad_two = product_over_rows(normed_second, grad_query)
    qk_grad_three = product_over_rows(memory_rows, grad_key)
    value_grad_one = product_over_rows(memory_rows, grad_value)
    memory_grad = product_transposed(grad_key, qk_full[3]) + product_transposed(
        grad_value, value_full[1]
    )
    grad_from_second, gain_second = normalize_back(
        product_transposed(grad_query, qk_full[2]), unit_second, scale_second, gain_rows[1]
    )
    grad_first = grad_second + grad_from_second
    branch = grad_first.astype(jnp.bfloat16)
    output_grad_first = product_over_rows(mixed_first, branch)
    grad_mixed = product_transposed(branch, output_full[0]).astype(jnp.bfloat16)
    grad_query, grad_key, grad_value, grad_scores = attend_back(
        to_heads(query_first, sequences),
        to_heads(key_first, sequences),
        to_heads(value_first, sequences),
        bias_heads,
        self_mask,
        summary_first,
        to_heads(grad_mixed, sequences),
    )
    grad_query = grad_query.reshape(row_count, model_width).astype(jnp.bfloat16)
    grad_key = grad_key.reshape(row_count, model_width).astype(jnp.bfloat16)
    grad_value = grad_value.reshape(row_count, model_width).astype(jnp.bfloat16)
    qk_grad_zero = product_over_rows(normed_first, grad_query)
    qk_grad_one = product_over_rows(normed_first, grad_key)
    value_grad_zero = product_over_rows(normed_first, grad_value)
    grad_norm = (
        product_transposed(grad_query, qk_full[0])
        + product_transposed(grad_key, qk_full[1])
        + product_transposed(grad_value, value_full[0])
    )
    grad_from_first, gain_first = normalize_back(grad_norm, unit_first, scale_first, gain_rows[0])
    hidden_grad = grad_first + grad_from_first
    score_term = jnp.sum(grad_scores.astype(jnp.float32), axis=0)
    grad_terms = (
        jnp.stack([qk_grad_zero, qk_grad_one, qk_grad_two, qk_grad_three]),
        jnp.stack([value_grad_zero, value_grad_one]),
        jnp.stack([output_grad_first, output_grad_second]),
        inner_grad,
        outer_grad,
        jnp.stack([gain_first, gain_second, gain_third]),
    )
    return (
        grad_terms,
        score_term,
        hidden_grad.reshape(sequences, length, model_width),
        memory_grad.reshape(sequences, -1, model_width),
    )


def adam_step(master, first_moment, second_moment, gradient, rate, decay):
    first_next = beta_first * first_moment + (1.0 - beta_first) * gradient
    second_next = beta_second * second_moment + (1.0 - beta_second) * gradient * gradient
    corrected = (
        first_next
        / (1.0 - beta_first**STEP)
        / (jnp.sqrt(second_next / (1.0 - beta_second**STEP)) + adam_epsilon)
    )
    master_next = master - rate * (corrected + decay * master)
    return (master_next, first_next, second_next)


def shards(
    hidden,
    memory,
    cotangent,
    target_lengths,
    memory_lengths,
    qk_master,
    value_master,
    output_master,
    inner_master,
    outer_master,
    gain_master,
    table_master,
    qk_first,
    value_first,
    output_first,
    inner_first,
    outer_first,
    gain_first,
    table_first,
    qk_second,
    value_second,
    output_second,
    inner_second,
    outer_second,
    gain_second,
    table_second,
):
    micro_count = hidden.shape[0]
    length = hidden.shape[2]
    model_width = hidden.shape[3]
    hidden_units = inner_master.shape[1]
    qk_low = qk_master.astype(jnp.bfloat16)
    value_low = value_master.astype(jnp.bfloat16)
    output_low = output_master.astype(jnp.bfloat16)
    inner_low = inner_master.astype(jnp.bfloat16)
    outer_low = outer_master.astype(jnp.bfloat16)
    gain_low = gain_master.astype(jnp.bfloat16)
    onehot = bucket_onehot(length)
    bias_heads = jnp.einsum("bij,bh->hij", onehot, table_master, precision=highest)
    masters = (qk_master, value_master, output_master, inner_master, outer_master, gain_master)
    totals = (
        jnp.zeros((4, model_width, model_width), jnp.float32),
        jnp.zeros((2, model_width, model_width), jnp.float32),
        jnp.zeros((2, model_width, model_width), jnp.float32),
        jnp.zeros((model_width, hidden_units), jnp.float32),
        jnp.zeros((hidden_units, model_width), jnp.float32),
        jnp.zeros((3, model_width), jnp.float32),
    )
    reduced = tuple((jnp.zeros_like(master) for master in masters))
    score_total = jnp.zeros((HEADS, length, length), jnp.float32)
    produced_list = []
    hidden_list = []
    memory_list = []
    for micro_index in range(micro_count):
        gathered = (
            lax.all_gather(qk_low, ("dp", "fsdp"), axis=1, tiled=True),
            lax.all_gather(value_low, ("dp", "fsdp"), axis=1, tiled=True),
            lax.all_gather(output_low, ("dp", "fsdp"), axis=1, tiled=True),
            lax.all_gather(inner_low, ("dp", "fsdp"), axis=0, tiled=True),
            lax.all_gather(outer_low, ("dp", "fsdp"), axis=0, tiled=True),
            lax.all_gather(gain_low, ("dp", "fsdp"), axis=1, tiled=True),
        )
        stored, produced = forward_pass(
            gathered,
            bias_heads,
            hidden[micro_index],
            memory[micro_index],
            target_lengths[micro_index],
            memory_lengths[micro_index],
        )
        gathered = (
            lax.all_gather(qk_low, ("dp", "fsdp"), axis=1, tiled=True),
            lax.all_gather(value_low, ("dp", "fsdp"), axis=1, tiled=True),
            lax.all_gather(output_low, ("dp", "fsdp"), axis=1, tiled=True),
            lax.all_gather(inner_low, ("dp", "fsdp"), axis=0, tiled=True),
            lax.all_gather(outer_low, ("dp", "fsdp"), axis=0, tiled=True),
            lax.all_gather(gain_low, ("dp", "fsdp"), axis=1, tiled=True),
        )
        grad_terms, score_term, hidden_grad, memory_grad = backward_pass(
            gathered, bias_heads, stored, cotangent[micro_index], target_lengths[micro_index]
        )
        totals = tuple((running + addition for running, addition in zip(totals, grad_terms)))
        score_total = score_total + score_term
        produced_list.append(produced)
        hidden_list.append(hidden_grad)
        memory_list.append(memory_grad)
    reduced = (
        lax.psum_scatter(totals[0], ("dp", "fsdp"), scatter_dimension=1, tiled=True),
        lax.psum_scatter(totals[1], ("dp", "fsdp"), scatter_dimension=1, tiled=True),
        lax.psum_scatter(totals[2], ("dp", "fsdp"), scatter_dimension=1, tiled=True),
        lax.psum_scatter(totals[3], ("dp", "fsdp"), scatter_dimension=0, tiled=True),
        lax.psum_scatter(totals[4], ("dp", "fsdp"), scatter_dimension=0, tiled=True),
        lax.psum_scatter(totals[5], ("dp", "fsdp"), scatter_dimension=1, tiled=True),
    )
    table_grad = jnp.einsum("bij,hij->bh", onehot, score_total, precision=highest)
    table_grad = lax.psum(table_grad, ("dp", "fsdp"))
    all_masters = (
        qk_master,
        value_master,
        output_master,
        inner_master,
        outer_master,
        gain_master,
        table_master,
    )
    firsts = (
        qk_first,
        value_first,
        output_first,
        inner_first,
        outer_first,
        gain_first,
        table_first,
    )
    seconds = (
        qk_second,
        value_second,
        output_second,
        inner_second,
        outer_second,
        gain_second,
        table_second,
    )
    gradients = (reduced[0], reduced[1], reduced[2], reduced[3], reduced[4], reduced[5], table_grad)
    rates = (
        rate_matrix,
        rate_matrix,
        rate_matrix,
        rate_matrix,
        rate_matrix,
        rate_small,
        rate_small,
    )
    decays = (weight_decay, weight_decay, weight_decay, weight_decay, weight_decay, 0.0, 0.0)
    updated = [
        adam_step(
            all_masters[index],
            firsts[index],
            seconds[index],
            gradients[index],
            rates[index],
            decays[index],
        )
        for index in range(7)
    ]
    news = [entry[0] for entry in updated]
    first_news = [entry[1] for entry in updated]
    second_news = [entry[2] for entry in updated]
    copies = [entry.astype(jnp.bfloat16) for entry in news]
    layer_out = jnp.stack(produced_list)
    hidden_out = jnp.stack(hidden_list)
    memory_out = jnp.stack(memory_list)
    return (
        layer_out,
        hidden_out,
        memory_out,
        news[0],
        news[1],
        news[2],
        news[3],
        news[4],
        news[5],
        news[6],
        first_news[0],
        first_news[1],
        first_news[2],
        first_news[3],
        first_news[4],
        first_news[5],
        first_news[6],
        second_news[0],
        second_news[1],
        second_news[2],
        second_news[3],
        second_news[4],
        second_news[5],
        second_news[6],
        copies[0],
        copies[1],
        copies[2],
        copies[3],
        copies[4],
        copies[5],
        copies[6],
    )


MESH = pl.DeviceIdType.MESH
PAIRS = 6
ORDERS = ("ax", "ay", "ax", "ay", "ax", "ay", "cx", "cy")


class Place:
    def __init__(self, wa, wf):
        self.wa, self.wf = wa, wf
        dp, fs = lax.axis_index("dp"), lax.axis_index("fsdp")
        self.z, self.y = dp // 2, dp % 2
        self.x, self.c = fs // 2, fs % 2
        self.to = {
            "x": (dp, (1 - self.x) * 2 + self.c),
            "y": (self.z * 2 + 1 - self.y, fs),
            "c": (dp, self.x * 2 + 1 - self.c),
            "r": (dp + 2, fs),
            "l": (dp - 2, fs),
        }

    def enter(self):
        bar = pltpu.get_barrier_semaphore()

        def greet(way):
            pl.semaphore_signal(bar, inc=1, device_id=self.to[way], device_id_type=MESH)

        for way in ("x", "y", "c"):
            greet(way)

        @pl.when(self.z < 3)
        def _():
            greet("r")

        @pl.when(self.z > 0)
        def _():
            greet("l")

        inner = (self.z > 0) & (self.z < 3)

        @pl.when(inner)
        def _():
            pl.semaphore_wait(bar, 5)

        @pl.when(jnp.logical_not(inner))
        def _():
            pl.semaphore_wait(bar, 4)

    def pick(self, f, zs, ps, qs, core=None):
        c = self.c if core is None else core
        xs, ys = (ps, qs) if ORDERS[f][1] == "x" else (qs, ps)
        if f < PAIRS:
            return self.wa.at[2 * f + c, zs, ys, xs]
        return self.wf.at[zs, ys, xs, c, f - PAIRS]

    def own(self, f):
        return (self.x, self.y) if ORDERS[f][1] == "x" else (self.y, self.x)

    def ways(self, f):
        return ("x", "y") if ORDERS[f][1] == "x" else ("y", "x")


def push(place, src, dst, send, recv, way):
    pltpu.make_async_remote_copy(
        src_ref=src, dst_ref=dst, send_sem=send, recv_sem=recv,
        device_id=place.to[way], device_id_type=MESH,
    ).start()


def got(place, ref, sem, way):
    pltpu.make_async_remote_copy(
        src_ref=ref, dst_ref=ref, send_sem=sem, recv_sem=sem,
        device_id=place.to[way], device_id_type=MESH,
    ).wait_recv()


def left_out(place, ref, sem, way):
    pltpu.make_async_remote_copy(
        src_ref=ref, dst_ref=ref, send_sem=sem, recv_sem=sem,
        device_id=place.to[way], device_id_type=MESH,
    ).wait_send()


ALL = slice(None)


class Gather:
    def __init__(self, place, f, send, recv):
        self.k, self.f = place, f
        self.send, self.recv = send, recv
        self.first_cross = ORDERS[f][0] == "a"

    def do(self, name):
        if name[0] in "LR":
            self.step(int(name[1]), name[0])
        else:
            getattr(self, name)()

    def blk(self, zi):
        p, q = self.k.own(self.f)
        return self.k.pick(self.f, zi, ALL if self.first_cross else p, q)

    def move(self, ref, s, r, way):
        push(self.k, ref, ref, self.send.at[self.f, s], self.recv.at[self.f, r], way)

    def start(self):
        p, q = self.k.own(self.f)
        pw, qw = self.k.ways(self.f)
        if self.first_cross:
            self.move(self.k.pick(self.f, self.k.z, p, q), 0, 0, pw)
        else:
            self.spread(self.k.z, 1)

    def cross(self):
        p, q = self.k.own(self.f)
        pw, qw = self.k.ways(self.f)
        if self.first_cross:
            got(self.k, self.k.pick(self.f, self.k.z, 1 - p, q), self.recv.at[self.f, 0], pw)
            self.spread(self.k.z, 1)
        else:
            got(self.k, self.k.pick(self.f, ALL, 1 - p, q), self.recv.at[self.f, 0], pw)
            half = self.k.pick(self.f, ALL, ALL, q)
            self.move(half, 3, 7, qw)
            self.move(half, 4, 8, "c")

    def sideways(self, zi):
        pw, qw = self.k.ways(self.f)
        if self.first_cross:
            self.move(self.blk(zi), 3, 7, qw)
            self.move(self.blk(zi), 4, 8, "c")
        else:
            self.move(self.blk(zi), 0, 0, pw)

    def spread(self, zi, t):
        z = self.k.z

        @pl.when(z < 3)
        def _():
            self.move(self.blk(zi), 1, t, "r")

        @pl.when(z > 0)
        def _():
            self.move(self.blk(zi), 2, 3 + t, "l")

        self.sideways(zi)

    def step(self, t, side):
        z = self.k.z

        if side == "L":
            @pl.when(z >= t)
            def _():
                got(self.k, self.blk(z - t), self.recv.at[self.f, t], "l")

                if t < 3:
                    @pl.when(z < 3)
                    def _():
                        self.move(self.blk(z - t), 1, t + 1, "r")

                self.sideways(z - t)
        else:
            @pl.when(z <= 3 - t)
            def _():
                got(self.k, self.blk(z + t), self.recv.at[self.f, 3 + t], "r")

                if t < 3:
                    @pl.when(z > 0)
                    def _():
                        self.move(self.blk(z + t), 2, 3 + t + 1, "l")

                self.sideways(z + t)

    def second(self):
        p, q = self.k.own(self.f)
        pw, qw = self.k.ways(self.f)
        other = self.k.pick(self.f, ALL, ALL, 1 - q)
        got(self.k, other, self.recv.at[self.f, 7], qw)
        self.move(other, 4, 8, "c")

    def finish(self):
        theirs = self.k.pick(self.f, ALL, ALL, ALL, 1 - self.k.c)
        got(self.k, theirs, self.recv.at[self.f, 8], "c")

    def drain(self):
        p, q = self.k.own(self.f)
        pw, qw = self.k.ways(self.f)
        z, f = self.k.z, self.f
        some = (lambda n: self.k.pick(f, pl.ds(0, n), ALL if self.first_cross else p, q))
        first = self.k.pick(f, z, p, q) if self.first_cross else self.k.pick(f, ALL, p, q)
        left_out(self.k, first, self.send.at[f, 0], pw)
        for n in (1, 2, 3):
            @pl.when(z == n - 1)
            def _():
                left_out(self.k, some(n), self.send.at[f, 1], "r")

            @pl.when(z == 4 - n)
            def _():
                left_out(self.k, some(n), self.send.at[f, 2], "l")
        left_out(self.k, self.k.pick(f, ALL, ALL, q), self.send.at[f, 3], qw)
        left_out(self.k, self.k.pick(f, ALL, ALL, ALL), self.send.at[f, 4], "c")


def add_into(dst, srcs, lead):
    sizes = lead
    count = 1
    for s in sizes:
        count *= s

    def body(i, _):
        idx, rest = [], i
        for s in reversed(sizes):
            idx.append(rest % s)
            rest = rest // s
        idx = tuple(reversed(idx)) or Ellipsis
        total = dst[idx].astype(jnp.float32)
        for src in srcs:
            total = total + src[idx].astype(jnp.float32)
        dst[idx] = total.astype(jnp.bfloat16)
        return 0

    lax.fori_loop(0, count, body, 0)


class Scatter:
    def __init__(self, place, f, send, recv, slots, final, result, credit):
        self.k, self.f = place, f
        self.wait_credit, self.give_credit, self.credit = credit
        self.send, self.recv = send, recv
        self.rd, self.rq, self.rp, self.rl, self.rr = slots
        self.final, self.result = final, result
        self.wide = ORDERS[f][0] == "a"

    def do(self, name):
        if name[0] == "z":
            self.step_in(int(name[1]))
        else:
            getattr(self, name)()

    def move(self, src, dst, s, way):
        push(self.k, src, dst, self.send.at[self.f, s], self.recv.at[self.f, s], way)

    def blk(self, zi):
        p, q = self.k.own(self.f)
        return self.k.pick(self.f, zi, ALL if self.wide else p, q)

    def start(self):
        if self.wait_credit:
            pl.semaphore_wait(self.credit, 1)
        self.move(self.k.pick(self.f, ALL, ALL, ALL, 1 - self.k.c), self.rd, 0, "c")

    def rpick(self, ps, qs):
        xs, ys = (ps, qs) if ORDERS[self.f][1] == "x" else (qs, ps)
        return self.rd.at[:, ys, xs]

    def core(self):
        p, q = self.k.own(self.f)
        pw, qw = self.k.ways(self.f)
        got(self.k, self.rd, self.recv.at[self.f, 0], "c")
        away = self.k.pick(self.f, ALL, ALL, 1 - q)
        add_into(away, [self.rpick(ALL, 1 - q)], (4, 2))
        self.move(away, self.rq, 1, qw)

    def half(self):
        p, q = self.k.own(self.f)
        pw, qw = self.k.ways(self.f)
        got(self.k, self.rq, self.recv.at[self.f, 1], qw)
        add_into(self.k.pick(self.f, ALL, ALL, q), [self.rpick(ALL, q), self.rq], (4, 2))
        if self.give_credit:
            pl.semaphore_signal(self.credit, inc=1, device_id=self.k.to["c"], device_id_type=MESH)
        if self.wide:
            self.step_out(1)
        else:
            self.move(self.k.pick(self.f, ALL, 1 - p, q), self.rp, 2, pw)

    def cross_in(self):
        p, q = self.k.own(self.f)
        pw, qw = self.k.ways(self.f)
        got(self.k, self.rp, self.recv.at[self.f, 2], pw)
        add_into(self.k.pick(self.f, ALL, p, q), [self.rp], (4,))
        self.step_out(1)

    def step_out(self, t):
        z = self.k.z

        @pl.when(z <= t - 1)
        def _():
            self.move(self.blk(z + 4 - t), self.rl.at[t - 1], 2 + t, "r")

        @pl.when(z >= 4 - t)
        def _():
            self.move(self.blk(z - 4 + t), self.rr.at[t - 1], 5 + t, "l")

    def step_in(self, t):
        z, f = self.k.z, self.f
        lead = (2,) if self.wide else ()

        @pl.when((z >= 1) & (z <= t))
        def _():
            got(self.k, self.rl.at[t - 1], self.recv.at[f, 2 + t], "l")
            add_into(self.blk(z + 3 - t), [self.rl.at[t - 1]], lead)

        @pl.when((z <= 2) & (z >= 3 - t))
        def _():
            got(self.k, self.rr.at[t - 1], self.recv.at[f, 5 + t], "r")
            add_into(self.blk(z - 3 + t), [self.rr.at[t - 1]], lead)

        if t < 3:
            self.step_out(t + 1)
        else:
            p, q = self.k.own(f)
            pw, qw = self.k.ways(f)
            if self.wide:
                self.move(self.k.pick(f, z, 1 - p, q), self.rp, 2, pw)
            else:
                self.total(None)

    def last(self):
        pw, qw = self.k.ways(self.f)
        got(self.k, self.rp, self.recv.at[self.f, 2], pw)
        self.total(self.rp)

    def total(self, more):
        p, q = self.k.own(self.f)
        c = self.k.c
        mine = self.k.pick(self.f, self.k.z, p, q)[...].astype(jnp.float32)
        if more is not None:
            mine = mine + more[...].astype(jnp.float32)
        if self.f < PAIRS:
            self.final[...] = mine
            kept = pl.ds(pl.multiple_of(c * 24, 8), 24)
            away = pl.ds(pl.multiple_of(24 - c * 24, 8), 24)
            self.move(self.final.at[away], self.result.at[2 * self.f + c], 9, "c")
            self.result[2 * self.f + c] = self.final[kept]
        else:
            self.final[...] = mine

    def finish(self):
        if self.f < PAIRS:
            got(self.k, self.result.at[2 * self.f + 1 - self.k.c], self.recv.at[self.f, 9], "c")

    def drain(self):
        p, q = self.k.own(self.f)
        pw, qw = self.k.ways(self.f)
        z, f, k = self.k.z, self.f, self.k
        left_out(k, self.rd, self.send.at[f, 0], "c")
        left_out(k, self.rq, self.send.at[f, 1], qw)
        left_out(k, self.rp, self.send.at[f, 2], pw)
        for t in (1, 2, 3):
            @pl.when(z <= t - 1)
            def _():
                left_out(k, self.rl.at[t - 1], self.send.at[f, 2 + t], "r")

            @pl.when(z >= 4 - t)
            def _():
                left_out(k, self.rr.at[t - 1], self.send.at[f, 5 + t], "l")
        if f < PAIRS:
            left_out(k, self.final.at[pl.ds(0, 24)], self.send.at[f, 9], "c")


class Line:
    def __init__(self, place, buf, send, recv):
        self.k, self.buf, self.send, self.recv = place, buf, send, recv

    def move(self, zi, s, r, way):
        push(self.k, self.buf.at[zi], self.buf.at[zi], self.send.at[s], self.recv.at[r], way)

    def start(self):
        z = self.k.z

        @pl.when(z < 3)
        def _():
            self.move(z, 3, 3, "r")

        @pl.when(z > 0)
        def _():
            self.move(z, 6, 6, "l")

    def step(self, t):
        z = self.k.z

        @pl.when(z >= t)
        def _():
            got(self.k, self.buf.at[z - t], self.recv.at[2 + t], "l")

            if t < 3:
                @pl.when(z < 3)
                def _():
                    self.move(z - t, 3 + t, 3 + t, "r")

        @pl.when(z <= 3 - t)
        def _():
            got(self.k, self.buf.at[z + t], self.recv.at[5 + t], "r")

            if t < 3:
                @pl.when(z > 0)
                def _():
                    self.move(z + t, 6 + t, 6 + t, "l")

    def drain(self):
        z = self.k.z
        for t in range(3):
            @pl.when((z < 3) & (z >= t))
            def _():
                left_out(self.k, self.buf.at[0], self.send.at[3 + t], "r")

            @pl.when((z > 0) & (z <= 3 - t))
            def _():
                left_out(self.k, self.buf.at[0], self.send.at[6 + t], "l")


class Gains:
    def __init__(self, place, buf, send, recv):
        self.k, self.buf, self.send, self.recv = place, buf, send, recv
        self.line = Line(place, buf, send, recv)
        z, y, x, c = place.z, place.y, place.x, place.c
        self.mine = [buf.at[z, y, x, c], buf.at[z, y, x], buf.at[z, y]]
        self.other = [buf.at[z, y, x, 1 - c], buf.at[z, y, 1 - x], buf.at[z, 1 - y]]

    def go(self, i):
        if 1 <= i <= 3:
            got(self.k, self.other[i - 1], self.recv.at[i - 1], "cxy"[i - 1])
        if i < 3:
            push(self.k, self.mine[i], self.mine[i], self.send.at[i], self.recv.at[i], "cxy"[i])
        elif i == 3:
            self.line.start()
        else:
            self.line.step(i - 3)

    def drain(self):
        for i in range(3):
            left_out(self.k, self.mine[i], self.send.at[i], "cxy"[i])
        self.line.drain()


class Small:
    def __init__(self, place, bufs, got_bufs, along, send, recv):
        self.k, self.bufs, self.got_bufs, self.along = place, bufs, got_bufs, along
        self.send, self.recv = send, recv
        self.line = Line(place, along, send, recv)

    def go(self, i):
        if 1 <= i <= 3:
            got(self.k, self.got_bufs.at[i - 1], self.recv.at[i - 1], "cxy"[i - 1])
            total = self.bufs[i - 1] + self.got_bufs[i - 1]
            if i < 3:
                self.bufs[i] = total
            else:
                self.along[self.k.z] = total
        if i < 3:
            push(self.k, self.bufs.at[i], self.got_bufs.at[i], self.send.at[i], self.recv.at[i], "cxy"[i])
        elif i == 3:
            self.line.start()
        else:
            self.line.step(i - 3)

    def drain(self):
        for i in range(3):
            left_out(self.k, self.bufs.at[i], self.send.at[i], "cxy"[i])
        self.line.drain()
BF, F32 = jnp.bfloat16, jnp.float32
ROOT = math.sqrt(2.0 / math.pi)
CUBE = 0.044715


def dot_nn(a, b):
    return lax.dot_general(a, b, (((1,), (0,)), ((), ())), preferred_element_type=F32)


def dot_nt(a, b):
    return lax.dot_general(a, b, (((1,), (1,)), ((), ())), preferred_element_type=F32)


def dot_tn(a, b):
    return lax.dot_general(a, b, (((0,), (0,)), ((), ())), preferred_element_type=F32)


def unit_of(values):
    scale = lax.rsqrt(jnp.mean(values * values, axis=-1, keepdims=True) + epsilon_norm)
    return values * scale, scale


class Layer:
    def __init__(self, wa, wf, b):
        self.wa, self.wf, self.b = wa, wf, b

    def cols(self, u, t):
        return self.wa[u, :, :, :, :, pl.ds(pl.multiple_of(256 * t, 256), 256)].reshape(768, 256)

    def half_rows(self, u, t):
        return self.wa[u, pl.ds(2 * t, 2)].reshape(384, 768)

    def times(self, a, u, put):
        def body(t, _):
            put(pl.ds(pl.multiple_of(256 * t, 256), 256), dot_nn(a[...], self.cols(u, t)))
            return 0

        lax.fori_loop(0, 3, body, 0)

    def times_back(self, pairs, put):
        def body(t, _):
            total = None
            for a, u in pairs:
                term = dot_nt(a[...], self.half_rows(u, t))
                total = term if total is None else total + term
            put(pl.ds(pl.multiple_of(384 * t, 384), 384), total)
            return 0

        lax.fori_loop(0, 2, body, 0)

    def weight_grad(self, a, d, u):
        def body(t, _):
            tile = a[:, pl.ds(pl.multiple_of(384 * t, 384), 384)]
            self.wa[u, pl.ds(2 * t, 2)] = dot_tn(tile, d[...]).astype(BF).reshape(2, 2, 2, 48, 768)
            return 0

        lax.fori_loop(0, 2, body, 0)

    def project(self, a, u, dst):
        def put(tile, value):
            dst[:, tile] = value.astype(BF)

        self.times(a, u, put)

    def add_project(self, base, a, u, dst):
        def put(tile, value):
            dst[:, tile] = base[:, tile].astype(F32) + value

        self.times(a, u, put)

    def norm(self, src, g, dst):
        gain = self.b["gain"][pl.ds(g, 1), :]

        def body(i, _):
            rows = pl.ds(pl.multiple_of(64 * i, 64), 64)
            unit, _unused = unit_of(src[rows].astype(F32))
            dst[rows] = (unit * gain).astype(BF)
            return 0

        lax.fori_loop(0, 8, body, 0)

    def norm_back(self, dn, src, g, base, dst, low):
        gain = self.b["gain"][pl.ds(g, 1), :]

        def body(i, acc):
            rows = pl.ds(pl.multiple_of(64 * i, 64), 64)
            unit, scale = unit_of(src[rows].astype(F32))
            grad = dn[rows]
            acc = acc + jnp.sum(grad * unit, axis=0, keepdims=True)
            pulled = grad * gain
            value = base(rows, i) + scale * (pulled - unit * jnp.mean(pulled * unit, axis=-1, keepdims=True))
            dst[rows] = value
            if low is not None:
                low[rows] = value.astype(BF)
            return acc

        total = lax.fori_loop(0, 8, body, jnp.zeros((1, 768), F32))
        for i in range(3):
            self.b["small"][3 * g + i:3 * g + i + 1, :] = total[:, 256 * i:256 * i + 256]

    def head_masks(self):
        lane = lax.broadcasted_iota(jnp.int32, (1, 128), 1)
        low = (lane < 64).astype(F32)
        return low.astype(BF), (1.0 - low).astype(BF)

    def allowed(self, s, kind):
        row = lax.broadcasted_iota(jnp.int32, (256, 256), 0)
        col = lax.broadcasted_iota(jnp.int32, (256, 256), 1)
        if kind == 1:
            return (col <= row) & (col < self.b["lens"][s])
        return col < self.b["lens"][2 + s]

    def bias(self, head):
        row = self.b["bias_row"][pl.ds(head, 1), :]
        return pltpu.roll(jnp.broadcast_to(row, (256, 256)), 0, axis=1, stride=1, stride_axis=0)

    def weights(self, queries, keys, bias, allowed):
        scores = dot_nt(queries, keys) * score_scale
        if bias is not None:
            scores = scores + bias
        scores = jnp.where(allowed, scores, masked_score)
        expanded = jnp.exp(scores - jnp.max(scores, axis=-1, keepdims=True))
        return expanded / jnp.sum(expanded, axis=-1, keepdims=True)

    def attend(self, kind, first, last):
        b = self.b
        q, k, v, o = (b[n + str(kind)] for n in "qkvo")
        masks = self.head_masks()
        keep = masks[0].astype(F32)

        def body(i, _):
            hp, s = i // 2, i % 2
            lanes = pl.ds(pl.multiple_of(128 * hp, 128), 128)
            rows = pl.ds(pl.multiple_of(256 * s, 256), 256)
            queries, keys, values = q[rows, lanes], k[rows, lanes], v[rows, lanes]
            allowed = self.allowed(s, kind)
            mixed = []
            for e in range(2):
                bias = self.bias(2 * hp + e) if kind == 1 else None
                p = self.weights(queries * masks[e], keys, bias, allowed)
                mixed.append(dot_nn(p.astype(BF), values))
            o[rows, lanes] = (mixed[0] * keep + mixed[1] * (1.0 - keep)).astype(BF)
            return 0

        lax.fori_loop(2 * first, 2 * last, body, 0)

    def attend_back(self, kind, first, last):
        b = self.b
        q, k, v = (b[n + str(kind)] for n in "qkv")
        masks = self.head_masks()
        row = lax.broadcasted_iota(jnp.int32, (256, 256), 0)
        col = lax.broadcasted_iota(jnp.int32, (256, 256), 1)
        flip = (row + col == 255).astype(F32).astype(BF)

        def body(i, _):
            hp, s = i // 2, i % 2
            lanes = pl.ds(pl.multiple_of(128 * hp, 128), 128)
            rows = pl.ds(pl.multiple_of(256 * s, 256), 256)
            queries, keys, values = q[rows, lanes], k[rows, lanes], v[rows, lanes]
            given = b["do"][rows, lanes]
            allowed = self.allowed(s, kind)
            dq = dk = dv = None
            for e in range(2):
                bias = self.bias(2 * hp + e) if kind == 1 else None
                qe = queries * masks[e]
                ge = given * masks[e]
                p = self.weights(qe, keys, bias, allowed)
                dp = dot_nt(ge, values)
                ds = (p * (dp - jnp.sum(p * dp, axis=-1, keepdims=True))).astype(BF)
                if kind == 1:
                    turned = pltpu.roll(dot_nn(flip, ds), 0, axis=1, stride=1, stride_axis=0)
                    b["small"][pl.ds(9 + 2 * hp + e, 1), :] += jnp.sum(turned, axis=0, keepdims=True)
                terms = (dot_nn(ds, keys * masks[e]), dot_tn(ds, qe), dot_tn(p.astype(BF), ge))
                if dq is None:
                    dq, dk, dv = terms
                else:
                    dq, dk, dv = dq + terms[0], dk + terms[1], dv + terms[2]
            q[rows, lanes] = (dq * score_scale).astype(BF)
            k[rows, lanes] = (dk * score_scale).astype(BF)
            v[rows, lanes] = dv.astype(BF)
            return 0

        lax.fori_loop(2 * first, 2 * last, body, 0)

    def live(self, i):
        row = lax.broadcasted_iota(jnp.int32, (64, 1), 0) + 64 * lax.rem(i, 4)
        bound = jnp.where(i < 4, self.b["lens"][0], self.b["lens"][1])
        return (row < bound).astype(F32)

    def cotangent(self):
        b = self.b

        def body(i, _):
            rows = pl.ds(pl.multiple_of(64 * i, 64), 64)
            b["df"][rows] = (b["cot"][rows].astype(F32) * self.live(i)).astype(BF)
            return 0

        lax.fori_loop(0, 8, body, 0)

    def ffn_act(self, j):
        b = self.b

        def body(t, _):
            cols = pl.ds(pl.multiple_of(384 * t, 384), 384)
            wi = self.wa[8 + j, :, :, :, :, cols].reshape(768, 384)
            wf = self.wf[j, t].reshape(384, 768)
            u = dot_nn(b["n3"][...], wi)
            square = u * u
            th = jnp.tanh(ROOT * (u + CUBE * (u * square)))
            half = 0.5 * (1.0 + th)
            b["act"][:, cols] = (u * half).astype(BF)
            slope = half + (0.5 * ROOT) * u * (1.0 - th * th) * (1.0 + (3.0 * CUBE) * square)
            da = dot_nt(b["df"][...], wf)
            b["du"][:, cols] = (da * slope).astype(BF)
            return 0

        lax.fori_loop(0, 2, body, 0)

    def ffn_out(self, j):
        b = self.b

        def body(t, _):
            cols = pl.ds(pl.multiple_of(256 * t, 256), 256)
            wf = self.wf[j, :, :, :, :, :, cols].reshape(768, 256)
            b["y"][:, cols] += dot_nn(b["act"][...], wf)
            return 0

        lax.fori_loop(0, 3, body, 0)

    def ffn_back(self, j):
        b = self.b

        def put(tile, value):
            if j == 0:
                b["dn"][:, tile] = value
            else:
                b["dn"][:, tile] += value

        self.times_back([(b["du"], 8 + j)], put)

    def ffn_grads(self, j):
        b = self.b

        def body(t, _):
            tile = b["act"][:, pl.ds(pl.multiple_of(384 * t, 384), 384)]
            self.wf[j, t] = dot_tn(tile, b["df"][...]).astype(BF).reshape(2, 2, 2, 48, 768)
            return 0

        lax.fori_loop(0, 2, body, 0)
        self.weight_grad(b["n3"], b["du"], 8 + j)


SCATTER_ORDER = (4, 5, 6, 7, 3, 2, 1, 0)


def layer_kernel(
    program, lens, hid, mem, cot, masters, outer, gain_tile, spread, owner, bias_row,
    low_out, hidden_grad, memory_grad, res, last, small_out,
    wa, wf, n1, q1, k1, v1, o1, n2, q2, k2, v2, o2, n3, act, du, df, x1, x2, dn,
    rd, rq, rlw, rrw, rpw, rln, rrn, rpn, fin, tiles, gain, small, small_got, along,
    gs, gr, ss, sr, xs, xr, ks, kr, ms, mr, credit,
):
    k = Place(wa, wf)
    z, y, x, c = k.z, k.y, k.x, k.c
    b = dict(
        lens=lens, hid=hid, mem=mem, cot=cot, bias_row=bias_row, gain=gain, small=small.at[0],
        n1=n1, q1=q1, k1=k1, v1=v1, o1=o1, n2=n2, q2=q2, k2=k2, v2=v2, o2=o2, n3=n3,
        act=act, du=du, df=df, do=act, y=memory_grad, dn=dn,
    )
    net = Layer(wa, wf, b)
    gathers = [Gather(k, f, gs, gr) for f in range(8)]
    scatters = {}
    for i, f in enumerate(SCATTER_ORDER):
        if f < PAIRS:
            slots = (rd.at[i % 4], rq.at[f], rpw.at[f], rlw.at[f], rrw.at[f])
        else:
            slots = (rd.at[i % 4], rq.at[f], rpn.at[f - PAIRS], rln.at[f - PAIRS], rrn.at[f - PAIRS])
        final = fin.at[f] if f < PAIRS else last.at[f - PAIRS]
        scatters[f] = Scatter(k, f, ss, sr, slots, final, res, (i >= 4, i < 4, credit))
    gains = Gains(k, tiles, ks, kr)
    sums = Small(k, small, small_got, along, ms, mr)
    mine = pl.ds(pl.multiple_of(24 * c, 8), 24)
    other = pl.ds(pl.multiple_of(24 - 24 * c, 8), 24)

    def enter():
        k.enter()
        push(k, masters.at[:, 1 - c], fin.at[:, mine], xs, xr, "c")
        tiles[z, y, x, c] = gain_tile[...].astype(BF).astype(F32)
        gains.go(0)
        for h in range(2):
            wf[z, y, x, c, h] = outer[48 * h:48 * h + 48].astype(BF)
        for p in range(PAIRS):
            fin[p, mine] = masters[p, c]

    def swap():
        got(k, fin.at[:, other], xr, "c")

    def own(f):
        if f < PAIRS:
            wa[2 * f + c, z, y, x] = fin[f].astype(BF)
        gathers[f].start()

    def spread_gains():
        flat = tiles[...].reshape(32, 8, 128)
        for g in range(3):
            lanes = dot_nn(flat[:, g].astype(BF), spread[...])
            gain[g:g + 1, :] = jnp.sum(lanes * owner[...], axis=0, keepdims=True)

    def put_do(tile, value):
        act[:, tile] = value.astype(BF)

    def put_dn(tile, value):
        dn[:, tile] = value

    def put_memory(tile, value):
        memory_grad[:, tile] = value

    def begin():
        memory_grad[...] = x2[...]
        small[0] = jnp.zeros_like(small[0])
        net.cotangent()

    def finish_low():
        low_out[...] = memory_grad[...].astype(BF)

    def total_small():
        small_out[...] = along[0] + along[1] + along[2] + along[3]

    grad = hidden_grad
    tasks = {
        "gain": spread_gains,
        "n1": lambda: net.norm(hid, 0, n1),
        "q1": lambda: net.project(n1, 0, q1),
        "k1": lambda: net.project(n1, 1, k1),
        "v1": lambda: net.project(n1, 2, v1),
        "o1": lambda: net.add_project(hid, o1, 3, x1),
        "n2": lambda: net.norm(x1, 1, n2),
        "k2": lambda: net.project(mem, 4, k2),
        "v2": lambda: net.project(mem, 5, v2),
        "q2": lambda: net.project(n2, 6, q2),
        "o2": lambda: net.add_project(x1, o2, 7, x2),
        "n3": lambda: net.norm(x2, 2, n3),
        "begin": begin,
        "low": finish_low,
        "nb3": lambda: net.norm_back(dn, x2, 2, lambda rows, i: cot[rows].astype(F32) * net.live(i), grad, df),
        "do2": lambda: net.times_back([(df, 7)], put_do),
        "w7": lambda: net.weight_grad(o2, df, 7),
        "dn2": lambda: net.times_back([(q2, 6)], put_dn),
        "w6": lambda: net.weight_grad(n2, q2, 6),
        "mg": lambda: net.times_back([(k2, 4), (v2, 5)], put_memory),
        "w4": lambda: net.weight_grad(mem, k2, 4),
        "w5": lambda: net.weight_grad(mem, v2, 5),
        "nb2": lambda: net.norm_back(dn, x1, 1, lambda rows, i: grad[rows], grad, df),
        "do1": lambda: net.times_back([(df, 3)], put_do),
        "w3": lambda: net.weight_grad(o1, df, 3),
        "dn1": lambda: net.times_back([(q1, 0), (k1, 1), (v1, 2)], put_dn),
        "w0": lambda: net.weight_grad(n1, q1, 0),
        "w1": lambda: net.weight_grad(n1, k1, 1),
        "w2": lambda: net.weight_grad(n1, v1, 2),
        "nb1": lambda: net.norm_back(dn, hid, 0, lambda rows, i: grad[rows], grad, None),
    }
    families = {
        "act": net.ffn_act, "out": net.ffn_out, "back": net.ffn_back, "grads": net.ffn_grads,
        "A1": lambda i: net.attend(1, 2 * i, 2 * i + 2),
        "A2": lambda i: net.attend(2, 2 * i, 2 * i + 2),
        "B1": lambda i: net.attend_back(1, 2 * i, 2 * i + 2),
        "B2": lambda i: net.attend_back(2, 2 * i, 2 * i + 2),
    }
    enter()
    for kind, index, name in program:
        if kind == "G":
            if name == "own":
                own(index)
            else:
                gathers[index].do(name)
        elif kind == "S":
            scatters[index].do(name)
        elif kind == "K":
            gains.go(index)
        elif kind == "R":
            if index < 7:
                sums.go(index)
            else:
                total_small()
        elif kind == "X":
            swap()
        elif name in tasks:
            tasks[name]()
        else:
            families[name](index)
    left_out(k, masters.at[:, 1 - c], xs, "c")
    gains.drain()
    sums.drain()
    for f in SCATTER_ORDER:
        scatters[f].drain()


def run_layer(program, lens, hid, mem, cot, masters, outer, gain_tile, spread, owner, bias_row):
    vm, sm = pl.BlockSpec(memory_space=pltpu.VMEM), pl.BlockSpec(memory_space=pltpu.SMEM)
    low, wide = pltpu.VMEM((512, 768), BF), pltpu.VMEM((512, 768), F32)
    dma = pltpu.SemaphoreType.DMA
    shape = jax.ShapeDtypeStruct
    return pl.pallas_call(
        functools.partial(layer_kernel, program),
        out_shape=(
            shape((512, 768), BF), shape((512, 768), F32), shape((512, 768), F32),
            shape((12, 24, 768), F32), shape((2, 48, 768), F32), shape((24, 256), F32),
        ),
        in_specs=[sm] + [vm] * 9,
        out_specs=[vm] * 6,
        scratch_shapes=[
            pltpu.VMEM((12, 4, 2, 2, 48, 768), BF),
            pltpu.VMEM((4, 2, 2, 2, 2, 48, 768), BF),
            *[low] * 14, *[wide] * 3,
            pltpu.VMEM((4, 4, 2, 2, 48, 768), BF),
            pltpu.VMEM((8, 4, 2, 48, 768), BF),
            pltpu.VMEM((6, 3, 2, 48, 768), BF),
            pltpu.VMEM((6, 3, 2, 48, 768), BF),
            pltpu.VMEM((6, 48, 768), BF),
            pltpu.VMEM((2, 3, 48, 768), BF),
            pltpu.VMEM((2, 3, 48, 768), BF),
            pltpu.VMEM((2, 4, 48, 768), BF),
            pltpu.VMEM((6, 48, 768), F32),
            pltpu.VMEM((4, 2, 2, 2, 8, 128), F32),
            pltpu.VMEM((8, 768), F32),
            pltpu.VMEM((3, 24, 256), F32),
            pltpu.VMEM((3, 24, 256), F32),
            pltpu.VMEM((4, 24, 256), F32),
            dma((8, 5)), dma((8, 9)), dma((8, 10)), dma((8, 10)), dma, dma,
            dma((9,)), dma((9,)), dma((9,)), dma((9,)),
            pltpu.SemaphoreType.REGULAR,
        ],
        compiler_params=pltpu.CompilerParams(
            collective_id=0, has_side_effects=True, vmem_limit_bytes=63 * 2**20
        ),
    )(lens, hid, mem, cot, masters, outer, gain_tile, spread, owner, bias_row)


def simple_program():
    prog = [("K", 1, ""), ("X", 0, "")]
    prog += [("G", f, "own") for f in range(8)]
    prog += [("K", 2, ""), ("K", 3, ""), ("T", 0, "n1")][:2]
    for name in ("cross", "L1", "R1", "L2", "R2", "L3", "R3"):
        prog += [("G", f, name) for f in range(6)]
        if name != "cross":
            prog += [("G", f, name) for f in (6, 7)]
    prog += [("G", f, "cross") for f in (6, 7)]
    prog += [("K", 4, ""), ("K", 5, ""), ("K", 6, ""), ("T", 0, "gain")]
    prog += [("G", f, "second") for f in range(8)] + [("G", f, "finish") for f in range(8)]
    prog += [("G", f, "drain") for f in range(8)]
    task = lambda *names: [("T", 0, n) for n in names]
    many = lambda name, n: [("T", i, name) for i in range(n)]
    prog += task("n1", "q1", "k1", "v1") + many("A1", 3) + task("o1", "n2", "k2", "v2", "q2") + many("A2", 3)
    prog += task("o2", "n3", "begin")
    for j in range(4):
        prog += [("T", j, n) for n in ("act", "out", "back", "grads")]
        if j == 1:
            prog += [("S", 4, "start")]
    prog += [("S", f, "start") for f in (5, 6, 7)]
    prog += task("low", "nb3", "do2", "w7") + many("B2", 3) + task("dn2", "w6")
    for s in ("core", "half"):
        prog += [("S", f, s) for f in (4, 5, 6, 7)]
    prog += [("S", 3, "start")] + task("mg", "w4", "w5") + [("S", 2, "start")]
    prog += task("nb2", "do1", "w3") + many("B1", 3) + task("dn1", "w2") + [("S", 1, "start")]
    prog += task("w0", "w1") + [("S", 0, "start")] + task("nb1") + [("R", 0, "")]
    for s in ("core", "half"):
        prog += [("S", f, s) for f in (3, 2, 1, 0)]
    prog += [("S", f, "cross_in") for f in (6, 7)]
    for s in ("z1", "z2", "z3"):
        prog += [("S", f, s) for f in SCATTER_ORDER]
        prog += [("R", int(s[1]), "")]
    prog += [("S", f, "last") for f in SCATTER_ORDER if f < 6]
    prog += [("S", f, "finish") for f in SCATTER_ORDER] + [("R", i, "") for i in range(4, 8)]
    return tuple(prog)


def shards_block(
    hidden, memory, cotangent, target_lengths, memory_lengths,
    qk_master, value_master, output_master, inner_master, outer_master, gain_master, table_master,
    qk_first, value_first, output_first, inner_first, outer_first, gain_first, table_first,
    qk_second, value_second, output_second, inner_second, outer_second, gain_second, table_second,
):
    axes = ("dp", "fsdp")
    inner4 = inner_master.reshape(24, 4, 768).transpose(1, 0, 2)
    m = jnp.concatenate(
        [qk_master[0:2], value_master[0:1], output_master[0:1], qk_master[3:4], value_master[1:2],
         qk_master[2:3], output_master[1:2], inner4]
    ).reshape(6, 2, 24, 768)
    gain_tile = jnp.zeros((8, 128), F32).at[:3, :24].set(gain_master)
    place = jnp.arange(768)
    spread = (place[None, :] % 24 == jnp.arange(128)[:, None]).astype(BF)
    owner = (place[None, :] // 24 == jnp.arange(32)[:, None]).astype(F32)
    by_distance = bucket_onehot(256)[:, :, 0]
    row = jnp.einsum("bd,bh->hd", by_distance, table_master, precision=highest)
    bias_row = jnp.zeros((16, 256), F32).at[:HEADS].set(jnp.roll(row[:, ::-1], 1, axis=1))
    lens = jnp.concatenate([target_lengths[:, 0], memory_lengths[:, 0]])
    flat = lambda a: a.reshape(512, 768)
    low_out, hidden_grad, memory_grad, res, last, small = run_layer(
        simple_program(), lens, flat(hidden), flat(memory), flat(cotangent), m, outer_master,
        gain_tile, spread, owner, bias_row,
    )
    device = lax.axis_index(axes)
    gain_grad = lax.dynamic_slice(small[:9].reshape(3, 768), (0, 24 * device), (3, 24))
    table_grad = jnp.einsum("bd,hd->bh", by_distance, small[9:21, ::-1], precision=highest)
    gradients = (
        jnp.stack([res[0], res[1], res[6], res[4]]),
        jnp.stack([res[2], res[5]]),
        jnp.stack([res[3], res[7]]),
        res[8:12].transpose(1, 0, 2).reshape(24, 3072),
        last.reshape(96, 768),
        gain_grad,
        table_grad,
    )
    masters = (qk_master, value_master, output_master, inner_master, outer_master, gain_master, table_master)
    firsts = (qk_first, value_first, output_first, inner_first, outer_first, gain_first, table_first)
    seconds = (qk_second, value_second, output_second, inner_second, outer_second, gain_second, table_second)
    updated = [
        adam_step(a, b, c, g, rate_matrix if i < 5 else rate_small, weight_decay if i < 5 else 0.0)
        for i, (a, b, c, g) in enumerate(zip(masters, firsts, seconds, gradients))
    ]
    whole = lambda a: a.reshape(2, 1, 256, 768)
    return (
        whole(low_out),
        whole(hidden_grad),
        whole(memory_grad),
        *[u[0] for u in updated],
        *[u[1] for u in updated],
        *[u[2] for u in updated],
        *[u[0].astype(BF) for u in updated],
    )


def solution(mesh):
    placed = (
        P(None, ("dp", "fsdp"), None, None),
        P(None, ("dp", "fsdp"), None, None),
        P(None, ("dp", "fsdp"), None, None),
        P(None, ("dp", "fsdp")),
        P(None, ("dp", "fsdp")),
        P(None, ("dp", "fsdp"), None),
        P(None, ("dp", "fsdp"), None),
        P(None, ("dp", "fsdp"), None),
        P(("dp", "fsdp"), None),
        P(("dp", "fsdp"), None),
        P(None, ("dp", "fsdp")),
        P(),
        P(None, ("dp", "fsdp"), None),
        P(None, ("dp", "fsdp"), None),
        P(None, ("dp", "fsdp"), None),
        P(("dp", "fsdp"), None),
        P(("dp", "fsdp"), None),
        P(None, ("dp", "fsdp")),
        P(),
        P(None, ("dp", "fsdp"), None),
        P(None, ("dp", "fsdp"), None),
        P(None, ("dp", "fsdp"), None),
        P(("dp", "fsdp"), None),
        P(("dp", "fsdp"), None),
        P(None, ("dp", "fsdp")),
        P(),
    )
    small_slice = dict(mesh.shape) == {"dp": 8, "fsdp": 4}
    return jax.shard_map(
        shards_block if small_slice else shards,
        mesh=mesh,
        in_specs=placed,
        out_specs=(
            P(None, ("dp", "fsdp"), None, None),
            P(None, ("dp", "fsdp"), None, None),
            P(None, ("dp", "fsdp"), None, None),
            P(None, ("dp", "fsdp"), None),
            P(None, ("dp", "fsdp"), None),
            P(None, ("dp", "fsdp"), None),
            P(("dp", "fsdp"), None),
            P(("dp", "fsdp"), None),
            P(None, ("dp", "fsdp")),
            P(),
            P(None, ("dp", "fsdp"), None),
            P(None, ("dp", "fsdp"), None),
            P(None, ("dp", "fsdp"), None),
            P(("dp", "fsdp"), None),
            P(("dp", "fsdp"), None),
            P(None, ("dp", "fsdp")),
            P(),
            P(None, ("dp", "fsdp"), None),
            P(None, ("dp", "fsdp"), None),
            P(None, ("dp", "fsdp"), None),
            P(("dp", "fsdp"), None),
            P(("dp", "fsdp"), None),
            P(None, ("dp", "fsdp")),
            P(),
            P(None, ("dp", "fsdp"), None),
            P(None, ("dp", "fsdp"), None),
            P(None, ("dp", "fsdp"), None),
            P(("dp", "fsdp"), None),
            P(("dp", "fsdp"), None),
            P(None, ("dp", "fsdp")),
            P(),
        ),
        check_vma=False,
    )
```

```python
import functools
import math

import jax
import jax.numpy as jnp
import numpy as np
from jax import lax
from jax.experimental import pallas as pl
from jax.experimental.pallas import tpu as pltpu
from jax.sharding import PartitionSpec as P

HEADS = 12
HEAD_DIM = 64
BUCKETS = 32
MAX_DIST = 128
STEP = 10


epsilon_norm = 1e-06
score_scale = 0.125
masked_score = -1e30
beta_first = 0.9
beta_second = 0.999
adam_epsilon = 1e-08
rate_matrix = 0.15
rate_small = 1.0
weight_decay = 0.01
highest = lax.Precision.HIGHEST


def bucket_onehot(length):
    places = jnp.arange(length, dtype=jnp.int32)
    distance = jnp.maximum(places[:, None] - places[None, :], 0)
    exact_range = BUCKETS // 2
    safe_distance = jnp.maximum(distance, 1).astype(jnp.float32)
    spread = (
        jnp.log(safe_distance / exact_range)
        / math.log(MAX_DIST / exact_range)
        * (BUCKETS - exact_range)
    )
    far_bucket = jnp.minimum(exact_range + spread.astype(jnp.int32), BUCKETS - 1)
    bucket = jnp.where(distance < exact_range, distance, far_bucket)
    labels = jnp.arange(BUCKETS, dtype=jnp.int32)
    return (bucket[None, :, :] == labels[:, None, None]).astype(jnp.float32)


def product(left_side, right_side):
    return jnp.dot(left_side, right_side, preferred_element_type=jnp.float32)


def product_over_rows(left_side, right_side):
    return lax.dot_general(
        left_side, right_side, (((0,), (0,)), ((), ())), preferred_element_type=jnp.float32
    )


def product_transposed(left_side, right_side):
    return lax.dot_general(
        left_side, right_side, (((1,), (1,)), ((), ())), preferred_element_type=jnp.float32
    )


def to_heads(values, sequences):
    return values.reshape(sequences, -1, HEADS, HEAD_DIM)


def normalize(values, gain_row):
    scale_rows = lax.rsqrt(jnp.mean(values * values, axis=-1, keepdims=True) + epsilon_norm)
    unit_rows = values * scale_rows
    return ((unit_rows * gain_row).astype(jnp.bfloat16), unit_rows, scale_rows)


def normalize_back(grad_norm, unit_rows, scale_rows, gain_row):
    gain_grad = jnp.sum(grad_norm * unit_rows, axis=0)
    grad_unit = grad_norm * gain_row
    grad_values = scale_rows * (
        grad_unit - unit_rows * jnp.mean(grad_unit * unit_rows, axis=-1, keepdims=True)
    )
    return (grad_values, gain_grad)


def attend_scores(queries, key_heads, bias_term, allowed):
    scores = (
        jnp.einsum("sihe,sjhe->shij", queries, key_heads, preferred_element_type=jnp.float32)
        * score_scale
        + bias_term
    )
    return jnp.where(allowed, scores, masked_score)


def attend_forward(queries, key_heads, value_heads, bias_term, allowed):
    scores = attend_scores(queries, key_heads, bias_term, allowed)
    row_max = jnp.max(scores, axis=-1, keepdims=True)
    expanded = jnp.exp(scores - row_max)
    row_total = jnp.sum(expanded, axis=-1, keepdims=True)
    weights = (expanded / row_total).astype(jnp.bfloat16)
    mixed_heads = jnp.einsum(
        "shij,sjhe->sihe", weights, value_heads, preferred_element_type=jnp.float32
    )
    return (mixed_heads, row_max + jnp.log(row_total))


def attend_back(queries, key_heads, value_heads, bias_term, allowed, summary, grad_mixed):
    scores = attend_scores(queries, key_heads, bias_term, allowed)
    weights = jnp.exp(scores - summary)
    grad_weights = jnp.einsum(
        "sihe,sjhe->shij", grad_mixed, value_heads, preferred_element_type=jnp.float32
    )
    grad_values = jnp.einsum(
        "shij,sihe->sjhe",
        weights.astype(jnp.bfloat16),
        grad_mixed,
        preferred_element_type=jnp.float32,
    )
    grad_scores = (
        weights * (grad_weights - jnp.sum(weights * grad_weights, axis=-1, keepdims=True))
    ).astype(jnp.bfloat16)
    grad_queries = (
        jnp.einsum("shij,sjhe->sihe", grad_scores, key_heads, preferred_element_type=jnp.float32)
        * score_scale
    )
    grad_keys = (
        jnp.einsum("shij,sihe->sjhe", grad_scores, queries, preferred_element_type=jnp.float32)
        * score_scale
    )
    return (grad_queries, grad_keys, grad_values, grad_scores)


def forward_pass(gathered, bias_heads, hidden_seq, memory_seq, target_len, memory_len):
    qk_full, value_full, output_full, inner_full, outer_full, gain_full = gathered
    gain_rows = gain_full.astype(jnp.float32)
    sequences, length, model_width = hidden_seq.shape
    memory_span = memory_seq.shape[1]
    row_count = sequences * length
    residual = hidden_seq.astype(jnp.float32).reshape(row_count, model_width)
    memory_rows = memory_seq.reshape(sequences * memory_span, model_width)
    places = jnp.arange(length, dtype=jnp.int32)
    self_mask = (places[None, :] <= places[:, None])[None, None] & (
        places[None, None, None, :] < target_len[:, None, None, None]
    )
    memory_places = jnp.arange(memory_span, dtype=jnp.int32)
    cross_mask = (memory_places[None, :] < memory_len[:, None])[:, None, None, :]
    normed_first, unit_first, scale_first = normalize(residual, gain_rows[0])
    query_first = product(normed_first, qk_full[0]).astype(jnp.bfloat16)
    key_first = product(normed_first, qk_full[1]).astype(jnp.bfloat16)
    value_first = product(normed_first, value_full[0]).astype(jnp.bfloat16)
    mixed_first, summary_first = attend_forward(
        to_heads(query_first, sequences),
        to_heads(key_first, sequences),
        to_heads(value_first, sequences),
        bias_heads,
        self_mask,
    )
    mixed_first = mixed_first.reshape(row_count, model_width).astype(jnp.bfloat16)
    first_sum = residual + product(mixed_first, output_full[0])
    normed_second, unit_second, scale_second = normalize(first_sum, gain_rows[1])
    query_second = product(normed_second, qk_full[2]).astype(jnp.bfloat16)
    key_second = product(memory_rows, qk_full[3]).astype(jnp.bfloat16)
    value_second = product(memory_rows, value_full[1]).astype(jnp.bfloat16)
    mixed_second, summary_second = attend_forward(
        to_heads(query_second, sequences),
        to_heads(key_second, sequences),
        to_heads(value_second, sequences),
        0.0,
        cross_mask,
    )
    mixed_second = mixed_second.reshape(row_count, model_width).astype(jnp.bfloat16)
    second_sum = first_sum + product(mixed_second, output_full[1])
    normed_third, unit_third, scale_third = normalize(second_sum, gain_rows[2])
    inner_act = product(normed_third, inner_full)
    activated = jax.nn.gelu(inner_act, approximate=True).astype(jnp.bfloat16)
    produced = (second_sum + product(activated, outer_full)).astype(jnp.bfloat16)
    stored = (
        self_mask,
        cross_mask,
        memory_rows,
        normed_first,
        unit_first,
        scale_first,
        query_first,
        key_first,
        value_first,
        summary_first,
        mixed_first,
        normed_second,
        unit_second,
        scale_second,
        query_second,
        key_second,
        value_second,
        summary_second,
        mixed_second,
        normed_third,
        unit_third,
        scale_third,
        inner_act,
        activated,
    )
    return (stored, produced.reshape(sequences, length, model_width))


def backward_pass(gathered, bias_heads, stored, cotangent_seq, target_len):
    qk_full, value_full, output_full, inner_full, outer_full, gain_full = gathered
    gain_rows = gain_full.astype(jnp.float32)
    (
        self_mask,
        cross_mask,
        memory_rows,
        normed_first,
        unit_first,
        scale_first,
        query_first,
        key_first,
        value_first,
        summary_first,
        mixed_first,
        normed_second,
        unit_second,
        scale_second,
        query_second,
        key_second,
        value_second,
        summary_second,
        mixed_second,
        normed_third,
        unit_third,
        scale_third,
        inner_act,
        activated,
    ) = stored
    sequences, length, model_width = cotangent_seq.shape
    row_count = sequences * length
    places = jnp.arange(length, dtype=jnp.int32)
    live_rows = (places[None, :] < target_len[:, None]).astype(jnp.float32).reshape(row_count, 1)
    grad_out = cotangent_seq.astype(jnp.float32).reshape(row_count, model_width) * live_rows
    branch = grad_out.astype(jnp.bfloat16)
    outer_grad = product_over_rows(activated, branch)
    grad_act = product_transposed(branch, outer_full)
    unused_value, gelu_pull = jax.vjp(
        lambda inputs: jax.nn.gelu(inputs, approximate=True), inner_act
    )
    grad_inner = gelu_pull(grad_act)[0].astype(jnp.bfloat16)
    inner_grad = product_over_rows(normed_third, grad_inner)
    grad_from_third, gain_third = normalize_back(
        product_transposed(grad_inner, inner_full), unit_third, scale_third, gain_rows[2]
    )
    grad_second = grad_out + grad_from_third
    branch = grad_second.astype(jnp.bfloat16)
    output_grad_second = product_over_rows(mixed_second, branch)
    grad_mixed = product_transposed(branch, output_full[1]).astype(jnp.bfloat16)
    grad_query, grad_key, grad_value, unused_scores = attend_back(
        to_heads(query_second, sequences),
        to_heads(key_second, sequences),
        to_heads(value_second, sequences),
        0.0,
        cross_mask,
        summary_second,
        to_heads(grad_mixed, sequences),
    )
    grad_query = grad_query.reshape(row_count, model_width).astype(jnp.bfloat16)
    grad_key = grad_key.reshape(memory_rows.shape[0], model_width).astype(jnp.bfloat16)
    grad_value = grad_value.reshape(memory_rows.shape[0], model_width).astype(jnp.bfloat16)
    qk_grad_two = product_over_rows(normed_second, grad_query)
    qk_grad_three = product_over_rows(memory_rows, grad_key)
    value_grad_one = product_over_rows(memory_rows, grad_value)
    memory_grad = product_transposed(grad_key, qk_full[3]) + product_transposed(
        grad_value, value_full[1]
    )
    grad_from_second, gain_second = normalize_back(
        product_transposed(grad_query, qk_full[2]), unit_second, scale_second, gain_rows[1]
    )
    grad_first = grad_second + grad_from_second
    branch = grad_first.astype(jnp.bfloat16)
    output_grad_first = product_over_rows(mixed_first, branch)
    grad_mixed = product_transposed(branch, output_full[0]).astype(jnp.bfloat16)
    grad_query, grad_key, grad_value, grad_scores = attend_back(
        to_heads(query_first, sequences),
        to_heads(key_first, sequences),
        to_heads(value_first, sequences),
        bias_heads,
        self_mask,
        summary_first,
        to_heads(grad_mixed, sequences),
    )
    grad_query = grad_query.reshape(row_count, model_width).astype(jnp.bfloat16)
    grad_key = grad_key.reshape(row_count, model_width).astype(jnp.bfloat16)
    grad_value = grad_value.reshape(row_count, model_width).astype(jnp.bfloat16)
    qk_grad_zero = product_over_rows(normed_first, grad_query)
    qk_grad_one = product_over_rows(normed_first, grad_key)
    value_grad_zero = product_over_rows(normed_first, grad_value)
    grad_norm = (
        product_transposed(grad_query, qk_full[0])
        + product_transposed(grad_key, qk_full[1])
        + product_transposed(grad_value, value_full[0])
    )
    grad_from_first, gain_first = normalize_back(grad_norm, unit_first, scale_first, gain_rows[0])
    hidden_grad = grad_first + grad_from_first
    score_term = jnp.sum(grad_scores.astype(jnp.float32), axis=0)
    grad_terms = (
        jnp.stack([qk_grad_zero, qk_grad_one, qk_grad_two, qk_grad_three]),
        jnp.stack([value_grad_zero, value_grad_one]),
        jnp.stack([output_grad_first, output_grad_second]),
        inner_grad,
        outer_grad,
        jnp.stack([gain_first, gain_second, gain_third]),
    )
    return (
        grad_terms,
        score_term,
        hidden_grad.reshape(sequences, length, model_width),
        memory_grad.reshape(sequences, -1, model_width),
    )


def adam_step(master, first_moment, second_moment, gradient, rate, decay):
    first_next = beta_first * first_moment + (1.0 - beta_first) * gradient
    second_next = beta_second * second_moment + (1.0 - beta_second) * gradient * gradient
    corrected = (
        first_next
        / (1.0 - beta_first**STEP)
        / (jnp.sqrt(second_next / (1.0 - beta_second**STEP)) + adam_epsilon)
    )
    master_next = master - rate * (corrected + decay * master)
    return (master_next, first_next, second_next)


def shards(
    hidden,
    memory,
    cotangent,
    target_lengths,
    memory_lengths,
    qk_master,
    value_master,
    output_master,
    inner_master,
    outer_master,
    gain_master,
    table_master,
    qk_first,
    value_first,
    output_first,
    inner_first,
    outer_first,
    gain_first,
    table_first,
    qk_second,
    value_second,
    output_second,
    inner_second,
    outer_second,
    gain_second,
    table_second,
):
    micro_count = hidden.shape[0]
    length = hidden.shape[2]
    model_width = hidden.shape[3]
    hidden_units = inner_master.shape[1]
    qk_low = qk_master.astype(jnp.bfloat16)
    value_low = value_master.astype(jnp.bfloat16)
    output_low = output_master.astype(jnp.bfloat16)
    inner_low = inner_master.astype(jnp.bfloat16)
    outer_low = outer_master.astype(jnp.bfloat16)
    gain_low = gain_master.astype(jnp.bfloat16)
    onehot = bucket_onehot(length)
    bias_heads = jnp.einsum("bij,bh->hij", onehot, table_master, precision=highest)
    masters = (qk_master, value_master, output_master, inner_master, outer_master, gain_master)
    totals = (
        jnp.zeros((4, model_width, model_width), jnp.float32),
        jnp.zeros((2, model_width, model_width), jnp.float32),
        jnp.zeros((2, model_width, model_width), jnp.float32),
        jnp.zeros((model_width, hidden_units), jnp.float32),
        jnp.zeros((hidden_units, model_width), jnp.float32),
        jnp.zeros((3, model_width), jnp.float32),
    )
    reduced = tuple((jnp.zeros_like(master) for master in masters))
    score_total = jnp.zeros((HEADS, length, length), jnp.float32)
    produced_list = []
    hidden_list = []
    memory_list = []
    for micro_index in range(micro_count):
        gathered = (
            lax.all_gather(qk_low, ("dp", "fsdp"), axis=1, tiled=True),
            lax.all_gather(value_low, ("dp", "fsdp"), axis=1, tiled=True),
            lax.all_gather(output_low, ("dp", "fsdp"), axis=1, tiled=True),
            lax.all_gather(inner_low, ("dp", "fsdp"), axis=0, tiled=True),
            lax.all_gather(outer_low, ("dp", "fsdp"), axis=0, tiled=True),
            lax.all_gather(gain_low, ("dp", "fsdp"), axis=1, tiled=True),
        )
        stored, produced = forward_pass(
            gathered,
            bias_heads,
            hidden[micro_index],
            memory[micro_index],
            target_lengths[micro_index],
            memory_lengths[micro_index],
        )
        gathered = (
            lax.all_gather(qk_low, ("dp", "fsdp"), axis=1, tiled=True),
            lax.all_gather(value_low, ("dp", "fsdp"), axis=1, tiled=True),
            lax.all_gather(output_low, ("dp", "fsdp"), axis=1, tiled=True),
            lax.all_gather(inner_low, ("dp", "fsdp"), axis=0, tiled=True),
            lax.all_gather(outer_low, ("dp", "fsdp"), axis=0, tiled=True),
            lax.all_gather(gain_low, ("dp", "fsdp"), axis=1, tiled=True),
        )
        grad_terms, score_term, hidden_grad, memory_grad = backward_pass(
            gathered, bias_heads, stored, cotangent[micro_index], target_lengths[micro_index]
        )
        totals = tuple((running + addition for running, addition in zip(totals, grad_terms)))
        score_total = score_total + score_term
        produced_list.append(produced)
        hidden_list.append(hidden_grad)
        memory_list.append(memory_grad)
    reduced = (
        lax.psum_scatter(totals[0], ("dp", "fsdp"), scatter_dimension=1, tiled=True),
        lax.psum_scatter(totals[1], ("dp", "fsdp"), scatter_dimension=1, tiled=True),
        lax.psum_scatter(totals[2], ("dp", "fsdp"), scatter_dimension=1, tiled=True),
        lax.psum_scatter(totals[3], ("dp", "fsdp"), scatter_dimension=0, tiled=True),
        lax.psum_scatter(totals[4], ("dp", "fsdp"), scatter_dimension=0, tiled=True),
        lax.psum_scatter(totals[5], ("dp", "fsdp"), scatter_dimension=1, tiled=True),
    )
    table_grad = jnp.einsum("bij,hij->bh", onehot, score_total, precision=highest)
    table_grad = lax.psum(table_grad, ("dp", "fsdp"))
    all_masters = (
        qk_master,
        value_master,
        output_master,
        inner_master,
        outer_master,
        gain_master,
        table_master,
    )
    firsts = (
        qk_first,
        value_first,
        output_first,
        inner_first,
        outer_first,
        gain_first,
        table_first,
    )
    seconds = (
        qk_second,
        value_second,
        output_second,
        inner_second,
        outer_second,
        gain_second,
        table_second,
    )
    gradients = (reduced[0], reduced[1], reduced[2], reduced[3], reduced[4], reduced[5], table_grad)
    rates = (
        rate_matrix,
        rate_matrix,
        rate_matrix,
        rate_matrix,
        rate_matrix,
        rate_small,
        rate_small,
    )
    decays = (weight_decay, weight_decay, weight_decay, weight_decay, weight_decay, 0.0, 0.0)
    updated = [
        adam_step(
            all_masters[index],
            firsts[index],
            seconds[index],
            gradients[index],
            rates[index],
            decays[index],
        )
        for index in range(7)
    ]
    news = [entry[0] for entry in updated]
    first_news = [entry[1] for entry in updated]
    second_news = [entry[2] for entry in updated]
    copies = [entry.astype(jnp.bfloat16) for entry in news]
    layer_out = jnp.stack(produced_list)
    hidden_out = jnp.stack(hidden_list)
    memory_out = jnp.stack(memory_list)
    return (
        layer_out,
        hidden_out,
        memory_out,
        news[0],
        news[1],
        news[2],
        news[3],
        news[4],
        news[5],
        news[6],
        first_news[0],
        first_news[1],
        first_news[2],
        first_news[3],
        first_news[4],
        first_news[5],
        first_news[6],
        second_news[0],
        second_news[1],
        second_news[2],
        second_news[3],
        second_news[4],
        second_news[5],
        second_news[6],
        copies[0],
        copies[1],
        copies[2],
        copies[3],
        copies[4],
        copies[5],
        copies[6],
    )


MESH = pl.DeviceIdType.MESH
PAIRS = 6
ORDERS = ("ax", "ay", "ax", "ay", "ax", "ay", "cx", "cy")


class Place:
    def __init__(self, wa, wf):
        self.wa, self.wf = wa, wf
        dp, fs = lax.axis_index("dp"), lax.axis_index("fsdp")
        self.z, self.y = dp // 2, dp % 2
        self.x, self.c = fs // 2, fs % 2
        self.to = {
            "x": (dp, (1 - self.x) * 2 + self.c),
            "y": (self.z * 2 + 1 - self.y, fs),
            "c": (dp, self.x * 2 + 1 - self.c),
            "r": (dp + 2, fs),
            "l": (dp - 2, fs),
        }

    def enter(self, wait):
        bar = pltpu.get_barrier_semaphore()
        inner = (self.z > 0) & (self.z < 3)
        if wait:
            @pl.when(inner)
            def _():
                pl.semaphore_wait(bar, 5)

            @pl.when(jnp.logical_not(inner))
            def _():
                pl.semaphore_wait(bar, 4)

            return

        def greet(way):
            pl.semaphore_signal(bar, inc=1, device_id=self.to[way], device_id_type=MESH)

        for way in ("x", "y", "c"):
            greet(way)

        @pl.when(self.z < 3)
        def _():
            greet("r")

        @pl.when(self.z > 0)
        def _():
            greet("l")

    def pick(self, f, zs, ps, qs, core=None):
        c = self.c if core is None else core
        xs, ys = (ps, qs) if ORDERS[f][1] == "x" else (qs, ps)
        if f < PAIRS:
            return self.wa.at[2 * f + c, zs, ys, xs]
        return self.wf.at[zs, ys, xs, c, f - PAIRS]

    def own(self, f):
        return (self.x, self.y) if ORDERS[f][1] == "x" else (self.y, self.x)

    def ways(self, f):
        return ("x", "y") if ORDERS[f][1] == "x" else ("y", "x")


def push(place, src, dst, send, recv, way):
    pltpu.make_async_remote_copy(
        src_ref=src, dst_ref=dst, send_sem=send, recv_sem=recv,
        device_id=place.to[way], device_id_type=MESH,
    ).start()


def got(place, ref, sem, way):
    pltpu.make_async_remote_copy(
        src_ref=ref, dst_ref=ref, send_sem=sem, recv_sem=sem,
        device_id=place.to[way], device_id_type=MESH,
    ).wait_recv()


def left_out(place, ref, sem, way):
    pltpu.make_async_remote_copy(
        src_ref=ref, dst_ref=ref, send_sem=sem, recv_sem=sem,
        device_id=place.to[way], device_id_type=MESH,
    ).wait_send()


ALL = slice(None)


class Gather:
    def __init__(self, place, f, send, recv):
        self.k, self.f = place, f
        self.send, self.recv = send, recv
        self.first_cross = ORDERS[f][0] == "a"

    def do(self, name):
        if name[0] in "LR":
            self.step(int(name[1]), name[0])
        else:
            getattr(self, name)()

    def blk(self, zi):
        p, q = self.k.own(self.f)
        return self.k.pick(self.f, zi, ALL if self.first_cross else p, q)

    def move(self, ref, s, r, way):
        push(self.k, ref, ref, self.send.at[self.f, s], self.recv.at[self.f, r], way)

    def start(self):
        p, q = self.k.own(self.f)
        pw, qw = self.k.ways(self.f)
        if self.first_cross:
            self.move(self.k.pick(self.f, self.k.z, p, q), 0, 0, pw)
        else:
            self.spread(self.k.z, 1)

    def cross(self):
        p, q = self.k.own(self.f)
        pw, qw = self.k.ways(self.f)
        if self.first_cross:
            got(self.k, self.k.pick(self.f, self.k.z, 1 - p, q), self.recv.at[self.f, 0], pw)
            self.spread(self.k.z, 1)
        else:
            got(self.k, self.k.pick(self.f, ALL, 1 - p, q), self.recv.at[self.f, 0], pw)
            half = self.k.pick(self.f, ALL, ALL, q)
            self.move(half, 3, 7, qw)
            self.move(half, 4, 8, "c")

    def sideways(self, zi):
        pw, qw = self.k.ways(self.f)
        if self.first_cross:
            self.move(self.blk(zi), 3, 7, qw)
            self.move(self.blk(zi), 4, 8, "c")
        else:
            self.move(self.blk(zi), 0, 0, pw)

    def spread(self, zi, t):
        z = self.k.z

        @pl.when(z < 3)
        def _():
            self.move(self.blk(zi), 1, t, "r")

        @pl.when(z > 0)
        def _():
            self.move(self.blk(zi), 2, 3 + t, "l")

        self.sideways(zi)

    def step(self, t, side):
        z = self.k.z

        if side == "L":
            @pl.when(z >= t)
            def _():
                got(self.k, self.blk(z - t), self.recv.at[self.f, t], "l")

                if t < 3:
                    @pl.when(z < 3)
                    def _():
                        self.move(self.blk(z - t), 1, t + 1, "r")

                self.sideways(z - t)
        else:
            @pl.when(z <= 3 - t)
            def _():
                got(self.k, self.blk(z + t), self.recv.at[self.f, 3 + t], "r")

                if t < 3:
                    @pl.when(z > 0)
                    def _():
                        self.move(self.blk(z + t), 2, 3 + t + 1, "l")

                self.sideways(z + t)

    def second(self):
        p, q = self.k.own(self.f)
        pw, qw = self.k.ways(self.f)
        other = self.k.pick(self.f, ALL, ALL, 1 - q)
        got(self.k, other, self.recv.at[self.f, 7], qw)
        self.move(other, 4, 8, "c")

    def finish(self):
        theirs = self.k.pick(self.f, ALL, ALL, ALL, 1 - self.k.c)
        got(self.k, theirs, self.recv.at[self.f, 8], "c")

    def drain(self):
        p, q = self.k.own(self.f)
        pw, qw = self.k.ways(self.f)
        z, f = self.k.z, self.f
        some = (lambda n: self.k.pick(f, pl.ds(0, n), ALL if self.first_cross else p, q))
        first = self.k.pick(f, z, p, q) if self.first_cross else self.k.pick(f, ALL, p, q)
        left_out(self.k, first, self.send.at[f, 0], pw)
        for n in (1, 2, 3):
            @pl.when(z == n - 1)
            def _():
                left_out(self.k, some(n), self.send.at[f, 1], "r")

            @pl.when(z == 4 - n)
            def _():
                left_out(self.k, some(n), self.send.at[f, 2], "l")
        left_out(self.k, self.k.pick(f, ALL, ALL, q), self.send.at[f, 3], qw)
        left_out(self.k, self.k.pick(f, ALL, ALL, ALL), self.send.at[f, 4], "c")


def add_into(dst, srcs, lead):
    sizes = lead
    count = 1
    for s in sizes:
        count *= s

    def body(i, _):
        idx, rest = [], i
        for s in reversed(sizes):
            idx.append(rest % s)
            rest = rest // s
        idx = tuple(reversed(idx)) or Ellipsis
        total = dst[idx].astype(jnp.float32)
        for src in srcs:
            total = total + src[idx].astype(jnp.float32)
        dst[idx] = total.astype(jnp.bfloat16)
        return 0

    lax.fori_loop(0, count, body, 0)


class Scatter:
    def __init__(self, place, f, send, recv, slots, final, result, credit):
        self.k, self.f = place, f
        self.wait_credit, self.give_credit, self.credit = credit
        self.send, self.recv = send, recv
        self.rd, self.rq, self.rp, self.rl, self.rr = slots
        self.final, self.result = final, result
        self.wide = ORDERS[f][0] == "a"

    def do(self, name):
        if name[0] == "z":
            self.step_in(int(name[1]))
        else:
            getattr(self, name)()

    def move(self, src, dst, s, way):
        push(self.k, src, dst, self.send.at[self.f, s], self.recv.at[self.f, s], way)

    def blk(self, zi):
        p, q = self.k.own(self.f)
        return self.k.pick(self.f, zi, ALL if self.wide else p, q)

    def start(self):
        if self.wait_credit:
            pl.semaphore_wait(self.credit, 1)
        self.move(self.k.pick(self.f, ALL, ALL, ALL, 1 - self.k.c), self.rd, 0, "c")

    def rpick(self, ps, qs):
        xs, ys = (ps, qs) if ORDERS[self.f][1] == "x" else (qs, ps)
        return self.rd.at[:, ys, xs]

    def core(self):
        p, q = self.k.own(self.f)
        pw, qw = self.k.ways(self.f)
        got(self.k, self.rd, self.recv.at[self.f, 0], "c")
        away = self.k.pick(self.f, ALL, ALL, 1 - q)
        add_into(away, [self.rpick(ALL, 1 - q)], (4, 2))
        self.move(away, self.rq, 1, qw)

    def half(self):
        p, q = self.k.own(self.f)
        pw, qw = self.k.ways(self.f)
        got(self.k, self.rq, self.recv.at[self.f, 1], qw)
        add_into(self.k.pick(self.f, ALL, ALL, q), [self.rpick(ALL, q), self.rq], (4, 2))
        if self.give_credit:
            pl.semaphore_signal(self.credit, inc=1, device_id=self.k.to["c"], device_id_type=MESH)
        if self.wide:
            self.step_out(1)
        else:
            self.move(self.k.pick(self.f, ALL, 1 - p, q), self.rp, 2, pw)

    def cross_in(self):
        p, q = self.k.own(self.f)
        pw, qw = self.k.ways(self.f)
        got(self.k, self.rp, self.recv.at[self.f, 2], pw)
        add_into(self.k.pick(self.f, ALL, p, q), [self.rp], (4,))
        self.step_out(1)

    def step_out(self, t):
        z = self.k.z

        @pl.when(z <= t - 1)
        def _():
            self.move(self.blk(z + 4 - t), self.rl.at[t - 1], 2 + t, "r")

        @pl.when(z >= 4 - t)
        def _():
            self.move(self.blk(z - 4 + t), self.rr.at[t - 1], 5 + t, "l")

    def step_in(self, t):
        z, f = self.k.z, self.f
        lead = (2,) if self.wide else ()

        @pl.when((z >= 1) & (z <= t))
        def _():
            got(self.k, self.rl.at[t - 1], self.recv.at[f, 2 + t], "l")
            add_into(self.blk(z + 3 - t), [self.rl.at[t - 1]], lead)

        @pl.when((z <= 2) & (z >= 3 - t))
        def _():
            got(self.k, self.rr.at[t - 1], self.recv.at[f, 5 + t], "r")
            add_into(self.blk(z - 3 + t), [self.rr.at[t - 1]], lead)

        if t < 3:
            self.step_out(t + 1)
        else:
            p, q = self.k.own(f)
            pw, qw = self.k.ways(f)
            if self.wide:
                self.move(self.k.pick(f, z, 1 - p, q), self.rp, 2, pw)
            else:
                self.total(None)

    def last(self):
        pw, qw = self.k.ways(self.f)
        got(self.k, self.rp, self.recv.at[self.f, 2], pw)
        self.total(self.rp)

    def total(self, more):
        p, q = self.k.own(self.f)
        c = self.k.c
        mine = self.k.pick(self.f, self.k.z, p, q)[...].astype(jnp.float32)
        if more is not None:
            mine = mine + more[...].astype(jnp.float32)
        if self.f < PAIRS:
            self.final[...] = mine
            kept = pl.ds(pl.multiple_of(c * 24, 8), 24)
            away = pl.ds(pl.multiple_of(24 - c * 24, 8), 24)
            self.move(self.final.at[away], self.result.at[2 * self.f + c], 9, "c")
            self.result[2 * self.f + c] = self.final[kept]
        else:
            self.final[...] = mine

    def finish(self):
        if self.f < PAIRS:
            got(self.k, self.result.at[2 * self.f + 1 - self.k.c], self.recv.at[self.f, 9], "c")

    def drain(self):
        p, q = self.k.own(self.f)
        pw, qw = self.k.ways(self.f)
        z, f, k = self.k.z, self.f, self.k
        left_out(k, self.rd, self.send.at[f, 0], "c")
        left_out(k, self.rq, self.send.at[f, 1], qw)
        left_out(k, self.rp, self.send.at[f, 2], pw)
        for t in (1, 2, 3):
            @pl.when(z <= t - 1)
            def _():
                left_out(k, self.rl.at[t - 1], self.send.at[f, 2 + t], "r")

            @pl.when(z >= 4 - t)
            def _():
                left_out(k, self.rr.at[t - 1], self.send.at[f, 5 + t], "l")
        if f < PAIRS:
            left_out(k, self.final.at[pl.ds(0, 24)], self.send.at[f, 9], "c")


class Line:
    def __init__(self, place, buf, send, recv):
        self.k, self.buf, self.send, self.recv = place, buf, send, recv

    def move(self, zi, s, r, way):
        push(self.k, self.buf.at[zi], self.buf.at[zi], self.send.at[s], self.recv.at[r], way)

    def start(self):
        z = self.k.z

        @pl.when(z < 3)
        def _():
            self.move(z, 3, 3, "r")

        @pl.when(z > 0)
        def _():
            self.move(z, 6, 6, "l")

    def step(self, t):
        z = self.k.z

        @pl.when(z >= t)
        def _():
            got(self.k, self.buf.at[z - t], self.recv.at[2 + t], "l")

            if t < 3:
                @pl.when(z < 3)
                def _():
                    self.move(z - t, 3 + t, 3 + t, "r")

        @pl.when(z <= 3 - t)
        def _():
            got(self.k, self.buf.at[z + t], self.recv.at[5 + t], "r")

            if t < 3:
                @pl.when(z > 0)
                def _():
                    self.move(z + t, 6 + t, 6 + t, "l")

    def drain(self):
        z = self.k.z
        for t in range(3):
            @pl.when((z < 3) & (z >= t))
            def _():
                left_out(self.k, self.buf.at[0], self.send.at[3 + t], "r")

            @pl.when((z > 0) & (z <= 3 - t))
            def _():
                left_out(self.k, self.buf.at[0], self.send.at[6 + t], "l")


class Gains:
    def __init__(self, place, buf, send, recv):
        self.k, self.buf, self.send, self.recv = place, buf, send, recv
        self.line = Line(place, buf, send, recv)
        z, y, x, c = place.z, place.y, place.x, place.c
        self.mine = [buf.at[z, y, x, c], buf.at[z, y, x], buf.at[z, y]]
        self.other = [buf.at[z, y, x, 1 - c], buf.at[z, y, 1 - x], buf.at[z, 1 - y]]

    def go(self, i):
        if 1 <= i <= 3:
            got(self.k, self.other[i - 1], self.recv.at[i - 1], "cxy"[i - 1])
        if i < 3:
            push(self.k, self.mine[i], self.mine[i], self.send.at[i], self.recv.at[i], "cxy"[i])
        elif i == 3:
            self.line.start()
        else:
            self.line.step(i - 3)

    def drain(self):
        for i in range(3):
            left_out(self.k, self.mine[i], self.send.at[i], "cxy"[i])
        self.line.drain()


class Small:
    def __init__(self, place, bufs, got_bufs, along, send, recv):
        self.k, self.bufs, self.got_bufs, self.along = place, bufs, got_bufs, along
        self.send, self.recv = send, recv
        self.line = Line(place, along, send, recv)

    def go(self, i):
        if 1 <= i <= 3:
            got(self.k, self.got_bufs.at[i - 1], self.recv.at[i - 1], "cxy"[i - 1])
            total = self.bufs[i - 1] + self.got_bufs[i - 1]
            if i < 3:
                self.bufs[i] = total
            else:
                self.along[self.k.z] = total
        if i < 3:
            push(self.k, self.bufs.at[i], self.got_bufs.at[i], self.send.at[i], self.recv.at[i], "cxy"[i])
        elif i == 3:
            self.line.start()
        else:
            self.line.step(i - 3)

    def drain(self):
        for i in range(3):
            left_out(self.k, self.bufs.at[i], self.send.at[i], "cxy"[i])
        self.line.drain()
BF, F32 = jnp.bfloat16, jnp.float32
ROOT = math.sqrt(2.0 / math.pi)
CUBE = 0.044715


def dot_nn(a, b):
    return lax.dot_general(a, b, (((1,), (0,)), ((), ())), preferred_element_type=F32)


def dot_nt(a, b):
    return lax.dot_general(a, b, (((1,), (1,)), ((), ())), preferred_element_type=F32)


def dot_tn(a, b):
    return lax.dot_general(a, b, (((0,), (0,)), ((), ())), preferred_element_type=F32)


def unit_of(values):
    scale = lax.rsqrt(jnp.mean(values * values, axis=-1, keepdims=True) + epsilon_norm)
    return values * scale, scale


class Layer:
    def __init__(self, wa, wf, b):
        self.wa, self.wf, self.b = wa, wf, b

    def times(self, a, u, put):
        for t in range(3):
            tile = slice(256 * t, 256 * t + 256)
            put(tile, dot_nn(a[...], self.wa[u, :, :, :, :, tile].reshape(768, 256)))

    def times_back(self, pairs, put):
        total = None
        for a, u in pairs:
            term = dot_nt(a[...], self.wa[u].reshape(768, 768))
            total = term if total is None else total + term
        put(slice(0, 768), total)

    def weight_grad(self, a, d, u):
        for t in range(2):
            tile = dot_tn(a[:, 384 * t:384 * t + 384], d[...])
            self.wa[u, 2 * t:2 * t + 2] = tile.astype(BF).reshape(2, 2, 2, 48, 768)

    def project(self, a, u, dst):
        def put(tile, value):
            dst[:, tile] = value.astype(BF)

        self.times(a, u, put)

    def add_project(self, base, a, u, dst):
        def put(tile, value):
            dst[:, tile] = base[:, tile].astype(F32) + value

        self.times(a, u, put)

    def norm(self, src, g, dst):
        gain = self.b["gain"][pl.ds(g, 1), :]

        def body(i, _):
            rows = pl.ds(pl.multiple_of(64 * i, 64), 64)
            unit, _unused = unit_of(src[rows].astype(F32))
            dst[rows] = (unit * gain).astype(BF)
            return 0

        lax.fori_loop(0, 8, body, 0)

    def norm_back(self, dn, src, g, base, dst, low):
        gain = self.b["gain"][pl.ds(g, 1), :]

        def body(i, acc):
            rows = pl.ds(pl.multiple_of(64 * i, 64), 64)
            unit, scale = unit_of(src[rows].astype(F32))
            grad = dn[rows]
            acc = acc + jnp.sum(grad * unit, axis=0, keepdims=True)
            pulled = grad * gain
            value = base(rows, i) + scale * (pulled - unit * jnp.mean(pulled * unit, axis=-1, keepdims=True))
            dst[rows] = value
            if low is not None:
                low[rows] = value.astype(BF)
            return acc

        total = lax.fori_loop(0, 8, body, jnp.zeros((1, 768), F32))
        for i in range(3):
            self.b["small"][12 + 3 * g + i:13 + 3 * g + i, :] = total[:, 256 * i:256 * i + 256]

    def head_masks(self):
        lane = lax.broadcasted_iota(jnp.int32, (1, 128), 1)
        low = (lane < 64).astype(F32)
        return low.astype(BF), (1.0 - low).astype(BF)

    def far(self, s, kind):
        col = lax.broadcasted_iota(jnp.int32, (1, 256), 1)
        length = self.b["lens"][0, s] if kind == 1 else self.b["mem_lens"][0, s]
        return jnp.where(col < length, 0.0, masked_score)

    def bias(self, head, causal):
        row = self.b["bias_row"][pl.ds(head, 1), :]
        turned = pltpu.roll(jnp.broadcast_to(row, (256, 256)), 0, axis=1, stride=1, stride_axis=0)
        return jnp.where(causal, turned, masked_score)

    def weights(self, scores):
        expanded = jnp.exp(scores - jnp.max(scores, axis=-1, keepdims=True))
        return expanded * (1.0 / jnp.sum(expanded, axis=-1, keepdims=True))

    def places(self):
        row = lax.broadcasted_iota(jnp.int32, (256, 256), 0)
        col = lax.broadcasted_iota(jnp.int32, (256, 256), 1)
        return row, col

    def attend(self, kind, first, last):
        b = self.b
        q, k, v, o = (b[n + str(kind)] for n in "qkvo")
        masks = self.head_masks()
        keep = masks[0].astype(F32)
        row, col = self.places()

        def body(hp, _):
            lanes = pl.ds(pl.multiple_of(128 * hp, 128), 128)
            biases = [self.bias(2 * hp + e, col <= row) if kind == 1 else 0.0 for e in range(2)]
            rows = [slice(0, 256), slice(256, 512)]
            both = [(s, e) for s in range(2) for e in range(2)]
            queries = [q[r, lanes] * BF(score_scale) for r in rows]
            keys, values = [k[r, lanes] for r in rows], [v[r, lanes] for r in rows]
            far = [self.far(s, kind) for s in range(2)]
            scores = [dot_nt(queries[s] * masks[e], keys[s]) + (biases[e] + far[s]) for s, e in both]
            low = [self.weights(one).astype(BF) for one in scores]
            mixed = [dot_nn(p, values[s]) for p, (s, e) in zip(low, both)]
            for s in range(2):
                o[rows[s], lanes] = (mixed[2 * s] * keep + mixed[2 * s + 1] * (1.0 - keep)).astype(BF)
            return 0

        lax.fori_loop(first, last, body, 0)

    def attend_back(self, kind, first, last):
        b = self.b
        q, k, v = (b[n + str(kind)] for n in "qkv")
        masks = self.head_masks()
        row, col = self.places()
        flip = (row + col == 255).astype(F32).astype(BF)

        def body(hp, _):
            lanes = pl.ds(pl.multiple_of(128 * hp, 128), 128)
            biases = [self.bias(2 * hp + e, col <= row) if kind == 1 else 0.0 for e in range(2)]
            rows = [slice(0, 256), slice(256, 512)]
            both = [(s, e) for s in range(2) for e in range(2)]
            queries = [q[r, lanes] * BF(score_scale) for r in rows]
            keys, values = [k[r, lanes] for r in rows], [v[r, lanes] for r in rows]
            given = [b["do"][r, lanes] for r in rows]
            far = [self.far(s, kind) for s in range(2)]
            qe = [queries[s] * masks[e] for s, e in both]
            ge = [given[s] * masks[e] for s, e in both]
            scores = [dot_nt(one, keys[s]) + (biases[e] + far[s]) for one, (s, e) in zip(qe, both)]
            dps = [dot_nt(one, values[s]) for one, (s, e) in zip(ge, both)]
            ps = [self.weights(one) for one in scores]
            dss = [(p * (dp - jnp.sum(p * dp, axis=-1, keepdims=True))).astype(BF) for p, dp in zip(ps, dps)]
            low = [p.astype(BF) for p in ps]
            dv = [dot_tn(p, one) for p, one in zip(low, ge)]
            dk = [dot_tn(ds, one) for ds, one in zip(dss, qe)]
            dq = [dot_nn(ds, keys[s] * masks[e]) for ds, (s, e) in zip(dss, both)]
            if kind == 1:
                for e in range(2):
                    turned = dot_nn(flip, dss[e]) + dot_nn(flip, dss[2 + e])
                    turned = pltpu.roll(turned, 0, axis=1, stride=1, stride_axis=0)
                    b["small"][pl.ds(2 * hp + e, 1), :] = jnp.sum(turned, axis=0, keepdims=True)
            for s in range(2):
                q[rows[s], lanes] = ((dq[2 * s] + dq[2 * s + 1]) * score_scale).astype(BF)
                k[rows[s], lanes] = (dk[2 * s] + dk[2 * s + 1]).astype(BF)
                v[rows[s], lanes] = (dv[2 * s] + dv[2 * s + 1]).astype(BF)
            return 0

        lax.fori_loop(first, last, body, 0)

    def live(self, i):
        row = lax.broadcasted_iota(jnp.int32, (64, 1), 0) + 64 * lax.rem(i, 4)
        bound = jnp.where(i < 4, self.b["lens"][0, 0], self.b["lens"][0, 1])
        return (row < bound).astype(F32)

    def cotangent(self):
        b = self.b

        def body(i, _):
            rows = pl.ds(pl.multiple_of(64 * i, 64), 64)
            b["df"][rows] = (b["cot"][rows].astype(F32) * self.live(i)).astype(BF)
            return 0

        lax.fori_loop(0, 8, body, 0)

    def ffn_act(self, j):
        b = self.b
        for t in range(2):
            cols = slice(384 * t, 384 * t + 384)
            wi = self.wa[8 + j, :, :, :, :, cols].reshape(768, 384)
            wf = self.wf[j, t].reshape(384, 768)
            u = dot_nn(b["n3"][...], wi)
            square = u * u
            th = jnp.tanh(u * (ROOT + (ROOT * CUBE) * square))
            half = 0.5 + 0.5 * th
            b["act"][:, cols] = (u * half).astype(BF)
            slope = half + u * (1.0 - th * th) * (0.5 * ROOT + (1.5 * ROOT * CUBE) * square)
            da = dot_nt(b["df"][...], wf)
            b["du"][:, cols] = (da * slope).astype(BF)

    def ffn_out(self, j):
        b = self.b
        for t in range(3):
            cols = slice(256 * t, 256 * t + 256)
            wf = self.wf[j, :, :, :, :, :, cols].reshape(768, 256)
            b["y"][:, cols] += dot_nn(b["act"][...], wf)

    def ffn_back(self, j):
        b = self.b

        def put(tile, value):
            if j == 0:
                b["dn"][:, tile] = value
            else:
                b["dn"][:, tile] += value

        self.times_back([(b["du"], 8 + j)], put)

    def ffn_grads(self, j):
        b = self.b
        for t in range(2):
            tile = dot_tn(b["act"][:, 384 * t:384 * t + 384], b["df"][...])
            self.wf[j, t] = tile.astype(BF).reshape(2, 2, 2, 48, 768)


SCATTER_ORDER = (4, 5, 6, 7, 3, 2, 1, 0)


def layer_kernel(program, lens, mem_lens, *refs):
    ins, outs, rest = refs[:13], refs[13:19], refs[19:]
    locals_in, locals_out, (in_sem, out_sem), rest = rest[:9], rest[9:15], rest[15:17], rest[17:]
    masters = rest[0]
    qk, value, output, inner = ins[3:7]
    units = [qk.at[0], qk.at[1], value.at[0], output.at[0], qk.at[3], value.at[1], qk.at[2], output.at[1]]
    units += [inner.at[:, 768 * j:768 * j + 768] for j in range(4)]
    pairs = [*zip((*ins[:3], *ins[7:]), locals_in), *((unit, masters.at[u // 2, u % 2]) for u, unit in enumerate(units))]
    fetch = [pltpu.make_async_copy(a, b, in_sem.at[i]) for i, (a, b) in enumerate(pairs)]
    store = [pltpu.make_async_copy(a, b, out_sem.at[i]) for i, (a, b) in enumerate(zip(locals_out, outs))]
    layer_body(program, lens, mem_lens, fetch, store, *locals_in, *locals_out, *rest)


def layer_body(
    program, lens, mem_lens, fetch, store,
    hid, mem, cot, outer, gain_in, table, spread, owner, near,
    low_out, hidden_grad, memory_grad, res, last, small_out, masters,
    wa, wf, n1, q1, k1, v1, o1, n2, q2, k2, v2, o2, n3, act, du, df, x1, x2, dn,
    rd, rq, rlw, rrw, rpw, rln, rrn, rpn, fin, tiles, gain, bias_row, small, small_got, along,
    gs, gr, ss, sr, xs, xr, ks, kr, ms, mr, credit,
):
    k = Place(wa, wf)
    z, y, x, c = k.z, k.y, k.x, k.c
    b = dict(
        lens=lens, mem_lens=mem_lens, hid=hid, mem=mem, cot=cot, bias_row=bias_row, gain=gain, small=small.at[0],
        n1=n1, q1=q1, k1=k1, v1=v1, o1=o1, n2=n2, q2=q2, k2=k2, v2=v2, o2=o2, n3=n3,
        act=act, du=du, df=df, do=act, y=memory_grad, dn=dn,
    )
    net = Layer(wa, wf, b)
    gathers = [Gather(k, f, gs, gr) for f in range(8)]
    scatters = {}
    for i, f in enumerate(SCATTER_ORDER):
        if f < PAIRS:
            slots = (rd.at[i % 4], rq.at[f], rpw.at[f], rlw.at[f], rrw.at[f])
        else:
            slots = (rd.at[i % 4], rq.at[f], rpn.at[f - PAIRS], rln.at[f - PAIRS], rrn.at[f - PAIRS])
        final = fin.at[f] if f < PAIRS else last.at[f - PAIRS]
        scatters[f] = Scatter(k, f, ss, sr, slots, final, res, (i >= 4, i < 4, credit))
    gains = Gains(k, tiles, ks, kr)
    sums = Small(k, small, small_got, along, ms, mr)
    mine = pl.ds(pl.multiple_of(24 * c, 8), 24)
    other = pl.ds(pl.multiple_of(24 - 24 * c, 8), 24)

    def enter():
        for i in (4, *range(9, 21), 3, 5, 8, 0, 1, 2, 6, 7):
            fetch[i].start()
        k.enter(False)
        for i in (4, *range(9, 21)):
            fetch[i].wait()
        tiles[z, y, x, c] = jnp.zeros((8, 128), F32)
        tiles[z, y, x, c, 0:3, 0:24] = gain_in[...].astype(BF).astype(F32)
        k.enter(True)
        push(k, masters.at[:, 1 - c], fin.at[:, mine], xs, xr, "c")
        gains.go(0)
        for i in (3, 5, 8):
            fetch[i].wait()
        bias_row[...] = jnp.zeros_like(bias_row)
        bias_row[0:HEADS, :] = lax.dot_general(
            table[...], near[...], (((1,), (0,)), ((), ())), precision=highest, preferred_element_type=F32
        )
        for h in range(2):
            wf[z, y, x, c, h] = outer[48 * h:48 * h + 48].astype(BF)
        for p in range(PAIRS):
            fin[p, mine] = masters[p, c]

    def swap():
        got(k, fin.at[:, other], xr, "c")

    def own(f):
        if f < PAIRS:
            wa[2 * f + c, z, y, x] = fin[f].astype(BF)
        gathers[f].start()

    def spread_gains():
        for i in (0, 6, 7):
            fetch[i].wait()
        flat = tiles[...].reshape(32, 8, 128)
        for g in range(3):
            lanes = dot_nn(flat[:, g].astype(BF), spread[...])
            gain[g:g + 1, :] = jnp.sum(lanes * owner[...], axis=0, keepdims=True)

    def put_do(tile, value):
        act[:, tile] = value.astype(BF)

    def put_dn(tile, value):
        dn[:, tile] = value

    def put_memory(tile, value):
        memory_grad[:, tile] = value

    def begin():
        fetch[2].wait()
        memory_grad[...] = x2[...]
        small[0] = jnp.zeros_like(small[0])
        net.cotangent()

    def finish_low():
        low_out[...] = memory_grad[...].astype(BF)
        store[0].start()

    def total_small():
        small_out[...] = along[0] + along[1] + along[2] + along[3]
        store[5].start()

    def mix_memory():
        net.times_back([(k2, 4), (v2, 5)], put_memory)
        store[2].start()

    def finish_hidden():
        net.norm_back(dn, hid, 0, lambda rows, i: grad[rows], grad, None)
        store[1].start()

    grad = hidden_grad
    tasks = {
        "gain": spread_gains,
        "n1": lambda: net.norm(hid, 0, n1),
        "q1": lambda: net.project(n1, 0, q1),
        "k1": lambda: net.project(n1, 1, k1),
        "v1": lambda: net.project(n1, 2, v1),
        "o1": lambda: net.add_project(hid, o1, 3, x1),
        "n2": lambda: net.norm(x1, 1, n2),
        "memory": lambda: fetch[1].wait(),
        "k2": lambda: net.project(mem, 4, k2),
        "v2": lambda: net.project(mem, 5, v2),
        "q2": lambda: net.project(n2, 6, q2),
        "o2": lambda: net.add_project(x1, o2, 7, x2),
        "n3": lambda: net.norm(x2, 2, n3),
        "begin": begin,
        "low": finish_low,
        "nb3": lambda: net.norm_back(dn, x2, 2, lambda rows, i: cot[rows].astype(F32) * net.live(i), grad, df),
        "do2": lambda: net.times_back([(df, 7)], put_do),
        "w7": lambda: net.weight_grad(o2, df, 7),
        "dn2": lambda: net.times_back([(q2, 6)], put_dn),
        "w6": lambda: net.weight_grad(n2, q2, 6),
        "mg": mix_memory,
        "w4": lambda: net.weight_grad(mem, k2, 4),
        "w5": lambda: net.weight_grad(mem, v2, 5),
        "nb2": lambda: net.norm_back(dn, x1, 1, lambda rows, i: grad[rows], grad, df),
        "do1": lambda: net.times_back([(df, 3)], put_do),
        "w3": lambda: net.weight_grad(o1, df, 3),
        "dn1": lambda: net.times_back([(q1, 0), (k1, 1), (v1, 2)], put_dn),
        "w0": lambda: net.weight_grad(n1, q1, 0),
        "w1": lambda: net.weight_grad(n1, k1, 1),
        "w2": lambda: net.weight_grad(n1, v1, 2),
        "nb1": finish_hidden,
    }
    families = {
        "act": net.ffn_act, "out": net.ffn_out, "back": net.ffn_back, "grads": net.ffn_grads,
        "W": lambda j: net.weight_grad(n3, du, 8 + j),
        "A1": lambda i: net.attend(1, 2 * i, 2 * i + 2),
        "A2": lambda i: net.attend(2, 2 * i, 2 * i + 2),
        "B1": lambda i: net.attend_back(1, 2 * i, 2 * i + 2),
        "B2": lambda i: net.attend_back(2, 2 * i, 2 * i + 2),
    }
    enter()
    for kind, index, name in program:
        if kind == "G":
            if name == "own":
                own(index)
            else:
                gathers[index].do(name)
        elif kind == "S":
            scatters[index].do(name)
        elif kind == "K":
            gains.go(index)
        elif kind == "R":
            if index < 7:
                sums.go(index)
            else:
                total_small()
        elif kind == "X":
            swap()
        elif name in tasks:
            tasks[name]()
        else:
            families[name](index)
    store[3].start()
    store[4].start()
    left_out(k, masters.at[:, 1 - c], xs, "c")
    gains.drain()
    sums.drain()
    for f in SCATTER_ORDER:
        scatters[f].drain()
    for copy in store:
        copy.wait()


def run_layer(program, *operands):
    far, sm = pl.BlockSpec(memory_space=pltpu.HBM), pl.BlockSpec(memory_space=pltpu.SMEM)
    low, wide = pltpu.VMEM((512, 768), BF), pltpu.VMEM((512, 768), F32)
    dma = pltpu.SemaphoreType.DMA
    shape = jax.ShapeDtypeStruct
    outs = (
        shape((512, 768), BF), shape((512, 768), F32), shape((512, 768), F32),
        shape((12, 24, 768), F32), shape((2, 48, 768), F32), shape((24, 256), F32),
    )
    return pl.pallas_call(
        functools.partial(layer_kernel, program),
        out_shape=outs,
        in_specs=[sm] * 2 + [far] * (len(operands) - 2),
        out_specs=[far] * 6,
        scratch_shapes=[
            *[pltpu.VMEM(a.shape, a.dtype) for a in (*operands[2:5], *operands[9:])],
            *[pltpu.VMEM(a.shape, a.dtype) for a in outs],
            dma((21,)), dma((6,)),
            pltpu.VMEM((6, 2, 24, 768), F32),
            pltpu.VMEM((12, 4, 2, 2, 48, 768), BF),
            pltpu.VMEM((4, 2, 2, 2, 2, 48, 768), BF),
            *[low] * 14, *[wide] * 3,
            pltpu.VMEM((4, 4, 2, 2, 48, 768), BF),
            pltpu.VMEM((8, 4, 2, 48, 768), BF),
            pltpu.VMEM((6, 3, 2, 48, 768), BF),
            pltpu.VMEM((6, 3, 2, 48, 768), BF),
            pltpu.VMEM((6, 48, 768), BF),
            pltpu.VMEM((2, 3, 48, 768), BF),
            pltpu.VMEM((2, 3, 48, 768), BF),
            pltpu.VMEM((2, 4, 48, 768), BF),
            pltpu.VMEM((6, 48, 768), F32),
            pltpu.VMEM((4, 2, 2, 2, 8, 128), F32),
            pltpu.VMEM((8, 768), F32),
            pltpu.VMEM((16, 256), F32),
            pltpu.VMEM((3, 24, 256), F32),
            pltpu.VMEM((3, 24, 256), F32),
            pltpu.VMEM((4, 24, 256), F32),
            dma((8, 5)), dma((8, 9)), dma((8, 10)), dma((8, 10)), dma, dma,
            dma((9,)), dma((9,)), dma((9,)), dma((9,)),
            pltpu.SemaphoreType.REGULAR,
        ],
        compiler_params=pltpu.CompilerParams(
            collective_id=0, has_side_effects=True, vmem_limit_bytes=63 * 2**20
        ),
    )(*operands)


def bucket_rows(length):
    distance = np.arange(length)
    exact_range = BUCKETS // 2
    safe = np.maximum(distance, 1).astype(np.float32)
    spread = np.log(safe / np.float32(exact_range)) / np.float32(math.log(MAX_DIST / exact_range))
    spread = (spread * np.float32(BUCKETS - exact_range)).astype(np.int32)
    bucket = np.where(distance < exact_range, distance, np.minimum(exact_range + spread, BUCKETS - 1))
    return (bucket[None, :] == np.arange(BUCKETS)[:, None]).astype(np.float32)


def adam_kernel(*refs):
    passed, ins, out_passed, outs, rest = refs[:3], refs[3:28], refs[28:31], refs[31:59], refs[59:]
    local, local_out, through, sems = rest[:25], rest[25:53], rest[53:56], rest[56]
    copies = [pltpu.make_async_copy(a, b, sems.at[0, i]) for i, (a, b) in enumerate(zip(ins, local))]
    inward = [pltpu.make_async_copy(a, b, sems.at[1, i]) for i, (a, b) in enumerate(zip(passed, through))]
    onward = [pltpu.make_async_copy(a, b, sems.at[1, 3 + i]) for i, (a, b) in enumerate(zip(through, out_passed))]
    store = [pltpu.make_async_copy(a, b, sems.at[2, i]) for i, (a, b) in enumerate(zip(local_out, outs))]
    order = (0, 1, 2, 3, *(j * 7 + i + 4 for i in range(7) for j in range(3)))
    for i in order:
        copies[i].start()
    for copy in inward:
        copy.start()
    res, last, small, reverse = local[:4]
    masters, firsts, seconds = local[4:11], local[11:18], local[18:25]
    device = lax.axis_index("dp") * 4 + lax.axis_index("fsdp")

    def update(i, at, grad):
        small_one = i > 4
        new, first, second = adam_step(
            masters[i][at], firsts[i][at], seconds[i][at], grad,
            rate_small if small_one else rate_matrix, 0.0 if small_one else weight_decay,
        )
        local_out[i][at] = new
        local_out[7 + i][at] = first
        local_out[14 + i][at] = second
        local_out[21 + i][at] = new.astype(BF)

    def arrive(i):
        for j in range(3):
            copies[4 + 7 * j + i].wait()

    def leave(i):
        for j in range(4):
            store[7 * j + i].start()

    for i in range(4):
        copies[i].wait()
    where = (((0, 0), (1, 1), (2, 6), (3, 4)), ((0, 2), (1, 5)), ((0, 3), (1, 7)))
    for i, pairs in enumerate(where):
        arrive(i)
        for at, u in pairs:
            update(i, at, res[u])
        leave(i)
    arrive(3)
    for j in range(4):
        update(3, (slice(None), slice(768 * j, 768 * j + 768)), res[8 + j])
    leave(3)
    for one, two in zip(inward, onward):
        one.wait()
        two.start()
    arrive(4)
    for h in range(2):
        update(4, (slice(48 * h, 48 * h + 48), slice(None)), last[h])
    leave(4)
    arrive(5)
    place = lax.broadcasted_iota(jnp.int32, (256, 24), 0) - lax.broadcasted_iota(jnp.int32, (256, 24), 1)
    for g in range(3):
        total = jnp.zeros((8, 24), F32)
        for i in range(3):
            mine = (place + 256 * i == 24 * device).astype(F32)
            rows = jnp.broadcast_to(small[12 + 3 * g + i:13 + 3 * g + i, :], (8, 256))
            total = total + lax.dot_general(
                rows, mine, (((1,), (0,)), ((), ())), precision=highest, preferred_element_type=F32
            )
        update(5, (slice(g, g + 1), slice(None)), total[0:1])
    leave(5)
    arrive(6)
    table_grad = lax.dot_general(
        small[0:16, :], reverse[...], (((1,), (1,)), ((), ())), precision=highest, preferred_element_type=F32
    )
    update(6, (slice(None), slice(None)), table_grad[:HEADS])
    leave(6)
    for copy in (*store, *onward):
        copy.wait()


def run_adam(*operands):
    far = pl.BlockSpec(memory_space=pltpu.HBM)
    shapes = [jax.ShapeDtypeStruct(a.shape, a.dtype) for a in operands]
    masters = shapes[7:14]
    outs = (*masters * 3, *[jax.ShapeDtypeStruct(a.shape, BF) for a in masters])
    return pl.pallas_call(
        adam_kernel,
        out_shape=(*shapes[:3], *outs),
        in_specs=[far] * len(operands),
        out_specs=[far] * 31,
        scratch_shapes=[
            *[pltpu.VMEM(a.shape, a.dtype) for a in (*shapes[3:], *outs, *shapes[:3])],
            pltpu.SemaphoreType.DMA((3, 28)),
        ],
        compiler_params=pltpu.CompilerParams(vmem_limit_bytes=60 * 2**20),
    )(*operands)


SCHEDULE = (
    "X0", "G7own", "G6own", "K1", "G2own", "G1own", "G7L1", "G5own", "G7R1", "G6L1", "K2", "G0own", "G7L2",
    "G6R1", "G7R2", "G2cross", "K3", "G7R3", "G6R2", "G1cross", "G7L3", "G0cross", "G4own", "G2R1",
    "G7cross", "K4", "G3own", "G2L1", "G0R1", "G6L2", "K5", "G0L1", "G2R2", "G2L2", "G6L3", "K6", "G0L2",
    "G0R2", "G2L3", "G1R1", "G2R3", "G7second", "G1L1", "G6R3", "G0L3", "G3cross", "G0R3", "G7finish",
    "G2second", "T0gain", "G2finish", "G6cross", "T0memory", "G1R2", "G2drain", "G1L2", "T0n1", "T0v2",
    "G0second", "G3L1", "G7drain", "G3R1", "G0finish", "T0k2", "G0drain", "G1R3", "T0q1", "G1L3", "G3L2",
    "G3R2", "G4cross", "T0k1", "G1second", "G1finish", "T0v1", "G3R3", "G3L3", "T1A1", "T0A1", "G4L1",
    "G4R1", "T2A1", "G3second", "T0o1", "T0n2", "G4L2", "G4R2", "G3finish", "G5cross", "T0q2", "G6second",
    "T2A2", "G4L3", "G4R3", "T1A2", "T0A2", "G3drain", "G5L1", "G5R1", "T0o2", "G6finish", "G6drain",
    "G4second", "T0n3", "T0begin", "G5R2", "G4finish", "G5L2", "G4drain", "T0act", "T0back", "T0W", "T0out",
    "G5R3", "G5L3", "T0grads", "T1act", "T1back", "T1out", "G5second", "T1W", "T1grads", "S4start",
    "G5finish", "G5drain", "T2act", "T2out", "S4core", "T2back", "T2grads", "T2W", "T3act", "T3back", "T3W",
    "S5start", "G1drain", "T3out", "T3grads", "S6start", "T0low", "S5core", "T0nb3", "S7start", "T0do2",
    "T0w7", "T1B2", "S4half", "S7core", "S6core", "T0B2", "T2B2", "T0dn2", "T0w6", "S3start", "S5half",
    "S4z1", "T0mg", "T0w5", "T0w4", "S2start", "T0nb2", "S6half", "S2core", "T0do1", "S5z1", "S3core",
    "S5z2", "T2B1", "S7half", "S4z2", "T0B1", "T1B1", "S6cross_in", "S6z1", "S2half", "T0dn1", "S2z1",
    "T0w2", "T0w0", "T0w3", "S1start", "T0w1", "S2z2", "S0start", "S1core", "S7cross_in", "S3half", "S0core",
    "S3z1", "S2z3", "S3z2", "T0nb1", "S7z1", "S4z3", "S1half", "R0", "S0half", "S5z3", "S1z1", "R1", "S0z1",
    "S1z2", "S0z2", "S5last", "S4last", "S5finish", "S4finish", "R2", "S2last", "S3z3", "S1z3", "R3", "S7z2",
    "S3last", "S6z2", "S0z3", "S1last", "R4", "S7z3", "S1finish", "R5", "S0last", "S2finish", "R6",
    "S3finish", "R7", "S6z3", "S0finish",
)


def shards_block(
    hidden, memory, cotangent, target_lengths, memory_lengths,
    qk_master, value_master, output_master, inner_master, outer_master, gain_master, table_master,
    qk_first, value_first, output_first, inner_first, outer_first, gain_first, table_first,
    qk_second, value_second, output_second, inner_second, outer_second, gain_second, table_second,
):
    place = np.arange(768)
    spread = (place[None, :] % 24 == np.arange(128)[:, None]).astype(jnp.bfloat16)
    owner = (place[None, :] // 24 == np.arange(32)[:, None]).astype(np.float32)
    by_distance = bucket_rows(256)
    flat = lambda a: a.reshape(512, 768)
    low_out, hidden_grad, memory_grad, res, last, small = run_layer(
        tuple((s[0], int(s[1]), s[2:]) for s in SCHEDULE), target_lengths.T, memory_lengths.T, flat(hidden), flat(memory), flat(cotangent),
        qk_master, value_master, output_master, inner_master, outer_master, gain_master, table_master.T,
        spread, owner, np.roll(by_distance[:, ::-1], 1, axis=1),
    )
    low_out, hidden_grad, memory_grad, *rest = run_adam(
        low_out, hidden_grad, memory_grad, res, last, small, by_distance[:, ::-1],
        qk_master, value_master, output_master, inner_master, outer_master, gain_master, table_master.T,
        qk_first, value_first, output_first, inner_first, outer_first, gain_first, table_first.T,
        qk_second, value_second, output_second, inner_second, outer_second, gain_second, table_second.T,
    )
    for i in (6, 13, 20, 27):
        rest[i] = rest[i].T
    whole = lambda a: a.reshape(2, 1, 256, 768)
    return whole(low_out), whole(hidden_grad), whole(memory_grad), *rest


def solution(mesh):
    placed = (
        P(None, ("dp", "fsdp"), None, None),
        P(None, ("dp", "fsdp"), None, None),
        P(None, ("dp", "fsdp"), None, None),
        P(None, ("dp", "fsdp")),
        P(None, ("dp", "fsdp")),
        P(None, ("dp", "fsdp"), None),
        P(None, ("dp", "fsdp"), None),
        P(None, ("dp", "fsdp"), None),
        P(("dp", "fsdp"), None),
        P(("dp", "fsdp"), None),
        P(None, ("dp", "fsdp")),
        P(),
        P(None, ("dp", "fsdp"), None),
        P(None, ("dp", "fsdp"), None),
        P(None, ("dp", "fsdp"), None),
        P(("dp", "fsdp"), None),
        P(("dp", "fsdp"), None),
        P(None, ("dp", "fsdp")),
        P(),
        P(None, ("dp", "fsdp"), None),
        P(None, ("dp", "fsdp"), None),
        P(None, ("dp", "fsdp"), None),
        P(("dp", "fsdp"), None),
        P(("dp", "fsdp"), None),
        P(None, ("dp", "fsdp")),
        P(),
    )
    small_slice = dict(mesh.shape) == {"dp": 8, "fsdp": 4}
    return jax.shard_map(
        shards_block if small_slice else shards,
        mesh=mesh,
        in_specs=placed,
        out_specs=(
            P(None, ("dp", "fsdp"), None, None),
            P(None, ("dp", "fsdp"), None, None),
            P(None, ("dp", "fsdp"), None, None),
            P(None, ("dp", "fsdp"), None),
            P(None, ("dp", "fsdp"), None),
            P(None, ("dp", "fsdp"), None),
            P(("dp", "fsdp"), None),
            P(("dp", "fsdp"), None),
            P(None, ("dp", "fsdp")),
            P(),
            P(None, ("dp", "fsdp"), None),
            P(None, ("dp", "fsdp"), None),
            P(None, ("dp", "fsdp"), None),
            P(("dp", "fsdp"), None),
            P(("dp", "fsdp"), None),
            P(None, ("dp", "fsdp")),
            P(),
            P(None, ("dp", "fsdp"), None),
            P(None, ("dp", "fsdp"), None),
            P(None, ("dp", "fsdp"), None),
            P(("dp", "fsdp"), None),
            P(("dp", "fsdp"), None),
            P(None, ("dp", "fsdp")),
            P(),
            P(None, ("dp", "fsdp"), None),
            P(None, ("dp", "fsdp"), None),
            P(None, ("dp", "fsdp"), None),
            P(("dp", "fsdp"), None),
            P(("dp", "fsdp"), None),
            P(None, ("dp", "fsdp")),
            P(),
        ),
        check_vma=False,
    )
```

```python
import functools
import math

import jax
import jax.numpy as jnp
import numpy as np
from jax import lax
from jax.experimental import pallas as pl
from jax.experimental.pallas import tpu as pltpu
from jax.sharding import PartitionSpec as P

HEADS = 12
HEAD_DIM = 64
BUCKETS = 32
MAX_DIST = 128
STEP = 10


epsilon_norm = 1e-06
score_scale = 0.125
masked_score = -1e30
beta_first = 0.9
beta_second = 0.999
adam_epsilon = 1e-08
rate_matrix = 0.15
rate_small = 1.0
weight_decay = 0.01
highest = lax.Precision.HIGHEST


def bucket_onehot(length):
    places = jnp.arange(length, dtype=jnp.int32)
    distance = jnp.maximum(places[:, None] - places[None, :], 0)
    exact_range = BUCKETS // 2
    safe_distance = jnp.maximum(distance, 1).astype(jnp.float32)
    spread = (
        jnp.log(safe_distance / exact_range)
        / math.log(MAX_DIST / exact_range)
        * (BUCKETS - exact_range)
    )
    far_bucket = jnp.minimum(exact_range + spread.astype(jnp.int32), BUCKETS - 1)
    bucket = jnp.where(distance < exact_range, distance, far_bucket)
    labels = jnp.arange(BUCKETS, dtype=jnp.int32)
    return (bucket[None, :, :] == labels[:, None, None]).astype(jnp.float32)


def product(left_side, right_side):
    return jnp.dot(left_side, right_side, preferred_element_type=jnp.float32)


def product_over_rows(left_side, right_side):
    return lax.dot_general(
        left_side, right_side, (((0,), (0,)), ((), ())), preferred_element_type=jnp.float32
    )


def product_transposed(left_side, right_side):
    return lax.dot_general(
        left_side, right_side, (((1,), (1,)), ((), ())), preferred_element_type=jnp.float32
    )


def to_heads(values, sequences):
    return values.reshape(sequences, -1, HEADS, HEAD_DIM)


def normalize(values, gain_row):
    scale_rows = lax.rsqrt(jnp.mean(values * values, axis=-1, keepdims=True) + epsilon_norm)
    unit_rows = values * scale_rows
    return ((unit_rows * gain_row).astype(jnp.bfloat16), unit_rows, scale_rows)


def normalize_back(grad_norm, unit_rows, scale_rows, gain_row):
    gain_grad = jnp.sum(grad_norm * unit_rows, axis=0)
    grad_unit = grad_norm * gain_row
    grad_values = scale_rows * (
        grad_unit - unit_rows * jnp.mean(grad_unit * unit_rows, axis=-1, keepdims=True)
    )
    return (grad_values, gain_grad)


def attend_scores(queries, key_heads, bias_term, allowed):
    scores = (
        jnp.einsum("sihe,sjhe->shij", queries, key_heads, preferred_element_type=jnp.float32)
        * score_scale
        + bias_term
    )
    return jnp.where(allowed, scores, masked_score)


def attend_forward(queries, key_heads, value_heads, bias_term, allowed):
    scores = attend_scores(queries, key_heads, bias_term, allowed)
    row_max = jnp.max(scores, axis=-1, keepdims=True)
    expanded = jnp.exp(scores - row_max)
    row_total = jnp.sum(expanded, axis=-1, keepdims=True)
    weights = (expanded / row_total).astype(jnp.bfloat16)
    mixed_heads = jnp.einsum(
        "shij,sjhe->sihe", weights, value_heads, preferred_element_type=jnp.float32
    )
    return (mixed_heads, row_max + jnp.log(row_total))


def attend_back(queries, key_heads, value_heads, bias_term, allowed, summary, grad_mixed):
    scores = attend_scores(queries, key_heads, bias_term, allowed)
    weights = jnp.exp(scores - summary)
    grad_weights = jnp.einsum(
        "sihe,sjhe->shij", grad_mixed, value_heads, preferred_element_type=jnp.float32
    )
    grad_values = jnp.einsum(
        "shij,sihe->sjhe",
        weights.astype(jnp.bfloat16),
        grad_mixed,
        preferred_element_type=jnp.float32,
    )
    grad_scores = (
        weights * (grad_weights - jnp.sum(weights * grad_weights, axis=-1, keepdims=True))
    ).astype(jnp.bfloat16)
    grad_queries = (
        jnp.einsum("shij,sjhe->sihe", grad_scores, key_heads, preferred_element_type=jnp.float32)
        * score_scale
    )
    grad_keys = (
        jnp.einsum("shij,sihe->sjhe", grad_scores, queries, preferred_element_type=jnp.float32)
        * score_scale
    )
    return (grad_queries, grad_keys, grad_values, grad_scores)


def forward_pass(gathered, bias_heads, hidden_seq, memory_seq, target_len, memory_len):
    qk_full, value_full, output_full, inner_full, outer_full, gain_full = gathered
    gain_rows = gain_full.astype(jnp.float32)
    sequences, length, model_width = hidden_seq.shape
    memory_span = memory_seq.shape[1]
    row_count = sequences * length
    residual = hidden_seq.astype(jnp.float32).reshape(row_count, model_width)
    memory_rows = memory_seq.reshape(sequences * memory_span, model_width)
    places = jnp.arange(length, dtype=jnp.int32)
    self_mask = (places[None, :] <= places[:, None])[None, None] & (
        places[None, None, None, :] < target_len[:, None, None, None]
    )
    memory_places = jnp.arange(memory_span, dtype=jnp.int32)
    cross_mask = (memory_places[None, :] < memory_len[:, None])[:, None, None, :]
    normed_first, unit_first, scale_first = normalize(residual, gain_rows[0])
    query_first = product(normed_first, qk_full[0]).astype(jnp.bfloat16)
    key_first = product(normed_first, qk_full[1]).astype(jnp.bfloat16)
    value_first = product(normed_first, value_full[0]).astype(jnp.bfloat16)
    mixed_first, summary_first = attend_forward(
        to_heads(query_first, sequences),
        to_heads(key_first, sequences),
        to_heads(value_first, sequences),
        bias_heads,
        self_mask,
    )
    mixed_first = mixed_first.reshape(row_count, model_width).astype(jnp.bfloat16)
    first_sum = residual + product(mixed_first, output_full[0])
    normed_second, unit_second, scale_second = normalize(first_sum, gain_rows[1])
    query_second = product(normed_second, qk_full[2]).astype(jnp.bfloat16)
    key_second = product(memory_rows, qk_full[3]).astype(jnp.bfloat16)
    value_second = product(memory_rows, value_full[1]).astype(jnp.bfloat16)
    mixed_second, summary_second = attend_forward(
        to_heads(query_second, sequences),
        to_heads(key_second, sequences),
        to_heads(value_second, sequences),
        0.0,
        cross_mask,
    )
    mixed_second = mixed_second.reshape(row_count, model_width).astype(jnp.bfloat16)
    second_sum = first_sum + product(mixed_second, output_full[1])
    normed_third, unit_third, scale_third = normalize(second_sum, gain_rows[2])
    inner_act = product(normed_third, inner_full)
    activated = jax.nn.gelu(inner_act, approximate=True).astype(jnp.bfloat16)
    produced = (second_sum + product(activated, outer_full)).astype(jnp.bfloat16)
    stored = (
        self_mask,
        cross_mask,
        memory_rows,
        normed_first,
        unit_first,
        scale_first,
        query_first,
        key_first,
        value_first,
        summary_first,
        mixed_first,
        normed_second,
        unit_second,
        scale_second,
        query_second,
        key_second,
        value_second,
        summary_second,
        mixed_second,
        normed_third,
        unit_third,
        scale_third,
        inner_act,
        activated,
    )
    return (stored, produced.reshape(sequences, length, model_width))


def backward_pass(gathered, bias_heads, stored, cotangent_seq, target_len):
    qk_full, value_full, output_full, inner_full, outer_full, gain_full = gathered
    gain_rows = gain_full.astype(jnp.float32)
    (
        self_mask,
        cross_mask,
        memory_rows,
        normed_first,
        unit_first,
        scale_first,
        query_first,
        key_first,
        value_first,
        summary_first,
        mixed_first,
        normed_second,
        unit_second,
        scale_second,
        query_second,
        key_second,
        value_second,
        summary_second,
        mixed_second,
        normed_third,
        unit_third,
        scale_third,
        inner_act,
        activated,
    ) = stored
    sequences, length, model_width = cotangent_seq.shape
    row_count = sequences * length
    places = jnp.arange(length, dtype=jnp.int32)
    live_rows = (places[None, :] < target_len[:, None]).astype(jnp.float32).reshape(row_count, 1)
    grad_out = cotangent_seq.astype(jnp.float32).reshape(row_count, model_width) * live_rows
    branch = grad_out.astype(jnp.bfloat16)
    outer_grad = product_over_rows(activated, branch)
    grad_act = product_transposed(branch, outer_full)
    unused_value, gelu_pull = jax.vjp(
        lambda inputs: jax.nn.gelu(inputs, approximate=True), inner_act
    )
    grad_inner = gelu_pull(grad_act)[0].astype(jnp.bfloat16)
    inner_grad = product_over_rows(normed_third, grad_inner)
    grad_from_third, gain_third = normalize_back(
        product_transposed(grad_inner, inner_full), unit_third, scale_third, gain_rows[2]
    )
    grad_second = grad_out + grad_from_third
    branch = grad_second.astype(jnp.bfloat16)
    output_grad_second = product_over_rows(mixed_second, branch)
    grad_mixed = product_transposed(branch, output_full[1]).astype(jnp.bfloat16)
    grad_query, grad_key, grad_value, unused_scores = attend_back(
        to_heads(query_second, sequences),
        to_heads(key_second, sequences),
        to_heads(value_second, sequences),
        0.0,
        cross_mask,
        summary_second,
        to_heads(grad_mixed, sequences),
    )
    grad_query = grad_query.reshape(row_count, model_width).astype(jnp.bfloat16)
    grad_key = grad_key.reshape(memory_rows.shape[0], model_width).astype(jnp.bfloat16)
    grad_value = grad_value.reshape(memory_rows.shape[0], model_width).astype(jnp.bfloat16)
    qk_grad_two = product_over_rows(normed_second, grad_query)
    qk_grad_three = product_over_rows(memory_rows, grad_key)
    value_grad_one = product_over_rows(memory_rows, grad_value)
    memory_grad = product_transposed(grad_key, qk_full[3]) + product_transposed(
        grad_value, value_full[1]
    )
    grad_from_second, gain_second = normalize_back(
        product_transposed(grad_query, qk_full[2]), unit_second, scale_second, gain_rows[1]
    )
    grad_first = grad_second + grad_from_second
    branch = grad_first.astype(jnp.bfloat16)
    output_grad_first = product_over_rows(mixed_first, branch)
    grad_mixed = product_transposed(branch, output_full[0]).astype(jnp.bfloat16)
    grad_query, grad_key, grad_value, grad_scores = attend_back(
        to_heads(query_first, sequences),
        to_heads(key_first, sequences),
        to_heads(value_first, sequences),
        bias_heads,
        self_mask,
        summary_first,
        to_heads(grad_mixed, sequences),
    )
    grad_query = grad_query.reshape(row_count, model_width).astype(jnp.bfloat16)
    grad_key = grad_key.reshape(row_count, model_width).astype(jnp.bfloat16)
    grad_value = grad_value.reshape(row_count, model_width).astype(jnp.bfloat16)
    qk_grad_zero = product_over_rows(normed_first, grad_query)
    qk_grad_one = product_over_rows(normed_first, grad_key)
    value_grad_zero = product_over_rows(normed_first, grad_value)
    grad_norm = (
        product_transposed(grad_query, qk_full[0])
        + product_transposed(grad_key, qk_full[1])
        + product_transposed(grad_value, value_full[0])
    )
    grad_from_first, gain_first = normalize_back(grad_norm, unit_first, scale_first, gain_rows[0])
    hidden_grad = grad_first + grad_from_first
    score_term = jnp.sum(grad_scores.astype(jnp.float32), axis=0)
    grad_terms = (
        jnp.stack([qk_grad_zero, qk_grad_one, qk_grad_two, qk_grad_three]),
        jnp.stack([value_grad_zero, value_grad_one]),
        jnp.stack([output_grad_first, output_grad_second]),
        inner_grad,
        outer_grad,
        jnp.stack([gain_first, gain_second, gain_third]),
    )
    return (
        grad_terms,
        score_term,
        hidden_grad.reshape(sequences, length, model_width),
        memory_grad.reshape(sequences, -1, model_width),
    )


def adam_step(master, first_moment, second_moment, gradient, rate, decay):
    first_next = beta_first * first_moment + (1.0 - beta_first) * gradient
    second_next = beta_second * second_moment + (1.0 - beta_second) * gradient * gradient
    corrected = (
        first_next
        / (1.0 - beta_first**STEP)
        / (jnp.sqrt(second_next / (1.0 - beta_second**STEP)) + adam_epsilon)
    )
    master_next = master - rate * (corrected + decay * master)
    return (master_next, first_next, second_next)


def shards(
    hidden,
    memory,
    cotangent,
    target_lengths,
    memory_lengths,
    qk_master,
    value_master,
    output_master,
    inner_master,
    outer_master,
    gain_master,
    table_master,
    qk_first,
    value_first,
    output_first,
    inner_first,
    outer_first,
    gain_first,
    table_first,
    qk_second,
    value_second,
    output_second,
    inner_second,
    outer_second,
    gain_second,
    table_second,
):
    micro_count = hidden.shape[0]
    length = hidden.shape[2]
    model_width = hidden.shape[3]
    hidden_units = inner_master.shape[1]
    qk_low = qk_master.astype(jnp.bfloat16)
    value_low = value_master.astype(jnp.bfloat16)
    output_low = output_master.astype(jnp.bfloat16)
    inner_low = inner_master.astype(jnp.bfloat16)
    outer_low = outer_master.astype(jnp.bfloat16)
    gain_low = gain_master.astype(jnp.bfloat16)
    onehot = bucket_onehot(length)
    bias_heads = jnp.einsum("bij,bh->hij", onehot, table_master, precision=highest)
    masters = (qk_master, value_master, output_master, inner_master, outer_master, gain_master)
    totals = (
        jnp.zeros((4, model_width, model_width), jnp.float32),
        jnp.zeros((2, model_width, model_width), jnp.float32),
        jnp.zeros((2, model_width, model_width), jnp.float32),
        jnp.zeros((model_width, hidden_units), jnp.float32),
        jnp.zeros((hidden_units, model_width), jnp.float32),
        jnp.zeros((3, model_width), jnp.float32),
    )
    reduced = tuple((jnp.zeros_like(master) for master in masters))
    score_total = jnp.zeros((HEADS, length, length), jnp.float32)
    produced_list = []
    hidden_list = []
    memory_list = []
    for micro_index in range(micro_count):
        gathered = (
            lax.all_gather(qk_low, ("dp", "fsdp"), axis=1, tiled=True),
            lax.all_gather(value_low, ("dp", "fsdp"), axis=1, tiled=True),
            lax.all_gather(output_low, ("dp", "fsdp"), axis=1, tiled=True),
            lax.all_gather(inner_low, ("dp", "fsdp"), axis=0, tiled=True),
            lax.all_gather(outer_low, ("dp", "fsdp"), axis=0, tiled=True),
            lax.all_gather(gain_low, ("dp", "fsdp"), axis=1, tiled=True),
        )
        stored, produced = forward_pass(
            gathered,
            bias_heads,
            hidden[micro_index],
            memory[micro_index],
            target_lengths[micro_index],
            memory_lengths[micro_index],
        )
        gathered = (
            lax.all_gather(qk_low, ("dp", "fsdp"), axis=1, tiled=True),
            lax.all_gather(value_low, ("dp", "fsdp"), axis=1, tiled=True),
            lax.all_gather(output_low, ("dp", "fsdp"), axis=1, tiled=True),
            lax.all_gather(inner_low, ("dp", "fsdp"), axis=0, tiled=True),
            lax.all_gather(outer_low, ("dp", "fsdp"), axis=0, tiled=True),
            lax.all_gather(gain_low, ("dp", "fsdp"), axis=1, tiled=True),
        )
        grad_terms, score_term, hidden_grad, memory_grad = backward_pass(
            gathered, bias_heads, stored, cotangent[micro_index], target_lengths[micro_index]
        )
        totals = tuple((running + addition for running, addition in zip(totals, grad_terms)))
        score_total = score_total + score_term
        produced_list.append(produced)
        hidden_list.append(hidden_grad)
        memory_list.append(memory_grad)
    reduced = (
        lax.psum_scatter(totals[0], ("dp", "fsdp"), scatter_dimension=1, tiled=True),
        lax.psum_scatter(totals[1], ("dp", "fsdp"), scatter_dimension=1, tiled=True),
        lax.psum_scatter(totals[2], ("dp", "fsdp"), scatter_dimension=1, tiled=True),
        lax.psum_scatter(totals[3], ("dp", "fsdp"), scatter_dimension=0, tiled=True),
        lax.psum_scatter(totals[4], ("dp", "fsdp"), scatter_dimension=0, tiled=True),
        lax.psum_scatter(totals[5], ("dp", "fsdp"), scatter_dimension=1, tiled=True),
    )
    table_grad = jnp.einsum("bij,hij->bh", onehot, score_total, precision=highest)
    table_grad = lax.psum(table_grad, ("dp", "fsdp"))
    all_masters = (
        qk_master,
        value_master,
        output_master,
        inner_master,
        outer_master,
        gain_master,
        table_master,
    )
    firsts = (
        qk_first,
        value_first,
        output_first,
        inner_first,
        outer_first,
        gain_first,
        table_first,
    )
    seconds = (
        qk_second,
        value_second,
        output_second,
        inner_second,
        outer_second,
        gain_second,
        table_second,
    )
    gradients = (reduced[0], reduced[1], reduced[2], reduced[3], reduced[4], reduced[5], table_grad)
    rates = (
        rate_matrix,
        rate_matrix,
        rate_matrix,
        rate_matrix,
        rate_matrix,
        rate_small,
        rate_small,
    )
    decays = (weight_decay, weight_decay, weight_decay, weight_decay, weight_decay, 0.0, 0.0)
    updated = [
        adam_step(
            all_masters[index],
            firsts[index],
            seconds[index],
            gradients[index],
            rates[index],
            decays[index],
        )
        for index in range(7)
    ]
    news = [entry[0] for entry in updated]
    first_news = [entry[1] for entry in updated]
    second_news = [entry[2] for entry in updated]
    copies = [entry.astype(jnp.bfloat16) for entry in news]
    layer_out = jnp.stack(produced_list)
    hidden_out = jnp.stack(hidden_list)
    memory_out = jnp.stack(memory_list)
    return (
        layer_out,
        hidden_out,
        memory_out,
        news[0],
        news[1],
        news[2],
        news[3],
        news[4],
        news[5],
        news[6],
        first_news[0],
        first_news[1],
        first_news[2],
        first_news[3],
        first_news[4],
        first_news[5],
        first_news[6],
        second_news[0],
        second_news[1],
        second_news[2],
        second_news[3],
        second_news[4],
        second_news[5],
        second_news[6],
        copies[0],
        copies[1],
        copies[2],
        copies[3],
        copies[4],
        copies[5],
        copies[6],
    )


MESH = pl.DeviceIdType.MESH
PAIRS = 6
SCATTER_ORDERS = ("cx", "cy", "ax", "ay", "ax", "cy", "ax", "ay")
ORDERS = ("ax", "ay", "cx", "ay", "ax", "ay", "cx", "ay")


class Place:
    def __init__(self, wa, wf):
        self.wa, self.wf = wa, wf
        dp, fs = lax.axis_index("dp"), lax.axis_index("fsdp")
        self.z, self.y = dp // 2, dp % 2
        self.x, self.c = fs // 2, fs % 2
        self.to = {
            "x": (dp, (1 - self.x) * 2 + self.c),
            "y": (self.z * 2 + 1 - self.y, fs),
            "c": (dp, self.x * 2 + 1 - self.c),
            "r": (dp + 2, fs),
            "l": (dp - 2, fs),
        }

    def enter(self, wait):
        bar = pltpu.get_barrier_semaphore()
        inner = (self.z > 0) & (self.z < 3)
        if wait:
            @pl.when(inner)
            def _():
                pl.semaphore_wait(bar, 5)

            @pl.when(jnp.logical_not(inner))
            def _():
                pl.semaphore_wait(bar, 4)

            return

        def greet(way):
            pl.semaphore_signal(bar, inc=1, device_id=self.to[way], device_id_type=MESH)

        for way in ("x", "y", "c"):
            greet(way)

        @pl.when(self.z < 3)
        def _():
            greet("r")

        @pl.when(self.z > 0)
        def _():
            greet("l")

    def pick(self, f, zs, ps, qs, core=None):
        c = self.c if core is None else core
        xs, ys = (ps, qs) if ORDERS[f][1] == "x" else (qs, ps)
        return self.block(f, zs, ys, xs, c)

    def block(self, f, zs, ys, xs, c):
        if f < PAIRS:
            return self.wa.at[2 * f + c, zs, ys, xs]
        return self.wf.at[zs, ys, xs, c, f - PAIRS]

    def own(self, f):
        return (self.x, self.y) if ORDERS[f][1] == "x" else (self.y, self.x)

    def ways(self, f):
        return ("x", "y") if ORDERS[f][1] == "x" else ("y", "x")


def push(place, src, dst, send, recv, way):
    pltpu.make_async_remote_copy(
        src_ref=src, dst_ref=dst, send_sem=send, recv_sem=recv,
        device_id=place.to[way], device_id_type=MESH,
    ).start()


def got(place, ref, sem, way):
    pltpu.make_async_remote_copy(
        src_ref=ref, dst_ref=ref, send_sem=sem, recv_sem=sem,
        device_id=place.to[way], device_id_type=MESH,
    ).wait_recv()


def left_out(place, ref, sem, way):
    pltpu.make_async_remote_copy(
        src_ref=ref, dst_ref=ref, send_sem=sem, recv_sem=sem,
        device_id=place.to[way], device_id_type=MESH,
    ).wait_send()


ALL = slice(None)


class Gather:
    def __init__(self, place, f, send, recv):
        self.k, self.f = place, f
        self.send, self.recv = send, recv
        self.first_cross = ORDERS[f][0] == "a"

    def do(self, name):
        if name[0] in "LR":
            self.step(int(name[1]), name[0])
        else:
            getattr(self, name)()

    def blk(self, zi):
        p, q = self.k.own(self.f)
        return self.k.pick(self.f, zi, ALL if self.first_cross else p, q)

    def move(self, ref, s, r, way):
        push(self.k, ref, ref, self.send.at[self.f, s], self.recv.at[self.f, r], way)

    def start(self):
        p, q = self.k.own(self.f)
        pw, qw = self.k.ways(self.f)
        if self.first_cross:
            self.move(self.k.pick(self.f, self.k.z, p, q), 0, 0, pw)
        else:
            self.spread(self.k.z, 1)

    def cross(self):
        p, q = self.k.own(self.f)
        pw, qw = self.k.ways(self.f)
        if self.first_cross:
            got(self.k, self.k.pick(self.f, self.k.z, 1 - p, q), self.recv.at[self.f, 0], pw)
            self.spread(self.k.z, 1)
        else:
            got(self.k, self.k.pick(self.f, ALL, 1 - p, q), self.recv.at[self.f, 0], pw)
            half = self.k.pick(self.f, ALL, ALL, q)
            self.move(half, 3, 7, qw)
            self.move(half, 4, 8, "c")

    def sideways(self, zi):
        pw, qw = self.k.ways(self.f)
        if self.first_cross:
            self.move(self.blk(zi), 3, 7, qw)
            self.move(self.blk(zi), 4, 8, "c")
        else:
            self.move(self.blk(zi), 0, 0, pw)

    def spread(self, zi, t):
        z = self.k.z

        @pl.when(z < 3)
        def _():
            self.move(self.blk(zi), 1, t, "r")

        @pl.when(z > 0)
        def _():
            self.move(self.blk(zi), 2, 3 + t, "l")

        self.sideways(zi)

    def step(self, t, side):
        z = self.k.z

        if side == "L":
            @pl.when(z >= t)
            def _():
                got(self.k, self.blk(z - t), self.recv.at[self.f, t], "l")

                if t < 3:
                    @pl.when(z < 3)
                    def _():
                        self.move(self.blk(z - t), 1, t + 1, "r")

                self.sideways(z - t)
        else:
            @pl.when(z <= 3 - t)
            def _():
                got(self.k, self.blk(z + t), self.recv.at[self.f, 3 + t], "r")

                if t < 3:
                    @pl.when(z > 0)
                    def _():
                        self.move(self.blk(z + t), 2, 3 + t + 1, "l")

                self.sideways(z + t)

    def second(self):
        p, q = self.k.own(self.f)
        pw, qw = self.k.ways(self.f)
        other = self.k.pick(self.f, ALL, ALL, 1 - q)
        got(self.k, other, self.recv.at[self.f, 7], qw)
        self.move(other, 4, 8, "c")

    def finish(self):
        theirs = self.k.pick(self.f, ALL, ALL, ALL, 1 - self.k.c)
        got(self.k, theirs, self.recv.at[self.f, 8], "c")

    def drain(self):
        p, q = self.k.own(self.f)
        pw, qw = self.k.ways(self.f)
        z, f = self.k.z, self.f
        some = (lambda n: self.k.pick(f, pl.ds(0, n), ALL if self.first_cross else p, q))
        first = self.k.pick(f, z, p, q) if self.first_cross else self.k.pick(f, ALL, p, q)
        left_out(self.k, first, self.send.at[f, 0], pw)
        for n in (1, 2, 3):
            @pl.when(z == n - 1)
            def _():
                left_out(self.k, some(n), self.send.at[f, 1], "r")

            @pl.when(z == 4 - n)
            def _():
                left_out(self.k, some(n), self.send.at[f, 2], "l")
        left_out(self.k, self.k.pick(f, ALL, ALL, q), self.send.at[f, 3], qw)
        left_out(self.k, self.k.pick(f, ALL, ALL, ALL), self.send.at[f, 4], "c")


def add_into(dst, srcs, lead):
    sizes = lead
    count = 1
    for s in sizes:
        count *= s

    def body(i, _):
        idx, rest = [], i
        for s in reversed(sizes):
            idx.append(rest % s)
            rest = rest // s
        idx = tuple(reversed(idx)) or Ellipsis
        total = dst[idx].astype(jnp.float32)
        for src in srcs:
            total = total + src[idx].astype(jnp.float32)
        dst[idx] = total.astype(jnp.bfloat16)
        return 0

    lax.fori_loop(0, count, body, 0)


PIECES = (slice(3, 4), slice(0, 1), slice(1, 3))


class Scatter:
    def __init__(self, place, f, send, recv, slots, final, result, credit):
        self.k, self.f = place, f
        self.wait_credit, self.give_credit, self.credit = credit
        self.send, self.recv = send, recv
        self.rd, self.rq, self.rp, self.rl, self.rr = slots
        self.final, self.result = final, result
        self.wide = SCATTER_ORDERS[f][0] == "a"

    def do(self, name):
        if name[0] == "z":
            self.step_in(int(name[1]))
        elif name[-1] in "AB":
            getattr(self, name[:-1])((0, 1) if name[-1] == "A" else (2,))
        else:
            getattr(self, name)()

    def pick(self, zs, ps, qs, core=None):
        c = self.k.c if core is None else core
        xs, ys = (ps, qs) if SCATTER_ORDERS[self.f][1] == "x" else (qs, ps)
        return self.k.block(self.f, zs, ys, xs, c)

    def own(self):
        return (self.k.x, self.k.y) if SCATTER_ORDERS[self.f][1] == "x" else (self.k.y, self.k.x)

    def ways(self):
        return ("x", "y") if SCATTER_ORDERS[self.f][1] == "x" else ("y", "x")

    def move(self, src, dst, s, way):
        push(self.k, src, dst, self.send.at[self.f, s], self.recv.at[self.f, s], way)

    def blk(self, zi):
        p, q = self.own()
        return self.pick(zi, ALL if self.wide else p, q)

    def start(self, pieces):
        if self.wait_credit and 0 in pieces:
            pl.semaphore_wait(self.credit, 1)
        for i in pieces:
            self.move(self.pick(PIECES[i], ALL, ALL, 1 - self.k.c), self.rd.at[PIECES[i]], i, "c")

    def rpick(self, zs, ps, qs):
        xs, ys = (ps, qs) if SCATTER_ORDERS[self.f][1] == "x" else (qs, ps)
        return self.rd.at[zs, ys, xs]

    def core(self, pieces):
        p, q = self.own()
        pw, qw = self.ways()
        for i in pieces:
            zs = PIECES[i]
            n = zs.stop - zs.start
            got(self.k, self.rd.at[zs], self.recv.at[self.f, i], "c")
            away = self.pick(zs, ALL, 1 - q)
            add_into(away, [self.rpick(zs, ALL, 1 - q)], (n, 2))
            self.move(away, self.rq.at[zs], 3 + i, qw)

    def half(self, pieces):
        p, q = self.own()
        pw, qw = self.ways()
        for i in pieces:
            zs = PIECES[i]
            n = zs.stop - zs.start
            got(self.k, self.rq.at[zs], self.recv.at[self.f, 3 + i], qw)
            add_into(self.pick(zs, ALL, q), [self.rpick(zs, ALL, q), self.rq.at[zs]], (n, 2))
            if not self.wide:
                self.move(self.pick(zs, 1 - p, q), self.rp.at[zs], 6 + i, pw)
        if self.wide and 0 in pieces:
            self.step_out(1)
        if self.give_credit and 2 in pieces:
            pl.semaphore_signal(self.credit, inc=1, device_id=self.k.to["c"], device_id_type=MESH)

    def cross(self, pieces):
        p, q = self.own()
        pw, qw = self.ways()
        for i in pieces:
            zs = PIECES[i]
            n = zs.stop - zs.start
            got(self.k, self.rp.at[zs], self.recv.at[self.f, 6 + i], pw)
            add_into(self.pick(zs, p, q), [self.rp.at[zs]], (n,))
        if 0 in pieces:
            self.step_out(1)

    def step_out(self, t):
        z = self.k.z

        @pl.when(z <= t - 1)
        def _():
            self.move(self.blk(z + 4 - t), self.rl.at[t - 1], 8 + t, "r")

        @pl.when(z >= 4 - t)
        def _():
            self.move(self.blk(z - 4 + t), self.rr.at[t - 1], 11 + t, "l")

    def step_in(self, t):
        z, f = self.k.z, self.f
        lead = (2,) if self.wide else ()

        @pl.when((z >= 1) & (z <= t))
        def _():
            got(self.k, self.rl.at[t - 1], self.recv.at[f, 8 + t], "l")
            add_into(self.blk(z + 3 - t), [self.rl.at[t - 1]], lead)

        @pl.when((z <= 2) & (z >= 3 - t))
        def _():
            got(self.k, self.rr.at[t - 1], self.recv.at[f, 11 + t], "r")
            add_into(self.blk(z - 3 + t), [self.rr.at[t - 1]], lead)

        if t < 3:
            self.step_out(t + 1)
        else:
            p, q = self.own()
            pw, qw = self.ways()
            if self.wide:
                self.move(self.pick(z, 1 - p, q), self.rp, 6, pw)
            else:
                self.total(None)

    def last(self):
        pw, qw = self.ways()
        got(self.k, self.rp, self.recv.at[self.f, 6], pw)
        self.total(self.rp)

    def total(self, more):
        p, q = self.own()
        c = self.k.c
        mine = self.pick(self.k.z, p, q)[...].astype(jnp.float32)
        if more is not None:
            mine = mine + more[...].astype(jnp.float32)
        self.final[...] = mine
        if self.f < PAIRS:
            kept = pl.ds(pl.multiple_of(c * 24, 8), 24)
            away = pl.ds(pl.multiple_of(24 - c * 24, 8), 24)
            self.move(self.final.at[away], self.result.at[self.f, c], 15, "c")
            self.result[self.f, c] = self.final[kept]

    def finish(self):
        if self.f < PAIRS:
            got(self.k, self.result.at[self.f, 1 - self.k.c], self.recv.at[self.f, 15], "c")

    def drain(self):
        pw, qw = self.ways()
        z, f, k = self.k.z, self.f, self.k
        for i, zs in enumerate(PIECES):
            left_out(k, self.rd.at[zs], self.send.at[f, i], "c")
            left_out(k, self.rq.at[zs], self.send.at[f, 3 + i], qw)
            if not self.wide:
                left_out(k, self.rp.at[zs], self.send.at[f, 6 + i], pw)
        if self.wide:
            left_out(k, self.rp, self.send.at[f, 6], pw)
        for t in (1, 2, 3):
            @pl.when(z <= t - 1)
            def _():
                left_out(k, self.rl.at[t - 1], self.send.at[f, 8 + t], "r")

            @pl.when(z >= 4 - t)
            def _():
                left_out(k, self.rr.at[t - 1], self.send.at[f, 11 + t], "l")
        if f < PAIRS:
            left_out(k, self.final.at[pl.ds(0, 24)], self.send.at[f, 15], "c")


class Line:
    def __init__(self, place, buf, send, recv):
        self.k, self.buf, self.send, self.recv = place, buf, send, recv

    def move(self, zi, s, r, way):
        push(self.k, self.buf.at[zi], self.buf.at[zi], self.send.at[s], self.recv.at[r], way)

    def start(self):
        z = self.k.z

        @pl.when(z < 3)
        def _():
            self.move(z, 3, 3, "r")

        @pl.when(z > 0)
        def _():
            self.move(z, 6, 6, "l")

    def step(self, t):
        z = self.k.z

        @pl.when(z >= t)
        def _():
            got(self.k, self.buf.at[z - t], self.recv.at[2 + t], "l")

            if t < 3:
                @pl.when(z < 3)
                def _():
                    self.move(z - t, 3 + t, 3 + t, "r")

        @pl.when(z <= 3 - t)
        def _():
            got(self.k, self.buf.at[z + t], self.recv.at[5 + t], "r")

            if t < 3:
                @pl.when(z > 0)
                def _():
                    self.move(z + t, 6 + t, 6 + t, "l")

    def drain(self):
        z = self.k.z
        for t in range(3):
            @pl.when((z < 3) & (z >= t))
            def _():
                left_out(self.k, self.buf.at[0], self.send.at[3 + t], "r")

            @pl.when((z > 0) & (z <= 3 - t))
            def _():
                left_out(self.k, self.buf.at[0], self.send.at[6 + t], "l")


class Gains:
    def __init__(self, place, buf, send, recv):
        self.k, self.buf, self.send, self.recv = place, buf, send, recv
        self.line = Line(place, buf, send, recv)
        z, y, x, c = place.z, place.y, place.x, place.c
        self.mine = [buf.at[z, y, x, c], buf.at[z, y, x], buf.at[z, y]]
        self.other = [buf.at[z, y, x, 1 - c], buf.at[z, y, 1 - x], buf.at[z, 1 - y]]

    def go(self, i):
        if 1 <= i <= 3:
            got(self.k, self.other[i - 1], self.recv.at[i - 1], "cxy"[i - 1])
        if i < 3:
            push(self.k, self.mine[i], self.mine[i], self.send.at[i], self.recv.at[i], "cxy"[i])
        elif i == 3:
            self.line.start()
        else:
            self.line.step(i - 3)

    def drain(self):
        for i in range(3):
            left_out(self.k, self.mine[i], self.send.at[i], "cxy"[i])
        self.line.drain()


class Small:
    def __init__(self, place, bufs, got_bufs, along, send, recv):
        self.k, self.bufs, self.got_bufs, self.along = place, bufs, got_bufs, along
        self.send, self.recv = send, recv
        self.line = Line(place, along, send, recv)

    def go(self, i):
        if 1 <= i <= 3:
            got(self.k, self.got_bufs.at[i - 1], self.recv.at[i - 1], "cxy"[i - 1])
            total = self.bufs[i - 1] + self.got_bufs[i - 1]
            if i < 3:
                self.bufs[i] = total
            else:
                self.along[self.k.z] = total
        if i < 3:
            push(self.k, self.bufs.at[i], self.got_bufs.at[i], self.send.at[i], self.recv.at[i], "cxy"[i])
        elif i == 3:
            self.line.start()
        else:
            self.line.step(i - 3)

    def drain(self):
        for i in range(3):
            left_out(self.k, self.bufs.at[i], self.send.at[i], "cxy"[i])
        self.line.drain()
BF, F32 = jnp.bfloat16, jnp.float32
INNER_UNIT = (8, 10, 11, 9)
ROOT = math.sqrt(2.0 / math.pi)
CUBE = 0.044715


def dot_nn(a, b):
    return lax.dot_general(a, b, (((1,), (0,)), ((), ())), preferred_element_type=F32)


def dot_nt(a, b):
    return lax.dot_general(a, b, (((1,), (1,)), ((), ())), preferred_element_type=F32)


def dot_tn(a, b):
    return lax.dot_general(a, b, (((0,), (0,)), ((), ())), preferred_element_type=F32)


def unit_of(values):
    scale = lax.rsqrt(jnp.mean(values * values, axis=-1, keepdims=True) + epsilon_norm)
    return values * scale, scale


class Layer:
    def __init__(self, wa, wf, b):
        self.wa, self.wf, self.b = wa, wf, b

    def times(self, a, u, put):
        for t in range(3):
            tile = slice(256 * t, 256 * t + 256)
            put(tile, dot_nn(a[...], self.wa[u, :, :, :, :, tile].reshape(768, 256)))

    def times_back(self, pairs, put):
        total = None
        for a, u in pairs:
            term = dot_nt(a[...], self.wa[u].reshape(768, 768))
            total = term if total is None else total + term
        put(slice(0, 768), total)

    def weight_grad(self, a, d, u):
        for t in range(2):
            tile = dot_tn(a[:, 384 * t:384 * t + 384], d[...])
            self.wa[u, 2 * t:2 * t + 2] = tile.astype(BF).reshape(2, 2, 2, 48, 768)

    def project(self, a, u, dst):
        def put(tile, value):
            dst[:, tile] = value.astype(BF)

        self.times(a, u, put)

    def add_project(self, base, a, u, dst):
        def put(tile, value):
            dst[:, tile] = base[:, tile].astype(F32) + value

        self.times(a, u, put)

    def norm(self, src, g, dst):
        gain = self.b["gain"][pl.ds(g, 1), :]

        def body(i, _):
            rows = pl.ds(pl.multiple_of(64 * i, 64), 64)
            unit, _unused = unit_of(src[rows].astype(F32))
            dst[rows] = (unit * gain).astype(BF)
            return 0

        lax.fori_loop(0, 8, body, 0)

    def norm_back(self, dn, src, g, base, dst, low):
        gain = self.b["gain"][pl.ds(g, 1), :]

        def body(i, acc):
            rows = pl.ds(pl.multiple_of(64 * i, 64), 64)
            unit, scale = unit_of(src[rows].astype(F32))
            grad = dn[rows]
            acc = acc + jnp.sum(grad * unit, axis=0, keepdims=True)
            pulled = grad * gain
            value = base(rows, i) + scale * (pulled - unit * jnp.mean(pulled * unit, axis=-1, keepdims=True))
            dst[rows] = value
            if low is not None:
                low[rows] = value.astype(BF)
            return acc

        total = lax.fori_loop(0, 8, body, jnp.zeros((1, 768), F32))
        for i in range(3):
            self.b["small"][12 + 3 * g + i:13 + 3 * g + i, :] = total[:, 256 * i:256 * i + 256]

    def head_masks(self):
        lane = lax.broadcasted_iota(jnp.int32, (1, 128), 1)
        low = (lane < 64).astype(F32)
        return low.astype(BF), (1.0 - low).astype(BF)

    def far(self, s, kind):
        col = lax.broadcasted_iota(jnp.int32, (1, 256), 1)
        length = self.b["lens"][0, s] if kind == 1 else self.b["mem_lens"][0, s]
        return jnp.where(col < length, 0.0, masked_score)

    def bias(self, head, causal):
        row = self.b["bias_row"][pl.ds(head, 1), :]
        turned = pltpu.roll(jnp.broadcast_to(row, (256, 256)), 0, axis=1, stride=1, stride_axis=0)
        return jnp.where(causal, turned, masked_score)

    def weights(self, scores):
        expanded = jnp.exp(scores - jnp.max(scores, axis=-1, keepdims=True))
        return expanded * (1.0 / jnp.sum(expanded, axis=-1, keepdims=True))

    def places(self):
        row = lax.broadcasted_iota(jnp.int32, (256, 256), 0)
        col = lax.broadcasted_iota(jnp.int32, (256, 256), 1)
        return row, col

    def attend(self, kind, first, last):
        b = self.b
        q, k, v, o = (b[n + str(kind)] for n in "qkvo")
        masks = self.head_masks()
        keep = masks[0].astype(F32)
        row, col = self.places()

        def body(hp, _):
            lanes = pl.ds(pl.multiple_of(128 * hp, 128), 128)
            biases = [self.bias(2 * hp + e, col <= row) if kind == 1 else 0.0 for e in range(2)]
            rows = [slice(0, 256), slice(256, 512)]
            both = [(s, e) for s in range(2) for e in range(2)]
            queries = [q[r, lanes] * BF(score_scale) for r in rows]
            keys, values = [k[r, lanes] for r in rows], [v[r, lanes] for r in rows]
            far = [self.far(s, kind) for s in range(2)]
            scores = [dot_nt(queries[s] * masks[e], keys[s]) + (biases[e] + far[s]) for s, e in both]
            low = [self.weights(one).astype(BF) for one in scores]
            mixed = [dot_nn(p, values[s]) for p, (s, e) in zip(low, both)]
            for s in range(2):
                o[rows[s], lanes] = (mixed[2 * s] * keep + mixed[2 * s + 1] * (1.0 - keep)).astype(BF)
            return 0

        lax.fori_loop(first, last, body, 0)

    def attend_back(self, kind, first, last):
        b = self.b
        q, k, v = (b[n + str(kind)] for n in "qkv")
        masks = self.head_masks()
        row, col = self.places()
        flip = (row + col == 255).astype(F32).astype(BF)

        def body(hp, _):
            lanes = pl.ds(pl.multiple_of(128 * hp, 128), 128)
            biases = [self.bias(2 * hp + e, col <= row) if kind == 1 else 0.0 for e in range(2)]
            rows = [slice(0, 256), slice(256, 512)]
            both = [(s, e) for s in range(2) for e in range(2)]
            queries = [q[r, lanes] * BF(score_scale) for r in rows]
            keys, values = [k[r, lanes] for r in rows], [v[r, lanes] for r in rows]
            given = [b["do"][r, lanes] for r in rows]
            far = [self.far(s, kind) for s in range(2)]
            qe = [queries[s] * masks[e] for s, e in both]
            ge = [given[s] * masks[e] for s, e in both]
            scores = [dot_nt(one, keys[s]) + (biases[e] + far[s]) for one, (s, e) in zip(qe, both)]
            dps = [dot_nt(one, values[s]) for one, (s, e) in zip(ge, both)]
            ps = [self.weights(one) for one in scores]
            dss = [(p * (dp - jnp.sum(p * dp, axis=-1, keepdims=True))).astype(BF) for p, dp in zip(ps, dps)]
            low = [p.astype(BF) for p in ps]
            dv = [dot_tn(p, one) for p, one in zip(low, ge)]
            dk = [dot_tn(ds, one) for ds, one in zip(dss, qe)]
            dq = [dot_nn(ds, keys[s] * masks[e]) for ds, (s, e) in zip(dss, both)]
            if kind == 1:
                for e in range(2):
                    turned = dot_nn(flip, dss[e]) + dot_nn(flip, dss[2 + e])
                    turned = pltpu.roll(turned, 0, axis=1, stride=1, stride_axis=0)
                    b["small"][pl.ds(2 * hp + e, 1), :] = jnp.sum(turned, axis=0, keepdims=True)
            for s in range(2):
                q[rows[s], lanes] = ((dq[2 * s] + dq[2 * s + 1]) * score_scale).astype(BF)
                k[rows[s], lanes] = (dk[2 * s] + dk[2 * s + 1]).astype(BF)
                v[rows[s], lanes] = (dv[2 * s] + dv[2 * s + 1]).astype(BF)
            return 0

        lax.fori_loop(first, last, body, 0)

    def live(self, i):
        row = lax.broadcasted_iota(jnp.int32, (64, 1), 0) + 64 * lax.rem(i, 4)
        bound = jnp.where(i < 4, self.b["lens"][0, 0], self.b["lens"][0, 1])
        return (row < bound).astype(F32)

    def cotangent(self):
        b = self.b

        def body(i, _):
            rows = pl.ds(pl.multiple_of(64 * i, 64), 64)
            b["df"][rows] = (b["cot"][rows].astype(F32) * self.live(i)).astype(BF)
            return 0

        lax.fori_loop(0, 8, body, 0)

    def ffn_act(self, j):
        b = self.b
        for t in range(2):
            cols = slice(384 * t, 384 * t + 384)
            wi = self.wa[INNER_UNIT[j], :, :, :, :, cols].reshape(768, 384)
            wf = self.wf[j, t].reshape(384, 768)
            u = dot_nn(b["n3"][...], wi)
            square = u * u
            th = jnp.tanh(u * (ROOT + (ROOT * CUBE) * square))
            half = 0.5 + 0.5 * th
            b["act"][:, cols] = (u * half).astype(BF)
            slope = half + u * (1.0 - th * th) * (0.5 * ROOT + (1.5 * ROOT * CUBE) * square)
            da = dot_nt(b["df"][...], wf)
            b["du"][:, cols] = (da * slope).astype(BF)

    def ffn_out(self, j):
        b = self.b
        for t in range(3):
            cols = slice(256 * t, 256 * t + 256)
            wf = self.wf[j, :, :, :, :, :, cols].reshape(768, 256)
            b["y"][:, cols] += dot_nn(b["act"][...], wf)

    def ffn_back(self, j):
        b = self.b

        def put(tile, value):
            if j == 0:
                b["dn"][:, tile] = value
            else:
                b["dn"][:, tile] += value

        self.times_back([(b["du"], INNER_UNIT[j])], put)

    def ffn_grads(self, j):
        b = self.b
        for t in range(2):
            tile = dot_tn(b["act"][:, 384 * t:384 * t + 384], b["df"][...])
            self.wf[j, t] = tile.astype(BF).reshape(2, 2, 2, 48, 768)


SCATTER_ORDER = (4, 5, 6, 7, 3, 2, 1, 0)
WIDE = [f for f in range(8) if SCATTER_ORDERS[f][0] == "a"]
NARROW = [f for f in range(8) if SCATTER_ORDERS[f][0] == "c"]


def layer_kernel(program, lens, mem_lens, *refs):
    ins, outs, rest = refs[:13], refs[13:19], refs[19:]
    locals_in, locals_out, (in_sem, out_sem), rest = rest[:9], list(rest[9:13]), rest[13:15], rest[15:]
    masters, du = rest[0], rest[15]
    locals_out = [du, *locals_out[:2], masters, *locals_out[2:]]
    qk, value, output, inner = ins[3:7]
    units = [qk.at[0], qk.at[1], value.at[0], output.at[0], qk.at[3], value.at[1], qk.at[2], output.at[1]]
    units += [inner.at[:, 768 * j:768 * j + 768] for j in (0, 3, 1, 2)]
    pairs = [*zip((*ins[:3], *ins[7:]), locals_in), *((unit, masters.at[u // 2, u % 2]) for u, unit in enumerate(units))]
    fetch = [pltpu.make_async_copy(a, b, in_sem.at[i]) for i, (a, b) in enumerate(pairs)]
    store = [pltpu.make_async_copy(a, b, out_sem.at[i]) for i, (a, b) in enumerate(zip(locals_out, outs))]
    layer_body(program, lens, mem_lens, fetch, store, *locals_in, *locals_out[1:3], *locals_out[4:], *rest)


def layer_body(
    program, lens, mem_lens, fetch, store,
    hid, mem, cot, outer, gain_in, table, spread, owner, near,
    hidden_grad, memory_grad, last, small_out, masters,
    wa, wf, n1, q1, k1, v1, o1, n2, q2, k2, v2, o2, n3, act, du, df, x1, x2, dn,
    rd, rq, rlw, rrw, rpw, rln, rrn, rpn, fin, tiles, gain, bias_row, small, small_got, along,
    gs, gr, ss, sr, xs, xr, ks, kr, ms, mr, credit,
):
    k = Place(wa, wf)
    z, y, x, c = k.z, k.y, k.x, k.c
    b = dict(
        lens=lens, mem_lens=mem_lens, hid=hid, mem=mem, cot=cot, bias_row=bias_row, gain=gain, small=small.at[0],
        n1=n1, q1=q1, k1=k1, v1=v1, o1=o1, n2=n2, q2=q2, k2=k2, v2=v2, o2=o2, n3=n3,
        act=act, du=du, df=df, do=act, y=memory_grad, dn=dn,
    )
    net = Layer(wa, wf, b)
    gathers = [Gather(k, f, gs, gr) for f in range(8)]
    scatters = {}
    for i, f in enumerate(SCATTER_ORDER):
        if f in WIDE:
            n = WIDE.index(f)
            slots = (rd.at[i % 4], rq.at[f], rpw.at[n], rlw.at[n], rrw.at[n])
        else:
            n = NARROW.index(f)
            slots = (rd.at[i % 4], rq.at[f], rpn.at[n], rln.at[n], rrn.at[n])
        final = fin.at[f] if f < PAIRS else last.at[f - PAIRS]
        scatters[f] = Scatter(k, f, ss, sr, slots, final, masters, (i >= 4, i < 4, credit.at[i % 4]))
    gains = Gains(k, tiles, ks, kr)
    sums = Small(k, small, small_got, along, ms, mr)
    mine = pl.ds(pl.multiple_of(24 * c, 8), 24)
    other = pl.ds(pl.multiple_of(24 - 24 * c, 8), 24)

    def enter():
        for i in (4, *range(9, 21), 3, 5, 8, 0, 1, 2, 6, 7):
            fetch[i].start()
        k.enter(False)
        for i in (4, *range(9, 21)):
            fetch[i].wait()
        tiles[z, y, x, c] = jnp.zeros((8, 128), F32)
        tiles[z, y, x, c, 0:3, 0:24] = gain_in[...].astype(BF).astype(F32)
        k.enter(True)
        push(k, masters.at[:, 1 - c], fin.at[:, mine], xs, xr, "c")
        gains.go(0)
        for i in (3, 5, 8):
            fetch[i].wait()
        bias_row[...] = jnp.zeros_like(bias_row)
        bias_row[0:HEADS, :] = lax.dot_general(
            table[...], near[...], (((1,), (0,)), ((), ())), precision=highest, preferred_element_type=F32
        )
        for h in range(2):
            wf[z, y, x, c, h] = outer[48 * h:48 * h + 48].astype(BF)
        for p in range(PAIRS):
            fin[p, mine] = masters[p, c]

    def swap():
        got(k, fin.at[:, other], xr, "c")
        left_out(k, masters.at[:, 1 - c], xs, "c")

    def own(f):
        if f < PAIRS:
            wa[2 * f + c, z, y, x] = fin[f].astype(BF)
        gathers[f].start()

    def spread_gains():
        for i in (0, 6, 7):
            fetch[i].wait()
        flat = tiles[...].reshape(32, 8, 128)
        for g in range(3):
            lanes = dot_nn(flat[:, g].astype(BF), spread[...])
            gain[g:g + 1, :] = jnp.sum(lanes * owner[...], axis=0, keepdims=True)

    def put_do(tile, value):
        act[:, tile] = value.astype(BF)

    def put_dn(tile, value):
        dn[:, tile] = value

    def put_memory(tile, value):
        memory_grad[:, tile] = value

    def begin():
        fetch[2].wait()
        memory_grad[...] = x2[...]
        small[0] = jnp.zeros_like(small[0])
        net.cotangent()

    def finish_low():
        du[...] = memory_grad[...].astype(BF)
        store[0].start()

    def total_small():
        small_out[...] = along[0] + along[1] + along[2] + along[3]
        store[5].start()

    def mix_memory():
        net.times_back([(k2, 4), (v2, 5)], put_memory)
        store[2].start()

    def finish_hidden():
        net.norm_back(dn, hid, 0, lambda rows, i: grad[rows], grad, None)
        store[1].start()

    grad = hidden_grad
    tasks = {
        "gain": spread_gains,
        "n1": lambda: net.norm(hid, 0, n1),
        "q1": lambda: net.project(n1, 0, q1),
        "k1": lambda: net.project(n1, 1, k1),
        "v1": lambda: net.project(n1, 2, v1),
        "o1": lambda: net.add_project(hid, o1, 3, x1),
        "n2": lambda: net.norm(x1, 1, n2),
        "memory": lambda: fetch[1].wait(),
        "k2": lambda: net.project(mem, 4, k2),
        "v2": lambda: net.project(mem, 5, v2),
        "q2": lambda: net.project(n2, 6, q2),
        "o2": lambda: net.add_project(x1, o2, 7, x2),
        "n3": lambda: net.norm(x2, 2, n3),
        "begin": begin,
        "low": finish_low,
        "nb3": lambda: net.norm_back(dn, x2, 2, lambda rows, i: cot[rows].astype(F32) * net.live(i), grad, df),
        "do2": lambda: net.times_back([(df, 7)], put_do),
        "w7": lambda: net.weight_grad(o2, df, 7),
        "dn2": lambda: net.times_back([(q2, 6)], put_dn),
        "w6": lambda: net.weight_grad(n2, q2, 6),
        "mg": mix_memory,
        "w4": lambda: net.weight_grad(mem, k2, 4),
        "w5": lambda: net.weight_grad(mem, v2, 5),
        "nb2": lambda: net.norm_back(dn, x1, 1, lambda rows, i: grad[rows], grad, df),
        "do1": lambda: net.times_back([(df, 3)], put_do),
        "w3": lambda: net.weight_grad(o1, df, 3),
        "dn1": lambda: net.times_back([(q1, 0), (k1, 1), (v1, 2)], put_dn),
        "w0": lambda: net.weight_grad(n1, q1, 0),
        "w1": lambda: net.weight_grad(n1, k1, 1),
        "w2": lambda: net.weight_grad(n1, v1, 2),
        "nb1": finish_hidden,
    }
    families = {
        "act": net.ffn_act, "out": net.ffn_out, "back": net.ffn_back, "grads": net.ffn_grads,
        "W": lambda j: net.weight_grad(n3, du, INNER_UNIT[j]),
        "A1": lambda i: net.attend(1, 2 * i, 2 * i + 2),
        "A2": lambda i: net.attend(2, 2 * i, 2 * i + 2),
        "B1": lambda i: net.attend_back(1, i, i + 1),
        "B2": lambda i: net.attend_back(2, i, i + 1),
    }
    enter()
    for kind, index, name in program:
        if kind == "G":
            if name == "own":
                own(index)
            else:
                gathers[index].do(name)
        elif kind == "S":
            scatters[index].do(name)
        elif kind == "K":
            gains.go(index)
        elif kind == "R":
            if index < 7:
                sums.go(index)
            else:
                total_small()
        elif kind == "X":
            swap()
        elif name in tasks:
            tasks[name]()
        else:
            families[name](index)
    store[3].start()
    store[4].start()
    gains.drain()
    sums.drain()
    for f in SCATTER_ORDER:
        scatters[f].drain()
    for copy in store:
        copy.wait()


def run_layer(program, *operands):
    far, sm = pl.BlockSpec(memory_space=pltpu.HBM), pl.BlockSpec(memory_space=pltpu.SMEM)
    low, wide = pltpu.VMEM((512, 768), BF), pltpu.VMEM((512, 768), F32)
    dma = pltpu.SemaphoreType.DMA
    shape = jax.ShapeDtypeStruct
    outs = (
        shape((512, 768), BF), shape((512, 768), F32), shape((512, 768), F32),
        shape((6, 2, 24, 768), F32), shape((2, 48, 768), F32), shape((24, 256), F32),
    )
    return pl.pallas_call(
        functools.partial(layer_kernel, program),
        out_shape=outs,
        in_specs=[sm] * 2 + [far] * (len(operands) - 2),
        out_specs=[far] * 6,
        scratch_shapes=[
            *[pltpu.VMEM(a.shape, a.dtype) for a in (*operands[2:5], *operands[9:])],
            *[pltpu.VMEM(outs[i].shape, outs[i].dtype) for i in (1, 2, 4, 5)],
            dma((21,)), dma((6,)),
            pltpu.VMEM((6, 2, 24, 768), F32),
            pltpu.VMEM((12, 4, 2, 2, 48, 768), BF),
            pltpu.VMEM((4, 2, 2, 2, 2, 48, 768), BF),
            *[low] * 14, *[wide] * 3,
            pltpu.VMEM((4, 4, 2, 2, 48, 768), BF),
            pltpu.VMEM((8, 4, 2, 48, 768), BF),
            pltpu.VMEM((max(len(WIDE), 1), 3, 2, 48, 768), BF),
            pltpu.VMEM((max(len(WIDE), 1), 3, 2, 48, 768), BF),
            pltpu.VMEM((max(len(WIDE), 1), 48, 768), BF),
            pltpu.VMEM((max(len(NARROW), 1), 3, 48, 768), BF),
            pltpu.VMEM((max(len(NARROW), 1), 3, 48, 768), BF),
            pltpu.VMEM((max(len(NARROW), 1), 4, 48, 768), BF),
            pltpu.VMEM((6, 48, 768), F32),
            pltpu.VMEM((4, 2, 2, 2, 8, 128), F32),
            pltpu.VMEM((8, 768), F32),
            pltpu.VMEM((16, 256), F32),
            pltpu.VMEM((3, 24, 256), F32),
            pltpu.VMEM((3, 24, 256), F32),
            pltpu.VMEM((4, 24, 256), F32),
            dma((8, 5)), dma((8, 9)), dma((8, 16)), dma((8, 16)), dma, dma,
            dma((9,)), dma((9,)), dma((9,)), dma((9,)),
            pltpu.SemaphoreType.REGULAR((4,)),
        ],
        compiler_params=pltpu.CompilerParams(
            collective_id=0, has_side_effects=True, vmem_limit_bytes=63 * 2**20
        ),
    )(*operands)


def bucket_rows(length):
    distance = np.arange(length)
    exact_range = BUCKETS // 2
    safe = np.maximum(distance, 1).astype(np.float32)
    spread = np.log(safe / np.float32(exact_range)) / np.float32(math.log(MAX_DIST / exact_range))
    spread = (spread * np.float32(BUCKETS - exact_range)).astype(np.int32)
    bucket = np.where(distance < exact_range, distance, np.minimum(exact_range + spread, BUCKETS - 1))
    return (bucket[None, :] == np.arange(BUCKETS)[:, None]).astype(np.float32)


def adam_kernel(*refs):
    passed, ins, out_passed, outs, rest = refs[:3], refs[3:28], refs[28:31], refs[31:59], refs[59:]
    local, local_out, through, sems = rest[:25], rest[25:53], rest[53:56], rest[56]
    copies = [pltpu.make_async_copy(a, b, sems.at[0, i]) for i, (a, b) in enumerate(zip(ins, local))]
    inward = [pltpu.make_async_copy(a, b, sems.at[1, i]) for i, (a, b) in enumerate(zip(passed, through))]
    onward = [pltpu.make_async_copy(a, b, sems.at[1, 3 + i]) for i, (a, b) in enumerate(zip(through, out_passed))]
    store = [pltpu.make_async_copy(a, b, sems.at[2, i]) for i, (a, b) in enumerate(zip(local_out, outs))]
    order = (0, 1, 2, 3, *(j * 7 + i + 4 for i in range(7) for j in range(3)))
    for i in order:
        copies[i].start()
    for copy in inward:
        copy.start()
    res, last, small, reverse = local[:4]
    masters, firsts, seconds = local[4:11], local[11:18], local[18:25]
    device = lax.axis_index("dp") * 4 + lax.axis_index("fsdp")

    def update(i, at, grad):
        small_one = i > 4
        new, first, second = adam_step(
            masters[i][at], firsts[i][at], seconds[i][at], grad,
            rate_small if small_one else rate_matrix, 0.0 if small_one else weight_decay,
        )
        local_out[i][at] = new
        local_out[7 + i][at] = first
        local_out[14 + i][at] = second
        local_out[21 + i][at] = new.astype(BF)

    def arrive(i):
        for j in range(3):
            copies[4 + 7 * j + i].wait()

    def leave(i):
        for j in range(4):
            store[7 * j + i].start()

    for i in range(4):
        copies[i].wait()
    where = (((0, 0), (1, 1), (2, 6), (3, 4)), ((0, 2), (1, 5)), ((0, 3), (1, 7)))
    for i, pairs in enumerate(where):
        arrive(i)
        for at, u in pairs:
            update(i, at, res[u])
        leave(i)
    arrive(3)
    for j in range(4):
        update(3, (slice(None), slice(768 * j, 768 * j + 768)), res[INNER_UNIT[j]])
    leave(3)
    for one, two in zip(inward, onward):
        one.wait()
        two.start()
    arrive(4)
    for h in range(2):
        update(4, (slice(48 * h, 48 * h + 48), slice(None)), last[h])
    leave(4)
    arrive(5)
    place = lax.broadcasted_iota(jnp.int32, (256, 24), 0) - lax.broadcasted_iota(jnp.int32, (256, 24), 1)
    for g in range(3):
        total = jnp.zeros((8, 24), F32)
        for i in range(3):
            mine = (place + 256 * i == 24 * device).astype(F32)
            rows = jnp.broadcast_to(small[12 + 3 * g + i:13 + 3 * g + i, :], (8, 256))
            total = total + lax.dot_general(
                rows, mine, (((1,), (0,)), ((), ())), precision=highest, preferred_element_type=F32
            )
        update(5, (slice(g, g + 1), slice(None)), total[0:1])
    leave(5)
    arrive(6)
    table_grad = lax.dot_general(
        small[0:16, :], reverse[...], (((1,), (1,)), ((), ())), precision=highest, preferred_element_type=F32
    )
    update(6, (slice(None), slice(None)), table_grad[:HEADS])
    leave(6)
    for copy in (*store, *onward):
        copy.wait()


def run_adam(*operands):
    far = pl.BlockSpec(memory_space=pltpu.HBM)
    shapes = [jax.ShapeDtypeStruct(a.shape, a.dtype) for a in operands]
    masters = shapes[7:14]
    outs = (*masters * 3, *[jax.ShapeDtypeStruct(a.shape, BF) for a in masters])
    return pl.pallas_call(
        adam_kernel,
        out_shape=(*shapes[:3], *outs),
        in_specs=[far] * len(operands),
        out_specs=[far] * 31,
        scratch_shapes=[
            *[pltpu.VMEM(a.shape, a.dtype) for a in (*shapes[3:], *outs, *shapes[:3])],
            pltpu.SemaphoreType.DMA((3, 28)),
        ],
        compiler_params=pltpu.CompilerParams(vmem_limit_bytes=60 * 2**20),
    )(*operands)


SCHEDULE = (
    "X0", "G2own", "G0own", "G4own", "K1", "G1own", "G7own", "G6own", "G2L1", "G2R1", "G0cross", "G6L1",
    "K2", "G5own", "G2L2", "G6R1", "G0L1", "G2R2", "G3own", "G2R3", "G6R2", "K3", "G1cross", "G0R1", "G6R3",
    "G1R1", "G2L3", "K4", "G2cross", "G6L2", "G1L1", "G3cross", "K5", "K6", "G0L2", "G6L3", "G1R2", "G1L2",
    "T0gain", "G3L1", "G1L3", "G0R2", "G3R1", "G0L3", "T0n1", "G7cross", "G1R3", "G0R3", "G6cross",
    "G2second", "G2finish", "G3R2", "G0second", "G3L2", "G4cross", "T0memory", "G1second", "G0finish",
    "T0k2", "G7R1", "T0q1", "G1finish", "T0v1", "G3L3", "G7L1", "T0k1", "T2A1", "G3R3", "G4L1", "T0A1",
    "G4R1", "T1A1", "G7L2", "G7R2", "T0o1", "T0v2", "G3second", "G3finish", "G6second", "T0n2", "G4L2",
    "G1drain", "G4R2", "G0drain", "G5cross", "G6finish", "T0q2", "G6drain", "G2drain", "G7L3", "G7R3",
    "T2A2", "T1A2", "G4L3", "G3drain", "G4R3", "T0A2", "T0o2", "G7second", "G5R1", "G5L1", "T0begin",
    "G4second", "G7finish", "G7drain", "T0n3", "G4finish", "G5L2", "G4drain", "G5R2", "T0act", "T0back",
    "T0out", "G5R3", "G5L3", "T0grads", "T0W", "T3act", "T3back", "G5second", "T3out", "T3grads", "S6startA",
    "T3W", "S4startA", "G5finish", "T1act", "S7startA", "S4coreA", "T1out", "T1back", "T1grads", "S4startB",
    "S6coreA", "S7coreA", "G5drain", "T1W", "T2act", "T2out", "T2back", "T2grads", "S7startB", "S4halfA",
    "T0nb3", "S7coreB", "S4coreB", "T2W", "T0low", "S6startB", "T0do2", "S7halfA", "T1B2", "S5startA",
    "S5startB", "S6halfA", "T3B2", "T2B2", "S5coreA", "T5B2", "S5coreB", "S6coreB", "S4halfB", "T0B2",
    "T0w7", "S4z1", "T4B2", "T0dn2", "S7halfB", "T0nb2", "T0do1", "S7z1", "T0w6", "S5halfA", "S4z2", "T0mg",
    "T0w5", "S3startA", "T1B1", "S6halfB", "S3startB", "S6z1", "T0w4", "S3coreA", "S5halfB", "T5B1", "S7z2",
    "S2startA", "S5crossA", "T0B1", "S2startB", "S2coreA", "T4B1", "S5crossB", "T0w3", "S3coreB", "S6z2",
    "T2B1", "T3B1", "S5z1", "S2coreB", "S3halfA", "T0dn1", "T0w2", "S1startA", "T0w1", "T0w0", "S0startA",
    "S5z2", "S1coreA", "S0startB", "S3halfB", "S1startB", "S2halfA", "S0coreA", "T0nb1", "R0", "R1", "S3z1",
    "S2halfB", "S1coreB", "S0coreB", "S2z1", "S0halfA", "S2z2", "S3z2", "S5z3", "R2", "S1halfA", "S0halfB",
    "S1halfB", "S4z3", "R3", "S7z3", "S0crossA", "S5finish", "S1crossA", "S0crossB", "S0z1", "S3z3", "S2z3",
    "S6z3", "R4", "S1crossB", "S1z1", "S0z2", "S1z2", "R5", "S4last", "S7last", "S2last", "S3last", "S0z3",
    "S1z3", "S6last", "S4finish", "S2finish", "S3finish", "R6", "S0finish", "R7", "S1finish",
)


def shards_block(
    hidden, memory, cotangent, target_lengths, memory_lengths,
    qk_master, value_master, output_master, inner_master, outer_master, gain_master, table_master,
    qk_first, value_first, output_first, inner_first, outer_first, gain_first, table_first,
    qk_second, value_second, output_second, inner_second, outer_second, gain_second, table_second,
):
    place = np.arange(768)
    spread = (place[None, :] % 24 == np.arange(128)[:, None]).astype(jnp.bfloat16)
    owner = (place[None, :] // 24 == np.arange(32)[:, None]).astype(np.float32)
    by_distance = bucket_rows(256)
    flat = lambda a: a.reshape(512, 768)
    low_out, hidden_grad, memory_grad, res, last, small = run_layer(
        tuple((s[0], int(s[1]), s[2:]) for s in SCHEDULE), target_lengths.T, memory_lengths.T, flat(hidden), flat(memory), flat(cotangent),
        qk_master, value_master, output_master, inner_master, outer_master, gain_master, table_master.T,
        spread, owner, np.roll(by_distance[:, ::-1], 1, axis=1),
    )
    low_out, hidden_grad, memory_grad, *rest = run_adam(
        low_out, hidden_grad, memory_grad, res.reshape(12, 24, 768), last, small, by_distance[:, ::-1],
        qk_master, value_master, output_master, inner_master, outer_master, gain_master, table_master.T,
        qk_first, value_first, output_first, inner_first, outer_first, gain_first, table_first.T,
        qk_second, value_second, output_second, inner_second, outer_second, gain_second, table_second.T,
    )
    for i in (6, 13, 20, 27):
        rest[i] = rest[i].T
    whole = lambda a: a.reshape(2, 1, 256, 768)
    return whole(low_out), whole(hidden_grad), whole(memory_grad), *rest


def solution(mesh):
    placed = (
        P(None, ("dp", "fsdp"), None, None),
        P(None, ("dp", "fsdp"), None, None),
        P(None, ("dp", "fsdp"), None, None),
        P(None, ("dp", "fsdp")),
        P(None, ("dp", "fsdp")),
        P(None, ("dp", "fsdp"), None),
        P(None, ("dp", "fsdp"), None),
        P(None, ("dp", "fsdp"), None),
        P(("dp", "fsdp"), None),
        P(("dp", "fsdp"), None),
        P(None, ("dp", "fsdp")),
        P(),
        P(None, ("dp", "fsdp"), None),
        P(None, ("dp", "fsdp"), None),
        P(None, ("dp", "fsdp"), None),
        P(("dp", "fsdp"), None),
        P(("dp", "fsdp"), None),
        P(None, ("dp", "fsdp")),
        P(),
        P(None, ("dp", "fsdp"), None),
        P(None, ("dp", "fsdp"), None),
        P(None, ("dp", "fsdp"), None),
        P(("dp", "fsdp"), None),
        P(("dp", "fsdp"), None),
        P(None, ("dp", "fsdp")),
        P(),
    )
    small_slice = dict(mesh.shape) == {"dp": 8, "fsdp": 4}
    return jax.shard_map(
        shards_block if small_slice else shards,
        mesh=mesh,
        in_specs=placed,
        out_specs=(
            P(None, ("dp", "fsdp"), None, None),
            P(None, ("dp", "fsdp"), None, None),
            P(None, ("dp", "fsdp"), None, None),
            P(None, ("dp", "fsdp"), None),
            P(None, ("dp", "fsdp"), None),
            P(None, ("dp", "fsdp"), None),
            P(("dp", "fsdp"), None),
            P(("dp", "fsdp"), None),
            P(None, ("dp", "fsdp")),
            P(),
            P(None, ("dp", "fsdp"), None),
            P(None, ("dp", "fsdp"), None),
            P(None, ("dp", "fsdp"), None),
            P(("dp", "fsdp"), None),
            P(("dp", "fsdp"), None),
            P(None, ("dp", "fsdp")),
            P(),
            P(None, ("dp", "fsdp"), None),
            P(None, ("dp", "fsdp"), None),
            P(None, ("dp", "fsdp"), None),
            P(("dp", "fsdp"), None),
            P(("dp", "fsdp"), None),
            P(None, ("dp", "fsdp")),
            P(),
            P(None, ("dp", "fsdp"), None),
            P(None, ("dp", "fsdp"), None),
            P(None, ("dp", "fsdp"), None),
            P(("dp", "fsdp"), None),
            P(("dp", "fsdp"), None),
            P(None, ("dp", "fsdp")),
            P(),
        ),
        check_vma=False,
    )
```

```python
import functools
import math

import jax
import jax.numpy as jnp
import numpy as np
from jax import lax
from jax.experimental import pallas as pl
from jax.experimental.pallas import tpu as pltpu
from jax.sharding import PartitionSpec as P

HEADS = 12
HEAD_DIM = 64
BUCKETS = 32
MAX_DIST = 128
STEP = 10


epsilon_norm = 1e-06
score_scale = 0.125
masked_score = -1e30
beta_first = 0.9
beta_second = 0.999
adam_epsilon = 1e-08
rate_matrix = 0.15
rate_small = 1.0
weight_decay = 0.01
highest = lax.Precision.HIGHEST


def bucket_onehot(length):
    places = jnp.arange(length, dtype=jnp.int32)
    distance = jnp.maximum(places[:, None] - places[None, :], 0)
    exact_range = BUCKETS // 2
    safe_distance = jnp.maximum(distance, 1).astype(jnp.float32)
    spread = (
        jnp.log(safe_distance / exact_range)
        / math.log(MAX_DIST / exact_range)
        * (BUCKETS - exact_range)
    )
    far_bucket = jnp.minimum(exact_range + spread.astype(jnp.int32), BUCKETS - 1)
    bucket = jnp.where(distance < exact_range, distance, far_bucket)
    labels = jnp.arange(BUCKETS, dtype=jnp.int32)
    return (bucket[None, :, :] == labels[:, None, None]).astype(jnp.float32)


def product(left_side, right_side):
    return jnp.dot(left_side, right_side, preferred_element_type=jnp.float32)


def product_over_rows(left_side, right_side):
    return lax.dot_general(
        left_side, right_side, (((0,), (0,)), ((), ())), preferred_element_type=jnp.float32
    )


def product_transposed(left_side, right_side):
    return lax.dot_general(
        left_side, right_side, (((1,), (1,)), ((), ())), preferred_element_type=jnp.float32
    )


def to_heads(values, sequences):
    return values.reshape(sequences, -1, HEADS, HEAD_DIM)


def normalize(values, gain_row):
    scale_rows = lax.rsqrt(jnp.mean(values * values, axis=-1, keepdims=True) + epsilon_norm)
    unit_rows = values * scale_rows
    return ((unit_rows * gain_row).astype(jnp.bfloat16), unit_rows, scale_rows)


def normalize_back(grad_norm, unit_rows, scale_rows, gain_row):
    gain_grad = jnp.sum(grad_norm * unit_rows, axis=0)
    grad_unit = grad_norm * gain_row
    grad_values = scale_rows * (
        grad_unit - unit_rows * jnp.mean(grad_unit * unit_rows, axis=-1, keepdims=True)
    )
    return (grad_values, gain_grad)


def attend_scores(queries, key_heads, bias_term, allowed):
    scores = (
        jnp.einsum("sihe,sjhe->shij", queries, key_heads, preferred_element_type=jnp.float32)
        * score_scale
        + bias_term
    )
    return jnp.where(allowed, scores, masked_score)


def attend_forward(queries, key_heads, value_heads, bias_term, allowed):
    scores = attend_scores(queries, key_heads, bias_term, allowed)
    row_max = jnp.max(scores, axis=-1, keepdims=True)
    expanded = jnp.exp(scores - row_max)
    row_total = jnp.sum(expanded, axis=-1, keepdims=True)
    weights = (expanded / row_total).astype(jnp.bfloat16)
    mixed_heads = jnp.einsum(
        "shij,sjhe->sihe", weights, value_heads, preferred_element_type=jnp.float32
    )
    return (mixed_heads, row_max + jnp.log(row_total))


def attend_back(queries, key_heads, value_heads, bias_term, allowed, summary, grad_mixed):
    scores = attend_scores(queries, key_heads, bias_term, allowed)
    weights = jnp.exp(scores - summary)
    grad_weights = jnp.einsum(
        "sihe,sjhe->shij", grad_mixed, value_heads, preferred_element_type=jnp.float32
    )
    grad_values = jnp.einsum(
        "shij,sihe->sjhe",
        weights.astype(jnp.bfloat16),
        grad_mixed,
        preferred_element_type=jnp.float32,
    )
    grad_scores = (
        weights * (grad_weights - jnp.sum(weights * grad_weights, axis=-1, keepdims=True))
    ).astype(jnp.bfloat16)
    grad_queries = (
        jnp.einsum("shij,sjhe->sihe", grad_scores, key_heads, preferred_element_type=jnp.float32)
        * score_scale
    )
    grad_keys = (
        jnp.einsum("shij,sihe->sjhe", grad_scores, queries, preferred_element_type=jnp.float32)
        * score_scale
    )
    return (grad_queries, grad_keys, grad_values, grad_scores)


def forward_pass(gathered, bias_heads, hidden_seq, memory_seq, target_len, memory_len):
    qk_full, value_full, output_full, inner_full, outer_full, gain_full = gathered
    gain_rows = gain_full.astype(jnp.float32)
    sequences, length, model_width = hidden_seq.shape
    memory_span = memory_seq.shape[1]
    row_count = sequences * length
    residual = hidden_seq.astype(jnp.float32).reshape(row_count, model_width)
    memory_rows = memory_seq.reshape(sequences * memory_span, model_width)
    places = jnp.arange(length, dtype=jnp.int32)
    self_mask = (places[None, :] <= places[:, None])[None, None] & (
        places[None, None, None, :] < target_len[:, None, None, None]
    )
    memory_places = jnp.arange(memory_span, dtype=jnp.int32)
    cross_mask = (memory_places[None, :] < memory_len[:, None])[:, None, None, :]
    normed_first, unit_first, scale_first = normalize(residual, gain_rows[0])
    query_first = product(normed_first, qk_full[0]).astype(jnp.bfloat16)
    key_first = product(normed_first, qk_full[1]).astype(jnp.bfloat16)
    value_first = product(normed_first, value_full[0]).astype(jnp.bfloat16)
    mixed_first, summary_first = attend_forward(
        to_heads(query_first, sequences),
        to_heads(key_first, sequences),
        to_heads(value_first, sequences),
        bias_heads,
        self_mask,
    )
    mixed_first = mixed_first.reshape(row_count, model_width).astype(jnp.bfloat16)
    first_sum = residual + product(mixed_first, output_full[0])
    normed_second, unit_second, scale_second = normalize(first_sum, gain_rows[1])
    query_second = product(normed_second, qk_full[2]).astype(jnp.bfloat16)
    key_second = product(memory_rows, qk_full[3]).astype(jnp.bfloat16)
    value_second = product(memory_rows, value_full[1]).astype(jnp.bfloat16)
    mixed_second, summary_second = attend_forward(
        to_heads(query_second, sequences),
        to_heads(key_second, sequences),
        to_heads(value_second, sequences),
        0.0,
        cross_mask,
    )
    mixed_second = mixed_second.reshape(row_count, model_width).astype(jnp.bfloat16)
    second_sum = first_sum + product(mixed_second, output_full[1])
    normed_third, unit_third, scale_third = normalize(second_sum, gain_rows[2])
    inner_act = product(normed_third, inner_full)
    activated = jax.nn.gelu(inner_act, approximate=True).astype(jnp.bfloat16)
    produced = (second_sum + product(activated, outer_full)).astype(jnp.bfloat16)
    stored = (
        self_mask,
        cross_mask,
        memory_rows,
        normed_first,
        unit_first,
        scale_first,
        query_first,
        key_first,
        value_first,
        summary_first,
        mixed_first,
        normed_second,
        unit_second,
        scale_second,
        query_second,
        key_second,
        value_second,
        summary_second,
        mixed_second,
        normed_third,
        unit_third,
        scale_third,
        inner_act,
        activated,
    )
    return (stored, produced.reshape(sequences, length, model_width))


def backward_pass(gathered, bias_heads, stored, cotangent_seq, target_len):
    qk_full, value_full, output_full, inner_full, outer_full, gain_full = gathered
    gain_rows = gain_full.astype(jnp.float32)
    (
        self_mask,
        cross_mask,
        memory_rows,
        normed_first,
        unit_first,
        scale_first,
        query_first,
        key_first,
        value_first,
        summary_first,
        mixed_first,
        normed_second,
        unit_second,
        scale_second,
        query_second,
        key_second,
        value_second,
        summary_second,
        mixed_second,
        normed_third,
        unit_third,
        scale_third,
        inner_act,
        activated,
    ) = stored
    sequences, length, model_width = cotangent_seq.shape
    row_count = sequences * length
    places = jnp.arange(length, dtype=jnp.int32)
    live_rows = (places[None, :] < target_len[:, None]).astype(jnp.float32).reshape(row_count, 1)
    grad_out = cotangent_seq.astype(jnp.float32).reshape(row_count, model_width) * live_rows
    branch = grad_out.astype(jnp.bfloat16)
    outer_grad = product_over_rows(activated, branch)
    grad_act = product_transposed(branch, outer_full)
    unused_value, gelu_pull = jax.vjp(
        lambda inputs: jax.nn.gelu(inputs, approximate=True), inner_act
    )
    grad_inner = gelu_pull(grad_act)[0].astype(jnp.bfloat16)
    inner_grad = product_over_rows(normed_third, grad_inner)
    grad_from_third, gain_third = normalize_back(
        product_transposed(grad_inner, inner_full), unit_third, scale_third, gain_rows[2]
    )
    grad_second = grad_out + grad_from_third
    branch = grad_second.astype(jnp.bfloat16)
    output_grad_second = product_over_rows(mixed_second, branch)
    grad_mixed = product_transposed(branch, output_full[1]).astype(jnp.bfloat16)
    grad_query, grad_key, grad_value, unused_scores = attend_back(
        to_heads(query_second, sequences),
        to_heads(key_second, sequences),
        to_heads(value_second, sequences),
        0.0,
        cross_mask,
        summary_second,
        to_heads(grad_mixed, sequences),
    )
    grad_query = grad_query.reshape(row_count, model_width).astype(jnp.bfloat16)
    grad_key = grad_key.reshape(memory_rows.shape[0], model_width).astype(jnp.bfloat16)
    grad_value = grad_value.reshape(memory_rows.shape[0], model_width).astype(jnp.bfloat16)
    qk_grad_two = product_over_rows(normed_second, grad_query)
    qk_grad_three = product_over_rows(memory_rows, grad_key)
    value_grad_one = product_over_rows(memory_rows, grad_value)
    memory_grad = product_transposed(grad_key, qk_full[3]) + product_transposed(
        grad_value, value_full[1]
    )
    grad_from_second, gain_second = normalize_back(
        product_transposed(grad_query, qk_full[2]), unit_second, scale_second, gain_rows[1]
    )
    grad_first = grad_second + grad_from_second
    branch = grad_first.astype(jnp.bfloat16)
    output_grad_first = product_over_rows(mixed_first, branch)
    grad_mixed = product_transposed(branch, output_full[0]).astype(jnp.bfloat16)
    grad_query, grad_key, grad_value, grad_scores = attend_back(
        to_heads(query_first, sequences),
        to_heads(key_first, sequences),
        to_heads(value_first, sequences),
        bias_heads,
        self_mask,
        summary_first,
        to_heads(grad_mixed, sequences),
    )
    grad_query = grad_query.reshape(row_count, model_width).astype(jnp.bfloat16)
    grad_key = grad_key.reshape(row_count, model_width).astype(jnp.bfloat16)
    grad_value = grad_value.reshape(row_count, model_width).astype(jnp.bfloat16)
    qk_grad_zero = product_over_rows(normed_first, grad_query)
    qk_grad_one = product_over_rows(normed_first, grad_key)
    value_grad_zero = product_over_rows(normed_first, grad_value)
    grad_norm = (
        product_transposed(grad_query, qk_full[0])
        + product_transposed(grad_key, qk_full[1])
        + product_transposed(grad_value, value_full[0])
    )
    grad_from_first, gain_first = normalize_back(grad_norm, unit_first, scale_first, gain_rows[0])
    hidden_grad = grad_first + grad_from_first
    score_term = jnp.sum(grad_scores.astype(jnp.float32), axis=0)
    grad_terms = (
        jnp.stack([qk_grad_zero, qk_grad_one, qk_grad_two, qk_grad_three]),
        jnp.stack([value_grad_zero, value_grad_one]),
        jnp.stack([output_grad_first, output_grad_second]),
        inner_grad,
        outer_grad,
        jnp.stack([gain_first, gain_second, gain_third]),
    )
    return (
        grad_terms,
        score_term,
        hidden_grad.reshape(sequences, length, model_width),
        memory_grad.reshape(sequences, -1, model_width),
    )


def adam_step(master, first_moment, second_moment, gradient, rate, decay):
    first_next = beta_first * first_moment + (1.0 - beta_first) * gradient
    second_next = beta_second * second_moment + (1.0 - beta_second) * gradient * gradient
    corrected = (
        first_next
        / (1.0 - beta_first**STEP)
        / (jnp.sqrt(second_next / (1.0 - beta_second**STEP)) + adam_epsilon)
    )
    master_next = master - rate * (corrected + decay * master)
    return (master_next, first_next, second_next)


def shards(
    hidden,
    memory,
    cotangent,
    target_lengths,
    memory_lengths,
    qk_master,
    value_master,
    output_master,
    inner_master,
    outer_master,
    gain_master,
    table_master,
    qk_first,
    value_first,
    output_first,
    inner_first,
    outer_first,
    gain_first,
    table_first,
    qk_second,
    value_second,
    output_second,
    inner_second,
    outer_second,
    gain_second,
    table_second,
):
    micro_count = hidden.shape[0]
    length = hidden.shape[2]
    model_width = hidden.shape[3]
    hidden_units = inner_master.shape[1]
    qk_low = qk_master.astype(jnp.bfloat16)
    value_low = value_master.astype(jnp.bfloat16)
    output_low = output_master.astype(jnp.bfloat16)
    inner_low = inner_master.astype(jnp.bfloat16)
    outer_low = outer_master.astype(jnp.bfloat16)
    gain_low = gain_master.astype(jnp.bfloat16)
    onehot = bucket_onehot(length)
    bias_heads = jnp.einsum("bij,bh->hij", onehot, table_master, precision=highest)
    masters = (qk_master, value_master, output_master, inner_master, outer_master, gain_master)
    totals = (
        jnp.zeros((4, model_width, model_width), jnp.float32),
        jnp.zeros((2, model_width, model_width), jnp.float32),
        jnp.zeros((2, model_width, model_width), jnp.float32),
        jnp.zeros((model_width, hidden_units), jnp.float32),
        jnp.zeros((hidden_units, model_width), jnp.float32),
        jnp.zeros((3, model_width), jnp.float32),
    )
    reduced = tuple((jnp.zeros_like(master) for master in masters))
    score_total = jnp.zeros((HEADS, length, length), jnp.float32)
    produced_list = []
    hidden_list = []
    memory_list = []
    for micro_index in range(micro_count):
        gathered = (
            lax.all_gather(qk_low, ("dp", "fsdp"), axis=1, tiled=True),
            lax.all_gather(value_low, ("dp", "fsdp"), axis=1, tiled=True),
            lax.all_gather(output_low, ("dp", "fsdp"), axis=1, tiled=True),
            lax.all_gather(inner_low, ("dp", "fsdp"), axis=0, tiled=True),
            lax.all_gather(outer_low, ("dp", "fsdp"), axis=0, tiled=True),
            lax.all_gather(gain_low, ("dp", "fsdp"), axis=1, tiled=True),
        )
        stored, produced = forward_pass(
            gathered,
            bias_heads,
            hidden[micro_index],
            memory[micro_index],
            target_lengths[micro_index],
            memory_lengths[micro_index],
        )
        gathered = (
            lax.all_gather(qk_low, ("dp", "fsdp"), axis=1, tiled=True),
            lax.all_gather(value_low, ("dp", "fsdp"), axis=1, tiled=True),
            lax.all_gather(output_low, ("dp", "fsdp"), axis=1, tiled=True),
            lax.all_gather(inner_low, ("dp", "fsdp"), axis=0, tiled=True),
            lax.all_gather(outer_low, ("dp", "fsdp"), axis=0, tiled=True),
            lax.all_gather(gain_low, ("dp", "fsdp"), axis=1, tiled=True),
        )
        grad_terms, score_term, hidden_grad, memory_grad = backward_pass(
            gathered, bias_heads, stored, cotangent[micro_index], target_lengths[micro_index]
        )
        totals = tuple((running + addition for running, addition in zip(totals, grad_terms)))
        score_total = score_total + score_term
        produced_list.append(produced)
        hidden_list.append(hidden_grad)
        memory_list.append(memory_grad)
    reduced = (
        lax.psum_scatter(totals[0], ("dp", "fsdp"), scatter_dimension=1, tiled=True),
        lax.psum_scatter(totals[1], ("dp", "fsdp"), scatter_dimension=1, tiled=True),
        lax.psum_scatter(totals[2], ("dp", "fsdp"), scatter_dimension=1, tiled=True),
        lax.psum_scatter(totals[3], ("dp", "fsdp"), scatter_dimension=0, tiled=True),
        lax.psum_scatter(totals[4], ("dp", "fsdp"), scatter_dimension=0, tiled=True),
        lax.psum_scatter(totals[5], ("dp", "fsdp"), scatter_dimension=1, tiled=True),
    )
    table_grad = jnp.einsum("bij,hij->bh", onehot, score_total, precision=highest)
    table_grad = lax.psum(table_grad, ("dp", "fsdp"))
    all_masters = (
        qk_master,
        value_master,
        output_master,
        inner_master,
        outer_master,
        gain_master,
        table_master,
    )
    firsts = (
        qk_first,
        value_first,
        output_first,
        inner_first,
        outer_first,
        gain_first,
        table_first,
    )
    seconds = (
        qk_second,
        value_second,
        output_second,
        inner_second,
        outer_second,
        gain_second,
        table_second,
    )
    gradients = (reduced[0], reduced[1], reduced[2], reduced[3], reduced[4], reduced[5], table_grad)
    rates = (
        rate_matrix,
        rate_matrix,
        rate_matrix,
        rate_matrix,
        rate_matrix,
        rate_small,
        rate_small,
    )
    decays = (weight_decay, weight_decay, weight_decay, weight_decay, weight_decay, 0.0, 0.0)
    updated = [
        adam_step(
            all_masters[index],
            firsts[index],
            seconds[index],
            gradients[index],
            rates[index],
            decays[index],
        )
        for index in range(7)
    ]
    news = [entry[0] for entry in updated]
    first_news = [entry[1] for entry in updated]
    second_news = [entry[2] for entry in updated]
    copies = [entry.astype(jnp.bfloat16) for entry in news]
    layer_out = jnp.stack(produced_list)
    hidden_out = jnp.stack(hidden_list)
    memory_out = jnp.stack(memory_list)
    return (
        layer_out,
        hidden_out,
        memory_out,
        news[0],
        news[1],
        news[2],
        news[3],
        news[4],
        news[5],
        news[6],
        first_news[0],
        first_news[1],
        first_news[2],
        first_news[3],
        first_news[4],
        first_news[5],
        first_news[6],
        second_news[0],
        second_news[1],
        second_news[2],
        second_news[3],
        second_news[4],
        second_news[5],
        second_news[6],
        copies[0],
        copies[1],
        copies[2],
        copies[3],
        copies[4],
        copies[5],
        copies[6],
    )


MESH = pl.DeviceIdType.MESH
PAIRS = 6
SCATTER_ORDERS = ("cx", "cy", "ax", "ay", "ax", "ay", "cx", "cy")
ORDERS = ("ax", "ay", "cx", "cy", "ax", "ay", "cx", "ay")


class Place:
    def __init__(self, wa, wf):
        self.wa, self.wf = wa, wf
        dp, fs = lax.axis_index("dp"), lax.axis_index("fsdp")
        self.z, self.y = dp // 2, dp % 2
        self.x, self.c = fs // 2, fs % 2
        self.to = {
            "x": (dp, (1 - self.x) * 2 + self.c),
            "y": (self.z * 2 + 1 - self.y, fs),
            "c": (dp, self.x * 2 + 1 - self.c),
            "r": (dp + 2, fs),
            "l": (dp - 2, fs),
        }

    def enter(self, wait):
        bar = pltpu.get_barrier_semaphore()
        inner = (self.z > 0) & (self.z < 3)
        if wait:
            @pl.when(inner)
            def _():
                pl.semaphore_wait(bar, 5)

            @pl.when(jnp.logical_not(inner))
            def _():
                pl.semaphore_wait(bar, 4)

            return

        def greet(way):
            pl.semaphore_signal(bar, inc=1, device_id=self.to[way], device_id_type=MESH)

        for way in ("x", "y", "c"):
            greet(way)

        @pl.when(self.z < 3)
        def _():
            greet("r")

        @pl.when(self.z > 0)
        def _():
            greet("l")

    def pick(self, f, zs, ps, qs, core=None):
        c = self.c if core is None else core
        xs, ys = (ps, qs) if ORDERS[f][1] == "x" else (qs, ps)
        return self.block(f, zs, ys, xs, c)

    def block(self, f, zs, ys, xs, c):
        if f < PAIRS:
            return self.wa.at[2 * f + c, zs, ys, xs]
        return self.wf.at[zs, ys, xs, c, f - PAIRS]

    def own(self, f):
        return (self.x, self.y) if ORDERS[f][1] == "x" else (self.y, self.x)

    def ways(self, f):
        return ("x", "y") if ORDERS[f][1] == "x" else ("y", "x")


def push(place, src, dst, send, recv, way):
    pltpu.make_async_remote_copy(
        src_ref=src, dst_ref=dst, send_sem=send, recv_sem=recv,
        device_id=place.to[way], device_id_type=MESH,
    ).start()


def got(place, ref, sem, way):
    pltpu.make_async_remote_copy(
        src_ref=ref, dst_ref=ref, send_sem=sem, recv_sem=sem,
        device_id=place.to[way], device_id_type=MESH,
    ).wait_recv()


def left_out(place, ref, sem, way):
    pltpu.make_async_remote_copy(
        src_ref=ref, dst_ref=ref, send_sem=sem, recv_sem=sem,
        device_id=place.to[way], device_id_type=MESH,
    ).wait_send()


ALL = slice(None)


class Gather:
    def __init__(self, place, f, send, recv):
        self.k, self.f = place, f
        self.send, self.recv = send, recv
        self.first_cross = ORDERS[f][0] == "a"

    def do(self, name):
        if name[0] in "LR":
            self.step(int(name[1]), name[0])
        else:
            getattr(self, name)()

    def blk(self, zi):
        p, q = self.k.own(self.f)
        return self.k.pick(self.f, zi, ALL if self.first_cross else p, q)

    def move(self, ref, s, r, way):
        push(self.k, ref, ref, self.send.at[self.f, s], self.recv.at[self.f, r], way)

    def start(self):
        p, q = self.k.own(self.f)
        pw, qw = self.k.ways(self.f)
        if self.first_cross:
            self.move(self.k.pick(self.f, self.k.z, p, q), 0, 0, pw)
        else:
            self.spread(self.k.z, 1)

    def cross(self):
        p, q = self.k.own(self.f)
        pw, qw = self.k.ways(self.f)
        if self.first_cross:
            got(self.k, self.k.pick(self.f, self.k.z, 1 - p, q), self.recv.at[self.f, 0], pw)
            self.spread(self.k.z, 1)
        else:
            got(self.k, self.k.pick(self.f, ALL, 1 - p, q), self.recv.at[self.f, 0], pw)
            half = self.k.pick(self.f, ALL, ALL, q)
            self.move(half, 3, 7, qw)
            self.move(half, 4, 8, "c")

    def sideways(self, zi):
        pw, qw = self.k.ways(self.f)
        if self.first_cross:
            self.move(self.blk(zi), 3, 7, qw)
            self.move(self.blk(zi), 4, 8, "c")
        else:
            self.move(self.blk(zi), 0, 0, pw)

    def spread(self, zi, t):
        z = self.k.z

        @pl.when(z < 3)
        def _():
            self.move(self.blk(zi), 1, t, "r")

        @pl.when(z > 0)
        def _():
            self.move(self.blk(zi), 2, 3 + t, "l")

        self.sideways(zi)

    def step(self, t, side):
        z = self.k.z

        if side == "L":
            @pl.when(z >= t)
            def _():
                got(self.k, self.blk(z - t), self.recv.at[self.f, t], "l")

                if t < 3:
                    @pl.when(z < 3)
                    def _():
                        self.move(self.blk(z - t), 1, t + 1, "r")

                self.sideways(z - t)
        else:
            @pl.when(z <= 3 - t)
            def _():
                got(self.k, self.blk(z + t), self.recv.at[self.f, 3 + t], "r")

                if t < 3:
                    @pl.when(z > 0)
                    def _():
                        self.move(self.blk(z + t), 2, 3 + t + 1, "l")

                self.sideways(z + t)

    def second(self):
        p, q = self.k.own(self.f)
        pw, qw = self.k.ways(self.f)
        other = self.k.pick(self.f, ALL, ALL, 1 - q)
        got(self.k, other, self.recv.at[self.f, 7], qw)
        self.move(other, 4, 8, "c")

    def finish(self):
        theirs = self.k.pick(self.f, ALL, ALL, ALL, 1 - self.k.c)
        got(self.k, theirs, self.recv.at[self.f, 8], "c")

    def drain(self):
        p, q = self.k.own(self.f)
        pw, qw = self.k.ways(self.f)
        z, f = self.k.z, self.f
        some = (lambda n: self.k.pick(f, pl.ds(0, n), ALL if self.first_cross else p, q))
        first = self.k.pick(f, z, p, q) if self.first_cross else self.k.pick(f, ALL, p, q)
        left_out(self.k, first, self.send.at[f, 0], pw)
        for n in (1, 2, 3):
            @pl.when(z == n - 1)
            def _():
                left_out(self.k, some(n), self.send.at[f, 1], "r")

            @pl.when(z == 4 - n)
            def _():
                left_out(self.k, some(n), self.send.at[f, 2], "l")
        left_out(self.k, self.k.pick(f, ALL, ALL, q), self.send.at[f, 3], qw)
        left_out(self.k, self.k.pick(f, ALL, ALL, ALL), self.send.at[f, 4], "c")


def add_into(dst, srcs, lead):
    sizes = lead
    count = 1
    for s in sizes:
        count *= s

    def body(i, _):
        idx, rest = [], i
        for s in reversed(sizes):
            idx.append(rest % s)
            rest = rest // s
        idx = tuple(reversed(idx)) or Ellipsis
        total = dst[idx].astype(jnp.float32)
        for src in srcs:
            total = total + src[idx].astype(jnp.float32)
        dst[idx] = total.astype(jnp.bfloat16)
        return 0

    lax.fori_loop(0, count, body, 0)


PIECES = (slice(3, 4), slice(0, 1), slice(1, 3))


class Scatter:
    def __init__(self, place, f, send, recv, slots, final, result, credit):
        self.k, self.f = place, f
        self.wait_credit, self.give_credit, self.credit = credit
        self.send, self.recv = send, recv
        self.rd, self.rq, self.rp, self.rl, self.rr = slots
        self.final, self.result = final, result
        self.wide = SCATTER_ORDERS[f][0] == "a"

    def do(self, name):
        if name[0] == "z":
            self.step_in(int(name[1]))
        elif name[-1] in "AB":
            getattr(self, name[:-1])((0, 1) if name[-1] == "A" else (2,))
        else:
            getattr(self, name)()

    def pick(self, zs, ps, qs, core=None):
        c = self.k.c if core is None else core
        xs, ys = (ps, qs) if SCATTER_ORDERS[self.f][1] == "x" else (qs, ps)
        return self.k.block(self.f, zs, ys, xs, c)

    def own(self):
        return (self.k.x, self.k.y) if SCATTER_ORDERS[self.f][1] == "x" else (self.k.y, self.k.x)

    def ways(self):
        return ("x", "y") if SCATTER_ORDERS[self.f][1] == "x" else ("y", "x")

    def move(self, src, dst, s, way):
        push(self.k, src, dst, self.send.at[self.f, s], self.recv.at[self.f, s], way)

    def blk(self, zi):
        p, q = self.own()
        return self.pick(zi, ALL if self.wide else p, q)

    def start(self, pieces):
        if self.wait_credit and 0 in pieces:
            pl.semaphore_wait(self.credit, 1)
        for i in pieces:
            self.move(self.pick(PIECES[i], ALL, ALL, 1 - self.k.c), self.rd.at[PIECES[i]], i, "c")

    def rpick(self, zs, ps, qs):
        xs, ys = (ps, qs) if SCATTER_ORDERS[self.f][1] == "x" else (qs, ps)
        return self.rd.at[zs, ys, xs]

    def core(self, pieces):
        p, q = self.own()
        pw, qw = self.ways()
        for i in pieces:
            zs = PIECES[i]
            n = zs.stop - zs.start
            got(self.k, self.rd.at[zs], self.recv.at[self.f, i], "c")
            away = self.pick(zs, ALL, 1 - q)
            add_into(away, [self.rpick(zs, ALL, 1 - q)], (n, 2))
            self.move(away, self.rq.at[zs], 3 + i, qw)

    def half(self, pieces):
        p, q = self.own()
        pw, qw = self.ways()
        for i in pieces:
            zs = PIECES[i]
            n = zs.stop - zs.start
            got(self.k, self.rq.at[zs], self.recv.at[self.f, 3 + i], qw)
            add_into(self.pick(zs, ALL, q), [self.rpick(zs, ALL, q), self.rq.at[zs]], (n, 2))
            if not self.wide:
                self.move(self.pick(zs, 1 - p, q), self.rp.at[zs], 6 + i, pw)
        if self.wide and 0 in pieces:
            self.step_out(1)
        if self.give_credit and 2 in pieces:
            pl.semaphore_signal(self.credit, inc=1, device_id=self.k.to["c"], device_id_type=MESH)

    def cross(self, pieces):
        p, q = self.own()
        pw, qw = self.ways()
        for i in pieces:
            zs = PIECES[i]
            n = zs.stop - zs.start
            got(self.k, self.rp.at[zs], self.recv.at[self.f, 6 + i], pw)
            add_into(self.pick(zs, p, q), [self.rp.at[zs]], (n,))
        if 0 in pieces:
            self.step_out(1)

    def step_out(self, t):
        z = self.k.z

        @pl.when(z <= t - 1)
        def _():
            self.move(self.blk(z + 4 - t), self.rl.at[t - 1], 8 + t, "r")

        @pl.when(z >= 4 - t)
        def _():
            self.move(self.blk(z - 4 + t), self.rr.at[t - 1], 11 + t, "l")

    def step_in(self, t):
        z, f = self.k.z, self.f
        lead = (2,) if self.wide else ()

        @pl.when((z >= 1) & (z <= t))
        def _():
            got(self.k, self.rl.at[t - 1], self.recv.at[f, 8 + t], "l")
            add_into(self.blk(z + 3 - t), [self.rl.at[t - 1]], lead)

        @pl.when((z <= 2) & (z >= 3 - t))
        def _():
            got(self.k, self.rr.at[t - 1], self.recv.at[f, 11 + t], "r")
            add_into(self.blk(z - 3 + t), [self.rr.at[t - 1]], lead)

        if t < 3:
            self.step_out(t + 1)
        else:
            p, q = self.own()
            pw, qw = self.ways()
            if self.wide:
                self.move(self.pick(z, 1 - p, q), self.rp, 6, pw)
            else:
                self.total(None)

    def last(self):
        pw, qw = self.ways()
        got(self.k, self.rp, self.recv.at[self.f, 6], pw)
        self.total(self.rp)

    def total(self, more):
        p, q = self.own()
        c = self.k.c
        mine = self.pick(self.k.z, p, q)[...].astype(jnp.float32)
        if more is not None:
            mine = mine + more[...].astype(jnp.float32)
        self.final[...] = mine
        if self.f < PAIRS:
            kept = pl.ds(pl.multiple_of(c * 24, 8), 24)
            away = pl.ds(pl.multiple_of(24 - c * 24, 8), 24)
            self.move(self.final.at[away], self.result.at[self.f, c], 15, "c")
            self.result[self.f, c] = self.final[kept]

    def finish(self):
        if self.f < PAIRS:
            got(self.k, self.result.at[self.f, 1 - self.k.c], self.recv.at[self.f, 15], "c")

    def drain(self):
        pw, qw = self.ways()
        z, f, k = self.k.z, self.f, self.k
        for i, zs in enumerate(PIECES):
            left_out(k, self.rd.at[zs], self.send.at[f, i], "c")
            left_out(k, self.rq.at[zs], self.send.at[f, 3 + i], qw)
            if not self.wide:
                left_out(k, self.rp.at[zs], self.send.at[f, 6 + i], pw)
        if self.wide:
            left_out(k, self.rp, self.send.at[f, 6], pw)
        for t in (1, 2, 3):
            @pl.when(z <= t - 1)
            def _():
                left_out(k, self.rl.at[t - 1], self.send.at[f, 8 + t], "r")

            @pl.when(z >= 4 - t)
            def _():
                left_out(k, self.rr.at[t - 1], self.send.at[f, 11 + t], "l")
        if f < PAIRS:
            left_out(k, self.final.at[pl.ds(0, 24)], self.send.at[f, 15], "c")


class Line:
    def __init__(self, place, buf, send, recv):
        self.k, self.buf, self.send, self.recv = place, buf, send, recv

    def move(self, zi, s, r, way):
        push(self.k, self.buf.at[zi], self.buf.at[zi], self.send.at[s], self.recv.at[r], way)

    def start(self):
        z = self.k.z

        @pl.when(z < 3)
        def _():
            self.move(z, 3, 3, "r")

        @pl.when(z > 0)
        def _():
            self.move(z, 6, 6, "l")

    def step(self, t):
        z = self.k.z

        @pl.when(z >= t)
        def _():
            got(self.k, self.buf.at[z - t], self.recv.at[2 + t], "l")

            if t < 3:
                @pl.when(z < 3)
                def _():
                    self.move(z - t, 3 + t, 3 + t, "r")

        @pl.when(z <= 3 - t)
        def _():
            got(self.k, self.buf.at[z + t], self.recv.at[5 + t], "r")

            if t < 3:
                @pl.when(z > 0)
                def _():
                    self.move(z + t, 6 + t, 6 + t, "l")

    def drain(self):
        z = self.k.z
        for t in range(3):
            @pl.when((z < 3) & (z >= t))
            def _():
                left_out(self.k, self.buf.at[0], self.send.at[3 + t], "r")

            @pl.when((z > 0) & (z <= 3 - t))
            def _():
                left_out(self.k, self.buf.at[0], self.send.at[6 + t], "l")


class Gains:
    def __init__(self, place, buf, send, recv):
        self.k, self.buf, self.send, self.recv = place, buf, send, recv
        self.line = Line(place, buf, send, recv)
        z, y, x, c = place.z, place.y, place.x, place.c
        self.mine = [buf.at[z, y, x, c], buf.at[z, y, x], buf.at[z, y]]
        self.other = [buf.at[z, y, x, 1 - c], buf.at[z, y, 1 - x], buf.at[z, 1 - y]]

    def go(self, i):
        if 1 <= i <= 3:
            got(self.k, self.other[i - 1], self.recv.at[i - 1], "cxy"[i - 1])
        if i < 3:
            push(self.k, self.mine[i], self.mine[i], self.send.at[i], self.recv.at[i], "cxy"[i])
        elif i == 3:
            self.line.start()
        else:
            self.line.step(i - 3)

    def drain(self):
        for i in range(3):
            left_out(self.k, self.mine[i], self.send.at[i], "cxy"[i])
        self.line.drain()


class Small:
    def __init__(self, place, bufs, got_bufs, along, send, recv):
        self.k, self.bufs, self.got_bufs, self.along = place, bufs, got_bufs, along
        self.send, self.recv = send, recv
        self.line = Line(place, along, send, recv)

    def go(self, i):
        if 1 <= i <= 3:
            got(self.k, self.got_bufs.at[i - 1], self.recv.at[i - 1], "cxy"[i - 1])
            total = self.bufs[i - 1] + self.got_bufs[i - 1]
            if i < 3:
                self.bufs[i] = total
            else:
                self.along[self.k.z] = total
        if i < 3:
            push(self.k, self.bufs.at[i], self.got_bufs.at[i], self.send.at[i], self.recv.at[i], "cxy"[i])
        elif i == 3:
            self.line.start()
        else:
            self.line.step(i - 3)

    def drain(self):
        for i in range(3):
            left_out(self.k, self.bufs.at[i], self.send.at[i], "cxy"[i])
        self.line.drain()
BF, F32 = jnp.bfloat16, jnp.float32
INNER_UNIT = (8, 10, 11, 9)
ROOT = math.sqrt(2.0 / math.pi)
CUBE = 0.044715


def dot_nn(a, b):
    return lax.dot_general(a, b, (((1,), (0,)), ((), ())), preferred_element_type=F32)


def dot_nt(a, b):
    return lax.dot_general(a, b, (((1,), (1,)), ((), ())), preferred_element_type=F32)


def dot_tn(a, b):
    return lax.dot_general(a, b, (((0,), (0,)), ((), ())), preferred_element_type=F32)


def unit_of(values):
    scale = lax.rsqrt(jnp.mean(values * values, axis=-1, keepdims=True) + epsilon_norm)
    return values * scale, scale


class Layer:
    def __init__(self, wa, wf, b):
        self.wa, self.wf, self.b = wa, wf, b

    def times(self, a, u, put):
        for t in range(3):
            tile = slice(256 * t, 256 * t + 256)
            put(tile, dot_nn(a[...], self.wa[u, :, :, :, :, tile].reshape(768, 256)))

    def times_back(self, pairs, put):
        total = None
        for a, u in pairs:
            term = dot_nt(a[...], self.wa[u].reshape(768, 768))
            total = term if total is None else total + term
        put(slice(0, 768), total)

    def weight_grad(self, a, d, u):
        for t in range(2):
            tile = dot_tn(a[:, 384 * t:384 * t + 384], d[...])
            self.wa[u, 2 * t:2 * t + 2] = tile.astype(BF).reshape(2, 2, 2, 48, 768)

    def project(self, a, u, dst):
        def put(tile, value):
            dst[:, tile] = value.astype(BF)

        self.times(a, u, put)

    def add_project(self, base, a, u, dst):
        def put(tile, value):
            dst[:, tile] = base[:, tile].astype(F32) + value

        self.times(a, u, put)

    def norm(self, src, g, dst):
        gain = self.b["gain"][pl.ds(g, 1), :]

        for i in range(4):
            rows = slice(128 * i, 128 * i + 128)
            unit, _unused = unit_of(src[rows].astype(F32))
            dst[rows] = (unit * gain).astype(BF)

    def norm_back(self, dn, src, g, base, dst, low):
        gain = self.b["gain"][pl.ds(g, 1), :]

        total = jnp.zeros((1, 768), F32)
        for i in range(4):
            rows = slice(128 * i, 128 * i + 128)
            unit, scale = unit_of(src[rows].astype(F32))
            grad = dn[rows]
            total = total + jnp.sum(grad * unit, axis=0, keepdims=True)
            pulled = grad * gain
            value = base(rows, i) + scale * (pulled - unit * jnp.mean(pulled * unit, axis=-1, keepdims=True))
            dst[rows] = value
            if low is not None:
                low[rows] = value.astype(BF)
        for i in range(3):
            self.b["small"][12 + 3 * g + i:13 + 3 * g + i, :] = total[:, 256 * i:256 * i + 256]

    def head_masks(self):
        lane = lax.broadcasted_iota(jnp.int32, (1, 128), 1)
        low = (lane < 64).astype(F32)
        return low.astype(BF), (1.0 - low).astype(BF)

    def far(self, s, kind):
        col = lax.broadcasted_iota(jnp.int32, (1, 256), 1)
        length = self.b["lens"][0, s] if kind == 1 else self.b["mem_lens"][0, s]
        return jnp.where(col < length, 0.0, masked_score)

    def bias(self, head, causal):
        row = self.b["bias_row"][pl.ds(head, 1), :]
        turned = pltpu.roll(jnp.broadcast_to(row, (256, 256)), 0, axis=1, stride=1, stride_axis=0)
        return jnp.where(causal, turned, masked_score)

    def weights(self, scores):
        expanded = jnp.exp(scores - jnp.max(scores, axis=-1, keepdims=True))
        return expanded * (1.0 / jnp.sum(expanded, axis=-1, keepdims=True))

    def places(self):
        row = lax.broadcasted_iota(jnp.int32, (256, 256), 0)
        col = lax.broadcasted_iota(jnp.int32, (256, 256), 1)
        return row, col

    def attend(self, kind, first, last):
        b = self.b
        q, k, v, o = (b[n + str(kind)] for n in "qkvo")
        masks = self.head_masks()
        keep = masks[0].astype(F32)
        row, col = self.places()

        def body(hp, _):
            lanes = pl.ds(pl.multiple_of(128 * hp, 128), 128)
            biases = [self.bias(2 * hp + e, col <= row) if kind == 1 else 0.0 for e in range(2)]
            rows = [slice(0, 256), slice(256, 512)]
            both = [(s, e) for s in range(2) for e in range(2)]
            queries = [q[r, lanes] * BF(score_scale) for r in rows]
            keys, values = [k[r, lanes] for r in rows], [v[r, lanes] for r in rows]
            far = [self.far(s, kind) for s in range(2)]
            scores = [dot_nt(queries[s] * masks[e], keys[s]) + (biases[e] + far[s]) for s, e in both]
            low = [self.weights(one).astype(BF) for one in scores]
            mixed = [dot_nn(p, values[s]) for p, (s, e) in zip(low, both)]
            for s in range(2):
                o[rows[s], lanes] = (mixed[2 * s] * keep + mixed[2 * s + 1] * (1.0 - keep)).astype(BF)
            return 0

        lax.fori_loop(first, last, body, 0)

    def attend_back(self, kind, first, last):
        b = self.b
        q, k, v, o = (b[n + str(kind)] for n in "qkvo")
        masks = self.head_masks()
        keep = masks[0].astype(F32)
        row, col = self.places()
        flip = (row + col == 255).astype(F32).astype(BF)

        def body(hp, _):
            lanes = pl.ds(pl.multiple_of(128 * hp, 128), 128)
            biases = [self.bias(2 * hp + e, col <= row) if kind == 1 else 0.0 for e in range(2)]
            rows = [slice(0, 256), slice(256, 512)]
            both = [(s, e) for s in range(2) for e in range(2)]
            queries = [q[r, lanes] * BF(score_scale) for r in rows]
            keys, values = [k[r, lanes] for r in rows], [v[r, lanes] for r in rows]
            given = [b["do"][r, lanes] for r in rows]
            kept = [g.astype(F32) * o[r, lanes].astype(F32) for g, r in zip(given, rows)]
            sums = [jnp.sum(kept[s] * (keep if e == 0 else 1.0 - keep), axis=-1, keepdims=True) for s, e in both]
            far = [self.far(s, kind) for s in range(2)]
            qe = [queries[s] * masks[e] for s, e in both]
            ge = [given[s] * masks[e] for s, e in both]
            scores = [dot_nt(one, keys[s]) + (biases[e] + far[s]) for one, (s, e) in zip(qe, both)]
            dps = [dot_nt(one, values[s]) for one, (s, e) in zip(ge, both)]
            ps = [self.weights(one) for one in scores]
            dss = [(p * (dp - one)).astype(BF) for p, dp, one in zip(ps, dps, sums)]
            low = [p.astype(BF) for p in ps]
            dv, dk = [], []
            for s in range(2):
                for found, left, right in ((dv, given[s].T, low), (dk, queries[s].T, dss)):
                    halves = [dot_nn(left[64 * e:64 * e + 64], right[2 * s + e]) for e in range(2)]
                    found.append(jnp.concatenate(halves).astype(BF).T)
            dq = [dot_nn(ds, keys[s] * masks[e]) for ds, (s, e) in zip(dss, both)]
            if kind == 1:
                for e in range(2):
                    turned = dot_nn(flip, dss[e]) + dot_nn(flip, dss[2 + e])
                    turned = pltpu.roll(turned, 0, axis=1, stride=1, stride_axis=0)
                    b["small"][pl.ds(2 * hp + e, 1), :] = jnp.sum(turned, axis=0, keepdims=True)
            for s in range(2):
                q[rows[s], lanes] = ((dq[2 * s] + dq[2 * s + 1]) * score_scale).astype(BF)
                k[rows[s], lanes] = dk[s]
                v[rows[s], lanes] = dv[s]
            return 0

        lax.fori_loop(first, last, body, 0)

    def live(self, i):
        row = lax.broadcasted_iota(jnp.int32, (128, 1), 0) + 128 * (i % 2)
        return (row < self.b["lens"][0, i // 2]).astype(F32)

    def cotangent(self):
        b = self.b
        for i in range(4):
            rows = slice(128 * i, 128 * i + 128)
            b["df"][rows] = (b["cot"][rows].astype(F32) * self.live(i)).astype(BF)

    def ffn_act(self, j):
        b = self.b
        for t in range(2):
            cols = slice(384 * t, 384 * t + 384)
            wi = self.wa[INNER_UNIT[j], :, :, :, :, cols].reshape(768, 384)
            wf = self.wf[j, t].reshape(384, 768)
            u = dot_nn(b["n3"][...], wi)
            square = u * u
            th = jnp.tanh(u * (ROOT + (ROOT * CUBE) * square))
            half = 0.5 + 0.5 * th
            b["act"][:, cols] = (u * half).astype(BF)
            slope = half + u * (1.0 - th * th) * (0.5 * ROOT + (1.5 * ROOT * CUBE) * square)
            da = dot_nt(b["df"][...], wf)
            b["du"][:, cols] = (da * slope).astype(BF)

    def ffn_out(self, j):
        b = self.b
        for t in range(3):
            cols = slice(256 * t, 256 * t + 256)
            wf = self.wf[j, :, :, :, :, :, cols].reshape(768, 256)
            b["y"][:, cols] += dot_nn(b["act"][...], wf)

    def ffn_back(self, j):
        b = self.b

        def put(tile, value):
            if j == 0:
                b["dn"][:, tile] = value
            else:
                b["dn"][:, tile] += value

        self.times_back([(b["du"], INNER_UNIT[j])], put)

    def ffn_grads(self, j):
        b = self.b
        for t in range(2):
            tile = dot_tn(b["act"][:, 384 * t:384 * t + 384], b["df"][...])
            self.wf[j, t] = tile.astype(BF).reshape(2, 2, 2, 48, 768)


SCATTER_ORDER = (4, 5, 6, 7, 3, 2, 1, 0)
WIDE = [f for f in range(8) if SCATTER_ORDERS[f][0] == "a"]
NARROW = [f for f in range(8) if SCATTER_ORDERS[f][0] == "c"]


def layer_kernel(program, lens, mem_lens, *refs):
    ins, outs, rest = refs[:13], refs[13:19], refs[19:]
    locals_in, locals_out, (in_sem, out_sem), rest = rest[:9], list(rest[9:13]), rest[13:15], rest[15:]
    masters, du = rest[0], rest[15]
    locals_out = [du, *locals_out[:2], masters, *locals_out[2:]]
    qk, value, output, inner = ins[3:7]
    units = [qk.at[0], qk.at[1], value.at[0], output.at[0], qk.at[3], value.at[1], qk.at[2], output.at[1]]
    units += [inner.at[:, 768 * j:768 * j + 768] for j in (0, 3, 1, 2)]
    pairs = [*zip((*ins[:3], *ins[7:]), locals_in), *((unit, masters.at[u // 2, u % 2]) for u, unit in enumerate(units))]
    fetch = [pltpu.make_async_copy(a, b, in_sem.at[i]) for i, (a, b) in enumerate(pairs)]
    store = [pltpu.make_async_copy(a, b, out_sem.at[i]) for i, (a, b) in enumerate(zip(locals_out, outs))]
    layer_body(program, lens, mem_lens, fetch, store, *locals_in, *locals_out[1:3], *locals_out[4:], *rest)


def layer_body(
    program, lens, mem_lens, fetch, store,
    hid, mem, cot, outer, gain_in, table, spread, owner, near,
    hidden_grad, memory_grad, last, small_out, masters,
    wa, wf, n1, q1, k1, v1, o1, n2, q2, k2, v2, o2, n3, act, du, df, x1, x2, dn,
    rd, rq, rlw, rrw, rpw, rln, rrn, rpn, fin, tiles, gain, bias_row, small, small_got, along,
    gs, gr, ss, sr, xs, xr, ks, kr, ms, mr, credit,
):
    k = Place(wa, wf)
    z, y, x, c = k.z, k.y, k.x, k.c
    b = dict(
        lens=lens, mem_lens=mem_lens, hid=hid, mem=mem, cot=cot, bias_row=bias_row, gain=gain, small=small.at[0],
        n1=n1, q1=q1, k1=k1, v1=v1, o1=o1, n2=n2, q2=q2, k2=k2, v2=v2, o2=o2, n3=n3,
        act=act, du=du, df=df, do=act, y=memory_grad, dn=dn,
    )
    net = Layer(wa, wf, b)
    gathers = [Gather(k, f, gs, gr) for f in range(8)]
    scatters = {}
    for i, f in enumerate(SCATTER_ORDER):
        if f in WIDE:
            n = WIDE.index(f)
            slots = (rd.at[i % 4], rq.at[f], rpw.at[n], rlw.at[n], rrw.at[n])
        else:
            n = NARROW.index(f)
            slots = (rd.at[i % 4], rq.at[f], rpn.at[n], rln.at[n], rrn.at[n])
        final = fin.at[f] if f < PAIRS else last.at[f - PAIRS]
        scatters[f] = Scatter(k, f, ss, sr, slots, final, masters, (i >= 4, i < 4, credit.at[i % 4]))
    gains = Gains(k, tiles, ks, kr)
    sums = Small(k, small, small_got, along, ms, mr)
    mine = pl.ds(pl.multiple_of(24 * c, 8), 24)
    other = pl.ds(pl.multiple_of(24 - 24 * c, 8), 24)

    def enter():
        for i in (4, *range(9, 21), 3, 5, 8, 0, 1, 2, 6, 7):
            fetch[i].start()
        k.enter(False)
        for i in (4, *range(9, 21)):
            fetch[i].wait()
        tiles[z, y, x, c] = jnp.zeros((8, 128), F32)
        tiles[z, y, x, c, 0:3, 0:24] = gain_in[...].astype(BF).astype(F32)
        k.enter(True)
        push(k, masters.at[:, 1 - c], fin.at[:, mine], xs, xr, "c")
        gains.go(0)
        for i in (3, 5, 8):
            fetch[i].wait()
        bias_row[...] = jnp.zeros_like(bias_row)
        bias_row[0:HEADS, :] = lax.dot_general(
            table[...], near[...], (((1,), (0,)), ((), ())), precision=highest, preferred_element_type=F32
        )
        for h in range(2):
            wf[z, y, x, c, h] = outer[48 * h:48 * h + 48].astype(BF)
        for p in range(PAIRS):
            fin[p, mine] = masters[p, c]

    def swap():
        got(k, fin.at[:, other], xr, "c")
        left_out(k, masters.at[:, 1 - c], xs, "c")

    def own(f):
        if f < PAIRS:
            wa[2 * f + c, z, y, x] = fin[f].astype(BF)
        gathers[f].start()

    def spread_gains():
        for i in (0, 6, 7):
            fetch[i].wait()
        flat = tiles[...].reshape(32, 8, 128)
        for g in range(3):
            lanes = dot_nn(flat[:, g].astype(BF), spread[...])
            gain[g:g + 1, :] = jnp.sum(lanes * owner[...], axis=0, keepdims=True)

    def put_do(tile, value):
        act[:, tile] = value.astype(BF)

    def put_dn(tile, value):
        dn[:, tile] = value

    def put_memory(tile, value):
        memory_grad[:, tile] = value

    def begin():
        fetch[2].wait()
        memory_grad[...] = x2[...]
        small[0] = jnp.zeros_like(small[0])
        net.cotangent()

    def finish_low():
        du[...] = memory_grad[...].astype(BF)
        store[0].start()

    def total_small():
        small_out[...] = along[0] + along[1] + along[2] + along[3]
        store[5].start()

    def mix_memory():
        net.times_back([(k2, 4), (v2, 5)], put_memory)
        store[2].start()

    def finish_hidden():
        net.norm_back(dn, hid, 0, lambda rows, i: grad[rows], grad, None)
        store[1].start()

    grad = hidden_grad
    tasks = {
        "gain": spread_gains,
        "n1": lambda: net.norm(hid, 0, n1),
        "q1": lambda: net.project(n1, 0, q1),
        "k1": lambda: net.project(n1, 1, k1),
        "v1": lambda: net.project(n1, 2, v1),
        "o1": lambda: net.add_project(hid, o1, 3, x1),
        "n2": lambda: net.norm(x1, 1, n2),
        "memory": lambda: fetch[1].wait(),
        "k2": lambda: net.project(mem, 4, k2),
        "v2": lambda: net.project(mem, 5, v2),
        "q2": lambda: net.project(n2, 6, q2),
        "o2": lambda: net.add_project(x1, o2, 7, x2),
        "n3": lambda: net.norm(x2, 2, n3),
        "begin": begin,
        "low": finish_low,
        "nb3": lambda: net.norm_back(dn, x2, 2, lambda rows, i: cot[rows].astype(F32) * net.live(i), grad, df),
        "do2": lambda: net.times_back([(df, 7)], put_do),
        "w7": lambda: net.weight_grad(o2, df, 7),
        "dn2": lambda: net.times_back([(q2, 6)], put_dn),
        "w6": lambda: net.weight_grad(n2, q2, 6),
        "mg": mix_memory,
        "w4": lambda: net.weight_grad(mem, k2, 4),
        "w5": lambda: net.weight_grad(mem, v2, 5),
        "nb2": lambda: net.norm_back(dn, x1, 1, lambda rows, i: grad[rows], grad, df),
        "do1": lambda: net.times_back([(df, 3)], put_do),
        "w3": lambda: net.weight_grad(o1, df, 3),
        "dn1": lambda: net.times_back([(q1, 0), (k1, 1), (v1, 2)], put_dn),
        "w0": lambda: net.weight_grad(n1, q1, 0),
        "w1": lambda: net.weight_grad(n1, k1, 1),
        "w2": lambda: net.weight_grad(n1, v1, 2),
        "nb1": finish_hidden,
    }
    families = {
        "act": net.ffn_act, "out": net.ffn_out, "back": net.ffn_back, "grads": net.ffn_grads,
        "W": lambda j: net.weight_grad(n3, du, INNER_UNIT[j]),
        "A1": lambda i: net.attend(1, 2 * i, 2 * i + 2),
        "A2": lambda i: net.attend(2, 2 * i, 2 * i + 2),
        "B1": lambda i: net.attend_back(1, i, i + 1),
        "B2": lambda i: net.attend_back(2, i, i + 1),
    }
    enter()
    for kind, index, name in program:
        if kind == "G":
            if name == "own":
                own(index)
            else:
                gathers[index].do(name)
        elif kind == "S":
            scatters[index].do(name)
        elif kind == "K":
            gains.go(index)
        elif kind == "R":
            if index < 7:
                sums.go(index)
            else:
                total_small()
        elif kind == "X":
            swap()
        elif name in tasks:
            tasks[name]()
        else:
            families[name](index)
    store[3].start()
    store[4].start()
    gains.drain()
    sums.drain()
    for f in SCATTER_ORDER:
        scatters[f].drain()
    for copy in store:
        copy.wait()


def run_layer(program, *operands):
    far, sm = pl.BlockSpec(memory_space=pltpu.HBM), pl.BlockSpec(memory_space=pltpu.SMEM)
    low, wide = pltpu.VMEM((512, 768), BF), pltpu.VMEM((512, 768), F32)
    dma = pltpu.SemaphoreType.DMA
    shape = jax.ShapeDtypeStruct
    outs = (
        shape((512, 768), BF), shape((512, 768), F32), shape((512, 768), F32),
        shape((6, 2, 24, 768), F32), shape((2, 48, 768), F32), shape((24, 256), F32),
    )
    return pl.pallas_call(
        functools.partial(layer_kernel, program),
        out_shape=outs,
        in_specs=[sm] * 2 + [far] * (len(operands) - 2),
        out_specs=[far] * 6,
        scratch_shapes=[
            *[pltpu.VMEM(a.shape, a.dtype) for a in (*operands[2:5], *operands[9:])],
            *[pltpu.VMEM(outs[i].shape, outs[i].dtype) for i in (1, 2, 4, 5)],
            dma((21,)), dma((6,)),
            pltpu.VMEM((6, 2, 24, 768), F32),
            pltpu.VMEM((12, 4, 2, 2, 48, 768), BF),
            pltpu.VMEM((4, 2, 2, 2, 2, 48, 768), BF),
            *[low] * 14, *[wide] * 3,
            pltpu.VMEM((4, 4, 2, 2, 48, 768), BF),
            pltpu.VMEM((8, 4, 2, 48, 768), BF),
            pltpu.VMEM((max(len(WIDE), 1), 3, 2, 48, 768), BF),
            pltpu.VMEM((max(len(WIDE), 1), 3, 2, 48, 768), BF),
            pltpu.VMEM((max(len(WIDE), 1), 48, 768), BF),
            pltpu.VMEM((max(len(NARROW), 1), 3, 48, 768), BF),
            pltpu.VMEM((max(len(NARROW), 1), 3, 48, 768), BF),
            pltpu.VMEM((max(len(NARROW), 1), 4, 48, 768), BF),
            pltpu.VMEM((6, 48, 768), F32),
            pltpu.VMEM((4, 2, 2, 2, 8, 128), F32),
            pltpu.VMEM((8, 768), F32),
            pltpu.VMEM((16, 256), F32),
            pltpu.VMEM((3, 24, 256), F32),
            pltpu.VMEM((3, 24, 256), F32),
            pltpu.VMEM((4, 24, 256), F32),
            dma((8, 5)), dma((8, 9)), dma((8, 16)), dma((8, 16)), dma, dma,
            dma((9,)), dma((9,)), dma((9,)), dma((9,)),
            pltpu.SemaphoreType.REGULAR((4,)),
        ],
        compiler_params=pltpu.CompilerParams(
            collective_id=0, has_side_effects=True, vmem_limit_bytes=63 * 2**20
        ),
    )(*operands)


def bucket_rows(length):
    distance = np.arange(length)
    exact_range = BUCKETS // 2
    safe = np.maximum(distance, 1).astype(np.float32)
    spread = np.log(safe / np.float32(exact_range)) / np.float32(math.log(MAX_DIST / exact_range))
    spread = (spread * np.float32(BUCKETS - exact_range)).astype(np.int32)
    bucket = np.where(distance < exact_range, distance, np.minimum(exact_range + spread, BUCKETS - 1))
    return (bucket[None, :] == np.arange(BUCKETS)[:, None]).astype(np.float32)


def adam_lean(master, first_moment, second_moment, gradient, rate, decay):
    first_next = beta_first * first_moment + (1.0 - beta_first) * gradient
    second_next = beta_second * second_moment + ((1.0 - beta_second) * gradient) * gradient
    root = jnp.sqrt(second_next * (1.0 / (1.0 - beta_second**STEP))) + adam_epsilon
    step = first_next * (rate / (1.0 - beta_first**STEP)) / root
    return ((1.0 - rate * decay) * master - step, first_next, second_next)


def adam_kernel(*refs):
    passed, ins, out_passed, outs, rest = refs[:3], refs[3:28], refs[28:31], refs[31:59], refs[59:]
    local, local_out, through, sems = rest[:25], rest[25:53], rest[53:56], rest[56]
    copies = [pltpu.make_async_copy(a, b, sems.at[0, i]) for i, (a, b) in enumerate(zip(ins, local))]
    inward = [pltpu.make_async_copy(a, b, sems.at[1, i]) for i, (a, b) in enumerate(zip(passed, through))]
    onward = [pltpu.make_async_copy(a, b, sems.at[1, 3 + i]) for i, (a, b) in enumerate(zip(through, out_passed))]
    store = [pltpu.make_async_copy(a, b, sems.at[2, i]) for i, (a, b) in enumerate(zip(local_out, outs))]
    order = (0, 1, 2, 3, *(j * 7 + i + 4 for i in range(7) for j in range(3)))
    for copy in inward:
        copy.start()
    for i in order:
        copies[i].start()
    for one, two in zip(inward, onward):
        one.wait()
        two.start()
    res, last, small, reverse = local[:4]
    masters, firsts, seconds = local[4:11], local[11:18], local[18:25]
    device = lax.axis_index("dp") * 4 + lax.axis_index("fsdp")

    def update(i, at, grad):
        small_one = i > 4
        new, first, second = adam_lean(
            masters[i][at], firsts[i][at], seconds[i][at], grad,
            rate_small if small_one else rate_matrix, 0.0 if small_one else weight_decay,
        )
        local_out[i][at] = new
        local_out[7 + i][at] = first
        local_out[14 + i][at] = second
        local_out[21 + i][at] = new.astype(BF)

    def arrive(i):
        for j in range(3):
            copies[4 + 7 * j + i].wait()

    def leave(i):
        for j in range(4):
            store[7 * j + i].start()

    for i in range(4):
        copies[i].wait()
    where = (((0, 0), (1, 1), (2, 6), (3, 4)), ((0, 2), (1, 5)), ((0, 3), (1, 7)))
    for i, pairs in enumerate(where):
        arrive(i)
        for at, u in pairs:
            update(i, at, res[u])
        leave(i)
    arrive(3)
    for j in range(4):
        update(3, (slice(None), slice(768 * j, 768 * j + 768)), res[INNER_UNIT[j]])
    leave(3)
    arrive(4)
    for h in range(2):
        update(4, (slice(48 * h, 48 * h + 48), slice(None)), last[h])
    leave(4)
    arrive(5)
    place = lax.broadcasted_iota(jnp.int32, (256, 24), 0) - lax.broadcasted_iota(jnp.int32, (256, 24), 1)
    for g in range(3):
        total = jnp.zeros((8, 24), F32)
        for i in range(3):
            mine = (place + 256 * i == 24 * device).astype(F32)
            rows = jnp.broadcast_to(small[12 + 3 * g + i:13 + 3 * g + i, :], (8, 256))
            total = total + lax.dot_general(
                rows, mine, (((1,), (0,)), ((), ())), precision=highest, preferred_element_type=F32
            )
        update(5, (slice(g, g + 1), slice(None)), total[0:1])
    leave(5)
    arrive(6)
    table_grad = lax.dot_general(
        small[0:16, :], reverse[...], (((1,), (1,)), ((), ())), precision=highest, preferred_element_type=F32
    )
    update(6, (slice(None), slice(None)), table_grad[:HEADS])
    leave(6)
    for copy in (*store, *onward):
        copy.wait()


def run_adam(*operands):
    far = pl.BlockSpec(memory_space=pltpu.HBM)
    shapes = [jax.ShapeDtypeStruct(a.shape, a.dtype) for a in operands]
    masters = shapes[7:14]
    outs = (*masters * 3, *[jax.ShapeDtypeStruct(a.shape, BF) for a in masters])
    return pl.pallas_call(
        adam_kernel,
        out_shape=(*shapes[:3], *outs),
        in_specs=[far] * len(operands),
        out_specs=[far] * 31,
        scratch_shapes=[
            *[pltpu.VMEM(a.shape, a.dtype) for a in (*shapes[3:], *outs, *shapes[:3])],
            pltpu.SemaphoreType.DMA((3, 28)),
        ],
        compiler_params=pltpu.CompilerParams(vmem_limit_bytes=60 * 2**20),
    )(*operands)


SCHEDULE = (
    "X0", "G7own", "G2own", "G4own", "K1", "G5own", "G1own", "G3own", "G2L1", "G0own", "G2R1", "G3L1",
    "G3R1", "G2R2", "K2", "G2L2", "G3R2", "G3L2", "G6own", "G2L3", "G0cross", "G3L3", "K3", "G2R3",
    "G1cross", "G6L1", "G3R3", "G2cross", "G6R1", "G3cross", "G6R2", "G0R1", "G6L2", "G0L1", "G6L3", "K4",
    "G0L2", "K5", "K6", "T0gain", "G1L1", "T0memory", "G0R2", "G6R3", "T0n1", "G1R1", "G4cross", "G1R2",
    "G2second", "G2finish", "T0k2", "G1L2", "G7cross", "G0R3", "G0L3", "G3second", "G3finish", "G1R3",
    "G1L3", "G6cross", "G2drain", "G4L1", "G0second", "G7L1", "T0v2", "G3drain", "G7R1", "G0finish",
    "G1second", "G7L2", "T0q1", "T0k1", "G5cross", "G4R1", "G1finish", "T0v1", "G7R2", "T2A1", "T0A1",
    "T1A1", "G4L2", "T0o1", "G7R3", "G7L3", "G4R2", "T0n2", "T0q2", "G6second", "G5L1", "T0A2", "G4R3",
    "G0drain", "G6finish", "G4L3", "G1drain", "T2A2", "G7second", "G5R1", "G6drain", "T1A2", "G5L2",
    "G7finish", "G7drain", "T0o2", "G4second", "G5R2", "G5L3", "T0begin", "T0n3", "G4finish", "T0act",
    "T0back", "T0out", "G5R3", "G4drain", "T0W", "T0grads", "T3act", "T3back", "G5second", "T3out", "T3W",
    "T3grads", "S4startA", "S4startB", "G5finish", "S7startA", "T1act", "G5drain", "S4coreA", "T1out",
    "T1back", "S7coreA", "T1grads", "T1W", "T2act", "T2back", "T2W", "S5startA", "S4coreB", "T2out",
    "T2grads", "S5coreA", "S6startA", "S7startB", "T0nb3", "T0low", "S5startB", "S4halfA", "T0do2", "T1B2",
    "S6coreA", "T3B2", "S6startB", "S5coreB", "T0B2", "T5B2", "T4B2", "S7halfA", "S4halfB", "S5halfA",
    "S6coreB", "S4z1", "S7coreB", "T2B2", "T0mg", "T0dn2", "T0w7", "T0nb2", "S5halfB", "S5z1", "T0w6",
    "T0w4", "S3startA", "S6halfA", "T0do1", "T0w5", "S2startA", "S4z2", "S7crossA", "S3startB", "T0B1",
    "S2coreA", "S3coreA", "T0w3", "S2startB", "T3B1", "S5z2", "T1B1", "S7halfB", "S2coreB", "S3coreB",
    "T2B1", "S6crossA", "T4B1", "S2halfA", "S6halfB", "T5B1", "S3halfA", "T0dn1", "T0w2", "S1startA", "T0w0",
    "T0w1", "S0startA", "S7crossB", "S7z1", "S0startB", "S1startB", "S1coreA", "S3halfB", "S3z1", "S0coreA",
    "S7z2", "S6crossB", "S2halfB", "T0nb1", "S6z1", "S0coreB", "S2z1", "R0", "R1", "S1coreB", "S6z2", "R2",
    "S1halfA", "S0halfA", "S3z2", "S2z2", "R3", "S0halfB", "S4z3", "S1halfB", "S1crossA", "S5z3", "R4",
    "S3z3", "S0crossA", "S1crossB", "S1z1", "S0crossB", "S0z1", "R5", "S6z3", "S7z3", "R6", "S2z3", "S1z2",
    "S3last", "S0z2", "S5last", "S4last", "S2last", "R7", "S5finish", "S4finish", "S1z3", "S2finish",
    "S1finish", "S0z3", "S3finish", "S0finish",
)


def shards_block(
    hidden, memory, cotangent, target_lengths, memory_lengths,
    qk_master, value_master, output_master, inner_master, outer_master, gain_master, table_master,
    qk_first, value_first, output_first, inner_first, outer_first, gain_first, table_first,
    qk_second, value_second, output_second, inner_second, outer_second, gain_second, table_second,
):
    place = np.arange(768)
    spread = (place[None, :] % 24 == np.arange(128)[:, None]).astype(jnp.bfloat16)
    owner = (place[None, :] // 24 == np.arange(32)[:, None]).astype(np.float32)
    by_distance = bucket_rows(256)
    flat = lambda a: a.reshape(512, 768)
    low_out, hidden_grad, memory_grad, res, last, small = run_layer(
        tuple((s[0], int(s[1]), s[2:]) for s in SCHEDULE), target_lengths.T, memory_lengths.T, flat(hidden), flat(memory), flat(cotangent),
        qk_master, value_master, output_master, inner_master, outer_master, gain_master, table_master.T,
        spread, owner, np.roll(by_distance[:, ::-1], 1, axis=1),
    )
    low_out, hidden_grad, memory_grad, *rest = run_adam(
        low_out, hidden_grad, memory_grad, res.reshape(12, 24, 768), last, small, by_distance[:, ::-1],
        qk_master, value_master, output_master, inner_master, outer_master, gain_master, table_master.T,
        qk_first, value_first, output_first, inner_first, outer_first, gain_first, table_first.T,
        qk_second, value_second, output_second, inner_second, outer_second, gain_second, table_second.T,
    )
    for i in (6, 13, 20, 27):
        rest[i] = rest[i].T
    whole = lambda a: a.reshape(2, 1, 256, 768)
    return whole(low_out), whole(hidden_grad), whole(memory_grad), *rest


def solution(mesh):
    placed = (
        P(None, ("dp", "fsdp"), None, None),
        P(None, ("dp", "fsdp"), None, None),
        P(None, ("dp", "fsdp"), None, None),
        P(None, ("dp", "fsdp")),
        P(None, ("dp", "fsdp")),
        P(None, ("dp", "fsdp"), None),
        P(None, ("dp", "fsdp"), None),
        P(None, ("dp", "fsdp"), None),
        P(("dp", "fsdp"), None),
        P(("dp", "fsdp"), None),
        P(None, ("dp", "fsdp")),
        P(),
        P(None, ("dp", "fsdp"), None),
        P(None, ("dp", "fsdp"), None),
        P(None, ("dp", "fsdp"), None),
        P(("dp", "fsdp"), None),
        P(("dp", "fsdp"), None),
        P(None, ("dp", "fsdp")),
        P(),
        P(None, ("dp", "fsdp"), None),
        P(None, ("dp", "fsdp"), None),
        P(None, ("dp", "fsdp"), None),
        P(("dp", "fsdp"), None),
        P(("dp", "fsdp"), None),
        P(None, ("dp", "fsdp")),
        P(),
    )
    small_slice = dict(mesh.shape) == {"dp": 8, "fsdp": 4}
    return jax.shard_map(
        shards_block if small_slice else shards,
        mesh=mesh,
        in_specs=placed,
        out_specs=(
            P(None, ("dp", "fsdp"), None, None),
            P(None, ("dp", "fsdp"), None, None),
            P(None, ("dp", "fsdp"), None, None),
            P(None, ("dp", "fsdp"), None),
            P(None, ("dp", "fsdp"), None),
            P(None, ("dp", "fsdp"), None),
            P(("dp", "fsdp"), None),
            P(("dp", "fsdp"), None),
            P(None, ("dp", "fsdp")),
            P(),
            P(None, ("dp", "fsdp"), None),
            P(None, ("dp", "fsdp"), None),
            P(None, ("dp", "fsdp"), None),
            P(("dp", "fsdp"), None),
            P(("dp", "fsdp"), None),
            P(None, ("dp", "fsdp")),
            P(),
            P(None, ("dp", "fsdp"), None),
            P(None, ("dp", "fsdp"), None),
            P(None, ("dp", "fsdp"), None),
            P(("dp", "fsdp"), None),
            P(("dp", "fsdp"), None),
            P(None, ("dp", "fsdp")),
            P(),
            P(None, ("dp", "fsdp"), None),
            P(None, ("dp", "fsdp"), None),
            P(None, ("dp", "fsdp"), None),
            P(("dp", "fsdp"), None),
            P(("dp", "fsdp"), None),
            P(None, ("dp", "fsdp")),
            P(),
        ),
        check_vma=False,
    )
```

```python
import functools
import math

import jax
import jax.numpy as jnp
import numpy as np
from jax import lax
from jax.experimental import pallas as pl
from jax.experimental.pallas import tpu as pltpu
from jax.sharding import PartitionSpec as P

HEADS = 12
HEAD_DIM = 64
BUCKETS = 32
MAX_DIST = 128
STEP = 10


epsilon_norm = 1e-06
score_scale = 0.125
masked_score = -1e30
beta_first = 0.9
beta_second = 0.999
adam_epsilon = 1e-08
rate_matrix = 0.15
rate_small = 1.0
weight_decay = 0.01
highest = lax.Precision.HIGHEST


def bucket_onehot(length):
    places = jnp.arange(length, dtype=jnp.int32)
    distance = jnp.maximum(places[:, None] - places[None, :], 0)
    exact_range = BUCKETS // 2
    safe_distance = jnp.maximum(distance, 1).astype(jnp.float32)
    spread = (
        jnp.log(safe_distance / exact_range)
        / math.log(MAX_DIST / exact_range)
        * (BUCKETS - exact_range)
    )
    far_bucket = jnp.minimum(exact_range + spread.astype(jnp.int32), BUCKETS - 1)
    bucket = jnp.where(distance < exact_range, distance, far_bucket)
    labels = jnp.arange(BUCKETS, dtype=jnp.int32)
    return (bucket[None, :, :] == labels[:, None, None]).astype(jnp.float32)


def product(left_side, right_side):
    return jnp.dot(left_side, right_side, preferred_element_type=jnp.float32)


def product_over_rows(left_side, right_side):
    return lax.dot_general(
        left_side, right_side, (((0,), (0,)), ((), ())), preferred_element_type=jnp.float32
    )


def product_transposed(left_side, right_side):
    return lax.dot_general(
        left_side, right_side, (((1,), (1,)), ((), ())), preferred_element_type=jnp.float32
    )


def to_heads(values, sequences):
    return values.reshape(sequences, -1, HEADS, HEAD_DIM)


def normalize(values, gain_row):
    scale_rows = lax.rsqrt(jnp.mean(values * values, axis=-1, keepdims=True) + epsilon_norm)
    unit_rows = values * scale_rows
    return ((unit_rows * gain_row).astype(jnp.bfloat16), unit_rows, scale_rows)


def normalize_back(grad_norm, unit_rows, scale_rows, gain_row):
    gain_grad = jnp.sum(grad_norm * unit_rows, axis=0)
    grad_unit = grad_norm * gain_row
    grad_values = scale_rows * (
        grad_unit - unit_rows * jnp.mean(grad_unit * unit_rows, axis=-1, keepdims=True)
    )
    return (grad_values, gain_grad)


def attend_scores(queries, key_heads, bias_term, allowed):
    scores = (
        jnp.einsum("sihe,sjhe->shij", queries, key_heads, preferred_element_type=jnp.float32)
        * score_scale
        + bias_term
    )
    return jnp.where(allowed, scores, masked_score)


def attend_forward(queries, key_heads, value_heads, bias_term, allowed):
    scores = attend_scores(queries, key_heads, bias_term, allowed)
    row_max = jnp.max(scores, axis=-1, keepdims=True)
    expanded = jnp.exp(scores - row_max)
    row_total = jnp.sum(expanded, axis=-1, keepdims=True)
    weights = (expanded / row_total).astype(jnp.bfloat16)
    mixed_heads = jnp.einsum(
        "shij,sjhe->sihe", weights, value_heads, preferred_element_type=jnp.float32
    )
    return (mixed_heads, row_max + jnp.log(row_total))


def attend_back(queries, key_heads, value_heads, bias_term, allowed, summary, grad_mixed):
    scores = attend_scores(queries, key_heads, bias_term, allowed)
    weights = jnp.exp(scores - summary)
    grad_weights = jnp.einsum(
        "sihe,sjhe->shij", grad_mixed, value_heads, preferred_element_type=jnp.float32
    )
    grad_values = jnp.einsum(
        "shij,sihe->sjhe",
        weights.astype(jnp.bfloat16),
        grad_mixed,
        preferred_element_type=jnp.float32,
    )
    grad_scores = (
        weights * (grad_weights - jnp.sum(weights * grad_weights, axis=-1, keepdims=True))
    ).astype(jnp.bfloat16)
    grad_queries = (
        jnp.einsum("shij,sjhe->sihe", grad_scores, key_heads, preferred_element_type=jnp.float32)
        * score_scale
    )
    grad_keys = (
        jnp.einsum("shij,sihe->sjhe", grad_scores, queries, preferred_element_type=jnp.float32)
        * score_scale
    )
    return (grad_queries, grad_keys, grad_values, grad_scores)


def forward_pass(gathered, bias_heads, hidden_seq, memory_seq, target_len, memory_len):
    qk_full, value_full, output_full, inner_full, outer_full, gain_full = gathered
    gain_rows = gain_full.astype(jnp.float32)
    sequences, length, model_width = hidden_seq.shape
    memory_span = memory_seq.shape[1]
    row_count = sequences * length
    residual = hidden_seq.astype(jnp.float32).reshape(row_count, model_width)
    memory_rows = memory_seq.reshape(sequences * memory_span, model_width)
    places = jnp.arange(length, dtype=jnp.int32)
    self_mask = (places[None, :] <= places[:, None])[None, None] & (
        places[None, None, None, :] < target_len[:, None, None, None]
    )
    memory_places = jnp.arange(memory_span, dtype=jnp.int32)
    cross_mask = (memory_places[None, :] < memory_len[:, None])[:, None, None, :]
    normed_first, unit_first, scale_first = normalize(residual, gain_rows[0])
    query_first = product(normed_first, qk_full[0]).astype(jnp.bfloat16)
    key_first = product(normed_first, qk_full[1]).astype(jnp.bfloat16)
    value_first = product(normed_first, value_full[0]).astype(jnp.bfloat16)
    mixed_first, summary_first = attend_forward(
        to_heads(query_first, sequences),
        to_heads(key_first, sequences),
        to_heads(value_first, sequences),
        bias_heads,
        self_mask,
    )
    mixed_first = mixed_first.reshape(row_count, model_width).astype(jnp.bfloat16)
    first_sum = residual + product(mixed_first, output_full[0])
    normed_second, unit_second, scale_second = normalize(first_sum, gain_rows[1])
    query_second = product(normed_second, qk_full[2]).astype(jnp.bfloat16)
    key_second = product(memory_rows, qk_full[3]).astype(jnp.bfloat16)
    value_second = product(memory_rows, value_full[1]).astype(jnp.bfloat16)
    mixed_second, summary_second = attend_forward(
        to_heads(query_second, sequences),
        to_heads(key_second, sequences),
        to_heads(value_second, sequences),
        0.0,
        cross_mask,
    )
    mixed_second = mixed_second.reshape(row_count, model_width).astype(jnp.bfloat16)
    second_sum = first_sum + product(mixed_second, output_full[1])
    normed_third, unit_third, scale_third = normalize(second_sum, gain_rows[2])
    inner_act = product(normed_third, inner_full)
    activated = jax.nn.gelu(inner_act, approximate=True).astype(jnp.bfloat16)
    produced = (second_sum + product(activated, outer_full)).astype(jnp.bfloat16)
    stored = (
        self_mask,
        cross_mask,
        memory_rows,
        normed_first,
        unit_first,
        scale_first,
        query_first,
        key_first,
        value_first,
        summary_first,
        mixed_first,
        normed_second,
        unit_second,
        scale_second,
        query_second,
        key_second,
        value_second,
        summary_second,
        mixed_second,
        normed_third,
        unit_third,
        scale_third,
        inner_act,
        activated,
    )
    return (stored, produced.reshape(sequences, length, model_width))


def backward_pass(gathered, bias_heads, stored, cotangent_seq, target_len):
    qk_full, value_full, output_full, inner_full, outer_full, gain_full = gathered
    gain_rows = gain_full.astype(jnp.float32)
    (
        self_mask,
        cross_mask,
        memory_rows,
        normed_first,
        unit_first,
        scale_first,
        query_first,
        key_first,
        value_first,
        summary_first,
        mixed_first,
        normed_second,
        unit_second,
        scale_second,
        query_second,
        key_second,
        value_second,
        summary_second,
        mixed_second,
        normed_third,
        unit_third,
        scale_third,
        inner_act,
        activated,
    ) = stored
    sequences, length, model_width = cotangent_seq.shape
    row_count = sequences * length
    places = jnp.arange(length, dtype=jnp.int32)
    live_rows = (places[None, :] < target_len[:, None]).astype(jnp.float32).reshape(row_count, 1)
    grad_out = cotangent_seq.astype(jnp.float32).reshape(row_count, model_width) * live_rows
    branch = grad_out.astype(jnp.bfloat16)
    outer_grad = product_over_rows(activated, branch)
    grad_act = product_transposed(branch, outer_full)
    unused_value, gelu_pull = jax.vjp(
        lambda inputs: jax.nn.gelu(inputs, approximate=True), inner_act
    )
    grad_inner = gelu_pull(grad_act)[0].astype(jnp.bfloat16)
    inner_grad = product_over_rows(normed_third, grad_inner)
    grad_from_third, gain_third = normalize_back(
        product_transposed(grad_inner, inner_full), unit_third, scale_third, gain_rows[2]
    )
    grad_second = grad_out + grad_from_third
    branch = grad_second.astype(jnp.bfloat16)
    output_grad_second = product_over_rows(mixed_second, branch)
    grad_mixed = product_transposed(branch, output_full[1]).astype(jnp.bfloat16)
    grad_query, grad_key, grad_value, unused_scores = attend_back(
        to_heads(query_second, sequences),
        to_heads(key_second, sequences),
        to_heads(value_second, sequences),
        0.0,
        cross_mask,
        summary_second,
        to_heads(grad_mixed, sequences),
    )
    grad_query = grad_query.reshape(row_count, model_width).astype(jnp.bfloat16)
    grad_key = grad_key.reshape(memory_rows.shape[0], model_width).astype(jnp.bfloat16)
    grad_value = grad_value.reshape(memory_rows.shape[0], model_width).astype(jnp.bfloat16)
    qk_grad_two = product_over_rows(normed_second, grad_query)
    qk_grad_three = product_over_rows(memory_rows, grad_key)
    value_grad_one = product_over_rows(memory_rows, grad_value)
    memory_grad = product_transposed(grad_key, qk_full[3]) + product_transposed(
        grad_value, value_full[1]
    )
    grad_from_second, gain_second = normalize_back(
        product_transposed(grad_query, qk_full[2]), unit_second, scale_second, gain_rows[1]
    )
    grad_first = grad_second + grad_from_second
    branch = grad_first.astype(jnp.bfloat16)
    output_grad_first = product_over_rows(mixed_first, branch)
    grad_mixed = product_transposed(branch, output_full[0]).astype(jnp.bfloat16)
    grad_query, grad_key, grad_value, grad_scores = attend_back(
        to_heads(query_first, sequences),
        to_heads(key_first, sequences),
        to_heads(value_first, sequences),
        bias_heads,
        self_mask,
        summary_first,
        to_heads(grad_mixed, sequences),
    )
    grad_query = grad_query.reshape(row_count, model_width).astype(jnp.bfloat16)
    grad_key = grad_key.reshape(row_count, model_width).astype(jnp.bfloat16)
    grad_value = grad_value.reshape(row_count, model_width).astype(jnp.bfloat16)
    qk_grad_zero = product_over_rows(normed_first, grad_query)
    qk_grad_one = product_over_rows(normed_first, grad_key)
    value_grad_zero = product_over_rows(normed_first, grad_value)
    grad_norm = (
        product_transposed(grad_query, qk_full[0])
        + product_transposed(grad_key, qk_full[1])
        + product_transposed(grad_value, value_full[0])
    )
    grad_from_first, gain_first = normalize_back(grad_norm, unit_first, scale_first, gain_rows[0])
    hidden_grad = grad_first + grad_from_first
    score_term = jnp.sum(grad_scores.astype(jnp.float32), axis=0)
    grad_terms = (
        jnp.stack([qk_grad_zero, qk_grad_one, qk_grad_two, qk_grad_three]),
        jnp.stack([value_grad_zero, value_grad_one]),
        jnp.stack([output_grad_first, output_grad_second]),
        inner_grad,
        outer_grad,
        jnp.stack([gain_first, gain_second, gain_third]),
    )
    return (
        grad_terms,
        score_term,
        hidden_grad.reshape(sequences, length, model_width),
        memory_grad.reshape(sequences, -1, model_width),
    )


def adam_step(master, first_moment, second_moment, gradient, rate, decay):
    first_next = beta_first * first_moment + (1.0 - beta_first) * gradient
    second_next = beta_second * second_moment + (1.0 - beta_second) * gradient * gradient
    corrected = (
        first_next
        / (1.0 - beta_first**STEP)
        / (jnp.sqrt(second_next / (1.0 - beta_second**STEP)) + adam_epsilon)
    )
    master_next = master - rate * (corrected + decay * master)
    return (master_next, first_next, second_next)


def shards(
    hidden,
    memory,
    cotangent,
    target_lengths,
    memory_lengths,
    qk_master,
    value_master,
    output_master,
    inner_master,
    outer_master,
    gain_master,
    table_master,
    qk_first,
    value_first,
    output_first,
    inner_first,
    outer_first,
    gain_first,
    table_first,
    qk_second,
    value_second,
    output_second,
    inner_second,
    outer_second,
    gain_second,
    table_second,
):
    micro_count = hidden.shape[0]
    length = hidden.shape[2]
    model_width = hidden.shape[3]
    hidden_units = inner_master.shape[1]
    qk_low = qk_master.astype(jnp.bfloat16)
    value_low = value_master.astype(jnp.bfloat16)
    output_low = output_master.astype(jnp.bfloat16)
    inner_low = inner_master.astype(jnp.bfloat16)
    outer_low = outer_master.astype(jnp.bfloat16)
    gain_low = gain_master.astype(jnp.bfloat16)
    onehot = bucket_onehot(length)
    bias_heads = jnp.einsum("bij,bh->hij", onehot, table_master, precision=highest)
    masters = (qk_master, value_master, output_master, inner_master, outer_master, gain_master)
    totals = (
        jnp.zeros((4, model_width, model_width), jnp.float32),
        jnp.zeros((2, model_width, model_width), jnp.float32),
        jnp.zeros((2, model_width, model_width), jnp.float32),
        jnp.zeros((model_width, hidden_units), jnp.float32),
        jnp.zeros((hidden_units, model_width), jnp.float32),
        jnp.zeros((3, model_width), jnp.float32),
    )
    reduced = tuple((jnp.zeros_like(master) for master in masters))
    score_total = jnp.zeros((HEADS, length, length), jnp.float32)
    produced_list = []
    hidden_list = []
    memory_list = []
    for micro_index in range(micro_count):
        gathered = (
            lax.all_gather(qk_low, ("dp", "fsdp"), axis=1, tiled=True),
            lax.all_gather(value_low, ("dp", "fsdp"), axis=1, tiled=True),
            lax.all_gather(output_low, ("dp", "fsdp"), axis=1, tiled=True),
            lax.all_gather(inner_low, ("dp", "fsdp"), axis=0, tiled=True),
            lax.all_gather(outer_low, ("dp", "fsdp"), axis=0, tiled=True),
            lax.all_gather(gain_low, ("dp", "fsdp"), axis=1, tiled=True),
        )
        stored, produced = forward_pass(
            gathered,
            bias_heads,
            hidden[micro_index],
            memory[micro_index],
            target_lengths[micro_index],
            memory_lengths[micro_index],
        )
        gathered = (
            lax.all_gather(qk_low, ("dp", "fsdp"), axis=1, tiled=True),
            lax.all_gather(value_low, ("dp", "fsdp"), axis=1, tiled=True),
            lax.all_gather(output_low, ("dp", "fsdp"), axis=1, tiled=True),
            lax.all_gather(inner_low, ("dp", "fsdp"), axis=0, tiled=True),
            lax.all_gather(outer_low, ("dp", "fsdp"), axis=0, tiled=True),
            lax.all_gather(gain_low, ("dp", "fsdp"), axis=1, tiled=True),
        )
        grad_terms, score_term, hidden_grad, memory_grad = backward_pass(
            gathered, bias_heads, stored, cotangent[micro_index], target_lengths[micro_index]
        )
        totals = tuple((running + addition for running, addition in zip(totals, grad_terms)))
        score_total = score_total + score_term
        produced_list.append(produced)
        hidden_list.append(hidden_grad)
        memory_list.append(memory_grad)
    reduced = (
        lax.psum_scatter(totals[0], ("dp", "fsdp"), scatter_dimension=1, tiled=True),
        lax.psum_scatter(totals[1], ("dp", "fsdp"), scatter_dimension=1, tiled=True),
        lax.psum_scatter(totals[2], ("dp", "fsdp"), scatter_dimension=1, tiled=True),
        lax.psum_scatter(totals[3], ("dp", "fsdp"), scatter_dimension=0, tiled=True),
        lax.psum_scatter(totals[4], ("dp", "fsdp"), scatter_dimension=0, tiled=True),
        lax.psum_scatter(totals[5], ("dp", "fsdp"), scatter_dimension=1, tiled=True),
    )
    table_grad = jnp.einsum("bij,hij->bh", onehot, score_total, precision=highest)
    table_grad = lax.psum(table_grad, ("dp", "fsdp"))
    all_masters = (
        qk_master,
        value_master,
        output_master,
        inner_master,
        outer_master,
        gain_master,
        table_master,
    )
    firsts = (
        qk_first,
        value_first,
        output_first,
        inner_first,
        outer_first,
        gain_first,
        table_first,
    )
    seconds = (
        qk_second,
        value_second,
        output_second,
        inner_second,
        outer_second,
        gain_second,
        table_second,
    )
    gradients = (reduced[0], reduced[1], reduced[2], reduced[3], reduced[4], reduced[5], table_grad)
    rates = (
        rate_matrix,
        rate_matrix,
        rate_matrix,
        rate_matrix,
        rate_matrix,
        rate_small,
        rate_small,
    )
    decays = (weight_decay, weight_decay, weight_decay, weight_decay, weight_decay, 0.0, 0.0)
    updated = [
        adam_step(
            all_masters[index],
            firsts[index],
            seconds[index],
            gradients[index],
            rates[index],
            decays[index],
        )
        for index in range(7)
    ]
    news = [entry[0] for entry in updated]
    first_news = [entry[1] for entry in updated]
    second_news = [entry[2] for entry in updated]
    copies = [entry.astype(jnp.bfloat16) for entry in news]
    layer_out = jnp.stack(produced_list)
    hidden_out = jnp.stack(hidden_list)
    memory_out = jnp.stack(memory_list)
    return (
        layer_out,
        hidden_out,
        memory_out,
        news[0],
        news[1],
        news[2],
        news[3],
        news[4],
        news[5],
        news[6],
        first_news[0],
        first_news[1],
        first_news[2],
        first_news[3],
        first_news[4],
        first_news[5],
        first_news[6],
        second_news[0],
        second_news[1],
        second_news[2],
        second_news[3],
        second_news[4],
        second_news[5],
        second_news[6],
        copies[0],
        copies[1],
        copies[2],
        copies[3],
        copies[4],
        copies[5],
        copies[6],
    )


MESH = pl.DeviceIdType.MESH
PAIRS = 6
SCATTER_ORDERS = ("cx", "cy", "ax", "ay", "ax", "ay", "ax", "cy")
ORDERS = ("ax", "ay", "cx", "cy", "ax", "ay", "cx", "ay")


class Place:
    def __init__(self, wa, wf):
        self.wa, self.wf = wa, wf
        dp, fs = lax.axis_index("dp"), lax.axis_index("fsdp")
        self.z, self.y = dp // 2, dp % 2
        self.x, self.c = fs // 2, fs % 2
        self.to = {
            "x": (dp, (1 - self.x) * 2 + self.c),
            "y": (self.z * 2 + 1 - self.y, fs),
            "c": (dp, self.x * 2 + 1 - self.c),
            "r": (dp + 2, fs),
            "l": (dp - 2, fs),
        }

    def enter(self, wait):
        bar = pltpu.get_barrier_semaphore()
        inner = (self.z > 0) & (self.z < 3)
        if wait:
            @pl.when(inner)
            def _():
                pl.semaphore_wait(bar, 5)

            @pl.when(jnp.logical_not(inner))
            def _():
                pl.semaphore_wait(bar, 4)

            return

        def greet(way):
            pl.semaphore_signal(bar, inc=1, device_id=self.to[way], device_id_type=MESH)

        for way in ("x", "y", "c"):
            greet(way)

        @pl.when(self.z < 3)
        def _():
            greet("r")

        @pl.when(self.z > 0)
        def _():
            greet("l")

    def pick(self, f, zs, ps, qs, core=None):
        c = self.c if core is None else core
        xs, ys = (ps, qs) if ORDERS[f][1] == "x" else (qs, ps)
        return self.block(f, zs, ys, xs, c)

    def block(self, f, zs, ys, xs, c):
        if f < PAIRS:
            return self.wa.at[2 * f + c, zs, ys, xs]
        return self.wf.at[zs, ys, xs, c, f - PAIRS]

    def own(self, f):
        return (self.x, self.y) if ORDERS[f][1] == "x" else (self.y, self.x)

    def ways(self, f):
        return ("x", "y") if ORDERS[f][1] == "x" else ("y", "x")


def push(place, src, dst, send, recv, way):
    pltpu.make_async_remote_copy(
        src_ref=src, dst_ref=dst, send_sem=send, recv_sem=recv,
        device_id=place.to[way], device_id_type=MESH,
    ).start()


def got(place, ref, sem, way):
    pltpu.make_async_remote_copy(
        src_ref=ref, dst_ref=ref, send_sem=sem, recv_sem=sem,
        device_id=place.to[way], device_id_type=MESH,
    ).wait_recv()


def left_out(place, ref, sem, way):
    pltpu.make_async_remote_copy(
        src_ref=ref, dst_ref=ref, send_sem=sem, recv_sem=sem,
        device_id=place.to[way], device_id_type=MESH,
    ).wait_send()


ALL = slice(None)


class Gather:
    def __init__(self, place, f, send, recv):
        self.k, self.f = place, f
        self.send, self.recv = send, recv
        self.first_cross = ORDERS[f][0] == "a"

    def do(self, name):
        if name[0] in "LR":
            self.step(int(name[1]), name[0])
        else:
            getattr(self, name)()

    def blk(self, zi):
        p, q = self.k.own(self.f)
        return self.k.pick(self.f, zi, ALL if self.first_cross else p, q)

    def move(self, ref, s, r, way):
        push(self.k, ref, ref, self.send.at[self.f, s], self.recv.at[self.f, r], way)

    def start(self):
        p, q = self.k.own(self.f)
        pw, qw = self.k.ways(self.f)
        if self.first_cross:
            self.move(self.k.pick(self.f, self.k.z, p, q), 0, 0, pw)
        else:
            self.spread(self.k.z, 1)

    def cross(self):
        p, q = self.k.own(self.f)
        pw, qw = self.k.ways(self.f)
        if self.first_cross:
            got(self.k, self.k.pick(self.f, self.k.z, 1 - p, q), self.recv.at[self.f, 0], pw)
            self.spread(self.k.z, 1)
        else:
            got(self.k, self.k.pick(self.f, ALL, 1 - p, q), self.recv.at[self.f, 0], pw)
            half = self.k.pick(self.f, ALL, ALL, q)
            self.move(half, 3, 7, qw)
            self.move(half, 4, 8, "c")

    def sideways(self, zi):
        pw, qw = self.k.ways(self.f)
        if self.first_cross:
            self.move(self.blk(zi), 3, 7, qw)
            self.move(self.blk(zi), 4, 8, "c")
        else:
            self.move(self.blk(zi), 0, 0, pw)

    def spread(self, zi, t):
        z = self.k.z

        @pl.when(z < 3)
        def _():
            self.move(self.blk(zi), 1, t, "r")

        @pl.when(z > 0)
        def _():
            self.move(self.blk(zi), 2, 3 + t, "l")

        self.sideways(zi)

    def step(self, t, side):
        z = self.k.z

        if side == "L":
            @pl.when(z >= t)
            def _():
                got(self.k, self.blk(z - t), self.recv.at[self.f, t], "l")

                if t < 3:
                    @pl.when(z < 3)
                    def _():
                        self.move(self.blk(z - t), 1, t + 1, "r")

                self.sideways(z - t)
        else:
            @pl.when(z <= 3 - t)
            def _():
                got(self.k, self.blk(z + t), self.recv.at[self.f, 3 + t], "r")

                if t < 3:
                    @pl.when(z > 0)
                    def _():
                        self.move(self.blk(z + t), 2, 3 + t + 1, "l")

                self.sideways(z + t)

    def second(self):
        p, q = self.k.own(self.f)
        pw, qw = self.k.ways(self.f)
        other = self.k.pick(self.f, ALL, ALL, 1 - q)
        got(self.k, other, self.recv.at[self.f, 7], qw)
        self.move(other, 4, 8, "c")

    def finish(self):
        theirs = self.k.pick(self.f, ALL, ALL, ALL, 1 - self.k.c)
        got(self.k, theirs, self.recv.at[self.f, 8], "c")

    def drain(self):
        p, q = self.k.own(self.f)
        pw, qw = self.k.ways(self.f)
        z, f = self.k.z, self.f
        some = (lambda n: self.k.pick(f, pl.ds(0, n), ALL if self.first_cross else p, q))
        first = self.k.pick(f, z, p, q) if self.first_cross else self.k.pick(f, ALL, p, q)
        left_out(self.k, first, self.send.at[f, 0], pw)
        for n in (1, 2, 3):
            @pl.when(z == n - 1)
            def _():
                left_out(self.k, some(n), self.send.at[f, 1], "r")

            @pl.when(z == 4 - n)
            def _():
                left_out(self.k, some(n), self.send.at[f, 2], "l")
        left_out(self.k, self.k.pick(f, ALL, ALL, q), self.send.at[f, 3], qw)
        left_out(self.k, self.k.pick(f, ALL, ALL, ALL), self.send.at[f, 4], "c")


def add_into(dst, srcs, lead):
    sizes = lead
    count = 1
    for s in sizes:
        count *= s

    def body(i, _):
        idx, rest = [], i
        for s in reversed(sizes):
            idx.append(rest % s)
            rest = rest // s
        idx = tuple(reversed(idx)) or Ellipsis
        if len(srcs) == 1:
            dst[idx] = dst[idx] + srcs[0][idx]
            return 0
        total = dst[idx].astype(jnp.float32)
        for src in srcs:
            total = total + src[idx].astype(jnp.float32)
        dst[idx] = total.astype(jnp.bfloat16)
        return 0

    lax.fori_loop(0, count, body, 0)


PIECES = (slice(3, 4), slice(0, 1), slice(1, 3))


class Scatter:
    def __init__(self, place, f, send, recv, slots, final, result, credit):
        self.k, self.f = place, f
        self.wait_credit, self.give_credit, self.credit = credit
        self.send, self.recv = send, recv
        self.rd, self.rq, self.rp, self.rl, self.rr = slots
        self.final, self.result = final, result
        self.wide = SCATTER_ORDERS[f][0] == "a"

    def do(self, name):
        if name[0] == "z":
            self.step_in(int(name[1]))
        elif name[-1] in "AB":
            getattr(self, name[:-1])((0, 1) if name[-1] == "A" else (2,))
        else:
            getattr(self, name)()

    def pick(self, zs, ps, qs, core=None):
        c = self.k.c if core is None else core
        xs, ys = (ps, qs) if SCATTER_ORDERS[self.f][1] == "x" else (qs, ps)
        return self.k.block(self.f, zs, ys, xs, c)

    def own(self):
        return (self.k.x, self.k.y) if SCATTER_ORDERS[self.f][1] == "x" else (self.k.y, self.k.x)

    def ways(self):
        return ("x", "y") if SCATTER_ORDERS[self.f][1] == "x" else ("y", "x")

    def move(self, src, dst, s, way):
        push(self.k, src, dst, self.send.at[self.f, s], self.recv.at[self.f, s], way)

    def blk(self, zi):
        p, q = self.own()
        return self.pick(zi, ALL if self.wide else p, q)

    def start(self, pieces):
        if self.wait_credit and 0 in pieces:
            pl.semaphore_wait(self.credit, 1)
        for i in pieces:
            self.move(self.pick(PIECES[i], ALL, ALL, 1 - self.k.c), self.rd.at[PIECES[i]], i, "c")

    def rpick(self, zs, ps, qs):
        xs, ys = (ps, qs) if SCATTER_ORDERS[self.f][1] == "x" else (qs, ps)
        return self.rd.at[zs, ys, xs]

    def core(self, pieces):
        p, q = self.own()
        pw, qw = self.ways()
        for i in pieces:
            zs = PIECES[i]
            n = zs.stop - zs.start
            got(self.k, self.rd.at[zs], self.recv.at[self.f, i], "c")
            away = self.pick(zs, ALL, 1 - q)
            add_into(away, [self.rpick(zs, ALL, 1 - q)], (n, 2))
            self.move(away, self.rq.at[zs], 3 + i, qw)

    def half(self, pieces):
        p, q = self.own()
        pw, qw = self.ways()
        for i in pieces:
            zs = PIECES[i]
            n = zs.stop - zs.start
            got(self.k, self.rq.at[zs], self.recv.at[self.f, 3 + i], qw)
            add_into(self.pick(zs, ALL, q), [self.rpick(zs, ALL, q), self.rq.at[zs]], (n, 2))
            if not self.wide:
                self.move(self.pick(zs, 1 - p, q), self.rp.at[zs], 6 + i, pw)
        if self.wide and 0 in pieces:
            self.step_out(1)
        if self.give_credit and 2 in pieces:
            pl.semaphore_signal(self.credit, inc=1, device_id=self.k.to["c"], device_id_type=MESH)

    def cross(self, pieces):
        p, q = self.own()
        pw, qw = self.ways()
        for i in pieces:
            zs = PIECES[i]
            n = zs.stop - zs.start
            got(self.k, self.rp.at[zs], self.recv.at[self.f, 6 + i], pw)
            add_into(self.pick(zs, p, q), [self.rp.at[zs]], (n,))
        if 0 in pieces:
            self.step_out(1)

    def step_out(self, t):
        z = self.k.z

        @pl.when(z <= t - 1)
        def _():
            self.move(self.blk(z + 4 - t), self.rl.at[t - 1], 8 + t, "r")

        @pl.when(z >= 4 - t)
        def _():
            self.move(self.blk(z - 4 + t), self.rr.at[t - 1], 11 + t, "l")

    def step_in(self, t):
        z, f = self.k.z, self.f
        lead = (2,) if self.wide else ()

        @pl.when((z >= 1) & (z <= t))
        def _():
            got(self.k, self.rl.at[t - 1], self.recv.at[f, 8 + t], "l")
            add_into(self.blk(z + 3 - t), [self.rl.at[t - 1]], lead)

        @pl.when((z <= 2) & (z >= 3 - t))
        def _():
            got(self.k, self.rr.at[t - 1], self.recv.at[f, 11 + t], "r")
            add_into(self.blk(z - 3 + t), [self.rr.at[t - 1]], lead)

        if t < 3:
            self.step_out(t + 1)
        else:
            p, q = self.own()
            pw, qw = self.ways()
            if self.wide:
                self.move(self.pick(z, 1 - p, q), self.rp, 6, pw)
            else:
                self.total(None)

    def last(self):
        pw, qw = self.ways()
        got(self.k, self.rp, self.recv.at[self.f, 6], pw)
        self.total(self.rp)

    def total(self, more):
        p, q = self.own()
        c = self.k.c
        mine = self.pick(self.k.z, p, q)[...].astype(jnp.float32)
        if more is not None:
            mine = mine + more[...].astype(jnp.float32)
        self.final[...] = mine
        if self.f < PAIRS:
            kept = pl.ds(pl.multiple_of(c * 24, 8), 24)
            away = pl.ds(pl.multiple_of(24 - c * 24, 8), 24)
            self.move(self.final.at[away], self.result.at[self.f, c], 15, "c")
            self.result[self.f, c] = self.final[kept]

    def finish(self):
        if self.f < PAIRS:
            got(self.k, self.result.at[self.f, 1 - self.k.c], self.recv.at[self.f, 15], "c")

    def drain(self):
        pw, qw = self.ways()
        z, f, k = self.k.z, self.f, self.k
        for i, zs in enumerate(PIECES):
            left_out(k, self.rd.at[zs], self.send.at[f, i], "c")
            left_out(k, self.rq.at[zs], self.send.at[f, 3 + i], qw)
            if not self.wide:
                left_out(k, self.rp.at[zs], self.send.at[f, 6 + i], pw)
        if self.wide:
            left_out(k, self.rp, self.send.at[f, 6], pw)
        for t in (1, 2, 3):
            @pl.when(z <= t - 1)
            def _():
                left_out(k, self.rl.at[t - 1], self.send.at[f, 8 + t], "r")

            @pl.when(z >= 4 - t)
            def _():
                left_out(k, self.rr.at[t - 1], self.send.at[f, 11 + t], "l")
        if f < PAIRS:
            left_out(k, self.final.at[pl.ds(0, 24)], self.send.at[f, 15], "c")


class Line:
    def __init__(self, place, buf, send, recv):
        self.k, self.buf, self.send, self.recv = place, buf, send, recv

    def move(self, zi, s, r, way):
        push(self.k, self.buf.at[zi], self.buf.at[zi], self.send.at[s], self.recv.at[r], way)

    def start(self):
        z = self.k.z

        @pl.when(z < 3)
        def _():
            self.move(z, 3, 3, "r")

        @pl.when(z > 0)
        def _():
            self.move(z, 6, 6, "l")

    def step(self, t):
        z = self.k.z

        @pl.when(z >= t)
        def _():
            got(self.k, self.buf.at[z - t], self.recv.at[2 + t], "l")

            if t < 3:
                @pl.when(z < 3)
                def _():
                    self.move(z - t, 3 + t, 3 + t, "r")

        @pl.when(z <= 3 - t)
        def _():
            got(self.k, self.buf.at[z + t], self.recv.at[5 + t], "r")

            if t < 3:
                @pl.when(z > 0)
                def _():
                    self.move(z + t, 6 + t, 6 + t, "l")

    def drain(self):
        z = self.k.z
        for t in range(3):
            @pl.when((z < 3) & (z >= t))
            def _():
                left_out(self.k, self.buf.at[0], self.send.at[3 + t], "r")

            @pl.when((z > 0) & (z <= 3 - t))
            def _():
                left_out(self.k, self.buf.at[0], self.send.at[6 + t], "l")


class Gains:
    def __init__(self, place, buf, send, recv):
        self.k, self.buf, self.send, self.recv = place, buf, send, recv
        self.line = Line(place, buf, send, recv)
        z, y, x, c = place.z, place.y, place.x, place.c
        self.mine = [buf.at[z, y, x, c], buf.at[z, y, x], buf.at[z, y]]
        self.other = [buf.at[z, y, x, 1 - c], buf.at[z, y, 1 - x], buf.at[z, 1 - y]]

    def go(self, i):
        if 1 <= i <= 3:
            got(self.k, self.other[i - 1], self.recv.at[i - 1], "cxy"[i - 1])
        if i < 3:
            push(self.k, self.mine[i], self.mine[i], self.send.at[i], self.recv.at[i], "cxy"[i])
        elif i == 3:
            self.line.start()
        else:
            self.line.step(i - 3)

    def drain(self):
        for i in range(3):
            left_out(self.k, self.mine[i], self.send.at[i], "cxy"[i])
        self.line.drain()


class Small:
    def __init__(self, place, bufs, got_bufs, along, send, recv):
        self.k, self.bufs, self.got_bufs, self.along = place, bufs, got_bufs, along
        self.send, self.recv = send, recv
        self.line = Line(place, along, send, recv)

    def go(self, i):
        if 1 <= i <= 3:
            got(self.k, self.got_bufs.at[i - 1], self.recv.at[i - 1], "cxy"[i - 1])
            total = self.bufs[i - 1] + self.got_bufs[i - 1]
            if i < 3:
                self.bufs[i] = total
            else:
                self.along[self.k.z] = total
        if i < 3:
            push(self.k, self.bufs.at[i], self.got_bufs.at[i], self.send.at[i], self.recv.at[i], "cxy"[i])
        elif i == 3:
            self.line.start()
        else:
            self.line.step(i - 3)

    def drain(self):
        for i in range(3):
            left_out(self.k, self.bufs.at[i], self.send.at[i], "cxy"[i])
        self.line.drain()
BF, F32 = jnp.bfloat16, jnp.float32
INNER_UNIT = (8, 10, 11, 9)
ROOT = math.sqrt(2.0 / math.pi)
CUBE = 0.044715


def dot_nn(a, b):
    return lax.dot_general(a, b, (((1,), (0,)), ((), ())), preferred_element_type=F32)


def dot_nt(a, b):
    return lax.dot_general(a, b, (((1,), (1,)), ((), ())), preferred_element_type=F32)


def dot_tn(a, b):
    return lax.dot_general(a, b, (((0,), (0,)), ((), ())), preferred_element_type=F32)


def unit_of(values):
    scale = lax.rsqrt(jnp.mean(values * values, axis=-1, keepdims=True) + epsilon_norm)
    return values * scale, scale


class Layer:
    def __init__(self, wa, wf, b):
        self.wa, self.wf, self.b = wa, wf, b

    def times(self, a, u, put):
        for t in range(3):
            tile = slice(256 * t, 256 * t + 256)
            put(tile, dot_nn(a[...], self.wa[u, :, :, :, :, tile].reshape(768, 256)))

    def times_back(self, pairs, put):
        total = None
        for a, u in pairs:
            term = dot_nt(a[...], self.wa[u].reshape(768, 768))
            total = term if total is None else total + term
        put(slice(0, 768), total)

    def weight_grad(self, a, d, u):
        for t in range(2):
            tile = dot_tn(a[:, 384 * t:384 * t + 384], d[...])
            self.wa[u, 2 * t:2 * t + 2] = tile.astype(BF).reshape(2, 2, 2, 48, 768)

    def project(self, a, u, dst):
        def put(tile, value):
            dst[:, tile] = value.astype(BF)

        self.times(a, u, put)

    def add_project(self, base, a, u, dst):
        def put(tile, value):
            dst[:, tile] = base[:, tile].astype(F32) + value

        self.times(a, u, put)

    def norm(self, src, g, dst):
        gain = self.b["gain"][pl.ds(g, 1), :]

        for i in range(4):
            rows = slice(128 * i, 128 * i + 128)
            unit, _unused = unit_of(src[rows].astype(F32))
            dst[rows] = (unit * gain).astype(BF)

    def norm_back(self, dn, src, g, base, dst, low):
        gain = self.b["gain"][pl.ds(g, 1), :]

        total = jnp.zeros((1, 768), F32)
        for i in range(4):
            rows = slice(128 * i, 128 * i + 128)
            unit, scale = unit_of(src[rows].astype(F32))
            grad = dn[rows]
            total = total + jnp.sum(grad * unit, axis=0, keepdims=True)
            pulled = grad * gain
            value = base(rows, i) + scale * (pulled - unit * jnp.mean(pulled * unit, axis=-1, keepdims=True))
            dst[rows] = value
            if low is not None:
                low[rows] = value.astype(BF)
        for i in range(3):
            self.b["small"][12 + 3 * g + i:13 + 3 * g + i, :] = total[:, 256 * i:256 * i + 256]

    def head_masks(self):
        lane = lax.broadcasted_iota(jnp.int32, (1, 128), 1)
        low = (lane < 64).astype(F32)
        return low.astype(BF), (1.0 - low).astype(BF)

    def far(self, s, kind):
        col = lax.broadcasted_iota(jnp.int32, (1, 256), 1)
        length = self.b["lens"][0, s] if kind == 1 else self.b["mem_lens"][0, s]
        return jnp.where(col < length, 0.0, masked_score)

    def bias(self, head, causal):
        row = self.b["bias_row"][pl.ds(head, 1), :]
        turned = pltpu.roll(jnp.broadcast_to(row, (256, 256)), 0, axis=1, stride=1, stride_axis=0)
        return jnp.where(causal, turned, masked_score)

    def weights(self, scores):
        expanded = jnp.exp(scores - jnp.max(scores, axis=-1, keepdims=True))
        return expanded * (1.0 / jnp.sum(expanded, axis=-1, keepdims=True))

    def places(self):
        row = lax.broadcasted_iota(jnp.int32, (256, 256), 0)
        col = lax.broadcasted_iota(jnp.int32, (256, 256), 1)
        return row, col

    def attend(self, kind, first, last):
        b = self.b
        q, k, v, o = (b[n + str(kind)] for n in "qkvo")
        masks = self.head_masks()
        keep = masks[0].astype(F32)
        row, col = self.places()

        def body(hp, _):
            lanes = pl.ds(pl.multiple_of(128 * hp, 128), 128)
            biases = [self.bias(2 * hp + e, col <= row) if kind == 1 else 0.0 for e in range(2)]
            rows = [slice(0, 256), slice(256, 512)]
            both = [(s, e) for s in range(2) for e in range(2)]
            queries = [q[r, lanes] * BF(score_scale) for r in rows]
            keys, values = [k[r, lanes] for r in rows], [v[r, lanes] for r in rows]
            far = [self.far(s, kind) for s in range(2)]
            scores = [dot_nt(queries[s] * masks[e], keys[s]) + (biases[e] + far[s]) for s, e in both]
            low = [self.weights(one).astype(BF) for one in scores]
            mixed = [dot_nn(p, values[s]) for p, (s, e) in zip(low, both)]
            for s in range(2):
                o[rows[s], lanes] = (mixed[2 * s] * keep + mixed[2 * s + 1] * (1.0 - keep)).astype(BF)
            return 0

        lax.fori_loop(first, last, body, 0)

    def attend_back(self, kind, first, last):
        b = self.b
        q, k, v, o = (b[n + str(kind)] for n in "qkvo")
        masks = self.head_masks()
        keep = masks[0].astype(F32)
        row, col = self.places()
        flip = (row + col == 255).astype(F32).astype(BF)

        def body(hp, _):
            lanes = pl.ds(pl.multiple_of(128 * hp, 128), 128)
            biases = [self.bias(2 * hp + e, col <= row) if kind == 1 else 0.0 for e in range(2)]
            rows = [slice(0, 256), slice(256, 512)]
            both = [(s, e) for s in range(2) for e in range(2)]
            queries = [q[r, lanes] * BF(score_scale) for r in rows]
            keys, values = [k[r, lanes] for r in rows], [v[r, lanes] for r in rows]
            given = [b["do"][r, lanes] for r in rows]
            kept = [g.astype(F32) * o[r, lanes].astype(F32) for g, r in zip(given, rows)]
            sums = [jnp.sum(kept[s] * (keep if e == 0 else 1.0 - keep), axis=-1, keepdims=True) for s, e in both]
            far = [self.far(s, kind) for s in range(2)]
            qe = [queries[s] * masks[e] for s, e in both]
            ge = [given[s] * masks[e] for s, e in both]
            scores = [dot_nt(one, keys[s]) + (biases[e] + far[s]) for one, (s, e) in zip(qe, both)]
            dps = [dot_nt(one, values[s]) for one, (s, e) in zip(ge, both)]
            ps = [self.weights(one) for one in scores]
            dss = [(p * (dp - one)).astype(BF) for p, dp, one in zip(ps, dps, sums)]
            low = [p.astype(BF) for p in ps]
            dv, dk = [], []
            for s in range(2):
                for found, left, right in ((dv, given[s].T, low), (dk, queries[s].T, dss)):
                    halves = [dot_nn(left[64 * e:64 * e + 64], right[2 * s + e]) for e in range(2)]
                    found.append(jnp.concatenate(halves).astype(BF).T)
            dq = [dot_nn(ds, keys[s] * masks[e]) for ds, (s, e) in zip(dss, both)]
            if kind == 1:
                for e in range(2):
                    turned = dot_nn(flip, dss[e]) + dot_nn(flip, dss[2 + e])
                    turned = pltpu.roll(turned, 0, axis=1, stride=1, stride_axis=0)
                    b["small"][pl.ds(2 * hp + e, 1), :] = jnp.sum(turned, axis=0, keepdims=True)
            for s in range(2):
                q[rows[s], lanes] = ((dq[2 * s] + dq[2 * s + 1]) * score_scale).astype(BF)
                k[rows[s], lanes] = dk[s]
                v[rows[s], lanes] = dv[s]
            return 0

        lax.fori_loop(first, last, body, 0)

    def live(self, i):
        row = lax.broadcasted_iota(jnp.int32, (128, 1), 0) + 128 * (i % 2)
        return (row < self.b["lens"][0, i // 2]).astype(F32)

    def cotangent(self):
        b = self.b
        for i in range(4):
            rows = slice(128 * i, 128 * i + 128)
            b["df"][rows] = (b["cot"][rows].astype(F32) * self.live(i)).astype(BF)

    def ffn_act(self, j):
        b = self.b
        for t in range(2):
            cols = slice(384 * t, 384 * t + 384)
            wi = self.wa[INNER_UNIT[j], :, :, :, :, cols].reshape(768, 384)
            wf = self.wf[j, t].reshape(384, 768)
            u = dot_nn(b["n3"][...], wi)
            square = u * u
            th = jnp.tanh(u * (ROOT + (ROOT * CUBE) * square))
            half = 0.5 + 0.5 * th
            b["act"][:, cols] = (u * half).astype(BF)
            slope = half + u * (1.0 - th * th) * (0.5 * ROOT + (1.5 * ROOT * CUBE) * square)
            da = dot_nt(b["df"][...], wf)
            b["du"][:, cols] = (da * slope).astype(BF)

    def ffn_out(self, j):
        b = self.b
        for t in range(3):
            cols = slice(256 * t, 256 * t + 256)
            wf = self.wf[j, :, :, :, :, :, cols].reshape(768, 256)
            b["y"][:, cols] += dot_nn(b["act"][...], wf)

    def ffn_back(self, j):
        b = self.b

        def put(tile, value):
            if j == 0:
                b["dn"][:, tile] = value
            else:
                b["dn"][:, tile] += value

        self.times_back([(b["du"], INNER_UNIT[j])], put)

    def ffn_grads(self, j):
        b = self.b
        for t in range(2):
            tile = dot_tn(b["act"][:, 384 * t:384 * t + 384], b["df"][...])
            self.wf[j, t] = tile.astype(BF).reshape(2, 2, 2, 48, 768)


SCATTER_ORDER = (4, 5, 6, 7, 3, 2, 1, 0)
WIDE = [f for f in range(8) if SCATTER_ORDERS[f][0] == "a"]
NARROW = [f for f in range(8) if SCATTER_ORDERS[f][0] == "c"]


def layer_kernel(program, lens, mem_lens, *refs):
    ins, outs, rest = refs[:13], refs[13:19], refs[19:]
    locals_in, locals_out, (in_sem, out_sem), rest = rest[:9], list(rest[9:13]), rest[13:15], rest[15:]
    masters, du = rest[0], rest[15]
    locals_out = [du, *locals_out[:2], masters, *locals_out[2:]]
    qk, value, output, inner = ins[3:7]
    units = [qk.at[0], qk.at[1], value.at[0], output.at[0], qk.at[3], value.at[1], qk.at[2], output.at[1]]
    units += [inner.at[:, 768 * j:768 * j + 768] for j in (0, 3, 1, 2)]
    pairs = [*zip((*ins[:3], *ins[7:]), locals_in), *((unit, masters.at[u // 2, u % 2]) for u, unit in enumerate(units))]
    fetch = [pltpu.make_async_copy(a, b, in_sem.at[i]) for i, (a, b) in enumerate(pairs)]
    store = [pltpu.make_async_copy(a, b, out_sem.at[i]) for i, (a, b) in enumerate(zip(locals_out, outs))]
    send_out = [pltpu.make_async_copy(masters.at[f], outs[3].at[f], out_sem.at[6 + f]) for f in range(PAIRS)]
    layer_body(program, lens, mem_lens, fetch, store, send_out, *locals_in, *locals_out[1:3], *locals_out[4:], *rest)


def layer_body(
    program, lens, mem_lens, fetch, store, send_out,
    hid, mem, cot, outer, gain_in, table, spread, owner, near,
    hidden_grad, memory_grad, last, small_out, masters,
    wa, wf, n1, q1, k1, v1, o1, n2, q2, k2, v2, o2, n3, act, du, df, x1, x2, dn,
    rd, rq, rlw, rrw, rpw, rln, rrn, rpn, fin, tiles, gain, bias_row, small, small_got, along,
    gs, gr, ss, sr, xs, xr, ks, kr, ms, mr, credit,
):
    k = Place(wa, wf)
    z, y, x, c = k.z, k.y, k.x, k.c
    b = dict(
        lens=lens, mem_lens=mem_lens, hid=hid, mem=mem, cot=cot, bias_row=bias_row, gain=gain, small=small.at[0],
        n1=n1, q1=q1, k1=k1, v1=v1, o1=o1, n2=n2, q2=q2, k2=k2, v2=v2, o2=o2, n3=n3,
        act=act, du=du, df=df, do=act, y=memory_grad, dn=dn,
    )
    net = Layer(wa, wf, b)
    gathers = [Gather(k, f, gs, gr) for f in range(8)]
    scatters = {}
    for i, f in enumerate(SCATTER_ORDER):
        if f in WIDE:
            n = WIDE.index(f)
            slots = (rd.at[i % 4], rq.at[f], rpw.at[n], rlw.at[n], rrw.at[n])
        else:
            n = NARROW.index(f)
            slots = (rd.at[i % 4], rq.at[f], rpn.at[n], rln.at[n], rrn.at[n])
        final = fin.at[f] if f < PAIRS else last.at[f - PAIRS]
        scatters[f] = Scatter(k, f, ss, sr, slots, final, masters, (i >= 4, i < 4, credit.at[i % 4]))
    gains = Gains(k, tiles, ks, kr)
    sums = Small(k, small, small_got, along, ms, mr)
    mine = pl.ds(pl.multiple_of(24 * c, 8), 24)
    other = pl.ds(pl.multiple_of(24 - 24 * c, 8), 24)

    def enter():
        for i in (4, *range(9, 21), 3, 5, 8, 0, 1, 2, 6, 7):
            fetch[i].start()
        k.enter(False)
        for i in (4, *range(9, 21)):
            fetch[i].wait()
        tiles[z, y, x, c] = jnp.zeros((8, 128), F32)
        tiles[z, y, x, c, 0:3, 0:24] = gain_in[...].astype(BF).astype(F32)
        k.enter(True)
        push(k, masters.at[:, 1 - c], fin.at[:, mine], xs, xr, "c")
        gains.go(0)
        fetch[3].wait()
        for h in range(2):
            wf[z, y, x, c, h] = outer[48 * h:48 * h + 48].astype(BF)
        for p in range(PAIRS):
            fin[p, mine] = masters[p, c]

    def swap():
        got(k, fin.at[:, other], xr, "c")
        left_out(k, masters.at[:, 1 - c], xs, "c")

    def own(f):
        if f < PAIRS:
            wa[2 * f + c, z, y, x] = fin[f].astype(BF)
        gathers[f].start()

    def spread_gains():
        for i in (0, 5, 6, 7, 8):
            fetch[i].wait()
        bias_row[...] = jnp.zeros_like(bias_row)
        bias_row[0:HEADS, :] = lax.dot_general(
            table[...], near[...], (((1,), (0,)), ((), ())), precision=highest, preferred_element_type=F32
        )
        flat = tiles[...].reshape(32, 8, 128)
        for g in range(3):
            lanes = dot_nn(flat[:, g].astype(BF), spread[...])
            gain[g:g + 1, :] = jnp.sum(lanes * owner[...], axis=0, keepdims=True)

    def put_do(tile, value):
        act[:, tile] = value.astype(BF)

    def put_dn(tile, value):
        dn[:, tile] = value

    def add_dn(tile, value):
        dn[:, tile] += value

    def put_memory(tile, value):
        memory_grad[:, tile] = value

    def add_memory(tile, value):
        memory_grad[:, tile] += value

    def begin():
        fetch[2].wait()
        memory_grad[...] = x2[...]
        small[0] = jnp.zeros_like(small[0])
        net.cotangent()

    def finish_low():
        du[...] = memory_grad[...].astype(BF)
        store[0].start()

    def total_small():
        small_out[...] = along[0] + along[1] + along[2] + along[3]
        store[5].start()

    def finish_memory():
        net.times_back([(v2, 5)], add_memory)
        store[2].start()

    def finish_hidden():
        net.norm_back(dn, hid, 0, lambda rows, i: grad[rows], grad, None)
        store[1].start()

    grad = hidden_grad
    tasks = {
        "gain": spread_gains,
        "n1": lambda: net.norm(hid, 0, n1),
        "q1": lambda: net.project(n1, 0, q1),
        "k1": lambda: net.project(n1, 1, k1),
        "v1": lambda: net.project(n1, 2, v1),
        "o1": lambda: net.add_project(hid, o1, 3, x1),
        "n2": lambda: net.norm(x1, 1, n2),
        "memory": lambda: fetch[1].wait(),
        "k2": lambda: net.project(mem, 4, k2),
        "v2": lambda: net.project(mem, 5, v2),
        "q2": lambda: net.project(n2, 6, q2),
        "o2": lambda: net.add_project(x1, o2, 7, x2),
        "n3": lambda: net.norm(x2, 2, n3),
        "begin": begin,
        "low": finish_low,
        "nb3": lambda: net.norm_back(dn, x2, 2, lambda rows, i: cot[rows].astype(F32) * net.live(i), grad, df),
        "do2": lambda: net.times_back([(df, 7)], put_do),
        "w7": lambda: net.weight_grad(o2, df, 7),
        "dn2": lambda: net.times_back([(q2, 6)], put_dn),
        "w6": lambda: net.weight_grad(n2, q2, 6),
        "mk": lambda: net.times_back([(k2, 4)], put_memory),
        "mv": finish_memory,
        "w4": lambda: net.weight_grad(mem, k2, 4),
        "w5": lambda: net.weight_grad(mem, v2, 5),
        "nb2": lambda: net.norm_back(dn, x1, 1, lambda rows, i: grad[rows], grad, df),
        "do1": lambda: net.times_back([(df, 3)], put_do),
        "w3": lambda: net.weight_grad(o1, df, 3),
        "dv1": lambda: net.times_back([(v1, 2)], put_dn),
        "dk1": lambda: net.times_back([(k1, 1)], add_dn),
        "dq1": lambda: net.times_back([(q1, 0)], add_dn),
        "w0": lambda: net.weight_grad(n1, q1, 0),
        "w1": lambda: net.weight_grad(n1, k1, 1),
        "w2": lambda: net.weight_grad(n1, v1, 2),
        "nb1": finish_hidden,
    }
    families = {
        "act": net.ffn_act, "out": net.ffn_out, "back": net.ffn_back, "grads": net.ffn_grads,
        "W": lambda j: net.weight_grad(n3, du, INNER_UNIT[j]),
        "A1": lambda i: net.attend(1, 2 * i, 2 * i + 2),
        "A2": lambda i: net.attend(2, 2 * i, 2 * i + 2),
        "B1": lambda i: net.attend_back(1, i, i + 1),
        "B2": lambda i: net.attend_back(2, i, i + 1),
    }
    enter()
    for kind, index, name in program:
        if kind == "G":
            if name == "own":
                own(index)
            else:
                gathers[index].do(name)
        elif kind == "S":
            scatters[index].do(name)
            if name == "finish":
                send_out[index].start()
        elif kind == "K":
            gains.go(index)
        elif kind == "R":
            if index < 7:
                sums.go(index)
            else:
                total_small()
        elif kind == "X":
            swap()
        elif name in tasks:
            tasks[name]()
        else:
            families[name](index)
    store[4].start()
    gains.drain()
    sums.drain()
    for f in SCATTER_ORDER:
        scatters[f].drain()
    for copy in (*store[:3], *store[4:], *send_out):
        copy.wait()


def run_layer(program, *operands):
    far, sm = pl.BlockSpec(memory_space=pltpu.HBM), pl.BlockSpec(memory_space=pltpu.SMEM)
    low, wide = pltpu.VMEM((512, 768), BF), pltpu.VMEM((512, 768), F32)
    dma = pltpu.SemaphoreType.DMA
    shape = jax.ShapeDtypeStruct
    outs = (
        shape((512, 768), BF), shape((512, 768), F32), shape((512, 768), F32),
        shape((6, 2, 24, 768), F32), shape((2, 48, 768), F32), shape((24, 256), F32),
    )
    return pl.pallas_call(
        functools.partial(layer_kernel, program),
        out_shape=outs,
        in_specs=[sm] * 2 + [far] * (len(operands) - 2),
        out_specs=[far] * 6,
        scratch_shapes=[
            *[pltpu.VMEM(a.shape, a.dtype) for a in (*operands[2:5], *operands[9:])],
            *[pltpu.VMEM(outs[i].shape, outs[i].dtype) for i in (1, 2, 4, 5)],
            dma((21,)), dma((12,)),
            pltpu.VMEM((6, 2, 24, 768), F32),
            pltpu.VMEM((12, 4, 2, 2, 48, 768), BF),
            pltpu.VMEM((4, 2, 2, 2, 2, 48, 768), BF),
            *[low] * 14, *[wide] * 3,
            pltpu.VMEM((4, 4, 2, 2, 48, 768), BF),
            pltpu.VMEM((8, 4, 2, 48, 768), BF),
            pltpu.VMEM((max(len(WIDE), 1), 3, 2, 48, 768), BF),
            pltpu.VMEM((max(len(WIDE), 1), 3, 2, 48, 768), BF),
            pltpu.VMEM((max(len(WIDE), 1), 48, 768), BF),
            pltpu.VMEM((max(len(NARROW), 1), 3, 48, 768), BF),
            pltpu.VMEM((max(len(NARROW), 1), 3, 48, 768), BF),
            pltpu.VMEM((max(len(NARROW), 1), 4, 48, 768), BF),
            pltpu.VMEM((6, 48, 768), F32),
            pltpu.VMEM((4, 2, 2, 2, 8, 128), F32),
            pltpu.VMEM((8, 768), F32),
            pltpu.VMEM((16, 256), F32),
            pltpu.VMEM((3, 24, 256), F32),
            pltpu.VMEM((3, 24, 256), F32),
            pltpu.VMEM((4, 24, 256), F32),
            dma((8, 5)), dma((8, 9)), dma((8, 16)), dma((8, 16)), dma, dma,
            dma((9,)), dma((9,)), dma((9,)), dma((9,)),
            pltpu.SemaphoreType.REGULAR((4,)),
        ],
        compiler_params=pltpu.CompilerParams(
            collective_id=0, has_side_effects=True, vmem_limit_bytes=63 * 2**20
        ),
    )(*operands)


def bucket_rows(length):
    distance = np.arange(length)
    exact_range = BUCKETS // 2
    safe = np.maximum(distance, 1).astype(np.float32)
    spread = np.log(safe / np.float32(exact_range)) / np.float32(math.log(MAX_DIST / exact_range))
    spread = (spread * np.float32(BUCKETS - exact_range)).astype(np.int32)
    bucket = np.where(distance < exact_range, distance, np.minimum(exact_range + spread, BUCKETS - 1))
    return (bucket[None, :] == np.arange(BUCKETS)[:, None]).astype(np.float32)


def adam_lean(master, first_moment, second_moment, gradient, rate, decay):
    first_next = beta_first * first_moment + (1.0 - beta_first) * gradient
    second_next = beta_second * second_moment + ((1.0 - beta_second) * gradient) * gradient
    root = jnp.sqrt(second_next * (1.0 / (1.0 - beta_second**STEP))) + adam_epsilon
    step = first_next * (rate / (1.0 - beta_first**STEP)) / root
    return ((1.0 - rate * decay) * master - step, first_next, second_next)


def adam_kernel(*refs):
    passed, ins, out_passed, outs, rest = refs[:3], refs[3:28], refs[28:31], refs[31:59], refs[59:]
    local, local_out, through, sems = rest[:25], rest[25:53], rest[53:56], rest[56]
    copies = [pltpu.make_async_copy(a, b, sems.at[0, i]) for i, (a, b) in enumerate(zip(ins, local))]
    inward = [pltpu.make_async_copy(a, b, sems.at[1, i]) for i, (a, b) in enumerate(zip(passed, through))]
    onward = [pltpu.make_async_copy(a, b, sems.at[1, 3 + i]) for i, (a, b) in enumerate(zip(through, out_passed))]
    store = [pltpu.make_async_copy(a, b, sems.at[2, i]) for i, (a, b) in enumerate(zip(local_out, outs))]
    order = (0, 1, 2, 3, *(j * 7 + i + 4 for i in range(7) for j in range(3)))
    for copy in inward:
        copy.start()
    for i in order:
        copies[i].start()
    for one, two in zip(inward, onward):
        one.wait()
        two.start()
    res, last, small, reverse = local[:4]
    masters, firsts, seconds = local[4:11], local[11:18], local[18:25]
    device = lax.axis_index("dp") * 4 + lax.axis_index("fsdp")

    def update(i, at, grad):
        small_one = i > 4
        new, first, second = adam_lean(
            masters[i][at], firsts[i][at], seconds[i][at], grad,
            rate_small if small_one else rate_matrix, 0.0 if small_one else weight_decay,
        )
        local_out[i][at] = new
        local_out[7 + i][at] = first
        local_out[14 + i][at] = second
        local_out[21 + i][at] = new.astype(BF)

    def arrive(i):
        for j in range(3):
            copies[4 + 7 * j + i].wait()

    def leave(i):
        for j in range(4):
            store[7 * j + i].start()

    for i in range(4):
        copies[i].wait()
    where = (((0, 0), (1, 1), (2, 6), (3, 4)), ((0, 2), (1, 5)), ((0, 3), (1, 7)))
    for i, pairs in enumerate(where):
        arrive(i)
        for at, u in pairs:
            update(i, at, res[u])
        leave(i)
    arrive(3)
    for j in range(4):
        update(3, (slice(None), slice(768 * j, 768 * j + 768)), res[INNER_UNIT[j]])
    leave(3)
    arrive(4)
    for h in range(2):
        update(4, (slice(48 * h, 48 * h + 48), slice(None)), last[h])
    leave(4)
    arrive(5)
    place = lax.broadcasted_iota(jnp.int32, (256, 24), 0) - lax.broadcasted_iota(jnp.int32, (256, 24), 1)
    for g in range(3):
        total = jnp.zeros((8, 24), F32)
        for i in range(3):
            mine = (place + 256 * i == 24 * device).astype(F32)
            rows = jnp.broadcast_to(small[12 + 3 * g + i:13 + 3 * g + i, :], (8, 256))
            total = total + lax.dot_general(
                rows, mine, (((1,), (0,)), ((), ())), precision=highest, preferred_element_type=F32
            )
        update(5, (slice(g, g + 1), slice(None)), total[0:1])
    leave(5)
    arrive(6)
    table_grad = lax.dot_general(
        small[0:16, :], reverse[...], (((1,), (1,)), ((), ())), precision=highest, preferred_element_type=F32
    )
    update(6, (slice(None), slice(None)), table_grad[:HEADS])
    leave(6)
    for copy in (*store, *onward):
        copy.wait()


def run_adam(*operands):
    far = pl.BlockSpec(memory_space=pltpu.HBM)
    shapes = [jax.ShapeDtypeStruct(a.shape, a.dtype) for a in operands]
    masters = shapes[7:14]
    outs = (*masters * 3, *[jax.ShapeDtypeStruct(a.shape, BF) for a in masters])
    return pl.pallas_call(
        adam_kernel,
        out_shape=(*shapes[:3], *outs),
        in_specs=[far] * len(operands),
        out_specs=[far] * 31,
        scratch_shapes=[
            *[pltpu.VMEM(a.shape, a.dtype) for a in (*shapes[3:], *outs, *shapes[:3])],
            pltpu.SemaphoreType.DMA((3, 28)),
        ],
        compiler_params=pltpu.CompilerParams(vmem_limit_bytes=60 * 2**20),
    )(*operands)


SCHEDULE = (
    "G7own", "G6own", "X0", "G1own", "G2own", "K1", "G5own", "G3own", "G4own", "G0own", "G6L1", "G6R1", "K2",
    "G2L1", "G2R1", "G3L1", "G3R1", "G0cross", "G2L2", "G6L2", "G6R2", "G2R2", "G3L2", "K3", "G3R2",
    "G1cross", "G4cross", "G6R3", "G0L1", "G2L3", "G6L3", "G0R1", "G3L3", "G2R3", "G7cross", "K4", "G3R3",
    "G2cross", "G3cross", "G0R2", "K5", "G0R3", "G1R1", "G0L2", "G0L3", "G1L1", "G6cross", "G1L2", "G1R2",
    "G3second", "K6", "G2second", "G1L3", "T0gain", "G1R3", "G7L1", "G7R1", "T0memory", "G4R1", "G2finish",
    "G0second", "G3finish", "G3drain", "T0k2", "T0v2", "G4L1", "G2drain", "T0n1", "G7R2", "G0finish",
    "G1second", "G7L2", "T0k1", "T0q1", "G5cross", "G4R2", "G4L2", "G1finish", "T0v1", "T0A1", "T1A1",
    "T2A1", "G7L3", "G7R3", "G6second", "G5R1", "T0o1", "G5L1", "T0n2", "G1drain", "T0q2", "G4L3", "G0drain",
    "T1A2", "G6finish", "G4R3", "G6drain", "T2A2", "G7second", "G5L2", "G5R2", "T0A2", "T0o2", "G7finish",
    "G4second", "T0begin", "T0n3", "G5R3", "G7drain", "G5L3", "G4finish", "T0act", "G4drain", "T0out",
    "T0back", "T0grads", "T0W", "G5second", "T3act", "T3back", "T3W", "S4startA", "S4startB", "G5finish",
    "T3out", "T3grads", "S7startA", "S4coreA", "G5drain", "T1act", "S7coreA", "T1back", "T1W", "T1out",
    "T1grads", "S4coreB", "T2act", "T2back", "T2W", "S5startA", "T2out", "S4halfA", "T2grads", "S5coreA",
    "S5startB", "S6startA", "T0low", "T0nb3", "T0do2", "S5coreB", "T5B2", "S4halfB", "S6startB", "S6coreA",
    "S4z1", "T1B2", "S7startB", "T3B2", "T4B2", "S5halfA", "T0B2", "S6coreB", "S4z2", "T2B2", "T0w7", "T0mk",
    "S7coreB", "S6halfA", "T0mv", "S7halfA", "T0dn2", "T0w6", "T0w4", "T0nb2", "S5halfB", "S5z1", "T0do1",
    "S3startA", "T0w5", "S6halfB", "S2startA", "S6z1", "T3B1", "S3coreA", "S2coreA", "T4B1", "S2startB",
    "T5B1", "S3startB", "S5z2", "T0w3", "T2B1", "S2coreB", "S6z2", "S3coreB", "T0B1", "T1B1", "T0dv1",
    "S3halfA", "T0w2", "S7halfB", "T0dq1", "S1startA", "T0dk1", "S2halfA", "T0w1", "T0w0", "S0startA",
    "S3halfB", "S1coreA", "S0startB", "S3z1", "S0coreA", "S2halfB", "S0coreB", "T0nb1", "S1startB",
    "S7crossA", "S7crossB", "S2z1", "S1coreB", "S3z2", "R0", "R1", "S7z1", "S2z2", "S1halfA", "S0halfA",
    "S0halfB", "R2", "S1halfB", "S7z2", "S0crossA", "S4z3", "S6z3", "S1crossA", "S3z3", "R3", "S0crossB",
    "S0z1", "S5z3", "S1crossB", "S1z1", "R4", "S2z3", "S0z2", "S7z3", "S3last", "S1z2", "S2last", "S5last",
    "S6last", "S4last", "S0z3", "R5", "S5finish", "S1z3", "S2finish", "S3finish", "R6", "S0finish", "R7",
    "S4finish", "S1finish",
)


def shards_block(
    hidden, memory, cotangent, target_lengths, memory_lengths,
    qk_master, value_master, output_master, inner_master, outer_master, gain_master, table_master,
    qk_first, value_first, output_first, inner_first, outer_first, gain_first, table_first,
    qk_second, value_second, output_second, inner_second, outer_second, gain_second, table_second,
):
    place = np.arange(768)
    spread = (place[None, :] % 24 == np.arange(128)[:, None]).astype(jnp.bfloat16)
    owner = (place[None, :] // 24 == np.arange(32)[:, None]).astype(np.float32)
    by_distance = bucket_rows(256)
    flat = lambda a: a.reshape(512, 768)
    low_out, hidden_grad, memory_grad, res, last, small = run_layer(
        tuple((s[0], int(s[1]), s[2:]) for s in SCHEDULE), target_lengths.T, memory_lengths.T, flat(hidden), flat(memory), flat(cotangent),
        qk_master, value_master, output_master, inner_master, outer_master, gain_master, table_master.T,
        spread, owner, np.roll(by_distance[:, ::-1], 1, axis=1),
    )
    low_out, hidden_grad, memory_grad, *rest = run_adam(
        low_out, hidden_grad, memory_grad, res.reshape(12, 24, 768), last, small, by_distance[:, ::-1],
        qk_master, value_master, output_master, inner_master, outer_master, gain_master, table_master.T,
        qk_first, value_first, output_first, inner_first, outer_first, gain_first, table_first.T,
        qk_second, value_second, output_second, inner_second, outer_second, gain_second, table_second.T,
    )
    for i in (6, 13, 20, 27):
        rest[i] = rest[i].T
    whole = lambda a: a.reshape(2, 1, 256, 768)
    return whole(low_out), whole(hidden_grad), whole(memory_grad), *rest


def solution(mesh):
    placed = (
        P(None, ("dp", "fsdp"), None, None),
        P(None, ("dp", "fsdp"), None, None),
        P(None, ("dp", "fsdp"), None, None),
        P(None, ("dp", "fsdp")),
        P(None, ("dp", "fsdp")),
        P(None, ("dp", "fsdp"), None),
        P(None, ("dp", "fsdp"), None),
        P(None, ("dp", "fsdp"), None),
        P(("dp", "fsdp"), None),
        P(("dp", "fsdp"), None),
        P(None, ("dp", "fsdp")),
        P(),
        P(None, ("dp", "fsdp"), None),
        P(None, ("dp", "fsdp"), None),
        P(None, ("dp", "fsdp"), None),
        P(("dp", "fsdp"), None),
        P(("dp", "fsdp"), None),
        P(None, ("dp", "fsdp")),
        P(),
        P(None, ("dp", "fsdp"), None),
        P(None, ("dp", "fsdp"), None),
        P(None, ("dp", "fsdp"), None),
        P(("dp", "fsdp"), None),
        P(("dp", "fsdp"), None),
        P(None, ("dp", "fsdp")),
        P(),
    )
    small_slice = dict(mesh.shape) == {"dp": 8, "fsdp": 4}
    return jax.shard_map(
        shards_block if small_slice else shards,
        mesh=mesh,
        in_specs=placed,
        out_specs=(
            P(None, ("dp", "fsdp"), None, None),
            P(None, ("dp", "fsdp"), None, None),
            P(None, ("dp", "fsdp"), None, None),
            P(None, ("dp", "fsdp"), None),
            P(None, ("dp", "fsdp"), None),
            P(None, ("dp", "fsdp"), None),
            P(("dp", "fsdp"), None),
            P(("dp", "fsdp"), None),
            P(None, ("dp", "fsdp")),
            P(),
            P(None, ("dp", "fsdp"), None),
            P(None, ("dp", "fsdp"), None),
            P(None, ("dp", "fsdp"), None),
            P(("dp", "fsdp"), None),
            P(("dp", "fsdp"), None),
            P(None, ("dp", "fsdp")),
            P(),
            P(None, ("dp", "fsdp"), None),
            P(None, ("dp", "fsdp"), None),
            P(None, ("dp", "fsdp"), None),
            P(("dp", "fsdp"), None),
            P(("dp", "fsdp"), None),
            P(None, ("dp", "fsdp")),
            P(),
            P(None, ("dp", "fsdp"), None),
            P(None, ("dp", "fsdp"), None),
            P(None, ("dp", "fsdp"), None),
            P(("dp", "fsdp"), None),
            P(("dp", "fsdp"), None),
            P(None, ("dp", "fsdp")),
            P(),
        ),
        check_vma=False,
    )
```

```python
import functools
import math

import jax
import jax.numpy as jnp
import numpy as np
from jax import lax
from jax.experimental import pallas as pl
from jax.experimental.pallas import tpu as pltpu
from jax.sharding import PartitionSpec as P

HEADS = 12
HEAD_DIM = 64
BUCKETS = 32
MAX_DIST = 128
STEP = 10


epsilon_norm = 1e-06
score_scale = 0.125
masked_score = -1e30
beta_first = 0.9
beta_second = 0.999
adam_epsilon = 1e-08
rate_matrix = 0.15
rate_small = 1.0
weight_decay = 0.01
highest = lax.Precision.HIGHEST


def bucket_onehot(length):
    places = jnp.arange(length, dtype=jnp.int32)
    distance = jnp.maximum(places[:, None] - places[None, :], 0)
    exact_range = BUCKETS // 2
    safe_distance = jnp.maximum(distance, 1).astype(jnp.float32)
    spread = (
        jnp.log(safe_distance / exact_range)
        / math.log(MAX_DIST / exact_range)
        * (BUCKETS - exact_range)
    )
    far_bucket = jnp.minimum(exact_range + spread.astype(jnp.int32), BUCKETS - 1)
    bucket = jnp.where(distance < exact_range, distance, far_bucket)
    labels = jnp.arange(BUCKETS, dtype=jnp.int32)
    return (bucket[None, :, :] == labels[:, None, None]).astype(jnp.float32)


def product(left_side, right_side):
    return jnp.dot(left_side, right_side, preferred_element_type=jnp.float32)


def product_over_rows(left_side, right_side):
    return lax.dot_general(
        left_side, right_side, (((0,), (0,)), ((), ())), preferred_element_type=jnp.float32
    )


def product_transposed(left_side, right_side):
    return lax.dot_general(
        left_side, right_side, (((1,), (1,)), ((), ())), preferred_element_type=jnp.float32
    )


def to_heads(values, sequences):
    return values.reshape(sequences, -1, HEADS, HEAD_DIM)


def normalize(values, gain_row):
    scale_rows = lax.rsqrt(jnp.mean(values * values, axis=-1, keepdims=True) + epsilon_norm)
    unit_rows = values * scale_rows
    return ((unit_rows * gain_row).astype(jnp.bfloat16), unit_rows, scale_rows)


def normalize_back(grad_norm, unit_rows, scale_rows, gain_row):
    gain_grad = jnp.sum(grad_norm * unit_rows, axis=0)
    grad_unit = grad_norm * gain_row
    grad_values = scale_rows * (
        grad_unit - unit_rows * jnp.mean(grad_unit * unit_rows, axis=-1, keepdims=True)
    )
    return (grad_values, gain_grad)


def attend_scores(queries, key_heads, bias_term, allowed):
    scores = (
        jnp.einsum("sihe,sjhe->shij", queries, key_heads, preferred_element_type=jnp.float32)
        * score_scale
        + bias_term
    )
    return jnp.where(allowed, scores, masked_score)


def attend_forward(queries, key_heads, value_heads, bias_term, allowed):
    scores = attend_scores(queries, key_heads, bias_term, allowed)
    row_max = jnp.max(scores, axis=-1, keepdims=True)
    expanded = jnp.exp(scores - row_max)
    row_total = jnp.sum(expanded, axis=-1, keepdims=True)
    weights = (expanded / row_total).astype(jnp.bfloat16)
    mixed_heads = jnp.einsum(
        "shij,sjhe->sihe", weights, value_heads, preferred_element_type=jnp.float32
    )
    return (mixed_heads, row_max + jnp.log(row_total))


def attend_back(queries, key_heads, value_heads, bias_term, allowed, summary, grad_mixed):
    scores = attend_scores(queries, key_heads, bias_term, allowed)
    weights = jnp.exp(scores - summary)
    grad_weights = jnp.einsum(
        "sihe,sjhe->shij", grad_mixed, value_heads, preferred_element_type=jnp.float32
    )
    grad_values = jnp.einsum(
        "shij,sihe->sjhe",
        weights.astype(jnp.bfloat16),
        grad_mixed,
        preferred_element_type=jnp.float32,
    )
    grad_scores = (
        weights * (grad_weights - jnp.sum(weights * grad_weights, axis=-1, keepdims=True))
    ).astype(jnp.bfloat16)
    grad_queries = (
        jnp.einsum("shij,sjhe->sihe", grad_scores, key_heads, preferred_element_type=jnp.float32)
        * score_scale
    )
    grad_keys = (
        jnp.einsum("shij,sihe->sjhe", grad_scores, queries, preferred_element_type=jnp.float32)
        * score_scale
    )
    return (grad_queries, grad_keys, grad_values, grad_scores)


def forward_pass(gathered, bias_heads, hidden_seq, memory_seq, target_len, memory_len):
    qk_full, value_full, output_full, inner_full, outer_full, gain_full = gathered
    gain_rows = gain_full.astype(jnp.float32)
    sequences, length, model_width = hidden_seq.shape
    memory_span = memory_seq.shape[1]
    row_count = sequences * length
    residual = hidden_seq.astype(jnp.float32).reshape(row_count, model_width)
    memory_rows = memory_seq.reshape(sequences * memory_span, model_width)
    places = jnp.arange(length, dtype=jnp.int32)
    self_mask = (places[None, :] <= places[:, None])[None, None] & (
        places[None, None, None, :] < target_len[:, None, None, None]
    )
    memory_places = jnp.arange(memory_span, dtype=jnp.int32)
    cross_mask = (memory_places[None, :] < memory_len[:, None])[:, None, None, :]
    normed_first, unit_first, scale_first = normalize(residual, gain_rows[0])
    query_first = product(normed_first, qk_full[0]).astype(jnp.bfloat16)
    key_first = product(normed_first, qk_full[1]).astype(jnp.bfloat16)
    value_first = product(normed_first, value_full[0]).astype(jnp.bfloat16)
    mixed_first, summary_first = attend_forward(
        to_heads(query_first, sequences),
        to_heads(key_first, sequences),
        to_heads(value_first, sequences),
        bias_heads,
        self_mask,
    )
    mixed_first = mixed_first.reshape(row_count, model_width).astype(jnp.bfloat16)
    first_sum = residual + product(mixed_first, output_full[0])
    normed_second, unit_second, scale_second = normalize(first_sum, gain_rows[1])
    query_second = product(normed_second, qk_full[2]).astype(jnp.bfloat16)
    key_second = product(memory_rows, qk_full[3]).astype(jnp.bfloat16)
    value_second = product(memory_rows, value_full[1]).astype(jnp.bfloat16)
    mixed_second, summary_second = attend_forward(
        to_heads(query_second, sequences),
        to_heads(key_second, sequences),
        to_heads(value_second, sequences),
        0.0,
        cross_mask,
    )
    mixed_second = mixed_second.reshape(row_count, model_width).astype(jnp.bfloat16)
    second_sum = first_sum + product(mixed_second, output_full[1])
    normed_third, unit_third, scale_third = normalize(second_sum, gain_rows[2])
    inner_act = product(normed_third, inner_full)
    activated = jax.nn.gelu(inner_act, approximate=True).astype(jnp.bfloat16)
    produced = (second_sum + product(activated, outer_full)).astype(jnp.bfloat16)
    stored = (
        self_mask,
        cross_mask,
        memory_rows,
        normed_first,
        unit_first,
        scale_first,
        query_first,
        key_first,
        value_first,
        summary_first,
        mixed_first,
        normed_second,
        unit_second,
        scale_second,
        query_second,
        key_second,
        value_second,
        summary_second,
        mixed_second,
        normed_third,
        unit_third,
        scale_third,
        inner_act,
        activated,
    )
    return (stored, produced.reshape(sequences, length, model_width))


def backward_pass(gathered, bias_heads, stored, cotangent_seq, target_len):
    qk_full, value_full, output_full, inner_full, outer_full, gain_full = gathered
    gain_rows = gain_full.astype(jnp.float32)
    (
        self_mask,
        cross_mask,
        memory_rows,
        normed_first,
        unit_first,
        scale_first,
        query_first,
        key_first,
        value_first,
        summary_first,
        mixed_first,
        normed_second,
        unit_second,
        scale_second,
        query_second,
        key_second,
        value_second,
        summary_second,
        mixed_second,
        normed_third,
        unit_third,
        scale_third,
        inner_act,
        activated,
    ) = stored
    sequences, length, model_width = cotangent_seq.shape
    row_count = sequences * length
    places = jnp.arange(length, dtype=jnp.int32)
    live_rows = (places[None, :] < target_len[:, None]).astype(jnp.float32).reshape(row_count, 1)
    grad_out = cotangent_seq.astype(jnp.float32).reshape(row_count, model_width) * live_rows
    branch = grad_out.astype(jnp.bfloat16)
    outer_grad = product_over_rows(activated, branch)
    grad_act = product_transposed(branch, outer_full)
    unused_value, gelu_pull = jax.vjp(
        lambda inputs: jax.nn.gelu(inputs, approximate=True), inner_act
    )
    grad_inner = gelu_pull(grad_act)[0].astype(jnp.bfloat16)
    inner_grad = product_over_rows(normed_third, grad_inner)
    grad_from_third, gain_third = normalize_back(
        product_transposed(grad_inner, inner_full), unit_third, scale_third, gain_rows[2]
    )
    grad_second = grad_out + grad_from_third
    branch = grad_second.astype(jnp.bfloat16)
    output_grad_second = product_over_rows(mixed_second, branch)
    grad_mixed = product_transposed(branch, output_full[1]).astype(jnp.bfloat16)
    grad_query, grad_key, grad_value, unused_scores = attend_back(
        to_heads(query_second, sequences),
        to_heads(key_second, sequences),
        to_heads(value_second, sequences),
        0.0,
        cross_mask,
        summary_second,
        to_heads(grad_mixed, sequences),
    )
    grad_query = grad_query.reshape(row_count, model_width).astype(jnp.bfloat16)
    grad_key = grad_key.reshape(memory_rows.shape[0], model_width).astype(jnp.bfloat16)
    grad_value = grad_value.reshape(memory_rows.shape[0], model_width).astype(jnp.bfloat16)
    qk_grad_two = product_over_rows(normed_second, grad_query)
    qk_grad_three = product_over_rows(memory_rows, grad_key)
    value_grad_one = product_over_rows(memory_rows, grad_value)
    memory_grad = product_transposed(grad_key, qk_full[3]) + product_transposed(
        grad_value, value_full[1]
    )
    grad_from_second, gain_second = normalize_back(
        product_transposed(grad_query, qk_full[2]), unit_second, scale_second, gain_rows[1]
    )
    grad_first = grad_second + grad_from_second
    branch = grad_first.astype(jnp.bfloat16)
    output_grad_first = product_over_rows(mixed_first, branch)
    grad_mixed = product_transposed(branch, output_full[0]).astype(jnp.bfloat16)
    grad_query, grad_key, grad_value, grad_scores = attend_back(
        to_heads(query_first, sequences),
        to_heads(key_first, sequences),
        to_heads(value_first, sequences),
        bias_heads,
        self_mask,
        summary_first,
        to_heads(grad_mixed, sequences),
    )
    grad_query = grad_query.reshape(row_count, model_width).astype(jnp.bfloat16)
    grad_key = grad_key.reshape(row_count, model_width).astype(jnp.bfloat16)
    grad_value = grad_value.reshape(row_count, model_width).astype(jnp.bfloat16)
    qk_grad_zero = product_over_rows(normed_first, grad_query)
    qk_grad_one = product_over_rows(normed_first, grad_key)
    value_grad_zero = product_over_rows(normed_first, grad_value)
    grad_norm = (
        product_transposed(grad_query, qk_full[0])
        + product_transposed(grad_key, qk_full[1])
        + product_transposed(grad_value, value_full[0])
    )
    grad_from_first, gain_first = normalize_back(grad_norm, unit_first, scale_first, gain_rows[0])
    hidden_grad = grad_first + grad_from_first
    score_term = jnp.sum(grad_scores.astype(jnp.float32), axis=0)
    grad_terms = (
        jnp.stack([qk_grad_zero, qk_grad_one, qk_grad_two, qk_grad_three]),
        jnp.stack([value_grad_zero, value_grad_one]),
        jnp.stack([output_grad_first, output_grad_second]),
        inner_grad,
        outer_grad,
        jnp.stack([gain_first, gain_second, gain_third]),
    )
    return (
        grad_terms,
        score_term,
        hidden_grad.reshape(sequences, length, model_width),
        memory_grad.reshape(sequences, -1, model_width),
    )


def adam_step(master, first_moment, second_moment, gradient, rate, decay):
    first_next = beta_first * first_moment + (1.0 - beta_first) * gradient
    second_next = beta_second * second_moment + (1.0 - beta_second) * gradient * gradient
    corrected = (
        first_next
        / (1.0 - beta_first**STEP)
        / (jnp.sqrt(second_next / (1.0 - beta_second**STEP)) + adam_epsilon)
    )
    master_next = master - rate * (corrected + decay * master)
    return (master_next, first_next, second_next)


def shards(
    hidden,
    memory,
    cotangent,
    target_lengths,
    memory_lengths,
    qk_master,
    value_master,
    output_master,
    inner_master,
    outer_master,
    gain_master,
    table_master,
    qk_first,
    value_first,
    output_first,
    inner_first,
    outer_first,
    gain_first,
    table_first,
    qk_second,
    value_second,
    output_second,
    inner_second,
    outer_second,
    gain_second,
    table_second,
):
    micro_count = hidden.shape[0]
    length = hidden.shape[2]
    model_width = hidden.shape[3]
    hidden_units = inner_master.shape[1]
    qk_low = qk_master.astype(jnp.bfloat16)
    value_low = value_master.astype(jnp.bfloat16)
    output_low = output_master.astype(jnp.bfloat16)
    inner_low = inner_master.astype(jnp.bfloat16)
    outer_low = outer_master.astype(jnp.bfloat16)
    gain_low = gain_master.astype(jnp.bfloat16)
    onehot = bucket_onehot(length)
    bias_heads = jnp.einsum("bij,bh->hij", onehot, table_master, precision=highest)
    masters = (qk_master, value_master, output_master, inner_master, outer_master, gain_master)
    totals = (
        jnp.zeros((4, model_width, model_width), jnp.float32),
        jnp.zeros((2, model_width, model_width), jnp.float32),
        jnp.zeros((2, model_width, model_width), jnp.float32),
        jnp.zeros((model_width, hidden_units), jnp.float32),
        jnp.zeros((hidden_units, model_width), jnp.float32),
        jnp.zeros((3, model_width), jnp.float32),
    )
    reduced = tuple((jnp.zeros_like(master) for master in masters))
    score_total = jnp.zeros((HEADS, length, length), jnp.float32)
    produced_list = []
    hidden_list = []
    memory_list = []
    for micro_index in range(micro_count):
        gathered = (
            lax.all_gather(qk_low, ("dp", "fsdp"), axis=1, tiled=True),
            lax.all_gather(value_low, ("dp", "fsdp"), axis=1, tiled=True),
            lax.all_gather(output_low, ("dp", "fsdp"), axis=1, tiled=True),
            lax.all_gather(inner_low, ("dp", "fsdp"), axis=0, tiled=True),
            lax.all_gather(outer_low, ("dp", "fsdp"), axis=0, tiled=True),
            lax.all_gather(gain_low, ("dp", "fsdp"), axis=1, tiled=True),
        )
        stored, produced = forward_pass(
            gathered,
            bias_heads,
            hidden[micro_index],
            memory[micro_index],
            target_lengths[micro_index],
            memory_lengths[micro_index],
        )
        gathered = (
            lax.all_gather(qk_low, ("dp", "fsdp"), axis=1, tiled=True),
            lax.all_gather(value_low, ("dp", "fsdp"), axis=1, tiled=True),
            lax.all_gather(output_low, ("dp", "fsdp"), axis=1, tiled=True),
            lax.all_gather(inner_low, ("dp", "fsdp"), axis=0, tiled=True),
            lax.all_gather(outer_low, ("dp", "fsdp"), axis=0, tiled=True),
            lax.all_gather(gain_low, ("dp", "fsdp"), axis=1, tiled=True),
        )
        grad_terms, score_term, hidden_grad, memory_grad = backward_pass(
            gathered, bias_heads, stored, cotangent[micro_index], target_lengths[micro_index]
        )
        totals = tuple((running + addition for running, addition in zip(totals, grad_terms)))
        score_total = score_total + score_term
        produced_list.append(produced)
        hidden_list.append(hidden_grad)
        memory_list.append(memory_grad)
    reduced = (
        lax.psum_scatter(totals[0], ("dp", "fsdp"), scatter_dimension=1, tiled=True),
        lax.psum_scatter(totals[1], ("dp", "fsdp"), scatter_dimension=1, tiled=True),
        lax.psum_scatter(totals[2], ("dp", "fsdp"), scatter_dimension=1, tiled=True),
        lax.psum_scatter(totals[3], ("dp", "fsdp"), scatter_dimension=0, tiled=True),
        lax.psum_scatter(totals[4], ("dp", "fsdp"), scatter_dimension=0, tiled=True),
        lax.psum_scatter(totals[5], ("dp", "fsdp"), scatter_dimension=1, tiled=True),
    )
    table_grad = jnp.einsum("bij,hij->bh", onehot, score_total, precision=highest)
    table_grad = lax.psum(table_grad, ("dp", "fsdp"))
    all_masters = (
        qk_master,
        value_master,
        output_master,
        inner_master,
        outer_master,
        gain_master,
        table_master,
    )
    firsts = (
        qk_first,
        value_first,
        output_first,
        inner_first,
        outer_first,
        gain_first,
        table_first,
    )
    seconds = (
        qk_second,
        value_second,
        output_second,
        inner_second,
        outer_second,
        gain_second,
        table_second,
    )
    gradients = (reduced[0], reduced[1], reduced[2], reduced[3], reduced[4], reduced[5], table_grad)
    rates = (
        rate_matrix,
        rate_matrix,
        rate_matrix,
        rate_matrix,
        rate_matrix,
        rate_small,
        rate_small,
    )
    decays = (weight_decay, weight_decay, weight_decay, weight_decay, weight_decay, 0.0, 0.0)
    updated = [
        adam_step(
            all_masters[index],
            firsts[index],
            seconds[index],
            gradients[index],
            rates[index],
            decays[index],
        )
        for index in range(7)
    ]
    news = [entry[0] for entry in updated]
    first_news = [entry[1] for entry in updated]
    second_news = [entry[2] for entry in updated]
    copies = [entry.astype(jnp.bfloat16) for entry in news]
    layer_out = jnp.stack(produced_list)
    hidden_out = jnp.stack(hidden_list)
    memory_out = jnp.stack(memory_list)
    return (
        layer_out,
        hidden_out,
        memory_out,
        news[0],
        news[1],
        news[2],
        news[3],
        news[4],
        news[5],
        news[6],
        first_news[0],
        first_news[1],
        first_news[2],
        first_news[3],
        first_news[4],
        first_news[5],
        first_news[6],
        second_news[0],
        second_news[1],
        second_news[2],
        second_news[3],
        second_news[4],
        second_news[5],
        second_news[6],
        copies[0],
        copies[1],
        copies[2],
        copies[3],
        copies[4],
        copies[5],
        copies[6],
    )


MESH = pl.DeviceIdType.MESH
PAIRS = 6
SCATTER_ORDERS = ("cx", "cy", "ax", "ay", "ax", "ay", "ax", "cy")
ORDERS = ("ax", "ay", "cx", "cy", "ax", "ay", "cx", "ay")


class Place:
    def __init__(self, wa, wf):
        self.wa, self.wf = wa, wf
        dp, fs = lax.axis_index("dp"), lax.axis_index("fsdp")
        self.z, self.y = dp // 2, dp % 2
        self.x, self.c = fs // 2, fs % 2
        self.to = {
            "x": (dp, (1 - self.x) * 2 + self.c),
            "y": (self.z * 2 + 1 - self.y, fs),
            "c": (dp, self.x * 2 + 1 - self.c),
            "r": (dp + 2, fs),
            "l": (dp - 2, fs),
        }

    def enter(self, wait):
        bar = pltpu.get_barrier_semaphore()
        inner = (self.z > 0) & (self.z < 3)
        if wait:
            @pl.when(inner)
            def _():
                pl.semaphore_wait(bar, 5)

            @pl.when(jnp.logical_not(inner))
            def _():
                pl.semaphore_wait(bar, 4)

            return

        def greet(way):
            pl.semaphore_signal(bar, inc=1, device_id=self.to[way], device_id_type=MESH)

        for way in ("x", "y", "c"):
            greet(way)

        @pl.when(self.z < 3)
        def _():
            greet("r")

        @pl.when(self.z > 0)
        def _():
            greet("l")

    def pick(self, f, zs, ps, qs, core=None):
        c = self.c if core is None else core
        xs, ys = (ps, qs) if ORDERS[f][1] == "x" else (qs, ps)
        return self.block(f, zs, ys, xs, c)

    def block(self, f, zs, ys, xs, c):
        if f < PAIRS:
            return self.wa.at[2 * f + c, zs, ys, xs]
        return self.wf.at[zs, ys, xs, c, f - PAIRS]

    def own(self, f):
        return (self.x, self.y) if ORDERS[f][1] == "x" else (self.y, self.x)

    def ways(self, f):
        return ("x", "y") if ORDERS[f][1] == "x" else ("y", "x")


def push(place, src, dst, send, recv, way):
    pltpu.make_async_remote_copy(
        src_ref=src, dst_ref=dst, send_sem=send, recv_sem=recv,
        device_id=place.to[way], device_id_type=MESH,
    ).start()


def got(place, ref, sem, way):
    pltpu.make_async_remote_copy(
        src_ref=ref, dst_ref=ref, send_sem=sem, recv_sem=sem,
        device_id=place.to[way], device_id_type=MESH,
    ).wait_recv()


def left_out(place, ref, sem, way):
    pltpu.make_async_remote_copy(
        src_ref=ref, dst_ref=ref, send_sem=sem, recv_sem=sem,
        device_id=place.to[way], device_id_type=MESH,
    ).wait_send()


ALL = slice(None)


class Gather:
    def __init__(self, place, f, send, recv):
        self.k, self.f = place, f
        self.send, self.recv = send, recv
        self.first_cross = ORDERS[f][0] == "a"

    def do(self, name):
        if name[0] in "LR":
            self.step(int(name[1]), name[0])
        else:
            getattr(self, name)()

    def blk(self, zi):
        p, q = self.k.own(self.f)
        return self.k.pick(self.f, zi, ALL if self.first_cross else p, q)

    def move(self, ref, s, r, way):
        push(self.k, ref, ref, self.send.at[self.f, s], self.recv.at[self.f, r], way)

    def start(self):
        p, q = self.k.own(self.f)
        pw, qw = self.k.ways(self.f)
        if self.first_cross:
            self.move(self.k.pick(self.f, self.k.z, p, q), 0, 0, pw)
        else:
            self.spread(self.k.z, 1)

    def cross(self):
        p, q = self.k.own(self.f)
        pw, qw = self.k.ways(self.f)
        if self.first_cross:
            got(self.k, self.k.pick(self.f, self.k.z, 1 - p, q), self.recv.at[self.f, 0], pw)
            self.spread(self.k.z, 1)
        else:
            got(self.k, self.k.pick(self.f, ALL, 1 - p, q), self.recv.at[self.f, 0], pw)
            half = self.k.pick(self.f, ALL, ALL, q)
            self.move(half, 3, 7, qw)
            self.move(half, 4, 8, "c")

    def sideways(self, zi):
        pw, qw = self.k.ways(self.f)
        if self.first_cross:
            self.move(self.blk(zi), 3, 7, qw)
            self.move(self.blk(zi), 4, 8, "c")
        else:
            self.move(self.blk(zi), 0, 0, pw)

    def spread(self, zi, t):
        z = self.k.z

        @pl.when(z < 3)
        def _():
            self.move(self.blk(zi), 1, t, "r")

        @pl.when(z > 0)
        def _():
            self.move(self.blk(zi), 2, 3 + t, "l")

        self.sideways(zi)

    def step(self, t, side):
        z = self.k.z

        if side == "L":
            @pl.when(z >= t)
            def _():
                got(self.k, self.blk(z - t), self.recv.at[self.f, t], "l")

                if t < 3:
                    @pl.when(z < 3)
                    def _():
                        self.move(self.blk(z - t), 1, t + 1, "r")

                self.sideways(z - t)
        else:
            @pl.when(z <= 3 - t)
            def _():
                got(self.k, self.blk(z + t), self.recv.at[self.f, 3 + t], "r")

                if t < 3:
                    @pl.when(z > 0)
                    def _():
                        self.move(self.blk(z + t), 2, 3 + t + 1, "l")

                self.sideways(z + t)

    def second(self):
        p, q = self.k.own(self.f)
        pw, qw = self.k.ways(self.f)
        other = self.k.pick(self.f, ALL, ALL, 1 - q)
        got(self.k, other, self.recv.at[self.f, 7], qw)
        self.move(other, 4, 8, "c")

    def finish(self):
        theirs = self.k.pick(self.f, ALL, ALL, ALL, 1 - self.k.c)
        got(self.k, theirs, self.recv.at[self.f, 8], "c")

    def drain(self):
        p, q = self.k.own(self.f)
        pw, qw = self.k.ways(self.f)
        z, f = self.k.z, self.f
        some = (lambda n: self.k.pick(f, pl.ds(0, n), ALL if self.first_cross else p, q))
        first = self.k.pick(f, z, p, q) if self.first_cross else self.k.pick(f, ALL, p, q)
        left_out(self.k, first, self.send.at[f, 0], pw)
        for n in (1, 2, 3):
            @pl.when(z == n - 1)
            def _():
                left_out(self.k, some(n), self.send.at[f, 1], "r")

            @pl.when(z == 4 - n)
            def _():
                left_out(self.k, some(n), self.send.at[f, 2], "l")
        left_out(self.k, self.k.pick(f, ALL, ALL, q), self.send.at[f, 3], qw)
        left_out(self.k, self.k.pick(f, ALL, ALL, ALL), self.send.at[f, 4], "c")


def add_into(dst, srcs, lead):
    sizes = lead
    count = 1
    for s in sizes:
        count *= s

    for i in range(count):
        idx, rest = [], i
        for s in reversed(sizes):
            idx.append(rest % s)
            rest = rest // s
        idx = tuple(reversed(idx)) or Ellipsis
        if len(srcs) == 1:
            dst[idx] = dst[idx] + srcs[0][idx]
        else:
            total = dst[idx].astype(jnp.float32)
            for src in srcs:
                total = total + src[idx].astype(jnp.float32)
            dst[idx] = total.astype(jnp.bfloat16)


PIECES = (slice(3, 4), slice(0, 1), slice(1, 3))


class Scatter:
    def __init__(self, place, f, send, recv, slots, final, result, credit):
        self.k, self.f = place, f
        self.wait_credit, self.give_credit, self.credit = credit
        self.send, self.recv = send, recv
        self.rd, self.rq, self.rp, self.rl, self.rr = slots
        self.final, self.result = final, result
        self.wide = SCATTER_ORDERS[f][0] == "a"

    def do(self, name):
        if name[0] == "z":
            self.step_in(int(name[1]))
        elif name[-1] in "AB":
            getattr(self, name[:-1])((0, 1) if name[-1] == "A" else (2,))
        else:
            getattr(self, name)()

    def pick(self, zs, ps, qs, core=None):
        c = self.k.c if core is None else core
        xs, ys = (ps, qs) if SCATTER_ORDERS[self.f][1] == "x" else (qs, ps)
        return self.k.block(self.f, zs, ys, xs, c)

    def own(self):
        return (self.k.x, self.k.y) if SCATTER_ORDERS[self.f][1] == "x" else (self.k.y, self.k.x)

    def ways(self):
        return ("x", "y") if SCATTER_ORDERS[self.f][1] == "x" else ("y", "x")

    def move(self, src, dst, s, way):
        push(self.k, src, dst, self.send.at[self.f, s], self.recv.at[self.f, s], way)

    def blk(self, zi):
        p, q = self.own()
        return self.pick(zi, ALL if self.wide else p, q)

    def start(self, pieces):
        if self.wait_credit and 0 in pieces:
            pl.semaphore_wait(self.credit, 1)
        for i in pieces:
            self.move(self.pick(PIECES[i], ALL, ALL, 1 - self.k.c), self.rd.at[PIECES[i]], i, "c")

    def rpick(self, zs, ps, qs):
        xs, ys = (ps, qs) if SCATTER_ORDERS[self.f][1] == "x" else (qs, ps)
        return self.rd.at[zs, ys, xs]

    def core(self, pieces):
        p, q = self.own()
        pw, qw = self.ways()
        for i in pieces:
            zs = PIECES[i]
            n = zs.stop - zs.start
            got(self.k, self.rd.at[zs], self.recv.at[self.f, i], "c")
            away = self.pick(zs, ALL, 1 - q)
            add_into(away, [self.rpick(zs, ALL, 1 - q)], (n, 2))
            self.move(away, self.rq.at[zs], 3 + i, qw)

    def half(self, pieces):
        p, q = self.own()
        pw, qw = self.ways()
        for i in pieces:
            zs = PIECES[i]
            n = zs.stop - zs.start
            got(self.k, self.rq.at[zs], self.recv.at[self.f, 3 + i], qw)
            add_into(self.pick(zs, ALL, q), [self.rpick(zs, ALL, q), self.rq.at[zs]], (n, 2))
            if not self.wide:
                self.move(self.pick(zs, 1 - p, q), self.rp.at[zs], 6 + i, pw)
        if self.wide and 0 in pieces:
            self.step_out(1)
        if self.give_credit and 2 in pieces:
            pl.semaphore_signal(self.credit, inc=1, device_id=self.k.to["c"], device_id_type=MESH)

    def cross(self, pieces):
        p, q = self.own()
        pw, qw = self.ways()
        for i in pieces:
            zs = PIECES[i]
            n = zs.stop - zs.start
            got(self.k, self.rp.at[zs], self.recv.at[self.f, 6 + i], pw)
            add_into(self.pick(zs, p, q), [self.rp.at[zs]], (n,))
        if 0 in pieces:
            self.step_out(1)

    def step_out(self, t):
        z = self.k.z

        @pl.when(z <= t - 1)
        def _():
            self.move(self.blk(z + 4 - t), self.rl.at[t - 1], 8 + t, "r")

        @pl.when(z >= 4 - t)
        def _():
            self.move(self.blk(z - 4 + t), self.rr.at[t - 1], 11 + t, "l")

    def step_in(self, t):
        z, f = self.k.z, self.f
        lead = (2,) if self.wide else ()

        @pl.when((z >= 1) & (z <= t))
        def _():
            got(self.k, self.rl.at[t - 1], self.recv.at[f, 8 + t], "l")
            add_into(self.blk(z + 3 - t), [self.rl.at[t - 1]], lead)

        @pl.when((z <= 2) & (z >= 3 - t))
        def _():
            got(self.k, self.rr.at[t - 1], self.recv.at[f, 11 + t], "r")
            add_into(self.blk(z - 3 + t), [self.rr.at[t - 1]], lead)

        if t < 3:
            self.step_out(t + 1)
        else:
            p, q = self.own()
            pw, qw = self.ways()
            if self.wide:
                self.move(self.pick(z, 1 - p, q), self.rp, 6, pw)
            else:
                self.total(None)

    def last(self):
        pw, qw = self.ways()
        got(self.k, self.rp, self.recv.at[self.f, 6], pw)
        self.total(self.rp)

    def total(self, more):
        p, q = self.own()
        c = self.k.c
        mine = self.pick(self.k.z, p, q)[...].astype(jnp.float32)
        if more is not None:
            mine = mine + more[...].astype(jnp.float32)
        self.final[...] = mine
        if self.f < PAIRS:
            kept = pl.ds(pl.multiple_of(c * 24, 8), 24)
            away = pl.ds(pl.multiple_of(24 - c * 24, 8), 24)
            self.move(self.final.at[away], self.result.at[self.f, c], 15, "c")
            self.result[self.f, c] = self.final[kept]

    def finish(self):
        if self.f < PAIRS:
            got(self.k, self.result.at[self.f, 1 - self.k.c], self.recv.at[self.f, 15], "c")

    def drain(self):
        pw, qw = self.ways()
        z, f, k = self.k.z, self.f, self.k
        for i, zs in enumerate(PIECES):
            left_out(k, self.rd.at[zs], self.send.at[f, i], "c")
            left_out(k, self.rq.at[zs], self.send.at[f, 3 + i], qw)
            if not self.wide:
                left_out(k, self.rp.at[zs], self.send.at[f, 6 + i], pw)
        if self.wide:
            left_out(k, self.rp, self.send.at[f, 6], pw)
        for t in (1, 2, 3):
            @pl.when(z <= t - 1)
            def _():
                left_out(k, self.rl.at[t - 1], self.send.at[f, 8 + t], "r")

            @pl.when(z >= 4 - t)
            def _():
                left_out(k, self.rr.at[t - 1], self.send.at[f, 11 + t], "l")
        if f < PAIRS:
            left_out(k, self.final.at[pl.ds(0, 24)], self.send.at[f, 15], "c")


class Line:
    def __init__(self, place, buf, send, recv):
        self.k, self.buf, self.send, self.recv = place, buf, send, recv

    def move(self, zi, s, r, way):
        push(self.k, self.buf.at[zi], self.buf.at[zi], self.send.at[s], self.recv.at[r], way)

    def start(self):
        z = self.k.z

        @pl.when(z < 3)
        def _():
            self.move(z, 3, 3, "r")

        @pl.when(z > 0)
        def _():
            self.move(z, 6, 6, "l")

    def step(self, t):
        z = self.k.z

        @pl.when(z >= t)
        def _():
            got(self.k, self.buf.at[z - t], self.recv.at[2 + t], "l")

            if t < 3:
                @pl.when(z < 3)
                def _():
                    self.move(z - t, 3 + t, 3 + t, "r")

        @pl.when(z <= 3 - t)
        def _():
            got(self.k, self.buf.at[z + t], self.recv.at[5 + t], "r")

            if t < 3:
                @pl.when(z > 0)
                def _():
                    self.move(z + t, 6 + t, 6 + t, "l")

    def drain(self):
        z = self.k.z
        for t in range(3):
            @pl.when((z < 3) & (z >= t))
            def _():
                left_out(self.k, self.buf.at[0], self.send.at[3 + t], "r")

            @pl.when((z > 0) & (z <= 3 - t))
            def _():
                left_out(self.k, self.buf.at[0], self.send.at[6 + t], "l")


class Gains:
    def __init__(self, place, buf, send, recv):
        self.k, self.buf, self.send, self.recv = place, buf, send, recv
        self.line = Line(place, buf, send, recv)
        z, y, x, c = place.z, place.y, place.x, place.c
        self.mine = [buf.at[z, y, x, c], buf.at[z, y, x], buf.at[z, y]]
        self.other = [buf.at[z, y, x, 1 - c], buf.at[z, y, 1 - x], buf.at[z, 1 - y]]

    def go(self, i):
        if 1 <= i <= 3:
            got(self.k, self.other[i - 1], self.recv.at[i - 1], "cxy"[i - 1])
        if i < 3:
            push(self.k, self.mine[i], self.mine[i], self.send.at[i], self.recv.at[i], "cxy"[i])
        elif i == 3:
            self.line.start()
        else:
            self.line.step(i - 3)

    def drain(self):
        for i in range(3):
            left_out(self.k, self.mine[i], self.send.at[i], "cxy"[i])
        self.line.drain()


class Small:
    def __init__(self, place, bufs, got_bufs, along, send, recv):
        self.k, self.bufs, self.got_bufs, self.along = place, bufs, got_bufs, along
        self.send, self.recv = send, recv
        self.line = Line(place, along, send, recv)

    def go(self, i):
        if 1 <= i <= 3:
            got(self.k, self.got_bufs.at[i - 1], self.recv.at[i - 1], "cxy"[i - 1])
            total = self.bufs[i - 1] + self.got_bufs[i - 1]
            if i < 3:
                self.bufs[i] = total
            else:
                self.along[self.k.z] = total
        if i < 3:
            push(self.k, self.bufs.at[i], self.got_bufs.at[i], self.send.at[i], self.recv.at[i], "cxy"[i])
        elif i == 3:
            self.line.start()
        else:
            self.line.step(i - 3)

    def drain(self):
        for i in range(3):
            left_out(self.k, self.bufs.at[i], self.send.at[i], "cxy"[i])
        self.line.drain()
BF, F32 = jnp.bfloat16, jnp.float32
INNER_UNIT = (8, 10, 11, 9)
ROOT = math.sqrt(2.0 / math.pi)
CUBE = 0.044715


def dot_nn(a, b):
    return lax.dot_general(a, b, (((1,), (0,)), ((), ())), preferred_element_type=F32)


def dot_nt(a, b):
    return lax.dot_general(a, b, (((1,), (1,)), ((), ())), preferred_element_type=F32)


def dot_tn(a, b):
    return lax.dot_general(a, b, (((0,), (0,)), ((), ())), preferred_element_type=F32)


def unit_of(values):
    scale = lax.rsqrt(jnp.mean(values * values, axis=-1, keepdims=True) + epsilon_norm)
    return values * scale, scale


class Layer:
    def __init__(self, wa, wf, b):
        self.wa, self.wf, self.b = wa, wf, b

    def times(self, a, u, put):
        for t in range(3):
            tile = slice(256 * t, 256 * t + 256)
            put(tile, dot_nn(a[...], self.wa[u, :, :, :, :, tile].reshape(768, 256)))

    def times_back(self, pairs, put):
        total = None
        for a, u in pairs:
            term = dot_nt(a[...], self.wa[u].reshape(768, 768))
            total = term if total is None else total + term
        put(slice(0, 768), total)

    def weight_grad(self, a, d, u):
        for t in range(2):
            tile = dot_tn(a[:, 384 * t:384 * t + 384], d[...])
            self.wa[u, 2 * t:2 * t + 2] = tile.astype(BF).reshape(2, 2, 2, 48, 768)

    def project(self, a, u, dst):
        def put(tile, value):
            dst[:, tile] = value.astype(BF)

        self.times(a, u, put)

    def add_project(self, base, a, u, dst):
        def put(tile, value):
            dst[:, tile] = base[:, tile].astype(F32) + value

        self.times(a, u, put)

    def norm(self, src, g, dst):
        gain = self.b["gain"][pl.ds(g, 1), :]

        for i in range(4):
            rows = slice(128 * i, 128 * i + 128)
            unit, _unused = unit_of(src[rows].astype(F32))
            dst[rows] = (unit * gain).astype(BF)

    def norm_back(self, dn, src, g, base, dst, low):
        gain = self.b["gain"][pl.ds(g, 1), :]

        total = jnp.zeros((1, 768), F32)
        for i in range(4):
            rows = slice(128 * i, 128 * i + 128)
            unit, scale = unit_of(src[rows].astype(F32))
            grad = dn[rows]
            total = total + jnp.sum(grad * unit, axis=0, keepdims=True)
            pulled = grad * gain
            value = base(rows, i) + scale * (pulled - unit * jnp.mean(pulled * unit, axis=-1, keepdims=True))
            dst[rows] = value
            if low is not None:
                low[rows] = value.astype(BF)
        for i in range(3):
            self.b["small"][12 + 3 * g + i:13 + 3 * g + i, :] = total[:, 256 * i:256 * i + 256]

    def head_masks(self):
        lane = lax.broadcasted_iota(jnp.int32, (1, 128), 1)
        low = (lane < 64).astype(F32)
        return low.astype(BF), (1.0 - low).astype(BF)

    def far(self, s, kind):
        col = lax.broadcasted_iota(jnp.int32, (1, 256), 1)
        length = self.b["lens"][0, s] if kind == 1 else self.b["mem_lens"][0, s]
        return jnp.where(col < length, 0.0, masked_score)

    def bias(self, head, causal):
        row = self.b["bias_row"][pl.ds(head, 1), :]
        turned = pltpu.roll(jnp.broadcast_to(row, (256, 256)), 0, axis=1, stride=1, stride_axis=0)
        return jnp.where(causal, turned, masked_score)

    def weights(self, scores):
        expanded = jnp.exp(scores - jnp.max(scores, axis=-1, keepdims=True))
        return expanded * (1.0 / jnp.sum(expanded, axis=-1, keepdims=True))

    def places(self):
        row = lax.broadcasted_iota(jnp.int32, (256, 256), 0)
        col = lax.broadcasted_iota(jnp.int32, (256, 256), 1)
        return row, col

    def attend(self, kind, first, last):
        b = self.b
        q, k, v, o = (b[n + str(kind)] for n in "qkvo")
        masks = self.head_masks()
        keep = masks[0].astype(F32)
        row, col = self.places()

        def body(hp, _):
            lanes = pl.ds(pl.multiple_of(128 * hp, 128), 128)
            biases = [self.bias(2 * hp + e, col <= row) if kind == 1 else 0.0 for e in range(2)]
            rows = [slice(0, 256), slice(256, 512)]
            both = [(s, e) for s in range(2) for e in range(2)]
            queries = [q[r, lanes] * BF(score_scale) for r in rows]
            keys, values = [k[r, lanes] for r in rows], [v[r, lanes] for r in rows]
            far = [self.far(s, kind) for s in range(2)]
            scores = [dot_nt(queries[s] * masks[e], keys[s]) + (biases[e] + far[s]) for s, e in both]
            low = [self.weights(one).astype(BF) for one in scores]
            mixed = [dot_nn(p, values[s]) for p, (s, e) in zip(low, both)]
            for s in range(2):
                o[rows[s], lanes] = (mixed[2 * s] * keep + mixed[2 * s + 1] * (1.0 - keep)).astype(BF)
            return 0

        lax.fori_loop(first, last, body, 0)

    def attend_back(self, kind, first, last):
        b = self.b
        q, k, v, o = (b[n + str(kind)] for n in "qkvo")
        masks = self.head_masks()
        keep = masks[0].astype(F32)
        row, col = self.places()
        flip = (row + col == 255).astype(F32).astype(BF)

        def body(hp, _):
            lanes = pl.ds(pl.multiple_of(128 * hp, 128), 128)
            biases = [self.bias(2 * hp + e, col <= row) if kind == 1 else 0.0 for e in range(2)]
            rows = [slice(0, 256), slice(256, 512)]
            both = [(s, e) for s in range(2) for e in range(2)]
            queries = [q[r, lanes] * BF(score_scale) for r in rows]
            keys, values = [k[r, lanes] for r in rows], [v[r, lanes] for r in rows]
            given = [b["do"][r, lanes] for r in rows]
            kept = [g.astype(F32) * o[r, lanes].astype(F32) for g, r in zip(given, rows)]
            sums = [jnp.sum(kept[s] * (keep if e == 0 else 1.0 - keep), axis=-1, keepdims=True) for s, e in both]
            far = [self.far(s, kind) for s in range(2)]
            qe = [queries[s] * masks[e] for s, e in both]
            ge = [given[s] * masks[e] for s, e in both]
            scores = [dot_nt(one, keys[s]) + (biases[e] + far[s]) for one, (s, e) in zip(qe, both)]
            dps = [dot_nt(one, values[s]) for one, (s, e) in zip(ge, both)]
            ps = [self.weights(one) for one in scores]
            dss = [(p * (dp - one)).astype(BF) for p, dp, one in zip(ps, dps, sums)]
            low = [p.astype(BF) for p in ps]
            dv, dk = [], []
            for s in range(2):
                for found, left, right in ((dv, given[s].T, low), (dk, queries[s].T, dss)):
                    halves = [dot_nn(left[64 * e:64 * e + 64], right[2 * s + e]) for e in range(2)]
                    found.append(jnp.concatenate(halves).astype(BF).T)
            dq = [dot_nn(ds, keys[s] * masks[e]) for ds, (s, e) in zip(dss, both)]
            if kind == 1:
                for e in range(2):
                    turned = dot_nn(flip, dss[e]) + dot_nn(flip, dss[2 + e])
                    turned = pltpu.roll(turned, 0, axis=1, stride=1, stride_axis=0)
                    b["small"][pl.ds(2 * hp + e, 1), :] = jnp.sum(turned, axis=0, keepdims=True)
            for s in range(2):
                q[rows[s], lanes] = ((dq[2 * s] + dq[2 * s + 1]) * score_scale).astype(BF)
                k[rows[s], lanes] = dk[s]
                v[rows[s], lanes] = dv[s]
            return 0

        lax.fori_loop(first, last, body, 0)

    def live(self, i):
        row = lax.broadcasted_iota(jnp.int32, (128, 1), 0) + 128 * (i % 2)
        return (row < self.b["lens"][0, i // 2]).astype(F32)

    def cotangent(self):
        b = self.b
        for i in range(4):
            rows = slice(128 * i, 128 * i + 128)
            b["df"][rows] = (b["cot"][rows].astype(F32) * self.live(i)).astype(BF)

    def ffn_act(self, j):
        b = self.b
        for t in range(2):
            cols = slice(384 * t, 384 * t + 384)
            wi = self.wa[INNER_UNIT[j], :, :, :, :, cols].reshape(768, 384)
            wf = self.wf[j, t].reshape(384, 768)
            u = dot_nn(b["n3"][...], wi)
            square = u * u
            th = jnp.tanh(u * (ROOT + (ROOT * CUBE) * square))
            half = 0.5 + 0.5 * th
            b["act"][:, cols] = (u * half).astype(BF)
            slope = half + u * (1.0 - th * th) * (0.5 * ROOT + (1.5 * ROOT * CUBE) * square)
            da = dot_nt(b["df"][...], wf)
            b["du"][:, cols] = (da * slope).astype(BF)

    def ffn_out(self, j):
        b = self.b
        for t in range(3):
            cols = slice(256 * t, 256 * t + 256)
            wf = self.wf[j, :, :, :, :, :, cols].reshape(768, 256)
            b["y"][:, cols] += dot_nn(b["act"][...], wf)

    def ffn_back(self, j):
        b = self.b

        def put(tile, value):
            if j == 0:
                b["dn"][:, tile] = value
            else:
                b["dn"][:, tile] += value

        self.times_back([(b["du"], INNER_UNIT[j])], put)

    def ffn_grads(self, j):
        b = self.b
        for t in range(2):
            tile = dot_tn(b["act"][:, 384 * t:384 * t + 384], b["df"][...])
            self.wf[j, t] = tile.astype(BF).reshape(2, 2, 2, 48, 768)


SCATTER_ORDER = (4, 5, 6, 7, 3, 2, 1, 0)
WIDE = [f for f in range(8) if SCATTER_ORDERS[f][0] == "a"]
NARROW = [f for f in range(8) if SCATTER_ORDERS[f][0] == "c"]


def layer_kernel(program, lens, mem_lens, *refs):
    ins, outs, rest = refs[:13], refs[13:19], refs[19:]
    locals_in, locals_out, (in_sem, out_sem), rest = rest[:9], list(rest[9:13]), rest[13:15], rest[15:]
    masters, du = rest[0], rest[15]
    locals_out = [du, *locals_out[:2], masters, *locals_out[2:]]
    qk, value, output, inner = ins[3:7]
    units = [qk.at[0], qk.at[1], value.at[0], output.at[0], qk.at[3], value.at[1], qk.at[2], output.at[1]]
    units += [inner.at[:, 768 * j:768 * j + 768] for j in (0, 3, 1, 2)]
    pairs = [*zip((*ins[:3], *ins[7:]), locals_in), *((unit, masters.at[u // 2, u % 2]) for u, unit in enumerate(units))]
    fetch = [pltpu.make_async_copy(a, b, in_sem.at[i]) for i, (a, b) in enumerate(pairs)]
    store = [pltpu.make_async_copy(a, b, out_sem.at[i]) for i, (a, b) in enumerate(zip(locals_out, outs))]
    send_out = [pltpu.make_async_copy(masters.at[f], outs[3].at[f], out_sem.at[6 + f]) for f in range(PAIRS)]
    layer_body(program, lens, mem_lens, fetch, store, send_out, *locals_in, *locals_out[1:3], *locals_out[4:], *rest)


def layer_body(
    program, lens, mem_lens, fetch, store, send_out,
    hid, mem, cot, outer, gain_in, table, spread, owner, near,
    hidden_grad, memory_grad, last, small_out, masters,
    wa, wf, n1, q1, k1, v1, o1, n2, q2, k2, v2, o2, n3, act, du, df, x1, x2, dn,
    rd, rq, rlw, rrw, rpw, rln, rrn, rpn, fin, tiles, gain, bias_row, small, small_got, along,
    gs, gr, ss, sr, xs, xr, ks, kr, ms, mr, credit,
):
    k = Place(wa, wf)
    z, y, x, c = k.z, k.y, k.x, k.c
    b = dict(
        lens=lens, mem_lens=mem_lens, hid=hid, mem=mem, cot=cot, bias_row=bias_row, gain=gain, small=small.at[0],
        n1=n1, q1=q1, k1=k1, v1=v1, o1=o1, n2=n2, q2=q2, k2=k2, v2=v2, o2=o2, n3=n3,
        act=act, du=du, df=df, do=act, y=memory_grad, dn=dn,
    )
    net = Layer(wa, wf, b)
    gathers = [Gather(k, f, gs, gr) for f in range(8)]
    scatters = {}
    for i, f in enumerate(SCATTER_ORDER):
        if f in WIDE:
            n = WIDE.index(f)
            slots = (rd.at[i % 4], rq.at[f], rpw.at[n], rlw.at[n], rrw.at[n])
        else:
            n = NARROW.index(f)
            slots = (rd.at[i % 4], rq.at[f], rpn.at[n], rln.at[n], rrn.at[n])
        final = fin.at[f] if f < PAIRS else last.at[f - PAIRS]
        scatters[f] = Scatter(k, f, ss, sr, slots, final, masters, (i >= 4, i < 4, credit.at[i % 4]))
    gains = Gains(k, tiles, ks, kr)
    sums = Small(k, small, small_got, along, ms, mr)
    mine = pl.ds(pl.multiple_of(24 * c, 8), 24)
    other = pl.ds(pl.multiple_of(24 - 24 * c, 8), 24)

    def enter():
        for i in (4, *range(9, 21), 3, 5, 8, 0, 1, 2, 6, 7):
            fetch[i].start()
        k.enter(False)
        for i in (4, *range(9, 21)):
            fetch[i].wait()
        tiles[z, y, x, c] = jnp.zeros((8, 128), F32)
        tiles[z, y, x, c, 0:3, 0:24] = gain_in[...].astype(BF).astype(F32)
        k.enter(True)
        push(k, masters.at[:, 1 - c], fin.at[:, mine], xs, xr, "c")
        gains.go(0)
        fetch[3].wait()
        for h in range(2):
            wf[z, y, x, c, h] = outer[48 * h:48 * h + 48].astype(BF)
        for p in range(PAIRS):
            fin[p, mine] = masters[p, c]

    def swap():
        got(k, fin.at[:, other], xr, "c")
        left_out(k, masters.at[:, 1 - c], xs, "c")

    def own(f):
        if f < PAIRS:
            wa[2 * f + c, z, y, x] = fin[f].astype(BF)
        gathers[f].start()

    def spread_gains():
        for i in (0, 5, 6, 7, 8):
            fetch[i].wait()
        bias_row[...] = jnp.zeros_like(bias_row)
        bias_row[0:HEADS, :] = lax.dot_general(
            table[...], near[...], (((1,), (0,)), ((), ())), precision=highest, preferred_element_type=F32
        )
        flat = tiles[...].reshape(32, 8, 128)
        for g in range(3):
            lanes = dot_nn(flat[:, g].astype(BF), spread[...])
            gain[g:g + 1, :] = jnp.sum(lanes * owner[...], axis=0, keepdims=True)

    def put_do(tile, value):
        act[:, tile] = value.astype(BF)

    def put_dn(tile, value):
        dn[:, tile] = value

    def add_dn(tile, value):
        dn[:, tile] += value

    def put_memory(tile, value):
        memory_grad[:, tile] = value

    def add_memory(tile, value):
        memory_grad[:, tile] += value

    def begin():
        fetch[2].wait()
        memory_grad[...] = x2[...]
        small[0] = jnp.zeros_like(small[0])
        net.cotangent()

    def finish_low():
        du[...] = memory_grad[...].astype(BF)
        store[0].start()

    def total_small():
        small_out[...] = along[0] + along[1] + along[2] + along[3]
        store[5].start()

    def finish_memory():
        net.times_back([(v2, 5)], add_memory)
        store[2].start()

    def finish_hidden():
        net.norm_back(dn, hid, 0, lambda rows, i: grad[rows], grad, None)
        store[1].start()

    grad = hidden_grad
    tasks = {
        "gain": spread_gains,
        "n1": lambda: net.norm(hid, 0, n1),
        "q1": lambda: net.project(n1, 0, q1),
        "k1": lambda: net.project(n1, 1, k1),
        "v1": lambda: net.project(n1, 2, v1),
        "o1": lambda: net.add_project(hid, o1, 3, x1),
        "n2": lambda: net.norm(x1, 1, n2),
        "memory": lambda: fetch[1].wait(),
        "k2": lambda: net.project(mem, 4, k2),
        "v2": lambda: net.project(mem, 5, v2),
        "q2": lambda: net.project(n2, 6, q2),
        "o2": lambda: net.add_project(x1, o2, 7, x2),
        "n3": lambda: net.norm(x2, 2, n3),
        "begin": begin,
        "low": finish_low,
        "nb3": lambda: net.norm_back(dn, x2, 2, lambda rows, i: cot[rows].astype(F32) * net.live(i), grad, df),
        "do2": lambda: net.times_back([(df, 7)], put_do),
        "w7": lambda: net.weight_grad(o2, df, 7),
        "dn2": lambda: net.times_back([(q2, 6)], put_dn),
        "w6": lambda: net.weight_grad(n2, q2, 6),
        "mk": lambda: net.times_back([(k2, 4)], put_memory),
        "mv": finish_memory,
        "w4": lambda: net.weight_grad(mem, k2, 4),
        "w5": lambda: net.weight_grad(mem, v2, 5),
        "nb2": lambda: net.norm_back(dn, x1, 1, lambda rows, i: grad[rows], grad, df),
        "do1": lambda: net.times_back([(df, 3)], put_do),
        "w3": lambda: net.weight_grad(o1, df, 3),
        "dv1": lambda: net.times_back([(v1, 2)], put_dn),
        "dk1": lambda: net.times_back([(k1, 1)], add_dn),
        "dq1": lambda: net.times_back([(q1, 0)], add_dn),
        "w0": lambda: net.weight_grad(n1, q1, 0),
        "w1": lambda: net.weight_grad(n1, k1, 1),
        "w2": lambda: net.weight_grad(n1, v1, 2),
        "nb1": finish_hidden,
    }
    families = {
        "act": net.ffn_act, "out": net.ffn_out, "back": net.ffn_back, "grads": net.ffn_grads,
        "W": lambda j: net.weight_grad(n3, du, INNER_UNIT[j]),
        "A1": lambda i: net.attend(1, 2 * i, 2 * i + 2),
        "A2": lambda i: net.attend(2, 2 * i, 2 * i + 2),
        "B1": lambda i: net.attend_back(1, i, i + 1),
        "B2": lambda i: net.attend_back(2, i, i + 1),
    }
    enter()
    for kind, index, name in program:
        if kind == "G":
            if name == "own":
                own(index)
            else:
                gathers[index].do(name)
        elif kind == "S":
            scatters[index].do(name)
            if name == "finish":
                send_out[index].start()
        elif kind == "K":
            gains.go(index)
        elif kind == "R":
            if index < 7:
                sums.go(index)
            else:
                total_small()
        elif kind == "X":
            swap()
        elif name in tasks:
            tasks[name]()
        else:
            families[name](index)
    store[4].start()
    gains.drain()
    sums.drain()
    for f in SCATTER_ORDER:
        scatters[f].drain()
    for copy in (*store[:3], *store[4:], *send_out):
        copy.wait()


def run_layer(program, *operands):
    far, sm = pl.BlockSpec(memory_space=pltpu.HBM), pl.BlockSpec(memory_space=pltpu.SMEM)
    low, wide = pltpu.VMEM((512, 768), BF), pltpu.VMEM((512, 768), F32)
    dma = pltpu.SemaphoreType.DMA
    shape = jax.ShapeDtypeStruct
    outs = (
        shape((512, 768), BF), shape((512, 768), F32), shape((512, 768), F32),
        shape((6, 2, 24, 768), F32), shape((2, 48, 768), F32), shape((24, 256), F32),
    )
    return pl.pallas_call(
        functools.partial(layer_kernel, program),
        out_shape=outs,
        in_specs=[sm] * 2 + [far] * (len(operands) - 2),
        out_specs=[far] * 6,
        scratch_shapes=[
            *[pltpu.VMEM(a.shape, a.dtype) for a in (*operands[2:5], *operands[9:])],
            *[pltpu.VMEM(outs[i].shape, outs[i].dtype) for i in (1, 2, 4, 5)],
            dma((21,)), dma((12,)),
            pltpu.VMEM((6, 2, 24, 768), F32),
            pltpu.VMEM((12, 4, 2, 2, 48, 768), BF),
            pltpu.VMEM((4, 2, 2, 2, 2, 48, 768), BF),
            *[low] * 14, *[wide] * 3,
            pltpu.VMEM((4, 4, 2, 2, 48, 768), BF),
            pltpu.VMEM((8, 4, 2, 48, 768), BF),
            pltpu.VMEM((max(len(WIDE), 1), 3, 2, 48, 768), BF),
            pltpu.VMEM((max(len(WIDE), 1), 3, 2, 48, 768), BF),
            pltpu.VMEM((max(len(WIDE), 1), 48, 768), BF),
            pltpu.VMEM((max(len(NARROW), 1), 3, 48, 768), BF),
            pltpu.VMEM((max(len(NARROW), 1), 3, 48, 768), BF),
            pltpu.VMEM((max(len(NARROW), 1), 4, 48, 768), BF),
            pltpu.VMEM((6, 48, 768), F32),
            pltpu.VMEM((4, 2, 2, 2, 8, 128), F32),
            pltpu.VMEM((8, 768), F32),
            pltpu.VMEM((16, 256), F32),
            pltpu.VMEM((3, 24, 256), F32),
            pltpu.VMEM((3, 24, 256), F32),
            pltpu.VMEM((4, 24, 256), F32),
            dma((8, 5)), dma((8, 9)), dma((8, 16)), dma((8, 16)), dma, dma,
            dma((9,)), dma((9,)), dma((9,)), dma((9,)),
            pltpu.SemaphoreType.REGULAR((4,)),
        ],
        compiler_params=pltpu.CompilerParams(
            collective_id=0, has_side_effects=True, vmem_limit_bytes=63 * 2**20
        ),
    )(*operands)


def bucket_rows(length):
    distance = np.arange(length)
    exact_range = BUCKETS // 2
    safe = np.maximum(distance, 1).astype(np.float32)
    spread = np.log(safe / np.float32(exact_range)) / np.float32(math.log(MAX_DIST / exact_range))
    spread = (spread * np.float32(BUCKETS - exact_range)).astype(np.int32)
    bucket = np.where(distance < exact_range, distance, np.minimum(exact_range + spread, BUCKETS - 1))
    return (bucket[None, :] == np.arange(BUCKETS)[:, None]).astype(np.float32)


def adam_lean(master, first_moment, second_moment, gradient, rate, decay):
    first_next = beta_first * first_moment + (1.0 - beta_first) * gradient
    second_next = beta_second * second_moment + ((1.0 - beta_second) * gradient) * gradient
    root = jnp.sqrt(second_next * (1.0 / (1.0 - beta_second**STEP))) + adam_epsilon
    step = first_next * (rate / (1.0 - beta_first**STEP)) / root
    return ((1.0 - rate * decay) * master - step, first_next, second_next)


def adam_kernel(*refs):
    passed, ins, out_passed, outs, rest = refs[:3], refs[3:28], refs[28:31], refs[31:59], refs[59:]
    local, local_out, through, sems = rest[:25], rest[25:53], rest[53:56], rest[56]
    copies = [pltpu.make_async_copy(a, b, sems.at[0, i]) for i, (a, b) in enumerate(zip(ins, local))]
    inward = [pltpu.make_async_copy(a, b, sems.at[1, i]) for i, (a, b) in enumerate(zip(passed, through))]
    onward = [pltpu.make_async_copy(a, b, sems.at[1, 3 + i]) for i, (a, b) in enumerate(zip(through, out_passed))]
    store = [pltpu.make_async_copy(a, b, sems.at[2, i]) for i, (a, b) in enumerate(zip(local_out, outs))]
    order = (0, 1, 2, 3, *(j * 7 + i + 4 for i in range(7) for j in range(3)))
    for copy in inward:
        copy.start()
    for i in order:
        copies[i].start()
    for one, two in zip(inward, onward):
        one.wait()
        two.start()
    res, last, small, reverse = local[:4]
    masters, firsts, seconds = local[4:11], local[11:18], local[18:25]
    device = lax.axis_index("dp") * 4 + lax.axis_index("fsdp")

    def update(i, at, grad):
        small_one = i > 4
        new, first, second = adam_lean(
            masters[i][at], firsts[i][at], seconds[i][at], grad,
            rate_small if small_one else rate_matrix, 0.0 if small_one else weight_decay,
        )
        local_out[i][at] = new
        local_out[7 + i][at] = first
        local_out[14 + i][at] = second
        local_out[21 + i][at] = new.astype(BF)

    def arrive(i):
        for j in range(3):
            copies[4 + 7 * j + i].wait()

    def leave(i):
        for j in range(4):
            store[7 * j + i].start()

    for i in range(4):
        copies[i].wait()
    where = (((0, 0), (1, 1), (2, 6), (3, 4)), ((0, 2), (1, 5)), ((0, 3), (1, 7)))
    for i, pairs in enumerate(where):
        arrive(i)
        for at, u in pairs:
            update(i, at, res[u])
        leave(i)
    arrive(3)
    for j in range(4):
        update(3, (slice(None), slice(768 * j, 768 * j + 768)), res[INNER_UNIT[j]])
    leave(3)
    arrive(4)
    for h in range(2):
        update(4, (slice(48 * h, 48 * h + 48), slice(None)), last[h])
    leave(4)
    arrive(5)
    place = lax.broadcasted_iota(jnp.int32, (256, 24), 0) - lax.broadcasted_iota(jnp.int32, (256, 24), 1)
    for g in range(3):
        total = jnp.zeros((8, 24), F32)
        for i in range(3):
            mine = (place + 256 * i == 24 * device).astype(F32)
            rows = jnp.broadcast_to(small[12 + 3 * g + i:13 + 3 * g + i, :], (8, 256))
            total = total + lax.dot_general(
                rows, mine, (((1,), (0,)), ((), ())), precision=highest, preferred_element_type=F32
            )
        update(5, (slice(g, g + 1), slice(None)), total[0:1])
    leave(5)
    arrive(6)
    table_grad = lax.dot_general(
        small[0:16, :], reverse[...], (((1,), (1,)), ((), ())), precision=highest, preferred_element_type=F32
    )
    update(6, (slice(None), slice(None)), table_grad[:HEADS])
    leave(6)
    for copy in (*store, *onward):
        copy.wait()


def run_adam(*operands):
    far = pl.BlockSpec(memory_space=pltpu.HBM)
    shapes = [jax.ShapeDtypeStruct(a.shape, a.dtype) for a in operands]
    masters = shapes[7:14]
    outs = (*masters * 3, *[jax.ShapeDtypeStruct(a.shape, BF) for a in masters])
    return pl.pallas_call(
        adam_kernel,
        out_shape=(*shapes[:3], *outs),
        in_specs=[far] * len(operands),
        out_specs=[far] * 31,
        scratch_shapes=[
            *[pltpu.VMEM(a.shape, a.dtype) for a in (*shapes[3:], *outs, *shapes[:3])],
            pltpu.SemaphoreType.DMA((3, 28)),
        ],
        compiler_params=pltpu.CompilerParams(vmem_limit_bytes=60 * 2**20),
    )(*operands)


SCHEDULE = (
    "G7own", "G6own", "X0", "G1own", "G2own", "K1", "G5own", "G3own", "G4own", "G0own", "G6L1", "G6R1", "K2",
    "G2L1", "G2R1", "G3L1", "G3R1", "G0cross", "G2L2", "G6L2", "G6R2", "G2R2", "G3L2", "K3", "G3R2",
    "G1cross", "G4cross", "G6R3", "G0L1", "G2L3", "G6L3", "G0R1", "G3L3", "G2R3", "G7cross", "K4", "G3R3",
    "G2cross", "G3cross", "G0R2", "K5", "G0R3", "G1R1", "G0L2", "G0L3", "G1L1", "G6cross", "G1L2", "G1R2",
    "G3second", "K6", "G2second", "G1L3", "T0gain", "G1R3", "G7L1", "G7R1", "T0memory", "G4R1", "G2finish",
    "G0second", "G3finish", "G3drain", "T0k2", "T0v2", "G4L1", "G2drain", "T0n1", "G7R2", "G0finish",
    "G1second", "G7L2", "T0k1", "T0q1", "G5cross", "G4R2", "G4L2", "G1finish", "T0v1", "T0A1", "T1A1",
    "T2A1", "G7L3", "G7R3", "G6second", "G5R1", "T0o1", "G5L1", "T0n2", "G1drain", "T0q2", "G4L3", "G0drain",
    "T1A2", "G6finish", "G4R3", "G6drain", "T2A2", "G7second", "G5L2", "G5R2", "T0A2", "T0o2", "G7finish",
    "G4second", "T0begin", "T0n3", "G5R3", "G7drain", "G5L3", "G4finish", "T0act", "G4drain", "T0out",
    "T0back", "T0grads", "T0W", "G5second", "T3act", "T3back", "T3W", "S4startA", "S4startB", "G5finish",
    "T3out", "T3grads", "S7startA", "S4coreA", "G5drain", "T1act", "S7coreA", "T1back", "T1W", "T1out",
    "T1grads", "S4coreB", "T2act", "T2back", "T2W", "S5startA", "T2out", "S4halfA", "T2grads", "S5coreA",
    "S5startB", "S6startA", "T0low", "T0nb3", "T0do2", "S5coreB", "T5B2", "S4halfB", "S6startB", "S6coreA",
    "S4z1", "T1B2", "S7startB", "T3B2", "T4B2", "S5halfA", "T0B2", "S6coreB", "S4z2", "T2B2", "T0w7", "T0mk",
    "S7coreB", "S6halfA", "T0mv", "S7halfA", "T0dn2", "T0w6", "T0w4", "T0nb2", "S5halfB", "S5z1", "T0do1",
    "S3startA", "T0w5", "S6halfB", "S2startA", "S6z1", "T3B1", "S3coreA", "S2coreA", "T4B1", "S2startB",
    "T5B1", "S3startB", "S5z2", "T0w3", "T2B1", "S2coreB", "S6z2", "S3coreB", "T0B1", "T1B1", "T0dv1",
    "S3halfA", "T0w2", "S7halfB", "T0dq1", "S1startA", "T0dk1", "S2halfA", "T0w1", "T0w0", "S0startA",
    "S3halfB", "S1coreA", "S0startB", "S3z1", "S0coreA", "S2halfB", "S0coreB", "T0nb1", "S1startB",
    "S7crossA", "S7crossB", "S2z1", "S1coreB", "S3z2", "R0", "R1", "S7z1", "S2z2", "S1halfA", "S0halfA",
    "S0halfB", "R2", "S1halfB", "S7z2", "S0crossA", "S4z3", "S6z3", "S1crossA", "S3z3", "R3", "S0crossB",
    "S0z1", "S5z3", "S1crossB", "S1z1", "R4", "S2z3", "S0z2", "S7z3", "S3last", "S1z2", "S2last", "S5last",
    "S6last", "S4last", "S0z3", "R5", "S5finish", "S1z3", "S2finish", "S3finish", "R6", "S0finish", "R7",
    "S4finish", "S1finish",
)


def shards_block(
    hidden, memory, cotangent, target_lengths, memory_lengths,
    qk_master, value_master, output_master, inner_master, outer_master, gain_master, table_master,
    qk_first, value_first, output_first, inner_first, outer_first, gain_first, table_first,
    qk_second, value_second, output_second, inner_second, outer_second, gain_second, table_second,
):
    place = np.arange(768)
    spread = (place[None, :] % 24 == np.arange(128)[:, None]).astype(jnp.bfloat16)
    owner = (place[None, :] // 24 == np.arange(32)[:, None]).astype(np.float32)
    by_distance = bucket_rows(256)
    flat = lambda a: a.reshape(512, 768)
    low_out, hidden_grad, memory_grad, res, last, small = run_layer(
        tuple((s[0], int(s[1]), s[2:]) for s in SCHEDULE), target_lengths.T, memory_lengths.T, flat(hidden), flat(memory), flat(cotangent),
        qk_master, value_master, output_master, inner_master, outer_master, gain_master, table_master.T,
        spread, owner, np.roll(by_distance[:, ::-1], 1, axis=1),
    )
    low_out, hidden_grad, memory_grad, *rest = run_adam(
        low_out, hidden_grad, memory_grad, res.reshape(12, 24, 768), last, small, by_distance[:, ::-1],
        qk_master, value_master, output_master, inner_master, outer_master, gain_master, table_master.T,
        qk_first, value_first, output_first, inner_first, outer_first, gain_first, table_first.T,
        qk_second, value_second, output_second, inner_second, outer_second, gain_second, table_second.T,
    )
    for i in (6, 13, 20, 27):
        rest[i] = rest[i].T
    whole = lambda a: a.reshape(2, 1, 256, 768)
    return whole(low_out), whole(hidden_grad), whole(memory_grad), *rest


def solution(mesh):
    placed = (
        P(None, ("dp", "fsdp"), None, None),
        P(None, ("dp", "fsdp"), None, None),
        P(None, ("dp", "fsdp"), None, None),
        P(None, ("dp", "fsdp")),
        P(None, ("dp", "fsdp")),
        P(None, ("dp", "fsdp"), None),
        P(None, ("dp", "fsdp"), None),
        P(None, ("dp", "fsdp"), None),
        P(("dp", "fsdp"), None),
        P(("dp", "fsdp"), None),
        P(None, ("dp", "fsdp")),
        P(),
        P(None, ("dp", "fsdp"), None),
        P(None, ("dp", "fsdp"), None),
        P(None, ("dp", "fsdp"), None),
        P(("dp", "fsdp"), None),
        P(("dp", "fsdp"), None),
        P(None, ("dp", "fsdp")),
        P(),
        P(None, ("dp", "fsdp"), None),
        P(None, ("dp", "fsdp"), None),
        P(None, ("dp", "fsdp"), None),
        P(("dp", "fsdp"), None),
        P(("dp", "fsdp"), None),
        P(None, ("dp", "fsdp")),
        P(),
    )
    small_slice = dict(mesh.shape) == {"dp": 8, "fsdp": 4}
    return jax.shard_map(
        shards_block if small_slice else shards,
        mesh=mesh,
        in_specs=placed,
        out_specs=(
            P(None, ("dp", "fsdp"), None, None),
            P(None, ("dp", "fsdp"), None, None),
            P(None, ("dp", "fsdp"), None, None),
            P(None, ("dp", "fsdp"), None),
            P(None, ("dp", "fsdp"), None),
            P(None, ("dp", "fsdp"), None),
            P(("dp", "fsdp"), None),
            P(("dp", "fsdp"), None),
            P(None, ("dp", "fsdp")),
            P(),
            P(None, ("dp", "fsdp"), None),
            P(None, ("dp", "fsdp"), None),
            P(None, ("dp", "fsdp"), None),
            P(("dp", "fsdp"), None),
            P(("dp", "fsdp"), None),
            P(None, ("dp", "fsdp")),
            P(),
            P(None, ("dp", "fsdp"), None),
            P(None, ("dp", "fsdp"), None),
            P(None, ("dp", "fsdp"), None),
            P(("dp", "fsdp"), None),
            P(("dp", "fsdp"), None),
            P(None, ("dp", "fsdp")),
            P(),
            P(None, ("dp", "fsdp"), None),
            P(None, ("dp", "fsdp"), None),
            P(None, ("dp", "fsdp"), None),
            P(("dp", "fsdp"), None),
            P(("dp", "fsdp"), None),
            P(None, ("dp", "fsdp")),
            P(),
        ),
        check_vma=False,
    )
```
